32 devices in a mesh: seq: 4 (over y, x), blk: 8 (over z, core).
Axes of the slice: x: 2, y: 2, z: 4, core: 2. Of those that a mesh axis runs over, the one named last changes fastest.
Arguments:
- tokens: bfloat16 [4, 1536, 768], P('seq', 'blk'), may hold values from -6 to 6
- segment_ids: int32 [4, 1536], P('seq', 'blk'), may hold values from 0 to 63, as said below
- out_grad: bfloat16 [4, 1536, 768], P('seq', 'blk'), may hold values from -6 to 6
- query_key_value_weight: bfloat16 [768, 2304], replicated, may hold values from -0.25 to 0.25
- query_bias: bfloat16 [768], replicated, may hold values from -3 to 3
- value_bias: bfloat16 [768], replicated, may hold values from -3 to 3
- attention_output_weight: bfloat16 [768, 768], replicated, may hold values from -2 to 2
- attention_output_bias: bfloat16 [768], replicated, may hold values from -3 to 3
- first_gain: bfloat16 [768], replicated, may hold values from 0.099609375 to 1.8984375
- first_shift: bfloat16 [768], replicated, may hold values from -1.75 to 1.75
- second_gain: bfloat16 [768], replicated, may hold values from 0.099609375 to 1.8984375
- second_shift: bfloat16 [768], replicated, may hold values from -1.75 to 1.75
- mlp_input_weight: bfloat16 [768, 3072], replicated, may hold values from -0.21875 to 0.21875
- mlp_input_bias: bfloat16 [3072], replicated, may hold values from -3 to 3
- mlp_output_weight: bfloat16 [3072, 768], replicated, may hold values from -0.15625 to 0.15625
- mlp_output_bias: bfloat16 [768], replicated, may hold values from -3 to 3
Outputs:
- layer_out: bfloat16 [4, 1536, 768], P('seq', 'blk')
- tokens_grad: bfloat16 [4, 1536, 768], P('seq', 'blk')
- qkv_weight_grad: float32 [768, 2304], P('blk')
- query_bias_grad: float32 [768], P('blk')
- value_bias_grad: float32 [768], P('blk')
- out_weight_grad: float32 [768, 768], P('blk')
- out_bias_grad: float32 [768], P('blk')
- first_gain_grad: float32 [768], P('blk')
- first_shift_grad: float32 [768], P('blk')
- second_gain_grad: float32 [768], P('blk')
- second_shift_grad: float32 [768], P('blk')
- up_weight_grad: float32 [768, 3072], P('blk')
- up_bias_grad: float32 [3072], P('blk')
- down_weight_grad: float32 [3072, 768], P(None, 'blk')
- down_bias_grad: float32 [768], P('blk')
The draws below stay inside these ranges and needn't reach their ends.
Inputs may be any that keep to these rules, and one draw needn't show every extreme that they name: `segment_ids`: each sequence is a packing of whole images laid end to end (coarse-patch images of 25 to 225 rows and one or two patch-8 images of 900 rows, at least one of these in every sequence), then one or more padding rows numbered 63; images are numbered from 0 in packing order. The packed rows are dealt in turn over blk: row t of the block of index b of blk is packed row t * 8 + b.
All inputs are finite; a program needn't handle non-finite values.
Results may differ from the reference program's by a relative error of at most 0.015.
Values may be sent and summed in bfloat16 or wider, within the bound.
A program may use at most 320 MiB of HBM per device.

```python
import math
from functools import partial
import jax
import jax.numpy as jnp
from jax import lax

D = 768
HEADS = 12
HEAD = 64
FF = 3072
TOK_DEV = 192
SHORT_LO = 25
SHORT_HI = 225
LONG_ROWS = 900
SEQS = 4
SEQ_LEN = 1536
SEG_PAD = 63


def draw_segment_ids(key, part):
    key = jax.random.fold_in(key, 7)
    item_count = SEQ_LEN // SHORT_LO + 1
    block_count = SEQ_LEN // TOK_DEV
    positions = jnp.arange(SEQ_LEN, dtype=jnp.int32)
    item_index = jnp.arange(item_count, dtype=jnp.int32)

    def one_sequence(seq_key):
        parts = jax.random.split(seq_key, 3)
        sizes = jax.random.randint(parts[0], (item_count,), SHORT_LO, SHORT_HI + 1, dtype=jnp.int32)
        first_long = jax.random.randint(parts[1], (), 0, 2, dtype=jnp.int32)
        second_long = first_long + 2 + jax.random.randint(parts[2], (), 0, 5, dtype=jnp.int32)
        is_long = (item_index == first_long) | (item_index == second_long)
        sizes = jnp.where(is_long, jnp.int32(LONG_ROWS), sizes)
        edges = jnp.cumsum(sizes).astype(jnp.int32)
        labels = jnp.sum((positions[:, None] >= edges[None, :]).astype(jnp.int32), axis=1)
        pad_start = jnp.max(jnp.where(edges < SEQ_LEN, edges, 0))
        packed = jnp.where(positions < pad_start, labels, SEG_PAD).astype(jnp.int32)
        order = positions % TOK_DEV * block_count + positions // TOK_DEV
        return packed[order].astype(jnp.int32)
    return jax.vmap(one_sequence)(jax.random.split(key, SEQS))


def raised(values, own_key, source, target, shards_of, factor):
    def block_of(dim):
        return (jnp.arange(values.shape[dim]) // (values.shape[dim] // shards_of)).reshape((-1,) + (1,) * (values.ndim - 1 - dim))

    one_side = jax.random.permutation(own_key, shards_of)[block_of(target)]
    far = (block_of(target) + shards_of // 2) % shards_of
    return jnp.where((block_of(source) == one_side) | (block_of(source) == far), factor * values, values)


def steps_of(own_key, extent, cuts, smallest, largest):
    def one(dim, blocks):
        heights = jax.random.uniform(jax.random.fold_in(jax.random.fold_in(own_key, 6), dim), (blocks,), jnp.float32, smallest / len(cuts), largest / len(cuts))
        return jnp.repeat(jnp.exp(heights), extent[dim] // blocks).reshape((-1,) + (1,) * (len(extent) - dim - 1))

    factor_of = one(*cuts[0])
    for cut in cuts[1:]:
        factor_of = factor_of * one(*cut)
    return factor_of


def normal_values(key, shape, scale, bound, shards=(), kind=jnp.bfloat16):
    entries = scale * jax.random.normal(key, shape, jnp.float32)
    if shards:
        entries = entries * steps_of(key, shape, shards, -0.22, 0.18)
    return jnp.clip(entries, -bound, bound).astype(kind)


def heavy_noise(own_key, extent, width, bound, shards, heavy, held_as=jnp.bfloat16):
    drawn = width * jax.random.normal(own_key, extent, jnp.float32)
    if shards:
        drawn = drawn * steps_of(own_key, extent, shards, -0.22, 0.18)
    return jnp.clip(raised(drawn, jax.random.fold_in(own_key, 3), *heavy), -bound, bound).astype(held_as)


def setup_inputs(seed: int = 0) -> dict:
    keys = jax.random.split(jax.random.key(seed), 17)
    return {
        "tokens": heavy_noise(keys[0], (SEQS, SEQ_LEN, D), 1.0, 6.0, ((0, 4), (1, 8)), (1, 2, 8, 2.0)),
        "segment_ids": draw_segment_ids(jax.random.fold_in(keys[16], 71), 0),
        "out_grad": heavy_noise(keys[2], (SEQS, SEQ_LEN, D), 1.0, 6.0, ((0, 4), (1, 8)), (1, 2, 8, 2.0)),
        "query_key_value_weight": normal_values(keys[3], (D, 3 * D), (D * 2 // 3) ** -0.5, 0.25),
        "query_bias": normal_values(keys[4], (D,), 0.5, 3.0),
        "value_bias": normal_values(keys[5], (D,), 0.5, 3.0),
        "attention_output_weight": normal_values(keys[6], (D, D), (max(D // 96, 1)) ** -0.5, 2.0),
        "attention_output_bias": normal_values(keys[7], (D,), 0.5, 3.0),
        "first_gain": jnp.clip(1.0 + 0.18 * jax.random.normal(keys[8], (D,), jnp.float32), 0.099609375, 1.8984375).astype(jnp.bfloat16),
        "first_shift": normal_values(keys[9], (D,), 0.3, 1.75),
        "second_gain": jnp.clip(1.0 + 0.18 * jax.random.normal(keys[10], (D,), jnp.float32), 0.099609375, 1.8984375).astype(jnp.bfloat16),
        "second_shift": normal_values(keys[11], (D,), 0.3, 1.75),
        "mlp_input_weight": normal_values(keys[12], (D, FF), D ** -0.5, 0.21875),
        "mlp_input_bias": normal_values(keys[13], (FF,), 0.5, 3.0),
        "mlp_output_weight": normal_values(keys[14], (FF, D), (FF // 2) ** -0.5, 0.15625),
        "mlp_output_bias": normal_values(keys[15], (D,), 0.5, 3.0),
    }


@jax.custom_vjp
def low(v):
    return lax.optimization_barrier(v.astype(jnp.bfloat16)).astype(jnp.float32)

@jax.custom_vjp
def reduced_backward(v):
    return v

def low_keep(v):
    return (low(v), None)

def low_pass(kept, grad):
    return (grad,)

def back_keep(v):
    return (v, None)

def back_low(kept, grad):
    return (low(grad),)
low.defvjp(low_keep, low_pass)
reduced_backward.defvjp(back_keep, back_low)
EPS = 1e-06
HIGH_ACCURACY = lax.Precision.HIGHEST

def layer_norm(inputs, norm_gain, norm_shift):
    centre = inputs - lax.optimization_barrier(jnp.mean(inputs, axis=-1, keepdims=True))
    spread = lax.optimization_barrier(jnp.mean(centre * centre, axis=-1, keepdims=True))
    return centre * lax.rsqrt(spread + EPS) * norm_gain + norm_shift

def query_block(key_rows, value_rows, key_segs, score_scale, inputs):
    queries, query_segs = inputs
    raw_scores = reduced_backward(jnp.einsum('qhd,khd->hqk', queries, key_rows, precision=HIGH_ACCURACY))
    same_image = (query_segs[:, None] == key_segs[None, :])[None]
    weights = jnp.where(same_image, jnp.exp(raw_scores * score_scale), 0.0)
    totals = reduced_backward(lax.optimization_barrier(jnp.sum(weights, axis=-1)))
    summed = reduced_backward(jnp.einsum('hqk,khd->qhd', low(weights), value_rows, precision=HIGH_ACCURACY))
    return summed / jnp.transpose(totals)[:, :, None]

def one_sequence(score_scale, inputs):
    queries, key_rows, value_rows, seg_rows = inputs
    length = queries.shape[0]
    block_rows = math.gcd(length, 512)
    query_blocks = queries.reshape(length // block_rows, block_rows, HEADS, HEAD)
    seg_blocks = seg_rows.reshape(length // block_rows, block_rows)
    worker = jax.checkpoint(partial(query_block, key_rows, value_rows, seg_rows, score_scale))
    attended = lax.map(worker, (query_blocks, seg_blocks))
    return attended.reshape(length, HEADS, HEAD)

def forward(segment_ids, tokens, query_key_value_weight, query_bias, value_bias, attention_output_weight, attention_output_bias, first_gain, first_shift, second_gain, second_shift, mlp_input_weight, mlp_input_bias, mlp_output_weight, mlp_output_bias):
    model_width = tokens.shape[-1]
    score_scale = 1.0 / math.sqrt(HEAD)
    live_rows = (segment_ids != SEG_PAD).astype(jnp.float32)[..., None, None]
    first_normed = low(layer_norm(tokens, first_gain, first_shift))
    query_key_value_bias = jnp.concatenate([query_bias, jnp.zeros_like(query_bias), value_bias])
    projected_rows = jnp.einsum('ipf,fh->iph', first_normed, query_key_value_weight, precision=HIGH_ACCURACY) + query_key_value_bias
    head_shape = tokens.shape[:2] + (HEADS, HEAD)
    queries = low(reduced_backward(projected_rows[..., :model_width])).reshape(head_shape)
    key_rows = low(reduced_backward(projected_rows[..., model_width:2 * model_width])).reshape(head_shape)
    value_rows = low(reduced_backward(projected_rows[..., 2 * model_width:])).reshape(head_shape)
    attended = lax.map(partial(one_sequence, score_scale), (queries, key_rows, value_rows, segment_ids))
    merged_heads = low((attended * live_rows).reshape(tokens.shape))
    branch_output = reduced_backward(jnp.einsum('vyn,na->vya', merged_heads, attention_output_weight, precision=HIGH_ACCURACY) + attention_output_bias)
    residual = tokens + branch_output
    second_normed = low(layer_norm(residual, second_gain, second_shift))
    hidden_rows = reduced_backward(jnp.einsum('bjr,re->bje', second_normed, mlp_input_weight, precision=HIGH_ACCURACY) + mlp_input_bias)
    gelu_active = low(jax.nn.gelu(hidden_rows, approximate=False))
    block_result = reduced_backward(jnp.einsum('vci,iz->vcz', gelu_active, mlp_output_weight, precision=HIGH_ACCURACY) + mlp_output_bias)
    return residual + block_result

def reference(tokens, segment_ids, out_grad, query_key_value_weight, query_bias, value_bias, attention_output_weight, attention_output_bias, first_gain, first_shift, second_gain, second_shift, mlp_input_weight, mlp_input_bias, mlp_output_weight, mlp_output_bias):
    floats = (tokens.astype(jnp.float32), query_key_value_weight.astype(jnp.float32), query_bias.astype(jnp.float32), value_bias.astype(jnp.float32), attention_output_weight.astype(jnp.float32), attention_output_bias.astype(jnp.float32), first_gain.astype(jnp.float32), first_shift.astype(jnp.float32), second_gain.astype(jnp.float32), second_shift.astype(jnp.float32), mlp_input_weight.astype(jnp.float32), mlp_input_bias.astype(jnp.float32), mlp_output_weight.astype(jnp.float32), mlp_output_bias.astype(jnp.float32))
    output, pullback = jax.vjp(partial(forward, segment_ids), *floats)
    gradients = pullback(out_grad.astype(jnp.float32))
    return (output.astype(jnp.bfloat16), gradients[0].astype(jnp.bfloat16), gradients[1], gradients[2], gradients[3], gradients[4], gradients[5], gradients[6], gradients[7], gradients[8], gradients[9], gradients[10], gradients[11], gradients[12], gradients[13])
```

```python
import functools
import math

import jax
import jax.numpy as jnp
from jax import lax
from jax.experimental import pallas as pl
from jax.experimental.pallas import tpu as pltpu
from jax.sharding import PartitionSpec as P

HEADS = 12
HEAD = 64
SHORT_LO = 25


EPS = 1e-06


def layer_norm(inputs, norm_gain, norm_shift):
    centre = inputs - jnp.mean(inputs, axis=-1, keepdims=True)
    spread = jnp.mean(centre * centre, axis=-1, keepdims=True)
    return centre * lax.rsqrt(spread + EPS) * norm_gain + norm_shift


def gelu_exact(inputs):
    return jax.nn.gelu(inputs, approximate=False)


def score_block(queries, query_segs, key_rows, key_segs):
    raw_scores = jnp.einsum("qhd,khd->hqk", queries, key_rows, preferred_element_type=jnp.float32)
    same_image = (query_segs[:, None] == key_segs[None, :])[None]
    return jnp.where(same_image, jnp.exp(raw_scores * (1.0 / math.sqrt(HEAD))), 0.0)


def forward_step(carried, queries, query_segs, key_rows, value_rows, key_segs):
    totals, summed = carried
    weights = score_block(queries, query_segs, key_rows, key_segs)
    totals = totals + jnp.transpose(jnp.sum(weights, axis=-1))
    summed = summed + jnp.einsum(
        "hqk,khd->qhd", weights.astype(jnp.bfloat16), value_rows, preferred_element_type=jnp.float32
    )
    return (totals, summed)


def back_step(queries, query_grads, query_corr, query_segs, key_rows, value_rows, key_segs):
    weights = score_block(queries, query_segs, key_rows, key_segs)
    product = jnp.einsum(
        "qhd,khd->hqk", query_grads, value_rows, preferred_element_type=jnp.float32
    )
    shifted = jnp.transpose(query_corr.astype(jnp.float32))[:, :, None]
    score_grads = (weights * (product - shifted) * (1.0 / math.sqrt(HEAD))).astype(jnp.bfloat16)
    return (weights.astype(jnp.bfloat16), score_grads)


def key_value_grads(queries, query_grads, query_corr, query_segs, key_rows, value_rows, key_segs):
    weights_low, score_grads = back_step(
        queries, query_grads, query_corr, query_segs, key_rows, value_rows, key_segs
    )
    key_part = jnp.einsum("hqk,qhd->khd", score_grads, queries, preferred_element_type=jnp.float32)
    value_part = jnp.einsum(
        "hqk,qhd->khd", weights_low, query_grads, preferred_element_type=jnp.float32
    )
    return (key_part, value_part)


def body(
    tokens,
    segment_ids,
    out_grad,
    query_key_value_weight,
    query_bias,
    value_bias,
    attention_output_weight,
    attention_output_bias,
    first_gain,
    first_shift,
    second_gain,
    second_shift,
    mlp_input_weight,
    mlp_input_bias,
    mlp_output_weight,
    mlp_output_bias,
):
    model_width = tokens.shape[-1]
    row_count = tokens.shape[0] * tokens.shape[1]
    head_shape = (row_count, HEADS, HEAD)
    pad_number = tokens.shape[1] * lax.axis_size("blk") // SHORT_LO + 2
    token_rows = tokens.reshape(row_count, model_width).astype(jnp.float32)
    seg_rows = segment_ids.reshape(row_count)
    live_rows = (seg_rows != pad_number).astype(jnp.float32)
    first_normed, first_back = jax.vjp(
        layer_norm, token_rows, first_gain.astype(jnp.float32), first_shift.astype(jnp.float32)
    )
    first_low = first_normed.astype(jnp.bfloat16)
    query_key_value_bias = jnp.concatenate(
        [
            query_bias.astype(jnp.float32),
            jnp.zeros((model_width,), jnp.float32),
            value_bias.astype(jnp.float32),
        ]
    )
    projected_rows = (
        jnp.dot(first_low, query_key_value_weight, preferred_element_type=jnp.float32)
        + query_key_value_bias
    )
    query_flat = projected_rows[:, :model_width].astype(jnp.bfloat16)
    key_flat = projected_rows[:, model_width : 2 * model_width].astype(jnp.bfloat16)
    value_flat = projected_rows[:, 2 * model_width :].astype(jnp.bfloat16)
    queries = query_flat.reshape(head_shape)
    gathered = (
        lax.all_gather(key_flat, "blk", axis=0, tiled=True),
        lax.all_gather(value_flat, "blk", axis=0, tiled=True),
        lax.all_gather(seg_rows, "blk", axis=0, tiled=True),
    )
    all_keys = gathered[0].reshape(-1, HEADS, HEAD)
    all_values = gathered[1].reshape(-1, HEADS, HEAD)
    all_segs = gathered[2]
    seq_rows = all_keys.shape[0]
    key_span = math.gcd(seq_rows, 2048)
    turns = seq_rows // key_span

    def forward_turn(index, carried):
        begin_row = index * key_span
        return forward_step(
            carried,
            queries,
            seg_rows,
            lax.dynamic_slice_in_dim(all_keys, begin_row, key_span, 0),
            lax.dynamic_slice_in_dim(all_values, begin_row, key_span, 0),
            lax.dynamic_slice_in_dim(all_segs, begin_row, key_span, 0),
        )

    totals, summed = lax.fori_loop(
        0,
        turns,
        forward_turn,
        (jnp.zeros((row_count, HEADS), jnp.float32), jnp.zeros(head_shape, jnp.float32)),
    )
    attended = summed / totals[:, :, None] * live_rows[:, None, None]
    merged_heads = attended.reshape(row_count, model_width).astype(jnp.bfloat16)
    residual = (
        token_rows
        + jnp.dot(merged_heads, attention_output_weight, preferred_element_type=jnp.float32)
        + attention_output_bias.astype(jnp.float32)
    )
    second_normed, second_back = jax.vjp(
        layer_norm, residual, second_gain.astype(jnp.float32), second_shift.astype(jnp.float32)
    )
    second_low = second_normed.astype(jnp.bfloat16)
    hidden_rows = jnp.dot(
        second_low, mlp_input_weight, preferred_element_type=jnp.float32
    ) + mlp_input_bias.astype(jnp.float32)
    gelu_active, gelu_back = jax.vjp(gelu_exact, hidden_rows)
    active_low = gelu_active.astype(jnp.bfloat16)
    layer_rows = (
        residual
        + jnp.dot(active_low, mlp_output_weight, preferred_element_type=jnp.float32)
        + mlp_output_bias.astype(jnp.float32)
    )
    layer_out = layer_rows.astype(jnp.bfloat16).reshape(tokens.shape)
    grad_rows = out_grad.reshape(row_count, model_width)
    down_weight_grad = jnp.einsum(
        "tf,td->fd", active_low, grad_rows, preferred_element_type=jnp.float32
    )
    down_bias_grad = jnp.sum(grad_rows.astype(jnp.float32), axis=0)
    active_grad = jnp.einsum(
        "td,fd->tf", grad_rows, mlp_output_weight, preferred_element_type=jnp.float32
    )
    (hidden_grad,) = gelu_back(active_grad)
    hidden_low = hidden_grad.astype(jnp.bfloat16)
    up_weight_grad = jnp.einsum(
        "td,tf->df", second_low, hidden_low, preferred_element_type=jnp.float32
    )
    up_bias_grad = jnp.sum(hidden_low.astype(jnp.float32), axis=0)
    normed_grad = jnp.einsum(
        "tf,df->td", hidden_low, mlp_input_weight, preferred_element_type=jnp.float32
    )
    resid_part, second_gain_grad, second_shift_grad = second_back(normed_grad)
    residual_grad = grad_rows.astype(jnp.float32) + resid_part
    branch_low = residual_grad.astype(jnp.bfloat16)
    out_weight_grad = jnp.einsum(
        "ti,to->io", merged_heads, branch_low, preferred_element_type=jnp.float32
    )
    out_bias_grad = jnp.sum(branch_low.astype(jnp.float32), axis=0)
    attended_grad = (
        jnp.einsum(
            "to,io->ti", branch_low, attention_output_weight, preferred_element_type=jnp.float32
        ).reshape(head_shape)
        * live_rows[:, None, None]
    )
    query_grads = (attended_grad / totals[:, :, None]).astype(jnp.bfloat16)
    corrections = (jnp.sum(attended_grad * attended, axis=-1) / totals).astype(jnp.bfloat16)

    def query_turn(index, carried):
        begin_row = index * key_span
        key_rows = lax.dynamic_slice_in_dim(all_keys, begin_row, key_span, 0)
        weights_low, score_grads = back_step(
            queries,
            query_grads,
            corrections,
            seg_rows,
            key_rows,
            lax.dynamic_slice_in_dim(all_values, begin_row, key_span, 0),
            lax.dynamic_slice_in_dim(all_segs, begin_row, key_span, 0),
        )
        return carried + jnp.einsum(
            "hqk,khd->qhd", score_grads, key_rows, preferred_element_type=jnp.float32
        )

    query_sum = lax.fori_loop(0, turns, query_turn, jnp.zeros(head_shape, jnp.float32))
    term_span = math.gcd(row_count * lax.axis_size("blk"), 2048)

    def term_block(index):
        begin_row = index * term_span
        key_part, value_part = key_value_grads(
            queries,
            query_grads,
            corrections,
            seg_rows,
            lax.dynamic_slice_in_dim(all_keys, begin_row, term_span, 0),
            lax.dynamic_slice_in_dim(all_values, begin_row, term_span, 0),
            lax.dynamic_slice_in_dim(all_segs, begin_row, term_span, 0),
        )
        return jnp.concatenate(
            [key_part.reshape(term_span, model_width), value_part.reshape(term_span, model_width)],
            axis=1,
        )

    blocks = lax.map(
        term_block, jnp.arange(row_count * lax.axis_size("blk") // term_span, dtype=jnp.int32)
    )
    key_terms = lax.psum_scatter(
        blocks.reshape(row_count * lax.axis_size("blk"), 2 * model_width),
        "blk",
        scatter_dimension=0,
        tiled=True,
    )
    query_low = query_sum.reshape(row_count, model_width).astype(jnp.bfloat16)
    key_low = key_terms[:, :model_width].astype(jnp.bfloat16)
    value_low = key_terms[:, model_width:].astype(jnp.bfloat16)
    qkv_grad = jnp.concatenate([query_low, key_low, value_low], axis=1)
    qkv_weight_grad = jnp.einsum(
        "td,tj->dj", first_low, qkv_grad, preferred_element_type=jnp.float32
    )
    query_bias_grad = jnp.sum(query_low.astype(jnp.float32), axis=0)
    value_bias_grad = jnp.sum(value_low.astype(jnp.float32), axis=0)
    first_grad = jnp.einsum(
        "tj,dj->td", qkv_grad, query_key_value_weight, preferred_element_type=jnp.float32
    )
    token_part, first_gain_grad, first_shift_grad = first_back(first_grad)
    tokens_grad = (residual_grad + token_part).astype(jnp.bfloat16).reshape(tokens.shape)
    local_grads = (
        qkv_weight_grad,
        query_bias_grad,
        value_bias_grad,
        out_weight_grad,
        out_bias_grad,
        first_gain_grad,
        first_shift_grad,
        second_gain_grad,
        second_shift_grad,
        up_weight_grad,
        up_bias_grad,
        down_weight_grad,
        down_bias_grad,
    )
    scattered = (
        lax.psum_scatter(local_grads[0], "blk", scatter_dimension=0, tiled=True),
        lax.psum_scatter(local_grads[1], "blk", scatter_dimension=0, tiled=True),
        lax.psum_scatter(local_grads[2], "blk", scatter_dimension=0, tiled=True),
        lax.psum_scatter(local_grads[3], "blk", scatter_dimension=0, tiled=True),
        lax.psum_scatter(local_grads[4], "blk", scatter_dimension=0, tiled=True),
        lax.psum_scatter(local_grads[5], "blk", scatter_dimension=0, tiled=True),
        lax.psum_scatter(local_grads[6], "blk", scatter_dimension=0, tiled=True),
        lax.psum_scatter(local_grads[7], "blk", scatter_dimension=0, tiled=True),
        lax.psum_scatter(local_grads[8], "blk", scatter_dimension=0, tiled=True),
        lax.psum_scatter(local_grads[9], "blk", scatter_dimension=0, tiled=True),
        lax.psum_scatter(local_grads[10], "blk", scatter_dimension=0, tiled=True),
        lax.psum_scatter(local_grads[11], "blk", scatter_dimension=1, tiled=True),
        lax.psum_scatter(local_grads[12], "blk", scatter_dimension=0, tiled=True),
    )
    summed_grads = lax.psum(
        (
            scattered[0],
            scattered[1],
            scattered[2],
            scattered[3],
            scattered[4],
            scattered[5],
            scattered[6],
            scattered[7],
            scattered[8],
            scattered[9],
            scattered[10],
            scattered[11],
            scattered[12],
        ),
        "seq",
    )
    return (layer_out, tokens_grad) + tuple(summed_grads)


VMEM_LIMIT = 64 * 1024 * 1024
D = 768
FF = 3072
ROWS = 192
CHIPS = 4
GROUP = 192
QKV = 3 * GROUP
HALF = FF // 2
OUT_HALF = D // 2
GRADS = 2 * HALF + OUT_HALF
PIECE = 48
KEYS = 1536
OWN = 768
LOW = jnp.bfloat16
F32 = jnp.float32
MESH = pl.DeviceIdType.MESH


def dot(a, b):
    return jnp.dot(a, b, preferred_element_type=F32)


def dot_nt(a, b):
    return lax.dot_general(a, b, (((1,), (1,)), ((), ())), preferred_element_type=F32)


def scratch_list():
    dma = pltpu.SemaphoreType.DMA
    vmem = pltpu.VMEM
    return dict(
        nrm=vmem((CHIPS, ROWS, D), LOW),
        xhat1=vmem((ROWS, D), F32),
        rstd1=vmem((ROWS, 1), F32),
        win=vmem((3, D, 256), LOW),
        wq=vmem((D, QKV), LOW),
        wo=vmem((D, D), LOW),
        w1=vmem((D, HALF), LOW),
        w2=vmem((HALF, D), LOW),
        q=vmem((3, OWN, HEAD), LOW),
        kvo=vmem((CHIPS, ROWS, 2 * GROUP), LOW),
        kvs=vmem((CHIPS, ROWS, 2 * GROUP), LOW),
        kh=vmem((3, KEYS, HEAD), LOW),
        vh=vmem((3, KEYS, 2 * HEAD), LOW),
        segs=vmem((2, CHIPS, 8, ROWS), jnp.int32),
        kseg=vmem((1, KEYS), jnp.int32),
        qseg=vmem((OWN, 128), jnp.int32),
        prob=vmem((3, OWN, KEYS), LOW),
        att=vmem((3, OWN, HEAD), F32),
        rtot=vmem((3, OWN, HEAD), F32),
        mgs=vmem((CHIPS, ROWS, GROUP), LOW),
        mg=vmem((CHIPS, ROWS, GROUP), LOW),
        mgo=vmem((CHIPS, ROWS, GROUP), LOW),
        mgt=vmem((CHIPS, GROUP, 2 * ROWS), LOW),
        og=vmem((2, ROWS, D), LOW),
        nt=vmem((2, ROWS, D), LOW),
        bl=vmem((2, ROWS, D), LOW),
        ogt=vmem((D, 2 * ROWS), LOW),
        ntt=vmem((D, 2 * ROWS), LOW),
        resid=vmem((ROWS, D), F32),
        xhat2=vmem((ROWS, D), F32),
        rstd2=vmem((ROWS, 1), F32),
        act=vmem((2 * ROWS, HALF), LOW),
        hg=vmem((2 * ROWS, HALF), LOW),
        lo=vmem((2, ROWS, D), F32),
        ng=vmem((2, ROWS, D), F32),
        lor=vmem((ROWS, D), F32),
        ngr=vmem((ROWS, D), F32),
        rgrad=vmem((ROWS, D), F32),
        ags=vmem((CHIPS, ROWS, GROUP), LOW),
        ag=vmem((CHIPS, ROWS, GROUP), LOW),
        dkt=vmem((3, HEAD, KEYS), F32),
        dvt=vmem((3, HEAD, KEYS), F32),
        dkr=vmem((3, HEAD, OWN), F32),
        dvr=vmem((3, HEAD, OWN), F32),
        dqkv=vmem((OWN, QKV), LOW),
        nrmt=vmem((CHIPS, D, ROWS), LOW),
        fgs=vmem((CHIPS, ROWS, D), LOW),
        fg=vmem((CHIPS, ROWS, D), LOW),
        dw=vmem((CHIPS, 4, PIECE, GRADS), LOW),
        rx=vmem((3, CHIPS, PIECE, GRADS), LOW),
        zs=vmem((CHIPS, PIECE, GRADS), LOW),
        rz=vmem((CHIPS, PIECE, GRADS), LOW),
        fin=vmem((PIECE, GRADS), LOW),
        dwq=vmem((CHIPS, 4, PIECE, QKV), LOW),
        dwqr=vmem((2, 4, PIECE, QKV), LOW),
        dwqx=vmem((2, 4, PIECE, QKV), LOW),
        rxq=vmem((3, 2, PIECE, QKV), LOW),
        zq=vmem((2, PIECE, QKV), LOW),
        rzq=vmem((CHIPS, PIECE, QKV), LOW),
        va=vmem((16, D), F32),
        var=vmem((8, 16, D), F32),
        vax=vmem((16, D), F32),
        vaxr=vmem((4, 16, D), F32),
        vb=vmem((16, D), F32),
        vbr=vmem((8, 16, D), F32),
        vbx=vmem((16, D), F32),
        vbxr=vmem((4, 16, D), F32),
        load_sem=dma((8,)),
        seg_s=dma((7,)), seg_r=dma((7,)),
        og_s=dma((1,)), og_r=dma((1,)),
        nu_s=dma((CHIPS,)), nd_s=dma((CHIPS,)), n_r=dma((CHIPS,)),
        kv_s=dma((CHIPS,)), kv_r=dma((CHIPS,)),
        mg_s=dma((CHIPS,)), mg_r=dma((CHIPS,)),
        mgo_s=dma((1,)), mgo_r=dma((1,)),
        nt_s=dma((1,)), nt_r=dma((1,)),
        lo_s=dma((1,)), lo_r=dma((1,)),
        ng_s=dma((1,)), ng_r=dma((1,)),
        bl_s=dma((1,)), bl_r=dma((1,)),
        ag_s=dma((CHIPS,)), ag_r=dma((CHIPS,)),
        dk_s=dma((3,)), dk_r=dma((3,)),
        dv_s=dma((3,)), dv_r=dma((3,)),
        fg_s=dma((CHIPS,)), fg_r=dma((CHIPS,)),
        x_s=dma((3,)), x_r=dma((3,)),
        z_s=dma((CHIPS,)), z_r=dma((CHIPS,)),
        f_s=dma((4,)), f_r=dma((4,)),
        q0_s=dma((1,)), q0_r=dma((1,)),
        qx_s=dma((3,)), qx_r=dma((3,)),
        qz_s=dma((2,)), qz_r=dma((CHIPS,)),
        qf_s=dma((3,)), qf_r=dma((3,)),
        va_s=dma((7,)), va_r=dma((7,)),
        vax_s=dma((3,)), vax_r=dma((3,)),
        vb_s=dma((7,)), vb_r=dma((7,)),
        vbx_s=dma((3,)), vbx_r=dma((3,)),
    )


class Box:
    pass


def kernel_body(names, pad_number, *refs):
    (tok, seg, ogi, wqkv, wo_h, w1_h, w2_h, par, qvb, b1) = refs[:10]
    (out_tok, out_layer, out_fin, out_finq, out_va, out_vb) = refs[10:16]
    r = Box()
    for name, ref in zip(names, refs[16:]):
        setattr(r, name, ref)

    s = lax.axis_index("seq")
    b = lax.axis_index("blk")
    z = b // 2
    c = b % 2
    sib = 2 * z + 1 - c
    flip = {1: s + 1 - 2 * (s % 2), 2: (s + 2) % 4, 3: 3 - s}
    swap = {1: 1, 2: 2, 3: 3}

    pending = []

    def send(src, dst, ssem, rsem, dev_s, dev_b):
        return pltpu.make_async_remote_copy(
            src_ref=src, dst_ref=dst, send_sem=ssem, recv_sem=rsem,
            device_id=(dev_s, dev_b), device_id_type=MESH,
        )

    def local_row(index):
        return par[index : index + 1, :]

    loads = []
    for part in range(3):
        start = pl.multiple_of(D * part + 384 * (z // 2) + 128 * (z % 2), 128)
        loads.append(
            pltpu.make_async_copy(wqkv.at[:, pl.ds(start, 256)], r.win.at[part], r.load_sem.at[part])
        )
    half = pl.multiple_of(c * HALF, 128)
    loads.append(pltpu.make_async_copy(wo_h, r.wo, r.load_sem.at[3]))
    loads.append(pltpu.make_async_copy(w1_h.at[:, pl.ds(half, HALF)], r.w1, r.load_sem.at[4]))
    loads.append(pltpu.make_async_copy(w2_h.at[pl.ds(half, HALF), :], r.w2, r.load_sem.at[5]))
    for item in loads:
        item.start()

    barrier = pltpu.get_barrier_semaphore()
    for step in range(1, 8):
        pl.semaphore_signal(barrier, inc=1, device_id=(s, (b + step) % 8), device_id_type=MESH)
    for step in (1, 2, 3):
        for core in range(2):
            pl.semaphore_signal(
                barrier, inc=1, device_id=(flip[step], 2 * z + core), device_id_type=MESH
            )
    pl.semaphore_wait(barrier, 13)

    r.segs[c, z] = jnp.broadcast_to(seg[...], (8, ROWS))
    seg_copies = []
    for step in range(1, 8):
        seg_copies.append(
            send(r.segs.at[c, z], r.segs.at[c, z], r.seg_s.at[step - 1], r.seg_r.at[step - 1],
                 s, (b + step) % 8)
        )
    for item in seg_copies:
        item.start()
    pending.extend(seg_copies)

    def first_norm(index, carried):
        rows = pl.ds(index * PIECE, PIECE)
        x = tok[rows, :].astype(F32)
        centre = x - jnp.mean(x, axis=-1, keepdims=True)
        spread = lax.rsqrt(jnp.mean(centre * centre, axis=-1, keepdims=True) + EPS)
        xhat = centre * spread
        r.xhat1[rows, :] = xhat
        r.rstd1[rows, :] = spread
        r.nrm[z, rows, :] = (xhat * local_row(3) + local_row(4)).astype(LOW)
        return carried

    lax.fori_loop(0, 4, first_norm, 0)

    def norm_copy(slot, up):
        if up:
            return send(r.nrm.at[slot], r.nrm.at[slot], r.nu_s.at[slot], r.n_r.at[slot], s, b + 2)
        return send(r.nrm.at[slot], r.nrm.at[slot], r.nd_s.at[slot], r.n_r.at[slot], s, b - 2)

    def norm_forward(slot):
        @pl.when(jnp.logical_and(slot <= z, z < 3))
        def _():
            norm_copy(slot, True).start()

        @pl.when(jnp.logical_and(slot >= z, z > 0))
        def _():
            norm_copy(slot, False).start()

    norm_forward(z)

    r.og[c] = ogi[...]
    og_copy = send(r.og.at[c], r.og.at[c], r.og_s.at[0], r.og_r.at[0], s, sib)
    og_copy.start()
    pending.append(og_copy)

    for part in range(3):
        loads[part].wait()
    for part in range(3):
        r.wq[:, part * GROUP : (part + 1) * GROUP] = jnp.where(
            z % 2 == 1, r.win[part, :, 64:256], r.win[part, :, 0:192]
        )

    upper = z // 2
    near = z * (1 - upper) + (3 - z) * upper
    qkv_bias = [qvb[0, pl.ds(z, 1), :], None, qvb[1, pl.ds(z, 1), :]]

    def split_keys(pair, row):
        for h in range(3):
            r.kh[h, pl.ds(row, ROWS), :] = pair[:, h * HEAD : (h + 1) * HEAD]
            r.vh[h, pl.ds(row, ROWS), 0:HEAD] = pair[:, GROUP + h * HEAD : GROUP + (h + 1) * HEAD]
            r.vh[h, pl.ds(row, ROWS), HEAD : 2 * HEAD] = jnp.ones((ROWS, HEAD), LOW)

    def kv_copy(slot):
        return send(r.kvo.at[slot], r.kvs.at[slot], r.kv_s.at[slot], r.kv_r.at[slot], s, sib)

    def project(index, carried):
        seq_slot = jnp.where(index == 0, near, jnp.where(index == 1, 1 - near, index))
        slot = seq_slot * (1 - upper) + (3 - seq_slot) * upper

        @pl.when(index > 0)
        def _():
            norm_copy(slot, True).wait_recv()
            norm_forward(slot)

        rows = r.nrm[slot]
        whole = dot(rows, r.wq[...])
        qs = (whole[:, :GROUP] + qkv_bias[0]).astype(LOW)
        ks = whole[:, GROUP : 2 * GROUP].astype(LOW)
        vs = (whole[:, 2 * GROUP :] + qkv_bias[2]).astype(LOW)
        for h in range(3):
            r.q[h, pl.ds(slot * ROWS, ROWS), :] = qs[:, h * HEAD : (h + 1) * HEAD]
        r.kvo[slot, :, 0:GROUP] = ks
        r.kvo[slot, :, GROUP : 2 * GROUP] = vs
        kv_copy(slot).start()
        split_keys(r.kvo[slot], slot * ROWS)
        return carried

    lax.fori_loop(0, CHIPS, project, 0)

    for item in seg_copies:
        item.wait_recv()
    for slot in range(CHIPS):
        for side, core in ((0, c), (1, 1 - c)):
            r.kseg[:, (side * CHIPS + slot) * ROWS : (side * CHIPS + slot + 1) * ROWS] = r.segs[
                core, slot, 0:1, :
            ]
        line = r.segs[c, slot, 0:1, :].astype(F32)
        r.qseg[slot * ROWS : (slot + 1) * ROWS, :] = jnp.transpose(
            jnp.broadcast_to(line, (128, ROWS))
        ).astype(jnp.int32)

    def take_sibling(slot, carried):
        kv_copy(slot).wait_recv()
        split_keys(r.kvs[slot], OWN + slot * ROWS)
        return carried

    lax.fori_loop(0, CHIPS, take_sibling, 0)

    SPAN = 256
    TURNS = KEYS // SPAN

    def mg_copy(block):
        return send(r.mgs.at[block], r.mg.at[z], r.mg_s.at[block], r.mg_r.at[z], s, 2 * block + c)

    def mg_arrival(slot):
        return send(r.mgs.at[slot], r.mg.at[slot], r.mg_s.at[slot], r.mg_r.at[slot], s, 2 * slot + c)

    def forward_block(index, carried):
        block = (z + 1 + index) % CHIPS
        rows = pl.ds(pl.multiple_of(block * ROWS, ROWS), ROWS)
        own_segs = r.qseg[rows, :]
        wide = jnp.concatenate([own_segs] * (SPAN // 128), axis=1)
        live = jnp.where(own_segs[:, :HEAD] != pad_number, 1.0, 0.0).astype(F32)
        for h in range(3):
            qs = r.q[h, rows, :]
            total = jnp.zeros((ROWS, 2 * HEAD), F32)
            for turn in range(TURNS):
                cols = slice(turn * SPAN, (turn + 1) * SPAN)
                raw = dot_nt(qs, r.kh[h, cols, :])
                weights = jnp.where(
                    wide == r.kseg[:, cols], jnp.exp(raw * (1.0 / math.sqrt(HEAD))), 0.0
                ).astype(LOW)
                r.prob[h, rows, cols] = weights
                total = total + dot(weights, r.vh[h, cols, :])
            inverse = 1.0 / total[:, HEAD:]
            attended = total[:, :HEAD] * inverse * live
            r.rtot[h, rows, :] = inverse
            r.att[h, rows, :] = attended
            r.mgs[block, :, h * HEAD : (h + 1) * HEAD] = attended.astype(LOW)

        @pl.when(block != z)
        def _():
            mg_copy(block).start()

        @pl.when(block == z)
        def _():
            r.mg[z] = r.mgs[z]

        return carried

    lax.fori_loop(0, CHIPS, forward_block, 0)

    def others(fn):
        def run(index, carried):
            fn((z + 1 + index) % CHIPS)
            return carried

        lax.fori_loop(0, CHIPS - 1, run, 0)

    others(lambda slot: mg_arrival(slot).wait_recv())
    mgo_copy = send(r.mg, r.mgo, r.mgo_s.at[0], r.mgo_r.at[0], s, sib)
    mgo_copy.start()
    pending.append(mgo_copy)

    loads[3].wait()

    def out_projection(index, carried):
        cols = pl.ds(pl.multiple_of(index * 256, 256), 256)
        total = tok[:, cols].astype(F32) + par[2:3, cols]
        for slot in range(CHIPS):
            total = total + dot(r.mg[slot], r.wo[slot * GROUP : (slot + 1) * GROUP, cols])
        r.resid[:, cols] = total
        return carried

    lax.fori_loop(0, 3, out_projection, 0)

    def second_norm(index, carried):
        rows = pl.ds(index * PIECE, PIECE)
        x = r.resid[rows, :]
        centre = x - jnp.mean(x, axis=-1, keepdims=True)
        spread = lax.rsqrt(jnp.mean(centre * centre, axis=-1, keepdims=True) + EPS)
        xhat = centre * spread
        r.xhat2[rows, :] = xhat
        r.rstd2[rows, :] = spread
        r.nt[c, rows, :] = (xhat * local_row(5) + local_row(6)).astype(LOW)
        return carried

    lax.fori_loop(0, 4, second_norm, 0)
    nt_copy = send(r.nt.at[c], r.nt.at[c], r.nt_s.at[0], r.nt_r.at[0], s, sib)
    nt_copy.start()
    pending.append(nt_copy)
    loads[4].wait()
    loads[5].wait()
    og_copy.wait_recv()
    r.va[...] = jnp.zeros((16, D), F32)
    r.vb[...] = jnp.zeros((16, D), F32)
    r.va[3:4, :] = jnp.sum(ogi[...].astype(F32), axis=0, keepdims=True)
    for core in range(2):
        r.ogt[:, core * ROWS : (core + 1) * ROWS] = jnp.transpose(r.og[core])
    nt_copy.wait_recv()

    TILE = 256
    r.lo[...] = jnp.zeros((2, ROWS, D), F32)
    r.ng[...] = jnp.zeros((2, ROWS, D), F32)

    def mlp_tile(index, carried):
        cols = pl.ds(pl.multiple_of(index * TILE, TILE), TILE)
        bias = b1[pl.ds(c, 1), cols]
        total = jnp.zeros((1, TILE), F32)
        for core in range(2):
            rows = slice(core * ROWS, (core + 1) * ROWS)
            hidden = dot(r.nt[core], r.w1[:, cols]) + bias
            gate = 0.5 * (1.0 + lax.erf(hidden * (1.0 / math.sqrt(2.0))))
            slope = gate + hidden * jnp.exp(-0.5 * hidden * hidden) * (1.0 / math.sqrt(2.0 * math.pi))
            active = (hidden * gate).astype(LOW)
            grad = (slope * dot_nt(r.og[core], r.w2[cols, :])).astype(LOW)
            r.act[rows, cols] = active
            r.hg[rows, cols] = grad
            total = total + jnp.sum(grad.astype(F32), axis=0, keepdims=True)
            r.lo[core] = r.lo[core] + dot(active, r.w2[cols, :])
            r.ng[core] = r.ng[core] + dot_nt(grad, r.w1[:, cols])
        r.va[pl.ds(4 + 2 * c + index // 3, 1), pl.ds(pl.multiple_of((index % 3) * TILE, TILE), TILE)] = total
        return carried

    lax.fori_loop(0, HALF // TILE, mlp_tile, 0)
    ng_copy = send(r.ng.at[1 - c], r.ngr, r.ng_s.at[0], r.ng_r.at[0], s, sib)
    lo_copy = send(r.lo.at[1 - c], r.lor, r.lo_s.at[0], r.lo_r.at[0], s, sib)
    ng_copy.start()
    lo_copy.start()
    pending.extend([ng_copy, lo_copy])
    for core in range(2):
        r.ntt[:, core * ROWS : (core + 1) * ROWS] = jnp.transpose(r.nt[core])
    mgo_copy.wait_recv()
    for slot in range(CHIPS):
        r.mgt[slot, :, pl.ds(pl.multiple_of(0, 1), ROWS)] = jnp.transpose(
            jnp.where(c == 0, r.mg[slot], r.mgo[slot])
        )
        r.mgt[slot, :, ROWS : 2 * ROWS] = jnp.transpose(jnp.where(c == 0, r.mgo[slot], r.mg[slot]))

    ng_copy.wait_recv()

    def second_back(index, carried):
        rows = pl.ds(index * PIECE, PIECE)
        grad = r.ng[c, rows, :] + r.ngr[rows, :]
        xhat = r.xhat2[rows, :]
        scaled = grad * local_row(5)
        mean_one = jnp.mean(scaled, axis=-1, keepdims=True)
        mean_two = jnp.mean(scaled * xhat, axis=-1, keepdims=True)
        through = r.rstd2[rows, :] * (scaled - mean_one - xhat * mean_two)
        resid_grad = ogi[rows, :].astype(F32) + through
        low = resid_grad.astype(LOW)
        r.rgrad[rows, :] = resid_grad
        r.bl[c, rows, :] = low
        r.va[0:1, :] += jnp.sum(low.astype(F32), axis=0, keepdims=True)
        r.va[1:2, :] += jnp.sum(grad * xhat, axis=0, keepdims=True)
        r.va[2:3, :] += jnp.sum(grad, axis=0, keepdims=True)
        return carried

    lax.fori_loop(0, 4, second_back, 0)
    bl_copy = send(r.bl.at[c], r.bl.at[c], r.bl_s.at[0], r.bl_r.at[0], s, sib)
    bl_copy.start()
    pending.append(bl_copy)

    def ag_copy(block):
        return send(r.ags.at[block], r.ag.at[z], r.ag_s.at[block], r.ag_r.at[z], s, 2 * block + c)

    def ag_arrival(slot):
        return send(r.ags.at[slot], r.ag.at[slot], r.ag_s.at[slot], r.ag_r.at[slot], s, 2 * slot + c)

    def attended_block(index, carried):
        block = (z + 1 + index) % CHIPS
        wide = pl.ds(pl.multiple_of(block * GROUP, GROUP), GROUP)
        r.ags[block] = dot_nt(r.bl[c], r.wo[wide, :]).astype(LOW)

        @pl.when(block != z)
        def _():
            ag_copy(block).start()

        @pl.when(block == z)
        def _():
            r.ag[z] = r.ags[z]

        return carried

    lax.fori_loop(0, CHIPS, attended_block, 0)

    va_copies = [
        send(r.va, r.var.at[b], r.va_s.at[step - 1], r.va_r.at[step - 1], s, (b + step) % 8)
        for step in range(1, 8)
    ]
    r.var[b] = r.va[...]
    for item in va_copies:
        item.start()
    pending.extend(va_copies)

    def mlp_grads(index, carried):
        tile = index // CHIPS
        block = index % CHIPS
        cols = pl.ds(pl.multiple_of(tile * TILE, TILE), TILE)
        late = pl.ds(pl.multiple_of(HALF + tile * TILE, TILE), TILE)
        rows = pl.ds(pl.multiple_of(block * ROWS, ROWS), ROWS)
        one = dot(r.ntt[rows, :], r.hg[:, cols]).astype(LOW)
        two = dot(r.ogt[rows, :], r.act[:, cols]).astype(LOW)
        for piece in range(4):
            part = slice(piece * PIECE, (piece + 1) * PIECE)
            r.dw[block, piece, :, cols] = one[part]
            r.dw[block, piece, :, late] = two[part]
        return carried

    lax.fori_loop(0, CHIPS * (HALF // TILE), mlp_grads, 0)
    bl_copy.wait_recv()

    def out_grads(block, carried):
        side = pl.ds(pl.multiple_of(c * OUT_HALF, OUT_HALF), OUT_HALF)
        grad = dot(r.mgt[block, :, 0:ROWS], r.bl[0, :, side]) + dot(
            r.mgt[block, :, ROWS : 2 * ROWS], r.bl[1, :, side]
        )
        low = grad.astype(LOW)
        for piece in range(4):
            r.dw[block, piece, :, 2 * HALF :] = low[piece * PIECE : (piece + 1) * PIECE]
        return carried

    lax.fori_loop(0, CHIPS, out_grads, 0)

    x_copies = [
        send(r.dw.at[:, flip[step]], r.rx.at[step - 1], r.x_s.at[step - 1], r.x_r.at[step - 1],
             flip[step], b)
        for step in (1, 2, 3)
    ]
    for item in x_copies:
        item.start()
    pending.extend(x_copies)

    lo_copy.wait_recv()

    def layer_rows(index, carried):
        rows = pl.ds(index * PIECE, PIECE)
        out_layer[rows, :] = (
            r.resid[rows, :] + r.lo[c, rows, :] + r.lor[rows, :] + local_row(7)
        ).astype(LOW)
        return carried

    lax.fori_loop(0, 4, layer_rows, 0)

    others(lambda slot: ag_arrival(slot).wait_recv())
    r.dkt[...] = jnp.zeros((3, HEAD, KEYS), F32)
    r.dvt[...] = jnp.zeros((3, HEAD, KEYS), F32)
    dk_copies, dv_copies = [], []
    for h in range(3):
        lanes = slice(h * HEAD, (h + 1) * HEAD)

        def backward_block(block, carried, h=h, lanes=lanes):
            rows = pl.ds(pl.multiple_of(block * ROWS, ROWS), ROWS)
            live = jnp.where(r.qseg[rows, :][:, :HEAD] != pad_number, 1.0, 0.0).astype(F32)
            grad = r.ag[block, :, lanes].astype(F32) * live
            inverse = r.rtot[h, rows, :]
            correct = jnp.sum(grad * r.att[h, rows, :], axis=-1, keepdims=True) * inverse[:, 0:1]
            correct = correct.astype(LOW).astype(F32)
            scaled = (grad * inverse).astype(LOW)
            scaled_t = jnp.transpose(scaled)
            query_t = jnp.transpose(r.q[h, rows, :])
            total = jnp.zeros((ROWS, HEAD), F32)
            for turn in range(TURNS):
                cols = slice(turn * SPAN, (turn + 1) * SPAN)
                product = dot_nt(scaled, r.vh[h, cols, 0:HEAD])
                weights = r.prob[h, rows, cols]
                slopes = (
                    weights.astype(F32) * (product - correct) * (1.0 / math.sqrt(HEAD))
                ).astype(LOW)
                total = total + dot(slopes, r.kh[h, cols, :])
                r.dkt[h, :, cols] += dot(query_t, slopes)
                r.dvt[h, :, cols] += dot(scaled_t, weights)
            r.dqkv[rows, lanes] = total.astype(LOW)
            return carried

        lax.fori_loop(0, CHIPS, backward_block, 0)
        dk_copies.append(
            send(r.dkt.at[h, :, pl.ds(OWN, OWN)], r.dkr.at[h], r.dk_s.at[h], r.dk_r.at[h], s, sib)
        )
        dv_copies.append(
            send(r.dvt.at[h, :, pl.ds(OWN, OWN)], r.dvr.at[h], r.dv_s.at[h], r.dv_r.at[h], s, sib)
        )
        dk_copies[h].start()
        dv_copies[h].start()
    pending.extend(dk_copies + dv_copies)

    for item in va_copies:
        item.wait_recv()
    total = r.var[0]
    for slot in range(1, 8):
        total = total + r.var[slot]
    r.vax[...] = total
    r.vaxr[s] = total
    vax_copies = [
        send(r.vax, r.vaxr.at[s], r.vax_s.at[step - 1], r.vax_r.at[step - 1], flip[step], b)
        for step in (1, 2, 3)
    ]
    for item in vax_copies:
        item.start()
    pending.extend(vax_copies)

    for slot in range(CHIPS):
        r.nrmt[slot] = jnp.transpose(r.nrm[slot])
    for h in range(3):
        dk_copies[h].wait_recv()
        dv_copies[h].wait_recv()
        key_grad = (r.dkt[h, :, 0:OWN] + r.dkr[h]).astype(LOW)
        value_grad = (r.dvt[h, :, 0:OWN] + r.dvr[h]).astype(LOW)
        r.dqkv[:, GROUP + h * HEAD : GROUP + (h + 1) * HEAD] = jnp.transpose(key_grad)
        r.dqkv[:, 2 * GROUP + h * HEAD : 2 * GROUP + (h + 1) * HEAD] = jnp.transpose(value_grad)

    def fg_copy(block):
        return send(r.fgs.at[block], r.fg.at[z], r.fg_s.at[block], r.fg_r.at[z], s, 2 * block + c)

    def fg_arrival(slot):
        return send(r.fgs.at[slot], r.fg.at[slot], r.fg_s.at[slot], r.fg_r.at[slot], s, 2 * slot + c)

    def first_grads(index, carried):
        block = (z + 1 + index) % CHIPS
        rows = pl.ds(pl.multiple_of(block * ROWS, ROWS), ROWS)
        r.fgs[block] = dot_nt(r.dqkv[rows, :], r.wq[...]).astype(LOW)

        @pl.when(block != z)
        def _():
            fg_copy(block).start()

        @pl.when(block == z)
        def _():
            r.fg[z] = r.fgs[z]

        return carried

    lax.fori_loop(0, CHIPS, first_grads, 0)

    def qkv_grads(block, carried):
        rows = pl.ds(pl.multiple_of(block * ROWS, ROWS), ROWS)
        grad = jnp.zeros((ROWS, QKV), F32)
        for slot in range(CHIPS):
            grad = grad + dot(
                r.nrmt[slot, rows, :], r.dqkv[slot * ROWS : (slot + 1) * ROWS, :]
            )
        low = grad.astype(LOW)
        for piece in range(4):
            r.dwq[block, piece] = low[piece * PIECE : (piece + 1) * PIECE]
        return carried

    lax.fori_loop(0, CHIPS, qkv_grads, 0)
    q0_copy = send(
        r.dwq.at[pl.ds(2 * (1 - c), 2)], r.dwqr, r.q0_s.at[0], r.q0_r.at[0], s, sib
    )
    q0_copy.start()
    pending.append(q0_copy)
    r.vb[pl.ds(z, 1), 0:GROUP] = jnp.sum(r.dqkv[:, 0:GROUP].astype(F32), axis=0, keepdims=True)
    r.vb[pl.ds(4 + z, 1), 0:GROUP] = jnp.sum(
        r.dqkv[:, 2 * GROUP :].astype(F32), axis=0, keepdims=True
    )
    q0_copy.wait_recv()
    for part in range(2):
        for piece in range(4):
            r.dwqx[part, piece] = (
                r.dwq[2 * c + part, piece].astype(F32) + r.dwqr[part, piece].astype(F32)
            ).astype(LOW)
    qx_copies = [
        send(r.dwqx.at[:, flip[step]], r.rxq.at[step - 1], r.qx_s.at[step - 1],
             r.qx_r.at[step - 1], flip[step], b)
        for step in (1, 2, 3)
    ]
    for item in qx_copies:
        item.start()
    pending.extend(qx_copies)

    for item in x_copies:
        item.wait_recv()

    def z_copy(block):
        return send(r.zs.at[block], r.rz.at[z], r.z_s.at[block], r.z_r.at[z], s, 2 * block + c)

    def z_arrival(slot):
        return send(r.zs.at[slot], r.rz.at[slot], r.z_s.at[slot], r.z_r.at[slot], s, 2 * slot + c)

    def x_sum(index, carried):
        block = (z + 1 + index) % CHIPS

        def columns(part, carried):
            cols = pl.ds(pl.multiple_of(part * 384, 384), 384)
            total = r.dw[block, s, :, cols].astype(F32)
            for step in range(3):
                total = total + r.rx[step, block, :, cols].astype(F32)
            r.zs[block, :, cols] = total.astype(LOW)
            return carried

        lax.fori_loop(0, GRADS // 384, columns, 0)

        @pl.when(block != z)
        def _():
            z_copy(block).start()

        @pl.when(block == z)
        def _():
            r.rz[z] = r.zs[z]

        return carried

    lax.fori_loop(0, CHIPS, x_sum, 0)

    others(lambda slot: fg_arrival(slot).wait_recv())

    def first_back(index, carried):
        rows = pl.ds(index * PIECE, PIECE)
        grad = r.fg[0, rows, :].astype(F32)
        for slot in range(1, CHIPS):
            grad = grad + r.fg[slot, rows, :].astype(F32)
        xhat = r.xhat1[rows, :]
        scaled = grad * local_row(3)
        mean_one = jnp.mean(scaled, axis=-1, keepdims=True)
        mean_two = jnp.mean(scaled * xhat, axis=-1, keepdims=True)
        through = r.rstd1[rows, :] * (scaled - mean_one - xhat * mean_two)
        out_tok[rows, :] = (r.rgrad[rows, :] + through).astype(LOW)
        r.vb[8:9, :] += jnp.sum(grad * xhat, axis=0, keepdims=True)
        r.vb[9:10, :] += jnp.sum(grad, axis=0, keepdims=True)
        return carried

    lax.fori_loop(0, 4, first_back, 0)

    vb_copies = [
        send(r.vb, r.vbr.at[b], r.vb_s.at[step - 1], r.vb_r.at[step - 1], s, (b + step) % 8)
        for step in range(1, 8)
    ]
    r.vbr[b] = r.vb[...]
    for item in vb_copies:
        item.start()
    pending.extend(vb_copies)

    for item in qx_copies:
        item.wait_recv()
    owner = s // 2
    mine = 2 * z + owner

    def qz_copy(part):
        return send(r.zq.at[part], r.rzq.at[z], r.qz_s.at[part], r.qz_r.at[z],
                    s, 2 * (2 * c + part) + owner)

    for part in range(2):
        total = r.dwqx[part, s].astype(F32)
        for step in range(3):
            total = total + r.rxq[step, part].astype(F32)
        r.zq[part] = total.astype(LOW)
        there = 2 * (2 * c + part) + owner

        @pl.when(there != b)
        def _(part=part):
            qz_copy(part).start()

        @pl.when(there == b)
        def _(part=part):
            r.rzq[z] = r.zq[part]

    for item in vb_copies:
        item.wait_recv()
    total = r.vbr[0]
    for slot in range(1, 8):
        total = total + r.vbr[slot]
    r.vbx[...] = total
    r.vbxr[s] = total
    vbx_copies = [
        send(r.vbx, r.vbxr.at[s], r.vbx_s.at[step - 1], r.vbx_r.at[step - 1], flip[step], b)
        for step in (1, 2, 3)
    ]
    for item in vbx_copies:
        item.start()
    pending.extend(vbx_copies)

    others(lambda slot: z_arrival(slot).wait_recv())

    def z_sum(part, carried):
        cols = pl.ds(pl.multiple_of(part * 384, 384), 384)
        total = r.rz[0, :, cols].astype(F32)
        for slot in range(1, CHIPS):
            total = total + r.rz[slot, :, cols].astype(F32)
        r.fin[:, cols] = total.astype(LOW)
        return carried

    lax.fori_loop(0, GRADS // 384, z_sum, 0)

    f_copies = [
        send(r.fin, out_fin.at[s % 2, c], r.f_s.at[step], r.f_r.at[2 * (s % 2) + c],
             s if step == 0 else flip[step], mine)
        for step in range(4)
    ]
    for item in f_copies[1:]:
        item.start()

    @pl.when(mine != b)
    def _():
        f_copies[0].start()

    @pl.when(mine == b)
    def _():
        out_fin[s % 2, c] = r.fin[...]

    def qf_copy(step):
        return send(r.rzq, out_finq.at[s % 2], r.qf_s.at[step - 1], r.qf_r.at[step - 1],
                    flip[step], b)

    def qz_arrival(slot):
        return send(r.zq.at[0], r.rzq.at[slot], r.qz_s.at[0], r.qz_r.at[slot], s, sib)

    @pl.when(owner == c)
    def _():
        for slot in range(CHIPS):
            @pl.when(jnp.logical_or(slot != z, z // 2 != c))
            def _(slot=slot):
                qz_arrival(slot).wait_recv()

        for step in (1, 2, 3):
            qf_copy(step).start()
        out_finq[s % 2] = r.rzq[...]

    for piece in range(2):
        for core in range(2):
            @pl.when(jnp.logical_or(2 * c + piece != s, core != c))
            def _(piece=piece, core=core):
                send(r.fin, out_fin.at[piece, core], r.f_s.at[0], r.f_r.at[2 * piece + core],
                     s, sib).wait_recv()

    for step in (1, 2, 3):
        @pl.when(flip[step] // 2 == c)
        def _(step=step):
            qf_copy(step).wait_recv()

    for item in vax_copies + vbx_copies:
        item.wait_recv()
    out_va[...] = r.vaxr[0] + r.vaxr[1] + r.vaxr[2] + r.vaxr[3]
    out_vb[...] = r.vbxr[0] + r.vbxr[1] + r.vbxr[2] + r.vbxr[3]

    for slot in range(CHIPS):
        @pl.when(jnp.logical_and(slot <= z, z < 3))
        def _(slot=slot):
            norm_copy(slot, True).wait_send()

        @pl.when(jnp.logical_and(slot >= z, z > 0))
        def _(slot=slot):
            norm_copy(slot, False).wait_send()

        kv_copy(slot).wait_send()
    for make in (mg_copy, ag_copy, fg_copy, z_copy):
        others(lambda slot, make=make: make(slot).wait_send())
    for item in pending:
        item.wait_send()
    for item in f_copies[1:]:
        item.wait_send()

    @pl.when(mine != b)
    def _():
        f_copies[0].wait_send()

    for part in range(2):
        @pl.when(2 * (2 * c + part) + owner != b)
        def _(part=part):
            qz_copy(part).wait_send()

    @pl.when(owner == c)
    def _():
        for step in (1, 2, 3):
            qf_copy(step).wait_send()


def chip_body(
    tokens, segment_ids, out_grad, query_key_value_weight, query_bias, value_bias,
    attention_output_weight, attention_output_bias, first_gain, first_shift,
    second_gain, second_shift, mlp_input_weight, mlp_input_bias, mlp_output_weight,
    mlp_output_bias,
):
    pad_number = tokens.shape[1] * lax.axis_size("blk") // SHORT_LO + 2
    par = jnp.stack(
        [query_bias, value_bias, attention_output_bias, first_gain, first_shift,
         second_gain, second_shift, mlp_output_bias]
    ).astype(F32)
    qvb = jnp.stack([query_bias.reshape(4, GROUP), value_bias.reshape(4, GROUP)]).astype(F32)
    b1 = mlp_input_bias.reshape(2, HALF).astype(F32)
    names = scratch_list()
    any_space = pl.BlockSpec(memory_space=pl.ANY)
    in_vmem = pl.BlockSpec(memory_space=pltpu.VMEM)
    tok_out, layer_out, fin, finq, va, vb = pl.pallas_call(
        functools.partial(kernel_body, tuple(names), pad_number),
        out_shape=(
            jax.ShapeDtypeStruct((ROWS, D), LOW),
            jax.ShapeDtypeStruct((ROWS, D), LOW),
            jax.ShapeDtypeStruct((2, 2, PIECE, GRADS), LOW),
            jax.ShapeDtypeStruct((2, CHIPS, PIECE, QKV), LOW),
            jax.ShapeDtypeStruct((16, D), F32),
            jax.ShapeDtypeStruct((16, D), F32),
        ),
        in_specs=[in_vmem, in_vmem, in_vmem, any_space, any_space, any_space, any_space,
                  in_vmem, in_vmem, in_vmem],
        out_specs=(in_vmem,) * 6,
        scratch_shapes=list(names.values()),
        compiler_params=pltpu.CompilerParams(
            collective_id=0, has_side_effects=True, vmem_limit_bytes=VMEM_LIMIT
        ),
        name="encoder_block",
    )(
        tokens.reshape(ROWS, D), segment_ids, out_grad.reshape(ROWS, D),
        query_key_value_weight, attention_output_weight, mlp_input_weight, mlp_output_weight,
        par, qvb, b1,
    )
    b = lax.axis_index("blk")
    up = jnp.transpose(fin[..., :HALF], (0, 2, 1, 3)).reshape(96, FF).astype(F32)
    down = jnp.transpose(fin[..., HALF : 2 * HALF], (1, 3, 0, 2)).reshape(FF, 96).astype(F32)
    out_w = jnp.transpose(fin[..., 2 * HALF :], (0, 2, 1, 3)).reshape(96, D).astype(F32)
    qkv_w = (
        jnp.transpose(finq.reshape(2, CHIPS, PIECE, 3, GROUP), (0, 2, 3, 1, 4))
        .reshape(96, 3 * D)
        .astype(F32)
    )

    def part(vector, width=96):
        return lax.dynamic_slice_in_dim(vector, b * width, width, 0)

    return (
        layer_out.reshape(tokens.shape),
        tok_out.reshape(tokens.shape),
        qkv_w,
        part(vb[0:4, :GROUP].reshape(D)),
        part(vb[4:8, :GROUP].reshape(D)),
        out_w,
        part(va[0]),
        part(vb[8]),
        part(vb[9]),
        part(va[1]),
        part(va[2]),
        up,
        part(va[4:8].reshape(FF), 384),
        down,
        part(va[3]),
    )


def solution(mesh):
    placed = (
        P("seq", "blk", None),
        P("seq", "blk"),
        P("seq", "blk", None),
        P(),
        P(),
        P(),
        P(),
        P(),
        P(),
        P(),
        P(),
        P(),
        P(),
        P(),
        P(),
        P(),
    )
    chosen = chip_body if mesh.shape["seq"] == 4 and mesh.shape["blk"] == 8 else body
    return jax.shard_map(
        chosen,
        mesh=mesh,
        in_specs=placed,
        out_specs=(
            P("seq", "blk", None),
            P("seq", "blk", None),
            P("blk", None),
            P("blk"),
            P("blk"),
            P("blk", None),
            P("blk"),
            P("blk"),
            P("blk"),
            P("blk"),
            P("blk"),
            P("blk", None),
            P("blk"),
            P(None, "blk"),
            P("blk"),
        ),
        check_vma=False,
    )
```

```python
import functools
import math

import jax
import jax.numpy as jnp
from jax import lax
from jax.experimental import pallas as pl
from jax.experimental.pallas import tpu as pltpu
from jax.sharding import PartitionSpec as P

HEADS = 12
HEAD = 64
SHORT_LO = 25


EPS = 1e-06


def layer_norm(inputs, norm_gain, norm_shift):
    centre = inputs - jnp.mean(inputs, axis=-1, keepdims=True)
    spread = jnp.mean(centre * centre, axis=-1, keepdims=True)
    return centre * lax.rsqrt(spread + EPS) * norm_gain + norm_shift


def gelu_exact(inputs):
    return jax.nn.gelu(inputs, approximate=False)


def score_block(queries, query_segs, key_rows, key_segs):
    raw_scores = jnp.einsum("qhd,khd->hqk", queries, key_rows, preferred_element_type=jnp.float32)
    same_image = (query_segs[:, None] == key_segs[None, :])[None]
    return jnp.where(same_image, jnp.exp(raw_scores * (1.0 / math.sqrt(HEAD))), 0.0)


def forward_step(carried, queries, query_segs, key_rows, value_rows, key_segs):
    totals, summed = carried
    weights = score_block(queries, query_segs, key_rows, key_segs)
    totals = totals + jnp.transpose(jnp.sum(weights, axis=-1))
    summed = summed + jnp.einsum(
        "hqk,khd->qhd", weights.astype(jnp.bfloat16), value_rows, preferred_element_type=jnp.float32
    )
    return (totals, summed)


def back_step(queries, query_grads, query_corr, query_segs, key_rows, value_rows, key_segs):
    weights = score_block(queries, query_segs, key_rows, key_segs)
    product = jnp.einsum(
        "qhd,khd->hqk", query_grads, value_rows, preferred_element_type=jnp.float32
    )
    shifted = jnp.transpose(query_corr.astype(jnp.float32))[:, :, None]
    score_grads = (weights * (product - shifted) * (1.0 / math.sqrt(HEAD))).astype(jnp.bfloat16)
    return (weights.astype(jnp.bfloat16), score_grads)


def key_value_grads(queries, query_grads, query_corr, query_segs, key_rows, value_rows, key_segs):
    weights_low, score_grads = back_step(
        queries, query_grads, query_corr, query_segs, key_rows, value_rows, key_segs
    )
    key_part = jnp.einsum("hqk,qhd->khd", score_grads, queries, preferred_element_type=jnp.float32)
    value_part = jnp.einsum(
        "hqk,qhd->khd", weights_low, query_grads, preferred_element_type=jnp.float32
    )
    return (key_part, value_part)


def body(
    tokens,
    segment_ids,
    out_grad,
    query_key_value_weight,
    query_bias,
    value_bias,
    attention_output_weight,
    attention_output_bias,
    first_gain,
    first_shift,
    second_gain,
    second_shift,
    mlp_input_weight,
    mlp_input_bias,
    mlp_output_weight,
    mlp_output_bias,
):
    model_width = tokens.shape[-1]
    row_count = tokens.shape[0] * tokens.shape[1]
    head_shape = (row_count, HEADS, HEAD)
    pad_number = tokens.shape[1] * lax.axis_size("blk") // SHORT_LO + 2
    token_rows = tokens.reshape(row_count, model_width).astype(jnp.float32)
    seg_rows = segment_ids.reshape(row_count)
    live_rows = (seg_rows != pad_number).astype(jnp.float32)
    first_normed, first_back = jax.vjp(
        layer_norm, token_rows, first_gain.astype(jnp.float32), first_shift.astype(jnp.float32)
    )
    first_low = first_normed.astype(jnp.bfloat16)
    query_key_value_bias = jnp.concatenate(
        [
            query_bias.astype(jnp.float32),
            jnp.zeros((model_width,), jnp.float32),
            value_bias.astype(jnp.float32),
        ]
    )
    projected_rows = (
        jnp.dot(first_low, query_key_value_weight, preferred_element_type=jnp.float32)
        + query_key_value_bias
    )
    query_flat = projected_rows[:, :model_width].astype(jnp.bfloat16)
    key_flat = projected_rows[:, model_width : 2 * model_width].astype(jnp.bfloat16)
    value_flat = projected_rows[:, 2 * model_width :].astype(jnp.bfloat16)
    queries = query_flat.reshape(head_shape)
    gathered = (
        lax.all_gather(key_flat, "blk", axis=0, tiled=True),
        lax.all_gather(value_flat, "blk", axis=0, tiled=True),
        lax.all_gather(seg_rows, "blk", axis=0, tiled=True),
    )
    all_keys = gathered[0].reshape(-1, HEADS, HEAD)
    all_values = gathered[1].reshape(-1, HEADS, HEAD)
    all_segs = gathered[2]
    seq_rows = all_keys.shape[0]
    key_span = math.gcd(seq_rows, 2048)
    turns = seq_rows // key_span

    def forward_turn(index, carried):
        begin_row = index * key_span
        return forward_step(
            carried,
            queries,
            seg_rows,
            lax.dynamic_slice_in_dim(all_keys, begin_row, key_span, 0),
            lax.dynamic_slice_in_dim(all_values, begin_row, key_span, 0),
            lax.dynamic_slice_in_dim(all_segs, begin_row, key_span, 0),
        )

    totals, summed = lax.fori_loop(
        0,
        turns,
        forward_turn,
        (jnp.zeros((row_count, HEADS), jnp.float32), jnp.zeros(head_shape, jnp.float32)),
    )
    attended = summed / totals[:, :, None] * live_rows[:, None, None]
    merged_heads = attended.reshape(row_count, model_width).astype(jnp.bfloat16)
    residual = (
        token_rows
        + jnp.dot(merged_heads, attention_output_weight, preferred_element_type=jnp.float32)
        + attention_output_bias.astype(jnp.float32)
    )
    second_normed, second_back = jax.vjp(
        layer_norm, residual, second_gain.astype(jnp.float32), second_shift.astype(jnp.float32)
    )
    second_low = second_normed.astype(jnp.bfloat16)
    hidden_rows = jnp.dot(
        second_low, mlp_input_weight, preferred_element_type=jnp.float32
    ) + mlp_input_bias.astype(jnp.float32)
    gelu_active, gelu_back = jax.vjp(gelu_exact, hidden_rows)
    active_low = gelu_active.astype(jnp.bfloat16)
    layer_rows = (
        residual
        + jnp.dot(active_low, mlp_output_weight, preferred_element_type=jnp.float32)
        + mlp_output_bias.astype(jnp.float32)
    )
    layer_out = layer_rows.astype(jnp.bfloat16).reshape(tokens.shape)
    grad_rows = out_grad.reshape(row_count, model_width)
    down_weight_grad = jnp.einsum(
        "tf,td->fd", active_low, grad_rows, preferred_element_type=jnp.float32
    )
    down_bias_grad = jnp.sum(grad_rows.astype(jnp.float32), axis=0)
    active_grad = jnp.einsum(
        "td,fd->tf", grad_rows, mlp_output_weight, preferred_element_type=jnp.float32
    )
    (hidden_grad,) = gelu_back(active_grad)
    hidden_low = hidden_grad.astype(jnp.bfloat16)
    up_weight_grad = jnp.einsum(
        "td,tf->df", second_low, hidden_low, preferred_element_type=jnp.float32
    )
    up_bias_grad = jnp.sum(hidden_low.astype(jnp.float32), axis=0)
    normed_grad = jnp.einsum(
        "tf,df->td", hidden_low, mlp_input_weight, preferred_element_type=jnp.float32
    )
    resid_part, second_gain_grad, second_shift_grad = second_back(normed_grad)
    residual_grad = grad_rows.astype(jnp.float32) + resid_part
    branch_low = residual_grad.astype(jnp.bfloat16)
    out_weight_grad = jnp.einsum(
        "ti,to->io", merged_heads, branch_low, preferred_element_type=jnp.float32
    )
    out_bias_grad = jnp.sum(branch_low.astype(jnp.float32), axis=0)
    attended_grad = (
        jnp.einsum(
            "to,io->ti", branch_low, attention_output_weight, preferred_element_type=jnp.float32
        ).reshape(head_shape)
        * live_rows[:, None, None]
    )
    query_grads = (attended_grad / totals[:, :, None]).astype(jnp.bfloat16)
    corrections = (jnp.sum(attended_grad * attended, axis=-1) / totals).astype(jnp.bfloat16)

    def query_turn(index, carried):
        begin_row = index * key_span
        key_rows = lax.dynamic_slice_in_dim(all_keys, begin_row, key_span, 0)
        weights_low, score_grads = back_step(
            queries,
            query_grads,
            corrections,
            seg_rows,
            key_rows,
            lax.dynamic_slice_in_dim(all_values, begin_row, key_span, 0),
            lax.dynamic_slice_in_dim(all_segs, begin_row, key_span, 0),
        )
        return carried + jnp.einsum(
            "hqk,khd->qhd", score_grads, key_rows, preferred_element_type=jnp.float32
        )

    query_sum = lax.fori_loop(0, turns, query_turn, jnp.zeros(head_shape, jnp.float32))
    term_span = math.gcd(row_count * lax.axis_size("blk"), 2048)

    def term_block(index):
        begin_row = index * term_span
        key_part, value_part = key_value_grads(
            queries,
            query_grads,
            corrections,
            seg_rows,
            lax.dynamic_slice_in_dim(all_keys, begin_row, term_span, 0),
            lax.dynamic_slice_in_dim(all_values, begin_row, term_span, 0),
            lax.dynamic_slice_in_dim(all_segs, begin_row, term_span, 0),
        )
        return jnp.concatenate(
            [key_part.reshape(term_span, model_width), value_part.reshape(term_span, model_width)],
            axis=1,
        )

    blocks = lax.map(
        term_block, jnp.arange(row_count * lax.axis_size("blk") // term_span, dtype=jnp.int32)
    )
    key_terms = lax.psum_scatter(
        blocks.reshape(row_count * lax.axis_size("blk"), 2 * model_width),
        "blk",
        scatter_dimension=0,
        tiled=True,
    )
    query_low = query_sum.reshape(row_count, model_width).astype(jnp.bfloat16)
    key_low = key_terms[:, :model_width].astype(jnp.bfloat16)
    value_low = key_terms[:, model_width:].astype(jnp.bfloat16)
    qkv_grad = jnp.concatenate([query_low, key_low, value_low], axis=1)
    qkv_weight_grad = jnp.einsum(
        "td,tj->dj", first_low, qkv_grad, preferred_element_type=jnp.float32
    )
    query_bias_grad = jnp.sum(query_low.astype(jnp.float32), axis=0)
    value_bias_grad = jnp.sum(value_low.astype(jnp.float32), axis=0)
    first_grad = jnp.einsum(
        "tj,dj->td", qkv_grad, query_key_value_weight, preferred_element_type=jnp.float32
    )
    token_part, first_gain_grad, first_shift_grad = first_back(first_grad)
    tokens_grad = (residual_grad + token_part).astype(jnp.bfloat16).reshape(tokens.shape)
    local_grads = (
        qkv_weight_grad,
        query_bias_grad,
        value_bias_grad,
        out_weight_grad,
        out_bias_grad,
        first_gain_grad,
        first_shift_grad,
        second_gain_grad,
        second_shift_grad,
        up_weight_grad,
        up_bias_grad,
        down_weight_grad,
        down_bias_grad,
    )
    scattered = (
        lax.psum_scatter(local_grads[0], "blk", scatter_dimension=0, tiled=True),
        lax.psum_scatter(local_grads[1], "blk", scatter_dimension=0, tiled=True),
        lax.psum_scatter(local_grads[2], "blk", scatter_dimension=0, tiled=True),
        lax.psum_scatter(local_grads[3], "blk", scatter_dimension=0, tiled=True),
        lax.psum_scatter(local_grads[4], "blk", scatter_dimension=0, tiled=True),
        lax.psum_scatter(local_grads[5], "blk", scatter_dimension=0, tiled=True),
        lax.psum_scatter(local_grads[6], "blk", scatter_dimension=0, tiled=True),
        lax.psum_scatter(local_grads[7], "blk", scatter_dimension=0, tiled=True),
        lax.psum_scatter(local_grads[8], "blk", scatter_dimension=0, tiled=True),
        lax.psum_scatter(local_grads[9], "blk", scatter_dimension=0, tiled=True),
        lax.psum_scatter(local_grads[10], "blk", scatter_dimension=0, tiled=True),
        lax.psum_scatter(local_grads[11], "blk", scatter_dimension=1, tiled=True),
        lax.psum_scatter(local_grads[12], "blk", scatter_dimension=0, tiled=True),
    )
    summed_grads = lax.psum(
        (
            scattered[0],
            scattered[1],
            scattered[2],
            scattered[3],
            scattered[4],
            scattered[5],
            scattered[6],
            scattered[7],
            scattered[8],
            scattered[9],
            scattered[10],
            scattered[11],
            scattered[12],
        ),
        "seq",
    )
    return (layer_out, tokens_grad) + tuple(summed_grads)


VMEM_LIMIT = 64 * 1024 * 1024
D = 768
FF = 3072
ROWS = 192
CHIPS = 4
GROUP = 192
QKV = 3 * GROUP
HALF = FF // 2
OUT_HALF = D // 2
PIECE = 48
TILE = 256
TILES = HALF // TILE
PACK = ROWS // 2
KEYS = 1536
OWN = 768
LOW = jnp.bfloat16
F32 = jnp.float32
MESH = pl.DeviceIdType.MESH


def dot(a, b):
    return jnp.dot(a, b, preferred_element_type=F32)


def dot_nt(a, b):
    return lax.dot_general(a, b, (((1,), (1,)), ((), ())), preferred_element_type=F32)


def scratch_list():
    dma = pltpu.SemaphoreType.DMA
    vmem = pltpu.VMEM
    return dict(
        nrm=vmem((CHIPS, ROWS, D), LOW),
        xhat1=vmem((ROWS, D), F32),
        rstd1=vmem((ROWS, 1), F32),
        par=vmem((8, D), F32),
        qvb=vmem((2, CHIPS, GROUP), F32),
        b1=vmem((1, FF), F32),
        wf=vmem((D, 3 * D), LOW),
        wo=vmem((D, D), LOW),
        w2=vmem((HALF, D), LOW),
        q=vmem((3, OWN, 2 * HEAD), LOW),
        kvo=vmem((CHIPS, ROWS, 2 * GROUP), LOW),
        kvs=vmem((CHIPS, ROWS, 2 * GROUP), LOW),
        kh=vmem((3, KEYS, HEAD), LOW),
        vh=vmem((3, KEYS, 2 * HEAD), LOW),
        segs=vmem((2, CHIPS, 8, ROWS), jnp.int32),
        kseg=vmem((1, KEYS), jnp.int32),
        qseg=vmem((OWN, 128), jnp.int32),
        prob=vmem((3, OWN, KEYS), LOW),
        att=vmem((3, OWN, 2 * HEAD), F32),
        mgs=vmem((CHIPS, PACK, 2 * GROUP), LOW),
        mgr=vmem((CHIPS, PACK, 2 * GROUP), LOW),
        mgo=vmem((CHIPS, PACK, 2 * GROUP), LOW),
        mg=vmem((CHIPS, ROWS, GROUP), LOW),
        mgt=vmem((CHIPS, GROUP, 2 * ROWS), LOW),
        og=vmem((2, ROWS, D), LOW),
        nt=vmem((2, ROWS, D), LOW),
        bl=vmem((2, ROWS, D), LOW),
        ogt=vmem((D, 2 * ROWS), LOW),
        ntt=vmem((D, 2 * ROWS), LOW),
        resid=vmem((ROWS, D), F32),
        xhat2=vmem((ROWS, D), F32),
        rstd2=vmem((ROWS, 1), F32),
        act=vmem((2 * ROWS, HALF), LOW),
        hg=vmem((2 * ROWS, HALF), LOW),
        lo=vmem((2, ROWS, D), F32),
        ng=vmem((2, ROWS, D), F32),
        lor=vmem((ROWS, D), F32),
        ngr=vmem((ROWS, D), F32),
        ags=vmem((CHIPS, PACK, 2 * GROUP), LOW),
        ag=vmem((CHIPS, PACK, 2 * GROUP), LOW),
        agh=vmem((3, OWN, HEAD), LOW),
        dqs=vmem((3, CHIPS, PACK, 2 * GROUP), LOW),
        dqr=vmem((3, CHIPS, PACK, 2 * GROUP), LOW),
        rowg=vmem((ROWS, 3 * D), LOW),
        dkt=vmem((3, HEAD, KEYS), F32),
        dvt=vmem((3, HEAD, KEYS), F32),
        dkr=vmem((3, HEAD, OWN), F32),
        dvr=vmem((3, HEAD, OWN), F32),
        dqkv=vmem((OWN, QKV), LOW),
        nrmt=vmem((CHIPS, D, ROWS), LOW),
        da=vmem((TILES, CHIPS, 2, 2, PIECE, TILE), LOW),
        db=vmem((TILES, CHIPS, 2, 2, PIECE, TILE), LOW),
        ra=vmem((TILES, CHIPS, 2, PIECE, TILE), LOW),
        rb=vmem((TILES, CHIPS, 2, PIECE, TILE), LOW),
        a2s=vmem((TILES, CHIPS, PIECE, TILE), LOW),
        b2s=vmem((TILES, CHIPS, PIECE, TILE), LOW),
        a2r=vmem((TILES, CHIPS, PIECE, TILE), LOW),
        b2r=vmem((TILES, CHIPS, PIECE, TILE), LOW),
        zs=vmem((TILES, CHIPS, 2, PIECE, TILE), LOW),
        rz=vmem((TILES, CHIPS, 2, PIECE, TILE), LOW),
        fin=vmem((TILES, 2, PIECE, TILE), LOW),
        oa=vmem((2, 2, 2, PIECE, OUT_HALF), LOW),
        ob=vmem((2, 2, 2, PIECE, OUT_HALF), LOW),
        roa=vmem((2, 2, PIECE, OUT_HALF), LOW),
        rob=vmem((2, 2, PIECE, OUT_HALF), LOW),
        oa2s=vmem((2, PIECE, OUT_HALF), LOW),
        ob2s=vmem((2, PIECE, OUT_HALF), LOW),
        oa2r=vmem((2, PIECE, OUT_HALF), LOW),
        ob2r=vmem((2, PIECE, OUT_HALF), LOW),
        zo=vmem((CHIPS, PIECE, OUT_HALF), LOW),
        rzo=vmem((CHIPS, PIECE, OUT_HALF), LOW),
        fo=vmem((PIECE, OUT_HALF), LOW),
        dwq=vmem((CHIPS, 4, PIECE, QKV), LOW),
        dwqr=vmem((2, 4, PIECE, QKV), LOW),
        dwqx=vmem((2, 4, PIECE, QKV), LOW),
        rxq=vmem((3, 2, PIECE, QKV), LOW),
        zq=vmem((2, PIECE, QKV), LOW),
        rzq=vmem((CHIPS, PIECE, QKV), LOW),
        va=vmem((16, D), F32),
        var=vmem((8, 16, D), F32),
        vax=vmem((16, D), F32),
        vaxr=vmem((4, 16, D), F32),
        vb=vmem((16, D), F32),
        vbr=vmem((8, 16, D), F32),
        vbx=vmem((16, D), F32),
        vbxr=vmem((4, 16, D), F32),
        load_sem=dma((3 + TILES,)),
        seg_s=dma((7,)), seg_r=dma((7,)),
        og_s=dma((1,)), og_r=dma((1,)),
        nu_s=dma((CHIPS,)), nd_s=dma((CHIPS,)), n_r=dma((CHIPS,)),
        kv_s=dma((CHIPS,)), kv_r=dma((CHIPS,)),
        mg_s=dma((CHIPS,)), mg_r=dma((CHIPS,)),
        mgo_s=dma((1,)), mgo_r=dma((1,)),
        nt_s=dma((1,)), nt_r=dma((1,)),
        lo_s=dma((1,)), lo_r=dma((1,)),
        ng_s=dma((1,)), ng_r=dma((1,)),
        bl_s=dma((1,)), bl_r=dma((1,)),
        ag_s=dma((CHIPS,)), ag_r=dma((CHIPS,)),
        dk_s=dma((3,)), dk_r=dma((3,)),
        dv_s=dma((3,)), dv_r=dma((3,)),
        dq_s=dma((3, CHIPS)), dq_r=dma((3, CHIPS)),
        a1_s=dma((TILES + 1,)), a1_r=dma((TILES + 1,)),
        b1_s=dma((TILES + 1,)), b1_r=dma((TILES + 1,)),
        a2_s=dma((TILES + 1,)), a2_r=dma((TILES + 1,)),
        b2_s=dma((TILES + 1,)), b2_r=dma((TILES + 1,)),
        z_s=dma((TILES + 1, CHIPS)), z_r=dma((TILES + 1, CHIPS)),
        f_s=dma((TILES + 1, 4)), f_r=dma((TILES + 1, 4)),
        q0_s=dma((1,)), q0_r=dma((1,)),
        qx_s=dma((3,)), qx_r=dma((3,)),
        qz_s=dma((2,)), qz_r=dma((CHIPS,)),
        qf_s=dma((3,)), qf_r=dma((3,)),
        va_s=dma((7,)), va_r=dma((7,)),
        vax_s=dma((3,)), vax_r=dma((3,)),
        vb_s=dma((7,)), vb_r=dma((7,)),
        vbx_s=dma((3,)), vbx_r=dma((3,)),
    )


EARLY = 2
SERVICE_ONE = ((1, 0), (3, 1), (5, 2), (7, 3), (9, 4), (11, 5))
SERVICE_TWO = ()
LATE_ONE = (6,)
LATE_TWO = (0, 1, 2, 3, 4, 5, 6)


class Box:
    pass


def kernel_body(names, pad_number, *refs):
    (tok, seg, ogi, wqkv, wo_h, w1_h, w2_h) = refs[:7]
    vectors = refs[7:15]
    b1_in = refs[15]
    (out_tok, out_layer, out_fin, out_fo, out_finq, out_va, out_vb) = refs[16:23]
    r = Box()
    for name, ref in zip(names, refs[23:]):
        setattr(r, name, ref)
    par, qvb, b1 = r.par, r.qvb, r.b1

    s = lax.axis_index("seq")
    b = lax.axis_index("blk")
    z = b // 2
    c = b % 2
    sib = 2 * z + 1 - c
    flip = {1: s + 1 - 2 * (s % 2), 2: (s + 2) % 4, 3: 3 - s}
    x = s % 2
    y = s // 2

    pending = []

    def send(src, dst, ssem, rsem, dev_s, dev_b):
        return pltpu.make_async_remote_copy(
            src_ref=src, dst_ref=dst, send_sem=ssem, recv_sem=rsem,
            device_id=(dev_s, dev_b), device_id_type=MESH,
        )

    def local_row(index):
        return par[index : index + 1, :]

    loads = []
    loads.append(pltpu.make_async_copy(wqkv, r.wf, r.load_sem.at[0]))
    half = pl.multiple_of(c * HALF, 128)
    loads.append(pltpu.make_async_copy(wo_h, r.wo, r.load_sem.at[1]))
    loads.append(pltpu.make_async_copy(w2_h.at[pl.ds(half, HALF), :], r.w2, r.load_sem.at[2]))
    for tile in range(TILES):
        cols = pl.ds(pl.multiple_of(c * HALF + tile * TILE, TILE), TILE)
        loads.append(
            pltpu.make_async_copy(
                w1_h.at[:, :, :, :, cols], r.da.at[tile], r.load_sem.at[3 + tile]
            )
        )
    for item in loads:
        item.start()

    for index, vector in enumerate(vectors):
        par[index : index + 1, :] = vector[...].astype(F32).reshape(1, D)
    for slot in range(CHIPS):
        part = slice(slot * GROUP, (slot + 1) * GROUP)
        qvb[0, slot : slot + 1, :] = par[0:1, part]
        qvb[1, slot : slot + 1, :] = par[1:2, part]
    b1[...] = b1_in[...].astype(F32).reshape(1, FF)

    barrier = pltpu.get_barrier_semaphore()
    for step in range(1, 8):
        pl.semaphore_signal(barrier, inc=1, device_id=(s, (b + step) % 8), device_id_type=MESH)
    for step in (1, 2, 3):
        for core in range(2):
            pl.semaphore_signal(
                barrier, inc=1, device_id=(flip[step], 2 * z + core), device_id_type=MESH
            )
    pl.semaphore_wait(barrier, 13)

    r.segs[c, z] = jnp.broadcast_to(seg[...], (8, ROWS))
    seg_copies = []
    for step in range(1, 8):
        seg_copies.append(
            send(r.segs.at[c, z], r.segs.at[c, z], r.seg_s.at[step - 1], r.seg_r.at[step - 1],
                 s, (b + step) % 8)
        )
    for item in seg_copies:
        item.start()
    pending.extend(seg_copies)

    def first_norm(index, carried):
        rows = pl.ds(index * PIECE, PIECE)
        x = tok[rows, :].astype(F32)
        centre = x - jnp.mean(x, axis=-1, keepdims=True)
        spread = lax.rsqrt(jnp.mean(centre * centre, axis=-1, keepdims=True) + EPS)
        xhat = centre * spread
        r.xhat1[rows, :] = xhat
        r.rstd1[rows, :] = spread
        r.nrm[z, rows, :] = (xhat * local_row(3) + local_row(4)).astype(LOW)
        return carried

    lax.fori_loop(0, 4, first_norm, 0)

    def norm_copy(slot, up):
        if up:
            return send(r.nrm.at[slot], r.nrm.at[slot], r.nu_s.at[slot], r.n_r.at[slot], s, b + 2)
        return send(r.nrm.at[slot], r.nrm.at[slot], r.nd_s.at[slot], r.n_r.at[slot], s, b - 2)

    def norm_forward(slot):
        @pl.when(jnp.logical_and(slot <= z, z < 3))
        def _():
            norm_copy(slot, True).start()

        @pl.when(jnp.logical_and(slot >= z, z > 0))
        def _():
            norm_copy(slot, False).start()

    norm_forward(z)

    r.og[c] = ogi[...]
    og_copy = send(r.og.at[c], r.og.at[c], r.og_s.at[0], r.og_r.at[0], s, sib)
    og_copy.start()
    pending.append(og_copy)

    loads[0].wait()
    for part in range(3):
        start = pl.multiple_of(D * part + 384 * (z // 2) + 128 * (z % 2), 128)
        window = r.wf[:, pl.ds(start, 256)]
        r.dqkv[:, part * GROUP : (part + 1) * GROUP] = jnp.where(
            z % 2 == 1, window[:, 64:256], window[:, 0:192]
        )

    upper = z // 2
    near = z * (1 - upper) + (3 - z) * upper
    qkv_bias = [qvb[0, pl.ds(z, 1), :], None, qvb[1, pl.ds(z, 1), :]]

    def split_keys(pair, row):
        for h in range(3):
            r.kh[h, pl.ds(row, ROWS), :] = pair[:, h * HEAD : (h + 1) * HEAD]
            r.vh[h, pl.ds(row, ROWS), 0:HEAD] = pair[:, GROUP + h * HEAD : GROUP + (h + 1) * HEAD]
            r.vh[h, pl.ds(row, ROWS), HEAD : 2 * HEAD] = jnp.ones((ROWS, HEAD), LOW)

    def kv_copy(slot):
        return send(r.kvo.at[slot], r.kvs.at[slot], r.kv_s.at[slot], r.kv_r.at[slot], s, sib)

    def project(index, carried):
        seq_slot = jnp.where(index == 0, near, jnp.where(index == 1, 1 - near, index))
        slot = seq_slot * (1 - upper) + (3 - seq_slot) * upper

        @pl.when(index > 0)
        def _():
            norm_copy(slot, True).wait_recv()
            norm_forward(slot)

        rows = r.nrm[slot]
        whole = dot(rows, r.dqkv[...])
        qs = (whole[:, :GROUP] + qkv_bias[0]).astype(LOW)
        ks = whole[:, GROUP : 2 * GROUP].astype(LOW)
        vs = (whole[:, 2 * GROUP :] + qkv_bias[2]).astype(LOW)
        for h in range(3):
            r.q[h, pl.ds(slot * ROWS, ROWS), 0:HEAD] = qs[:, h * HEAD : (h + 1) * HEAD]
        r.kvo[slot, :, 0:GROUP] = ks
        r.kvo[slot, :, GROUP : 2 * GROUP] = vs
        kv_copy(slot).start()
        split_keys(r.kvo[slot], slot * ROWS)
        return carried

    lax.fori_loop(0, CHIPS, project, 0)

    for item in seg_copies:
        item.wait_recv()
    for slot in range(CHIPS):
        for side, core in ((0, c), (1, 1 - c)):
            r.kseg[:, (side * CHIPS + slot) * ROWS : (side * CHIPS + slot + 1) * ROWS] = r.segs[
                core, slot, 0:1, :
            ]
        line = r.segs[c, slot, 0:1, :].astype(F32)
        r.qseg[slot * ROWS : (slot + 1) * ROWS, :] = jnp.transpose(
            jnp.broadcast_to(line, (128, ROWS))
        ).astype(jnp.int32)

    def take_sibling(slot, carried):
        kv_copy(slot).wait_recv()
        split_keys(r.kvs[slot], OWN + slot * ROWS)
        return carried

    lax.fori_loop(0, CHIPS, take_sibling, 0)

    SPAN = 256
    TURNS = KEYS // SPAN

    def pack(ref, index, lane, value):
        width = value.shape[1]
        ref[index, :, lane : lane + width] = value[0:PACK]
        ref[index, :, GROUP + lane : GROUP + lane + width] = value[PACK:ROWS]

    def mg_copy(block):
        return send(r.mgs.at[block], r.mgr.at[z], r.mg_s.at[block], r.mg_r.at[z], s, 2 * block + c)

    def mg_arrival(slot):
        return send(r.mgs.at[slot], r.mgr.at[slot], r.mg_s.at[slot], r.mg_r.at[slot], s, 2 * slot + c)

    def forward_block(index, carried):
        block = (z + 1 + index) % CHIPS
        rows = pl.ds(pl.multiple_of(block * ROWS, ROWS), ROWS)
        own_segs = r.qseg[rows, :]
        wide = jnp.concatenate([own_segs] * (SPAN // 128), axis=1)
        live = jnp.where(own_segs[:, :HEAD] != pad_number, 1.0, 0.0).astype(F32)
        for h in range(3):
            qs = r.q[h, rows, 0:HEAD]
            total = jnp.zeros((ROWS, 2 * HEAD), F32)
            for turn in range(TURNS):
                cols = slice(turn * SPAN, (turn + 1) * SPAN)
                raw = dot_nt(qs, r.kh[h, cols, :])
                weights = jnp.where(
                    wide == r.kseg[:, cols], jnp.exp(raw * (1.0 / math.sqrt(HEAD))), 0.0
                ).astype(LOW)
                r.prob[h, rows, cols] = weights
                total = total + dot(weights, r.vh[h, cols, :])
            inverse = 1.0 / total[:, HEAD:]
            attended = total[:, :HEAD] * inverse * live
            r.att[h, rows, 0:HEAD] = attended
            r.att[h, rows, HEAD : 2 * HEAD] = inverse
            pack(r.mgs, block, h * HEAD, attended.astype(LOW))

        @pl.when(block != z)
        def _():
            mg_copy(block).start()

        @pl.when(block == z)
        def _():
            r.mgr[z] = r.mgs[z]

        return carried

    lax.fori_loop(0, CHIPS, forward_block, 0)

    def others(fn):
        def run(index, carried):
            fn((z + 1 + index) % CHIPS)
            return carried

        lax.fori_loop(0, CHIPS - 1, run, 0)

    others(lambda slot: mg_arrival(slot).wait_recv())
    mgo_copy = send(r.mgr, r.mgo, r.mgo_s.at[0], r.mgo_r.at[0], s, sib)
    mgo_copy.start()
    pending.append(mgo_copy)

    for slot in range(CHIPS):
        r.mg[slot, 0:PACK, :] = r.mgr[slot, :, 0:GROUP]
        r.mg[slot, PACK:ROWS, :] = r.mgr[slot, :, GROUP : 2 * GROUP]

    loads[1].wait()

    def out_projection(index, carried):
        cols = pl.ds(pl.multiple_of(index * 256, 256), 256)
        total = tok[:, cols].astype(F32) + par[2:3, cols]
        for slot in range(CHIPS):
            total = total + dot(r.mg[slot], r.wo[slot * GROUP : (slot + 1) * GROUP, cols])
        r.resid[:, cols] = total
        return carried

    lax.fori_loop(0, 3, out_projection, 0)

    def second_norm(index, carried):
        rows = pl.ds(index * PIECE, PIECE)
        x = r.resid[rows, :]
        centre = x - jnp.mean(x, axis=-1, keepdims=True)
        spread = lax.rsqrt(jnp.mean(centre * centre, axis=-1, keepdims=True) + EPS)
        xhat = centre * spread
        r.xhat2[rows, :] = xhat
        r.rstd2[rows, :] = spread
        r.nt[c, rows, :] = (xhat * local_row(5) + local_row(6)).astype(LOW)
        return carried

    lax.fori_loop(0, 4, second_norm, 0)
    nt_copy = send(r.nt.at[c], r.nt.at[c], r.nt_s.at[0], r.nt_r.at[0], s, sib)
    nt_copy.start()
    pending.append(nt_copy)
    for item in loads[2:]:
        item.wait()
    og_copy.wait_recv()
    r.va[...] = jnp.zeros((16, D), F32)
    r.vb[...] = jnp.zeros((16, D), F32)
    r.va[3:4, :] = jnp.sum(ogi[...].astype(F32), axis=0, keepdims=True)
    for core in range(2):
        r.ogt[:, core * ROWS : (core + 1) * ROWS] = jnp.transpose(r.og[core])
    nt_copy.wait_recv()

    r.lo[...] = jnp.zeros((2, ROWS, D), F32)
    r.ng[...] = jnp.zeros((2, ROWS, D), F32)

    def mlp_tile(index, carried):
        cols = pl.ds(pl.multiple_of(index * TILE, TILE), TILE)
        bias = b1[:, pl.ds(pl.multiple_of(c * HALF + index * TILE, TILE), TILE)]
        total = jnp.zeros((1, TILE), F32)
        w1 = r.da[index].reshape(D, TILE)
        for core in range(2):
            rows = slice(core * ROWS, (core + 1) * ROWS)
            hidden = dot(r.nt[core], w1) + bias
            gate = 0.5 * (1.0 + lax.erf(hidden * (1.0 / math.sqrt(2.0))))
            slope = gate + hidden * jnp.exp(-0.5 * hidden * hidden) * (1.0 / math.sqrt(2.0 * math.pi))
            active = (hidden * gate).astype(LOW)
            grad = (slope * dot_nt(r.og[core], r.w2[cols, :])).astype(LOW)
            r.act[rows, cols] = active
            r.hg[rows, cols] = grad
            total = total + jnp.sum(grad.astype(F32), axis=0, keepdims=True)
            r.lo[core] = r.lo[core] + dot(active, r.w2[cols, :])
            r.ng[core] = r.ng[core] + dot_nt(grad, w1)
        r.va[pl.ds(4 + 2 * c + index // 3, 1), pl.ds(pl.multiple_of((index % 3) * TILE, TILE), TILE)] = total
        return carried

    lax.fori_loop(0, HALF // TILE, mlp_tile, 0)
    ng_copy = send(r.ng.at[1 - c], r.ngr, r.ng_s.at[0], r.ng_r.at[0], s, sib)
    lo_copy = send(r.lo.at[1 - c], r.lor, r.lo_s.at[0], r.lo_r.at[0], s, sib)
    ng_copy.start()
    lo_copy.start()
    pending.extend([ng_copy, lo_copy])

    def hop_one(unit):
        if isinstance(unit, int) and unit == TILES:
            one, two, to_one, to_two = r.oa, r.ob, r.roa, r.rob
        else:
            one, two, to_one, to_two = r.da.at[unit], r.db.at[unit], r.ra.at[unit], r.rb.at[unit]
        return (
            send(one.at[:, :, 1 - x], to_one, r.a1_s.at[unit], r.a1_r.at[unit], flip[1], b),
            send(two.at[:, 1 - y], to_two, r.b1_s.at[unit], r.b1_r.at[unit], flip[2], b),
        )

    def hop_two(unit):
        if isinstance(unit, int) and unit == TILES:
            one, two, to_one, to_two = r.oa2s, r.ob2s, r.oa2r, r.ob2r
        else:
            one, two, to_one, to_two = (
                r.a2s.at[unit], r.b2s.at[unit], r.a2r.at[unit], r.b2r.at[unit]
            )
        return (
            send(one, to_one, r.a2_s.at[unit], r.a2_r.at[unit], flip[2], b),
            send(two, to_two, r.b2_s.at[unit], r.b2_r.at[unit], flip[1], b),
        )

    def z_copy(unit, block):
        if isinstance(unit, int) and unit == TILES:
            here, there = r.zo.at[block], r.rzo.at[z]
        else:
            here, there = r.zs.at[unit, block], r.rz.at[unit, z]
        return send(here, there, r.z_s.at[unit, block], r.z_r.at[unit, z], s, 2 * block + c)

    def z_arrival(unit, slot):
        if isinstance(unit, int) and unit == TILES:
            here, there = r.zo.at[slot], r.rzo.at[slot]
        else:
            here, there = r.zs.at[unit, slot], r.rz.at[unit, slot]
        return send(here, there, r.z_s.at[unit, slot], r.z_r.at[unit, slot], s, 2 * slot + c)

    owner = s // 2
    mine = 2 * z + owner

    def fin_copy(unit, step):
        if isinstance(unit, int) and unit == TILES:
            here, there = r.fo, out_fo.at[s % 2, c]
        else:
            here, there = r.fin.at[unit], out_fin.at[unit, s % 2, c]
        return send(here, there, r.f_s.at[unit, step], r.f_r.at[unit, 2 * (s % 2) + c],
                    s if step == 0 else flip[step], mine)

    def fin_arrival(unit, piece, core):
        if isinstance(unit, int) and unit == TILES:
            here, there = r.fo, out_fo.at[piece, core]
        else:
            here, there = r.fin.at[unit], out_fin.at[unit, piece, core]
        return send(here, there, r.f_s.at[unit, 0], r.f_r.at[unit, 2 * piece + core], s, sib)

    def mlp_grads(tile):
        cols = pl.ds(pl.multiple_of(tile * TILE, TILE), TILE)

        def block_grads(block, carried):
            rows = pl.ds(pl.multiple_of(block * ROWS, ROWS), ROWS)
            one = dot(r.ntt[rows, :], r.hg[:, cols]).astype(LOW)
            two = dot(r.ogt[rows, :], r.act[:, cols]).astype(LOW)
            for piece in range(4):
                part = slice(piece * PIECE, (piece + 1) * PIECE)
                r.da[tile, block, piece // 2, piece % 2] = one[part]
                r.db[tile, block, piece // 2, piece % 2] = two[part]
            return carried

        lax.fori_loop(0, CHIPS, block_grads, 0)
        for item in hop_one(tile):
            item.start()

    def service_one(unit):
        for item in hop_one(unit):
            item.wait_recv()
        if isinstance(unit, int) and unit == TILES:
            for block in range(2):
                r.oa2s[block] = (
                    r.oa[block, 1 - y, x].astype(F32) + r.roa[block, 1 - y].astype(F32)
                ).astype(LOW)
                r.ob2s[block] = (
                    r.ob[block, y, 1 - x].astype(F32) + r.rob[block, 1 - x].astype(F32)
                ).astype(LOW)
        else:
            def add(block, carried):
                r.a2s[unit, block] = (
                    r.da[unit, block, 1 - y, x].astype(F32) + r.ra[unit, block, 1 - y].astype(F32)
                ).astype(LOW)
                r.b2s[unit, block] = (
                    r.db[unit, block, y, 1 - x].astype(F32) + r.rb[unit, block, 1 - x].astype(F32)
                ).astype(LOW)
                return carried

            lax.fori_loop(0, CHIPS, add, 0)
        for item in hop_two(unit):
            item.start()

    def service_two(unit):
        for item in hop_two(unit):
            item.wait_recv()
        if isinstance(unit, int) and unit == TILES:
            for block in range(2):
                r.zo[block] = (
                    r.oa[block, y, x].astype(F32) + r.roa[block, y].astype(F32)
                    + r.oa2r[block].astype(F32)
                ).astype(LOW)
                r.zo[2 + block] = (
                    r.ob[block, y, x].astype(F32) + r.rob[block, x].astype(F32)
                    + r.ob2r[block].astype(F32)
                ).astype(LOW)
        else:
            def add(block, carried):
                r.zs[unit, block, 0] = (
                    r.da[unit, block, y, x].astype(F32) + r.ra[unit, block, y].astype(F32)
                    + r.a2r[unit, block].astype(F32)
                ).astype(LOW)
                r.zs[unit, block, 1] = (
                    r.db[unit, block, y, x].astype(F32) + r.rb[unit, block, x].astype(F32)
                    + r.b2r[unit, block].astype(F32)
                ).astype(LOW)
                return carried

            lax.fori_loop(0, CHIPS, add, 0)
        others(lambda block: z_copy(unit, block).start())

    def service_three(unit):
        others(lambda slot: z_arrival(unit, slot).wait_recv())
        if isinstance(unit, int) and unit == TILES:
            total = r.zo[z].astype(F32)
            for step in range(1, CHIPS):
                total = total + r.rzo[(z + step) % CHIPS].astype(F32)
            r.fo[...] = total.astype(LOW)
        else:
            total = r.zs[unit, z].astype(F32)
            for step in range(1, CHIPS):
                total = total + r.rz[unit, (z + step) % CHIPS].astype(F32)
            r.fin[unit] = total.astype(LOW)
        for step in (1, 2, 3):
            fin_copy(unit, step).start()

        @pl.when(mine != b)
        def _():
            fin_copy(unit, 0).start()

        @pl.when(mine == b)
        def _():
            if isinstance(unit, int) and unit == TILES:
                out_fo[s % 2, c] = r.fo[...]
            else:
                out_fin[unit, s % 2, c] = r.fin[unit]

    for core in range(2):
        r.ntt[:, core * ROWS : (core + 1) * ROWS] = jnp.transpose(r.nt[core])
    def early_grads(tile, carried):
        mlp_grads(tile)
        return carried

    lax.fori_loop(0, EARLY, early_grads, 0)

    ng_copy.wait_recv()

    def second_back(index, carried):
        rows = pl.ds(index * PIECE, PIECE)
        grad = r.ng[c, rows, :] + r.ngr[rows, :]
        xhat = r.xhat2[rows, :]
        scaled = grad * local_row(5)
        mean_one = jnp.mean(scaled, axis=-1, keepdims=True)
        mean_two = jnp.mean(scaled * xhat, axis=-1, keepdims=True)
        through = r.rstd2[rows, :] * (scaled - mean_one - xhat * mean_two)
        resid_grad = ogi[rows, :].astype(F32) + through
        low = resid_grad.astype(LOW)
        r.xhat2[rows, :] = resid_grad
        r.bl[c, rows, :] = low
        r.va[0:1, :] += jnp.sum(low.astype(F32), axis=0, keepdims=True)
        r.va[1:2, :] += jnp.sum(grad * xhat, axis=0, keepdims=True)
        r.va[2:3, :] += jnp.sum(grad, axis=0, keepdims=True)
        return carried

    lax.fori_loop(0, 4, second_back, 0)
    bl_copy = send(r.bl.at[c], r.bl.at[c], r.bl_s.at[0], r.bl_r.at[0], s, sib)
    bl_copy.start()
    pending.append(bl_copy)

    def ag_copy(block):
        return send(r.ags.at[block], r.ag.at[z], r.ag_s.at[block], r.ag_r.at[z], s, 2 * block + c)

    def ag_arrival(slot):
        return send(r.ags.at[slot], r.ag.at[slot], r.ag_s.at[slot], r.ag_r.at[slot], s, 2 * slot + c)

    def attended_block(index, carried):
        block = (z + 1 + index) % CHIPS
        wide = pl.ds(pl.multiple_of(block * GROUP, GROUP), GROUP)
        pack(r.ags, block, 0, dot_nt(r.bl[c], r.wo[wide, :]).astype(LOW))

        @pl.when(block != z)
        def _():
            ag_copy(block).start()

        @pl.when(block == z)
        def _():
            r.ag[z] = r.ags[z]

        return carried

    lax.fori_loop(0, CHIPS, attended_block, 0)

    va_copies = [
        send(r.va, r.var.at[b], r.va_s.at[step - 1], r.va_r.at[step - 1], s, (b + step) % 8)
        for step in range(1, 8)
    ]
    r.var[b] = r.va[...]
    for item in va_copies:
        item.start()
    pending.extend(va_copies)

    def late_grads(tile, carried):
        mlp_grads(tile)
        return carried

    lax.fori_loop(EARLY, TILES, late_grads, 0)
    mgo_copy.wait_recv()
    for slot in range(CHIPS):
        theirs = jnp.concatenate(
            [r.mgo[slot, :, 0:GROUP], r.mgo[slot, :, GROUP : 2 * GROUP]], axis=0
        )
        r.mgt[slot, :, 0:ROWS] = jnp.transpose(jnp.where(c == 0, r.mg[slot], theirs))
        r.mgt[slot, :, ROWS : 2 * ROWS] = jnp.transpose(jnp.where(c == 0, theirs, r.mg[slot]))

    bl_copy.wait_recv()
    side = pl.ds(pl.multiple_of(c * OUT_HALF, OUT_HALF), OUT_HALF)
    for block in range(CHIPS):
        grad = dot(r.mgt[block, :, 0:ROWS], r.bl[0, :, side]) + dot(
            r.mgt[block, :, ROWS : 2 * ROWS], r.bl[1, :, side]
        )
        low = grad.astype(LOW)
        home = r.oa if block < 2 else r.ob
        for piece in range(4):
            home[block % 2, piece // 2, piece % 2] = low[piece * PIECE : (piece + 1) * PIECE]
    for item in hop_one(TILES):
        item.start()

    lo_copy.wait_recv()

    def layer_rows(index, carried):
        rows = pl.ds(index * PIECE, PIECE)
        out_layer[rows, :] = (
            r.resid[rows, :] + r.lo[c, rows, :] + r.lor[rows, :] + local_row(7)
        ).astype(LOW)
        return carried

    lax.fori_loop(0, 4, layer_rows, 0)

    others(lambda slot: ag_arrival(slot).wait_recv())
    for h in range(3):
        for slot in range(CHIPS):
            for part in range(2):
                start = slot * ROWS + part * PACK
                r.agh[h, start : start + PACK, :] = r.ag[
                    slot, :, part * GROUP + h * HEAD : part * GROUP + (h + 1) * HEAD
                ]
    r.dkt[...] = jnp.zeros((3, HEAD, KEYS), F32)
    r.dvt[...] = jnp.zeros((3, HEAD, KEYS), F32)

    def pair_copies(h):
        return (
            send(r.dkt.at[h, :, pl.ds(OWN, OWN)], r.dkr.at[h], r.dk_s.at[h], r.dk_r.at[h], s, sib),
            send(r.dvt.at[h, :, pl.ds(OWN, OWN)], r.dvr.at[h], r.dv_s.at[h], r.dv_r.at[h], s, sib),
        )

    def dq_copy(h, block):
        return send(r.dqs.at[h, block], r.dqr.at[h, z], r.dq_s.at[h, block], r.dq_r.at[h, z],
                    s, 2 * block + c)

    def dq_arrival(h, slot):
        return send(r.dqs.at[h, slot], r.dqr.at[h, slot], r.dq_s.at[h, slot], r.dq_r.at[h, slot],
                    s, 2 * slot + c)

    def finish_head(h):
        for item in pair_copies(h):
            item.wait_recv()
        key_grad = jnp.transpose((r.dkt[h, :, 0:OWN] + r.dkr[h]).astype(LOW))
        value_grad = jnp.transpose((r.dvt[h, :, 0:OWN] + r.dvr[h]).astype(LOW))
        for part, whole in enumerate((r.q[h, :, HEAD : 2 * HEAD], key_grad, value_grad)):
            lane = h * GROUP + part * HEAD
            r.dqkv[:, lane : lane + HEAD] = whole
            for block in range(CHIPS):
                pack(r.dqs.at[h], block, part * HEAD, whole[block * ROWS : (block + 1) * ROWS])
        others(lambda block: dq_copy(h, block).start())
        r.dqr[h, z] = r.dqs[h, z]

    def backward_block(index, carried):
        h = index // CHIPS
        block = index % CHIPS
        rows = pl.ds(pl.multiple_of(block * ROWS, ROWS), ROWS)
        live = jnp.where(r.qseg[rows, :][:, :HEAD] != pad_number, 1.0, 0.0).astype(F32)
        grad = r.agh[h, rows, :].astype(F32) * live
        inverse = r.att[h, rows, HEAD : 2 * HEAD]
        correct = jnp.sum(grad * r.att[h, rows, 0:HEAD], axis=-1, keepdims=True) * inverse[:, 0:1]
        correct = correct.astype(LOW).astype(F32)
        scaled = (grad * inverse).astype(LOW)
        scaled_t = jnp.transpose(scaled)
        query_t = jnp.transpose(r.q[h, rows, 0:HEAD])
        total = jnp.zeros((ROWS, HEAD), F32)
        for turn in range(TURNS):
            cols = slice(turn * SPAN, (turn + 1) * SPAN)
            product = dot_nt(scaled, r.vh[h, cols, 0:HEAD])
            weights = r.prob[h, rows, cols]
            slopes = (
                weights.astype(F32) * (product - correct) * (1.0 / math.sqrt(HEAD))
            ).astype(LOW)
            total = total + dot(slopes, r.kh[h, cols, :])
            r.dkt[h, :, cols] += dot(query_t, slopes)
            r.dvt[h, :, cols] += dot(scaled_t, weights)
        r.q[h, rows, HEAD : 2 * HEAD] = total.astype(LOW)

        @pl.when(block == CHIPS - 1)
        def _():
            for item in pair_copies(h):
                item.start()

        for turn, unit in SERVICE_ONE:
            @pl.when(index == turn)
            def _(unit=unit):
                service_one(unit)

        for turn, unit in SERVICE_TWO:
            @pl.when(index == turn)
            def _(unit=unit):
                service_two(unit)

        for turn, head in ((5, 0), (9, 1)):
            @pl.when(index == turn)
            def _(head=head):
                finish_head(head)

        return carried

    lax.fori_loop(0, 3 * CHIPS, backward_block, 0)

    for item in va_copies:
        item.wait_recv()
    total = r.var[0]
    for slot in range(1, 8):
        total = total + r.var[slot]
    r.vax[...] = total
    r.vaxr[s] = total
    vax_copies = [
        send(r.vax, r.vaxr.at[s], r.vax_s.at[step - 1], r.vax_r.at[step - 1], flip[step], b)
        for step in (1, 2, 3)
    ]
    for item in vax_copies:
        item.start()
    pending.extend(vax_copies)

    for slot in range(CHIPS):
        r.nrmt[slot] = jnp.transpose(r.nrm[slot])
    finish_head(2)

    def qkv_grads(block, carried):
        rows = pl.ds(pl.multiple_of(block * ROWS, ROWS), ROWS)
        grad = jnp.zeros((ROWS, QKV), F32)
        for slot in range(CHIPS):
            grad = grad + dot(
                r.nrmt[slot, rows, :], r.dqkv[slot * ROWS : (slot + 1) * ROWS, :]
            )
        low = grad.astype(LOW)
        for piece in range(4):
            r.dwq[block, piece] = low[piece * PIECE : (piece + 1) * PIECE]
        return carried

    lax.fori_loop(0, CHIPS, qkv_grads, 0)
    q0_copy = send(
        r.dwq.at[pl.ds(2 * (1 - c), 2)], r.dwqr, r.q0_s.at[0], r.q0_r.at[0], s, sib
    )
    q0_copy.start()
    pending.append(q0_copy)
    column_sums = jnp.sum(r.dqkv[...].astype(F32), axis=0, keepdims=True)
    for row, lane in ((0, 0), (CHIPS, 2 * HEAD)):
        r.vb[pl.ds(row + z, 1), 0:GROUP] = jnp.concatenate(
            [
                column_sums[:, h * GROUP + lane : h * GROUP + lane + HEAD]
                for h in range(3)
            ],
            axis=1,
        )
    q0_copy.wait_recv()
    for part in range(2):
        for piece in range(4):
            r.dwqx[part, piece] = (
                r.dwq[2 * c + part, piece].astype(F32) + r.dwqr[part, piece].astype(F32)
            ).astype(LOW)
    qx_copies = [
        send(r.dwqx.at[:, flip[step]], r.rxq.at[step - 1], r.qx_s.at[step - 1],
             r.qx_r.at[step - 1], flip[step], b)
        for step in (1, 2, 3)
    ]
    for item in qx_copies:
        item.start()
    pending.extend(qx_copies)

    for unit in LATE_ONE:
        service_one(unit)
    for unit in LATE_TWO[:2]:
        service_two(unit)

    for h in range(3):
        others(lambda slot, h=h: dq_arrival(h, slot).wait_recv())
        for slot in range(CHIPS):
            for part in range(3):
                lane = part * D + slot * GROUP + h * HEAD
                for side in range(2):
                    start = side * GROUP + part * HEAD
                    r.rowg[side * PACK : (side + 1) * PACK, lane : lane + HEAD] = r.dqr[
                        h, slot, :, start : start + HEAD
                    ]

    def first_grads(index, carried):
        rows = pl.ds(pl.multiple_of(index * 256, 256), 256)
        r.ngr[:, rows] = dot_nt(r.rowg[...], r.wf[rows, :])
        return carried

    lax.fori_loop(0, 3, first_grads, 0)

    def first_back(index, carried):
        rows = pl.ds(index * PIECE, PIECE)
        grad = r.ngr[rows, :]
        xhat = r.xhat1[rows, :]
        scaled = grad * local_row(3)
        mean_one = jnp.mean(scaled, axis=-1, keepdims=True)
        mean_two = jnp.mean(scaled * xhat, axis=-1, keepdims=True)
        through = r.rstd1[rows, :] * (scaled - mean_one - xhat * mean_two)
        out_tok[rows, :] = (r.xhat2[rows, :] + through).astype(LOW)
        r.vb[8:9, :] += jnp.sum(grad * xhat, axis=0, keepdims=True)
        r.vb[9:10, :] += jnp.sum(grad, axis=0, keepdims=True)
        return carried

    lax.fori_loop(0, 4, first_back, 0)

    vb_copies = [
        send(r.vb, r.vbr.at[b], r.vb_s.at[step - 1], r.vb_r.at[step - 1], s, (b + step) % 8)
        for step in range(1, 8)
    ]
    r.vbr[b] = r.vb[...]
    for item in vb_copies:
        item.start()
    pending.extend(vb_copies)

    for item in qx_copies:
        item.wait_recv()
    def qz_copy(part):
        return send(r.zq.at[part], r.rzq.at[z], r.qz_s.at[part], r.qz_r.at[z],
                    s, 2 * (2 * c + part) + owner)

    for part in range(2):
        total = r.dwqx[part, s].astype(F32)
        for step in range(3):
            total = total + r.rxq[step, part].astype(F32)
        r.zq[part] = total.astype(LOW)
        there = 2 * (2 * c + part) + owner

        @pl.when(there != b)
        def _(part=part):
            qz_copy(part).start()

        @pl.when(there == b)
        def _(part=part):
            r.rzq[z] = r.zq[part]

    for item in vb_copies:
        item.wait_recv()
    total = r.vbr[0]
    for slot in range(1, 8):
        total = total + r.vbr[slot]
    r.vbx[...] = total
    r.vbxr[s] = total
    vbx_copies = [
        send(r.vbx, r.vbxr.at[s], r.vbx_s.at[step - 1], r.vbx_r.at[step - 1], flip[step], b)
        for step in (1, 2, 3)
    ]
    for item in vbx_copies:
        item.start()
    pending.extend(vbx_copies)

    for unit in LATE_TWO[2:]:
        service_two(unit)

    for unit in range(TILES + 1):
        service_three(unit)

    def qf_copy(step):
        return send(r.rzq, out_finq.at[s % 2], r.qf_s.at[step - 1], r.qf_r.at[step - 1],
                    flip[step], b)

    def qz_arrival(slot):
        return send(r.zq.at[0], r.rzq.at[slot], r.qz_s.at[0], r.qz_r.at[slot], s, sib)

    @pl.when(owner == c)
    def _():
        for slot in range(CHIPS):
            @pl.when(jnp.logical_or(slot != z, z // 2 != c))
            def _(slot=slot):
                qz_arrival(slot).wait_recv()

        for step in (1, 2, 3):
            qf_copy(step).start()
        out_finq[s % 2] = r.rzq[...]

    for piece in range(2):
        for core in range(2):
            @pl.when(jnp.logical_or(2 * c + piece != s, core != c))
            def _(piece=piece, core=core):
                for unit in range(TILES + 1):
                    fin_arrival(unit, piece, core).wait_recv()

    for step in (1, 2, 3):
        @pl.when(flip[step] // 2 == c)
        def _(step=step):
            qf_copy(step).wait_recv()

    for item in vax_copies + vbx_copies:
        item.wait_recv()
    out_va[...] = r.vaxr[0] + r.vaxr[1] + r.vaxr[2] + r.vaxr[3]
    out_vb[...] = r.vbxr[0] + r.vbxr[1] + r.vbxr[2] + r.vbxr[3]

    for slot in range(CHIPS):
        @pl.when(jnp.logical_and(slot <= z, z < 3))
        def _(slot=slot):
            norm_copy(slot, True).wait_send()

        @pl.when(jnp.logical_and(slot >= z, z > 0))
        def _(slot=slot):
            norm_copy(slot, False).wait_send()

        kv_copy(slot).wait_send()
    for make in (mg_copy, ag_copy):
        others(lambda slot, make=make: make(slot).wait_send())
    for h in range(3):
        others(lambda slot, h=h: dq_copy(h, slot).wait_send())
        for item in pair_copies(h):
            item.wait_send()
    for item in pending:
        item.wait_send()
    for unit in range(TILES + 1):
        for item in hop_one(unit) + hop_two(unit):
            item.wait_send()
        others(lambda slot, unit=unit: z_copy(unit, slot).wait_send())
        for step in (1, 2, 3):
            fin_copy(unit, step).wait_send()

        @pl.when(mine != b)
        def _(unit=unit):
            fin_copy(unit, 0).wait_send()

    for part in range(2):
        @pl.when(2 * (2 * c + part) + owner != b)
        def _(part=part):
            qz_copy(part).wait_send()

    @pl.when(owner == c)
    def _():
        for step in (1, 2, 3):
            qf_copy(step).wait_send()


def finish_body(tok, layer, fin, fo, finq, va, vb, *outs):
    (layer_out, tok_out, qkv_w, out_w, up_w, down_w, qb, v_b, ob, g1, s1, g2, s2, down_b, up_b) = outs
    layer_out[...] = layer[...]
    tok_out[...] = tok[...]
    for piece in range(2):
        rows = slice(piece * PIECE, (piece + 1) * PIECE)
        for core in range(2):
            out_w[rows, core * OUT_HALF : (core + 1) * OUT_HALF] = fo[piece, core].astype(F32)
            for tile in range(TILES):
                start = core * HALF + tile * TILE
                up_w[rows, start : start + TILE] = fin[tile, piece, core, 0].astype(F32)
        for slot in range(CHIPS):
            for h in range(3):
                for part in range(3):
                    lane = part * D + slot * GROUP + h * HEAD
                    source = h * GROUP + part * HEAD
                    qkv_w[rows, lane : lane + HEAD] = finq[
                        piece, slot, :, source : source + HEAD
                    ].astype(F32)
    for core in range(2):
        for tile in range(TILES):
            start = core * HALF + tile * TILE
            both = jnp.concatenate(
                [fin[tile, 0, core, 1].astype(F32), fin[tile, 1, core, 1].astype(F32)], axis=0
            )
            down_w[start : start + TILE, :] = jnp.transpose(both)
    b = lax.axis_index("blk")
    for index in range(8):
        @pl.when(b == index)
        def _(index=index):
            cols = slice(index * 96, (index + 1) * 96)
            for ref, source, row in (
                (ob, va, 0), (g2, va, 1), (s2, va, 2), (down_b, va, 3), (g1, vb, 8), (s1, vb, 9)
            ):
                ref[...] = source[row, cols]
            slot = index // 2
            half = slice((index % 2) * 96, (index % 2 + 1) * 96)
            qb[...] = vb[slot, half]
            v_b[...] = vb[4 + slot, half]
            start = (index * 384) % D
            up_b[...] = va[4 + index * 384 // D, start : start + 384]


def chip_body(
    tokens, segment_ids, out_grad, query_key_value_weight, query_bias, value_bias,
    attention_output_weight, attention_output_bias, first_gain, first_shift,
    second_gain, second_shift, mlp_input_weight, mlp_input_bias, mlp_output_weight,
    mlp_output_bias,
):
    pad_number = tokens.shape[1] * lax.axis_size("blk") // SHORT_LO + 2
    names = scratch_list()
    any_space = pl.BlockSpec(memory_space=pl.ANY)
    in_vmem = pl.BlockSpec(memory_space=pltpu.VMEM)
    results = pl.pallas_call(
        functools.partial(kernel_body, tuple(names), pad_number),
        out_shape=(
            jax.ShapeDtypeStruct((ROWS, D), LOW),
            jax.ShapeDtypeStruct((ROWS, D), LOW),
            jax.ShapeDtypeStruct((TILES, 2, 2, 2, PIECE, TILE), LOW),
            jax.ShapeDtypeStruct((2, 2, PIECE, OUT_HALF), LOW),
            jax.ShapeDtypeStruct((2, CHIPS, PIECE, QKV), LOW),
            jax.ShapeDtypeStruct((16, D), F32),
            jax.ShapeDtypeStruct((16, D), F32),
        ),
        in_specs=[in_vmem] * 3 + [any_space] * 4 + [in_vmem] * 9,
        out_specs=(in_vmem,) * 7,
        scratch_shapes=list(names.values()),
        compiler_params=pltpu.CompilerParams(
            collective_id=0, has_side_effects=True, vmem_limit_bytes=VMEM_LIMIT
        ),
        name="encoder_block",
    )(
        tokens.reshape(ROWS, D), segment_ids, out_grad.reshape(ROWS, D),
        query_key_value_weight, attention_output_weight,
        mlp_input_weight.reshape(CHIPS, 2, 2, PIECE, FF), mlp_output_weight,
        query_bias, value_bias, attention_output_bias, first_gain, first_shift,
        second_gain, second_shift, mlp_output_bias, mlp_input_bias,
    )
    wide = [(96, 3 * D), (96, D), (96, FF), (FF, 96)]
    shapes = (
        [jax.ShapeDtypeStruct((ROWS, D), LOW)] * 2
        + [jax.ShapeDtypeStruct(shape, F32) for shape in wide]
        + [jax.ShapeDtypeStruct((96,), F32)] * 8
        + [jax.ShapeDtypeStruct((384,), F32)]
    )
    (layer_out, tok_out, qkv_w, out_w, up_w, down_w, qb, vb, ob, g1, s1, g2, s2, down_b, up_b) = (
        pl.pallas_call(
            finish_body,
            out_shape=tuple(shapes),
            in_specs=[in_vmem] * 7,
            out_specs=(in_vmem,) * len(shapes),
            compiler_params=pltpu.CompilerParams(vmem_limit_bytes=VMEM_LIMIT),
            name="place_results",
        )(*results)
    )
    return (
        layer_out.reshape(tokens.shape), tok_out.reshape(tokens.shape), qkv_w, qb, vb, out_w, ob,
        g1, s1, g2, s2, up_w, up_b, down_w, down_b,
    )


def solution(mesh):
    placed = (
        P("seq", "blk", None),
        P("seq", "blk"),
        P("seq", "blk", None),
        P(),
        P(),
        P(),
        P(),
        P(),
        P(),
        P(),
        P(),
        P(),
        P(),
        P(),
        P(),
        P(),
    )
    chosen = chip_body if mesh.shape["seq"] == 4 and mesh.shape["blk"] == 8 else body
    return jax.shard_map(
        chosen,
        mesh=mesh,
        in_specs=placed,
        out_specs=(
            P("seq", "blk", None),
            P("seq", "blk", None),
            P("blk", None),
            P("blk"),
            P("blk"),
            P("blk", None),
            P("blk"),
            P("blk"),
            P("blk"),
            P("blk"),
            P("blk"),
            P("blk", None),
            P("blk"),
            P(None, "blk"),
            P("blk"),
        ),
        check_vma=False,
    )
```

```python
import functools
import math

import jax
import jax.numpy as jnp
from jax import lax
from jax.experimental import pallas as pl
from jax.experimental.pallas import tpu as pltpu
from jax.sharding import PartitionSpec as P

HEADS = 12
HEAD = 64
SHORT_LO = 25


EPS = 1e-06


def layer_norm(inputs, norm_gain, norm_shift):
    centre = inputs - jnp.mean(inputs, axis=-1, keepdims=True)
    spread = jnp.mean(centre * centre, axis=-1, keepdims=True)
    return centre * lax.rsqrt(spread + EPS) * norm_gain + norm_shift


def gelu_exact(inputs):
    return jax.nn.gelu(inputs, approximate=False)


def score_block(queries, query_segs, key_rows, key_segs):
    raw_scores = jnp.einsum("qhd,khd->hqk", queries, key_rows, preferred_element_type=jnp.float32)
    same_image = (query_segs[:, None] == key_segs[None, :])[None]
    return jnp.where(same_image, jnp.exp(raw_scores * (1.0 / math.sqrt(HEAD))), 0.0)


def forward_step(carried, queries, query_segs, key_rows, value_rows, key_segs):
    totals, summed = carried
    weights = score_block(queries, query_segs, key_rows, key_segs)
    totals = totals + jnp.transpose(jnp.sum(weights, axis=-1))
    summed = summed + jnp.einsum(
        "hqk,khd->qhd", weights.astype(jnp.bfloat16), value_rows, preferred_element_type=jnp.float32
    )
    return (totals, summed)


def back_step(queries, query_grads, query_corr, query_segs, key_rows, value_rows, key_segs):
    weights = score_block(queries, query_segs, key_rows, key_segs)
    product = jnp.einsum(
        "qhd,khd->hqk", query_grads, value_rows, preferred_element_type=jnp.float32
    )
    shifted = jnp.transpose(query_corr.astype(jnp.float32))[:, :, None]
    score_grads = (weights * (product - shifted) * (1.0 / math.sqrt(HEAD))).astype(jnp.bfloat16)
    return (weights.astype(jnp.bfloat16), score_grads)


def key_value_grads(queries, query_grads, query_corr, query_segs, key_rows, value_rows, key_segs):
    weights_low, score_grads = back_step(
        queries, query_grads, query_corr, query_segs, key_rows, value_rows, key_segs
    )
    key_part = jnp.einsum("hqk,qhd->khd", score_grads, queries, preferred_element_type=jnp.float32)
    value_part = jnp.einsum(
        "hqk,qhd->khd", weights_low, query_grads, preferred_element_type=jnp.float32
    )
    return (key_part, value_part)


def body(
    tokens,
    segment_ids,
    out_grad,
    query_key_value_weight,
    query_bias,
    value_bias,
    attention_output_weight,
    attention_output_bias,
    first_gain,
    first_shift,
    second_gain,
    second_shift,
    mlp_input_weight,
    mlp_input_bias,
    mlp_output_weight,
    mlp_output_bias,
):
    model_width = tokens.shape[-1]
    row_count = tokens.shape[0] * tokens.shape[1]
    head_shape = (row_count, HEADS, HEAD)
    pad_number = tokens.shape[1] * lax.axis_size("blk") // SHORT_LO + 2
    token_rows = tokens.reshape(row_count, model_width).astype(jnp.float32)
    seg_rows = segment_ids.reshape(row_count)
    live_rows = (seg_rows != pad_number).astype(jnp.float32)
    first_normed, first_back = jax.vjp(
        layer_norm, token_rows, first_gain.astype(jnp.float32), first_shift.astype(jnp.float32)
    )
    first_low = first_normed.astype(jnp.bfloat16)
    query_key_value_bias = jnp.concatenate(
        [
            query_bias.astype(jnp.float32),
            jnp.zeros((model_width,), jnp.float32),
            value_bias.astype(jnp.float32),
        ]
    )
    projected_rows = (
        jnp.dot(first_low, query_key_value_weight, preferred_element_type=jnp.float32)
        + query_key_value_bias
    )
    query_flat = projected_rows[:, :model_width].astype(jnp.bfloat16)
    key_flat = projected_rows[:, model_width : 2 * model_width].astype(jnp.bfloat16)
    value_flat = projected_rows[:, 2 * model_width :].astype(jnp.bfloat16)
    queries = query_flat.reshape(head_shape)
    gathered = (
        lax.all_gather(key_flat, "blk", axis=0, tiled=True),
        lax.all_gather(value_flat, "blk", axis=0, tiled=True),
        lax.all_gather(seg_rows, "blk", axis=0, tiled=True),
    )
    all_keys = gathered[0].reshape(-1, HEADS, HEAD)
    all_values = gathered[1].reshape(-1, HEADS, HEAD)
    all_segs = gathered[2]
    seq_rows = all_keys.shape[0]
    key_span = math.gcd(seq_rows, 2048)
    turns = seq_rows // key_span

    def forward_turn(index, carried):
        begin_row = index * key_span
        return forward_step(
            carried,
            queries,
            seg_rows,
            lax.dynamic_slice_in_dim(all_keys, begin_row, key_span, 0),
            lax.dynamic_slice_in_dim(all_values, begin_row, key_span, 0),
            lax.dynamic_slice_in_dim(all_segs, begin_row, key_span, 0),
        )

    totals, summed = lax.fori_loop(
        0,
        turns,
        forward_turn,
        (jnp.zeros((row_count, HEADS), jnp.float32), jnp.zeros(head_shape, jnp.float32)),
    )
    attended = summed / totals[:, :, None] * live_rows[:, None, None]
    merged_heads = attended.reshape(row_count, model_width).astype(jnp.bfloat16)
    residual = (
        token_rows
        + jnp.dot(merged_heads, attention_output_weight, preferred_element_type=jnp.float32)
        + attention_output_bias.astype(jnp.float32)
    )
    second_normed, second_back = jax.vjp(
        layer_norm, residual, second_gain.astype(jnp.float32), second_shift.astype(jnp.float32)
    )
    second_low = second_normed.astype(jnp.bfloat16)
    hidden_rows = jnp.dot(
        second_low, mlp_input_weight, preferred_element_type=jnp.float32
    ) + mlp_input_bias.astype(jnp.float32)
    gelu_active, gelu_back = jax.vjp(gelu_exact, hidden_rows)
    active_low = gelu_active.astype(jnp.bfloat16)
    layer_rows = (
        residual
        + jnp.dot(active_low, mlp_output_weight, preferred_element_type=jnp.float32)
        + mlp_output_bias.astype(jnp.float32)
    )
    layer_out = layer_rows.astype(jnp.bfloat16).reshape(tokens.shape)
    grad_rows = out_grad.reshape(row_count, model_width)
    down_weight_grad = jnp.einsum(
        "tf,td->fd", active_low, grad_rows, preferred_element_type=jnp.float32
    )
    down_bias_grad = jnp.sum(grad_rows.astype(jnp.float32), axis=0)
    active_grad = jnp.einsum(
        "td,fd->tf", grad_rows, mlp_output_weight, preferred_element_type=jnp.float32
    )
    (hidden_grad,) = gelu_back(active_grad)
    hidden_low = hidden_grad.astype(jnp.bfloat16)
    up_weight_grad = jnp.einsum(
        "td,tf->df", second_low, hidden_low, preferred_element_type=jnp.float32
    )
    up_bias_grad = jnp.sum(hidden_low.astype(jnp.float32), axis=0)
    normed_grad = jnp.einsum(
        "tf,df->td", hidden_low, mlp_input_weight, preferred_element_type=jnp.float32
    )
    resid_part, second_gain_grad, second_shift_grad = second_back(normed_grad)
    residual_grad = grad_rows.astype(jnp.float32) + resid_part
    branch_low = residual_grad.astype(jnp.bfloat16)
    out_weight_grad = jnp.einsum(
        "ti,to->io", merged_heads, branch_low, preferred_element_type=jnp.float32
    )
    out_bias_grad = jnp.sum(branch_low.astype(jnp.float32), axis=0)
    attended_grad = (
        jnp.einsum(
            "to,io->ti", branch_low, attention_output_weight, preferred_element_type=jnp.float32
        ).reshape(head_shape)
        * live_rows[:, None, None]
    )
    query_grads = (attended_grad / totals[:, :, None]).astype(jnp.bfloat16)
    corrections = (jnp.sum(attended_grad * attended, axis=-1) / totals).astype(jnp.bfloat16)

    def query_turn(index, carried):
        begin_row = index * key_span
        key_rows = lax.dynamic_slice_in_dim(all_keys, begin_row, key_span, 0)
        weights_low, score_grads = back_step(
            queries,
            query_grads,
            corrections,
            seg_rows,
            key_rows,
            lax.dynamic_slice_in_dim(all_values, begin_row, key_span, 0),
            lax.dynamic_slice_in_dim(all_segs, begin_row, key_span, 0),
        )
        return carried + jnp.einsum(
            "hqk,khd->qhd", score_grads, key_rows, preferred_element_type=jnp.float32
        )

    query_sum = lax.fori_loop(0, turns, query_turn, jnp.zeros(head_shape, jnp.float32))
    term_span = math.gcd(row_count * lax.axis_size("blk"), 2048)

    def term_block(index):
        begin_row = index * term_span
        key_part, value_part = key_value_grads(
            queries,
            query_grads,
            corrections,
            seg_rows,
            lax.dynamic_slice_in_dim(all_keys, begin_row, term_span, 0),
            lax.dynamic_slice_in_dim(all_values, begin_row, term_span, 0),
            lax.dynamic_slice_in_dim(all_segs, begin_row, term_span, 0),
        )
        return jnp.concatenate(
            [key_part.reshape(term_span, model_width), value_part.reshape(term_span, model_width)],
            axis=1,
        )

    blocks = lax.map(
        term_block, jnp.arange(row_count * lax.axis_size("blk") // term_span, dtype=jnp.int32)
    )
    key_terms = lax.psum_scatter(
        blocks.reshape(row_count * lax.axis_size("blk"), 2 * model_width),
        "blk",
        scatter_dimension=0,
        tiled=True,
    )
    query_low = query_sum.reshape(row_count, model_width).astype(jnp.bfloat16)
    key_low = key_terms[:, :model_width].astype(jnp.bfloat16)
    value_low = key_terms[:, model_width:].astype(jnp.bfloat16)
    qkv_grad = jnp.concatenate([query_low, key_low, value_low], axis=1)
    qkv_weight_grad = jnp.einsum(
        "td,tj->dj", first_low, qkv_grad, preferred_element_type=jnp.float32
    )
    query_bias_grad = jnp.sum(query_low.astype(jnp.float32), axis=0)
    value_bias_grad = jnp.sum(value_low.astype(jnp.float32), axis=0)
    first_grad = jnp.einsum(
        "tj,dj->td", qkv_grad, query_key_value_weight, preferred_element_type=jnp.float32
    )
    token_part, first_gain_grad, first_shift_grad = first_back(first_grad)
    tokens_grad = (residual_grad + token_part).astype(jnp.bfloat16).reshape(tokens.shape)
    local_grads = (
        qkv_weight_grad,
        query_bias_grad,
        value_bias_grad,
        out_weight_grad,
        out_bias_grad,
        first_gain_grad,
        first_shift_grad,
        second_gain_grad,
        second_shift_grad,
        up_weight_grad,
        up_bias_grad,
        down_weight_grad,
        down_bias_grad,
    )
    scattered = (
        lax.psum_scatter(local_grads[0], "blk", scatter_dimension=0, tiled=True),
        lax.psum_scatter(local_grads[1], "blk", scatter_dimension=0, tiled=True),
        lax.psum_scatter(local_grads[2], "blk", scatter_dimension=0, tiled=True),
        lax.psum_scatter(local_grads[3], "blk", scatter_dimension=0, tiled=True),
        lax.psum_scatter(local_grads[4], "blk", scatter_dimension=0, tiled=True),
        lax.psum_scatter(local_grads[5], "blk", scatter_dimension=0, tiled=True),
        lax.psum_scatter(local_grads[6], "blk", scatter_dimension=0, tiled=True),
        lax.psum_scatter(local_grads[7], "blk", scatter_dimension=0, tiled=True),
        lax.psum_scatter(local_grads[8], "blk", scatter_dimension=0, tiled=True),
        lax.psum_scatter(local_grads[9], "blk", scatter_dimension=0, tiled=True),
        lax.psum_scatter(local_grads[10], "blk", scatter_dimension=0, tiled=True),
        lax.psum_scatter(local_grads[11], "blk", scatter_dimension=1, tiled=True),
        lax.psum_scatter(local_grads[12], "blk", scatter_dimension=0, tiled=True),
    )
    summed_grads = lax.psum(
        (
            scattered[0],
            scattered[1],
            scattered[2],
            scattered[3],
            scattered[4],
            scattered[5],
            scattered[6],
            scattered[7],
            scattered[8],
            scattered[9],
            scattered[10],
            scattered[11],
            scattered[12],
        ),
        "seq",
    )
    return (layer_out, tokens_grad) + tuple(summed_grads)


VMEM_LIMIT = 64 * 1024 * 1024
D = 768
FF = 3072
ROWS = 192
CHIPS = 4
GROUP = 192
QKV = 3 * GROUP
HALF = FF // 2
OUT_HALF = D // 2
PIECE = 48
TILE = 256
TILES = HALF // TILE
PACK = ROWS // 2
KEYS = 1536
OWN = 768
LOW = jnp.bfloat16
F32 = jnp.float32
MESH = pl.DeviceIdType.MESH


def dot(a, b):
    return jnp.dot(a, b, preferred_element_type=F32)


def dot_nt(a, b):
    return lax.dot_general(a, b, (((1,), (1,)), ((), ())), preferred_element_type=F32)


def dot_tn(a, b):
    return lax.dot_general(a, b, (((0,), (0,)), ((), ())), preferred_element_type=F32)


def scratch_list():
    dma = pltpu.SemaphoreType.DMA
    vmem = pltpu.VMEM
    return dict(
        nrm=vmem((CHIPS, ROWS, D), LOW),
        xhat1=vmem((ROWS, D), F32),
        rstd1=vmem((ROWS, 1), F32),
        par=vmem((8, D), F32),
        qvb=vmem((2, CHIPS, GROUP), F32),
        b1=vmem((1, FF), F32),
        wf=vmem((D, 3 * D), LOW),
        wo=vmem((D, D), LOW),
        w2=vmem((HALF, D), LOW),
        q=vmem((3, OWN, 2 * HEAD), LOW),
        kvo=vmem((CHIPS, ROWS, 2 * GROUP), LOW),
        kvs=vmem((CHIPS, ROWS, 2 * GROUP), LOW),
        kh=vmem((3, KEYS, HEAD), LOW),
        vh=vmem((3, KEYS, 2 * HEAD), LOW),
        kvt=vmem((6, HEAD, KEYS), LOW),
        segs=vmem((2, CHIPS, 8, ROWS), jnp.int32),
        kseg=vmem((1, KEYS), jnp.int32),
        qseg=vmem((OWN, 128), jnp.int32),
        prob=vmem((3, OWN, KEYS), LOW),
        att=vmem((3, OWN, 2 * HEAD), F32),
        mgs=vmem((CHIPS, PACK, 2 * GROUP), LOW),
        mgr=vmem((CHIPS, PACK, 2 * GROUP), LOW),
        mgo=vmem((CHIPS, PACK, 2 * GROUP), LOW),
        mg=vmem((CHIPS, ROWS, GROUP), LOW),
        og=vmem((2, ROWS, D), LOW),
        nt=vmem((2, ROWS, D), LOW),
        bl=vmem((2, ROWS, D), LOW),
        resid=vmem((ROWS, D), F32),
        xhat2=vmem((ROWS, D), F32),
        rstd2=vmem((ROWS, 1), F32),
        act=vmem((2 * ROWS, HALF), LOW),
        hg=vmem((2 * ROWS, HALF), LOW),
        lo=vmem((2, ROWS, D), F32),
        ng=vmem((2, ROWS, D), F32),
        lor=vmem((ROWS, D), F32),
        ngr=vmem((ROWS, D), F32),
        ags=vmem((CHIPS, PACK, 2 * GROUP), LOW),
        ag=vmem((CHIPS, PACK, 2 * GROUP), LOW),
        agh=vmem((3, OWN, HEAD), LOW),
        dqs=vmem((3, CHIPS, PACK, 2 * GROUP), LOW),
        dqr=vmem((3, CHIPS, PACK, 2 * GROUP), LOW),
        rowg=vmem((ROWS, 3 * D), LOW),
        dkr=vmem((3, 2, HEAD, OWN), LOW),
        dks=vmem((3, 2, HEAD, OWN), LOW),
        dqkv=vmem((OWN, QKV), LOW),
        da=vmem((TILES, CHIPS, 2, 2, PIECE, TILE), LOW),
        db=vmem((TILES, CHIPS, 2, 2, PIECE, TILE), LOW),
        ra=vmem((TILES, CHIPS, 2, PIECE, TILE), LOW),
        rb=vmem((TILES, CHIPS, 2, PIECE, TILE), LOW),
        a2s=vmem((TILES, CHIPS, PIECE, TILE), LOW),
        b2s=vmem((TILES, CHIPS, PIECE, TILE), LOW),
        a2r=vmem((TILES, CHIPS, PIECE, TILE), LOW),
        b2r=vmem((TILES, CHIPS, PIECE, TILE), LOW),
        zs=vmem((TILES, CHIPS, 2, PIECE, TILE), LOW),
        rz=vmem((TILES, CHIPS, 2, PIECE, TILE), LOW),
        zm=vmem((TILES, 2, 2, PIECE, TILE), LOW),
        fin=vmem((TILES, 2, PIECE, TILE), LOW),
        oa=vmem((2, 2, 2, PIECE, OUT_HALF), LOW),
        ob=vmem((2, 2, 2, PIECE, OUT_HALF), LOW),
        roa=vmem((2, 2, PIECE, OUT_HALF), LOW),
        rob=vmem((2, 2, PIECE, OUT_HALF), LOW),
        oa2s=vmem((2, PIECE, OUT_HALF), LOW),
        ob2s=vmem((2, PIECE, OUT_HALF), LOW),
        oa2r=vmem((2, PIECE, OUT_HALF), LOW),
        ob2r=vmem((2, PIECE, OUT_HALF), LOW),
        zo=vmem((CHIPS, PIECE, OUT_HALF), LOW),
        rzo=vmem((CHIPS, PIECE, OUT_HALF), LOW),
        zmo=vmem((2, PIECE, OUT_HALF), LOW),
        fo=vmem((PIECE, OUT_HALF), LOW),
        dwq=vmem((CHIPS, 4, PIECE, QKV), LOW),
        dwqr=vmem((2, 4, PIECE, QKV), LOW),
        dwqx=vmem((2, 4, PIECE, QKV), LOW),
        rxq=vmem((3, 2, PIECE, QKV), LOW),
        zq=vmem((2, PIECE, QKV), LOW),
        rzq=vmem((CHIPS, PIECE, QKV), LOW),
        va=vmem((8, D), F32),
        vh1=vmem((1, HALF), F32),
        vap=vmem((8, D), F32),
        vaz=vmem((CHIPS, 8, D), F32),
        vax=vmem((4, 8, D), F32),
        vq=vmem((8, TILE), F32),
        vqp=vmem((8, TILE), F32),
        vqz=vmem((CHIPS, 8, TILE), F32),
        vqx=vmem((4, 8, TILE), F32),
        vb=vmem((8, TILE), F32),
        vbr=vmem((8, 8, TILE), F32),
        vbx=vmem((4, 8, TILE), F32),
        load_sem=dma((3 + TILES,)),
        seg_s=dma((7,)), seg_r=dma((7,)),
        og_s=dma((1,)), og_r=dma((1,)),
        nu_s=dma((CHIPS, 2)), nd_s=dma((CHIPS, 2)), n_r=dma((CHIPS, 2)),
        kv_s=dma((CHIPS,)), kv_r=dma((CHIPS,)),
        mg_s=dma((CHIPS,)), mg_r=dma((CHIPS,)),
        mgo_s=dma((1,)), mgo_r=dma((1,)),
        nt_s=dma((1,)), nt_r=dma((1,)),
        lo_s=dma((1,)), lo_r=dma((1,)),
        ng_s=dma((1,)), ng_r=dma((1,)),
        bl_s=dma((1,)), bl_r=dma((1,)),
        ag_s=dma((CHIPS,)), ag_r=dma((CHIPS,)),
        dk_s=dma((3,)), dk_r=dma((3,)),
        dq_s=dma((3, CHIPS)), dq_r=dma((3, CHIPS)),
        a1_s=dma((TILES + 1,)), a1_r=dma((TILES + 1,)),
        b1_s=dma((TILES + 1,)), b1_r=dma((TILES + 1,)),
        a2_s=dma((TILES + 1,)), a2_r=dma((TILES + 1,)),
        b2_s=dma((TILES + 1,)), b2_r=dma((TILES + 1,)),
        z_s=dma((TILES + 1, CHIPS)), z_r=dma((TILES + 1, CHIPS)),
        f_s=dma((TILES + 1, 4)), f_r=dma((TILES + 1, 4)),
        q0_s=dma((1,)), q0_r=dma((1,)),
        qx_s=dma((3,)), qx_r=dma((3,)),
        qz_s=dma((2,)), qz_r=dma((CHIPS,)),
        qf_s=dma((3,)), qf_r=dma((3,)),
        va_s=dma((7,)), va_r=dma((7,)),
        vq_s=dma((7,)), vq_r=dma((7,)),
        vb_s=dma((7,)), vb_r=dma((7,)),
        vbx_s=dma((3,)), vbx_r=dma((3,)),
    )


EARLY = 4
STARTED = 2
PLAN = dict(
    before_norm=((0, 2),),
    after_norm=((1, 0), (0, 3)),
    before_loop=((1, 1), (0, 4)),
    loop=(
        (0, ((2, 0), (1, 2), (0, 5))),
        (1, ((2, 1), (3, 0))),
        (3, ((1, 3), (0, 6))),
    ),
    after_loop=((2, 2), (3, 1), (1, 4), (4, 0)),
    after_qkv=((1, 5), (2, 3), (3, 2), (4, 1), (1, 6)),
    after_rows=((2, 4), (3, 3), (4, 2), (2, 5), (3, 4)),
    before_sums=((2, 6), (3, 5), (4, 3)),
    last=((3, 6), (4, 4), (4, 5), (4, 6)),
)


class Box:
    pass


def kernel_body(names, pad_number, *refs):
    (tok, seg, ogi, wqkv, wo_h, w1_h, w2_h) = refs[:7]
    vectors = refs[7:15]
    b1_in = refs[15]
    (out_tok, out_layer, out_fin, out_fo, out_finq, out_va, out_vq, out_vb) = refs[16:24]
    r = Box()
    for name, ref in zip(names, refs[24:]):
        setattr(r, name, ref)
    par, qvb, b1 = r.par, r.qvb, r.b1

    s = lax.axis_index("seq")
    b = lax.axis_index("blk")
    z = b // 2
    c = b % 2
    sib = 2 * z + 1 - c
    flip = {1: s + 1 - 2 * (s % 2), 2: (s + 2) % 4, 3: 3 - s}
    x = s % 2
    y = s // 2

    pending = []

    def send(src, dst, ssem, rsem, dev_s, dev_b):
        return pltpu.make_async_remote_copy(
            src_ref=src, dst_ref=dst, send_sem=ssem, recv_sem=rsem,
            device_id=(dev_s, dev_b), device_id_type=MESH,
        )

    def local_row(index):
        return par[index : index + 1, :]

    loads = []
    loads.append(pltpu.make_async_copy(wqkv, r.wf, r.load_sem.at[0]))
    half = pl.multiple_of(c * HALF, 128)
    loads.append(pltpu.make_async_copy(wo_h, r.wo, r.load_sem.at[1]))
    loads.append(pltpu.make_async_copy(w2_h.at[pl.ds(half, HALF), :], r.w2, r.load_sem.at[2]))
    for tile in range(TILES):
        cols = pl.ds(pl.multiple_of(c * HALF + tile * TILE, TILE), TILE)
        loads.append(
            pltpu.make_async_copy(
                w1_h.at[:, :, :, :, cols], r.da.at[tile], r.load_sem.at[3 + tile]
            )
        )
    for item in loads:
        item.start()

    for index, vector in enumerate(vectors):
        par[index : index + 1, :] = vector[...].astype(F32).reshape(1, D)
    for slot in range(CHIPS):
        part = slice(slot * GROUP, (slot + 1) * GROUP)
        qvb[0, slot : slot + 1, :] = par[0:1, part]
        qvb[1, slot : slot + 1, :] = par[1:2, part]
    b1[...] = b1_in[...].astype(F32).reshape(1, FF)

    barrier = pltpu.get_barrier_semaphore()
    for step in range(1, 8):
        pl.semaphore_signal(barrier, inc=1, device_id=(s, (b + step) % 8), device_id_type=MESH)
    for step in (1, 2, 3):
        for core in range(2):
            pl.semaphore_signal(
                barrier, inc=1, device_id=(flip[step], 2 * z + core), device_id_type=MESH
            )
    pl.semaphore_wait(barrier, 13)

    r.segs[c, z] = jnp.broadcast_to(seg[...], (8, ROWS))
    seg_copies = []
    for step in range(1, 8):
        seg_copies.append(
            send(r.segs.at[c, z], r.segs.at[c, z], r.seg_s.at[step - 1], r.seg_r.at[step - 1],
                 s, (b + step) % 8)
        )
    for item in seg_copies:
        item.start()
    pending.extend(seg_copies)

    def first_norm(index, carried):
        rows = pl.ds(index * PIECE, PIECE)
        x = tok[rows, :].astype(F32)
        centre = x - jnp.mean(x, axis=-1, keepdims=True)
        spread = lax.rsqrt(jnp.mean(centre * centre, axis=-1, keepdims=True) + EPS)
        xhat = centre * spread
        r.xhat1[rows, :] = xhat
        r.rstd1[rows, :] = spread
        r.nrm[z, rows, :] = (xhat * local_row(3) + local_row(4)).astype(LOW)
        return carried

    lax.fori_loop(0, 4, first_norm, 0)

    def norm_copy(slot, side, up):
        part = r.nrm.at[slot, pl.ds(side * PACK, PACK)]
        sems = r.nu_s if up else r.nd_s
        return send(part, part, sems.at[slot, side], r.n_r.at[slot, side], s, b + 2 if up else b - 2)

    def norm_forward(slot, side):
        @pl.when(jnp.logical_and(slot <= z, z < 3))
        def _():
            norm_copy(slot, side, True).start()

        @pl.when(jnp.logical_and(slot >= z, z > 0))
        def _():
            norm_copy(slot, side, False).start()

    norm_forward(z, 0)
    norm_forward(z, 1)

    r.og[c] = ogi[...]
    og_copy = send(r.og.at[c], r.og.at[c], r.og_s.at[0], r.og_r.at[0], s, sib)
    og_copy.start()
    pending.append(og_copy)

    loads[0].wait()
    for part in range(3):
        start = pl.multiple_of(D * part + 384 * (z // 2) + 128 * (z % 2), 128)
        window = r.wf[:, pl.ds(start, 256)]
        r.dqkv[:, part * GROUP : (part + 1) * GROUP] = jnp.where(
            z % 2 == 1, window[:, 64:256], window[:, 0:192]
        )

    upper = z // 2
    qkv_bias = [qvb[0, pl.ds(z, 1), :], None, qvb[1, pl.ds(z, 1), :]]

    def split_keys(pair, row):
        for h in range(3):
            r.kh[h, pl.ds(row, ROWS), :] = pair[:, h * HEAD : (h + 1) * HEAD]
            r.vh[h, pl.ds(row, ROWS), 0:HEAD] = pair[:, GROUP + h * HEAD : GROUP + (h + 1) * HEAD]
            r.vh[h, pl.ds(row, ROWS), HEAD : 2 * HEAD] = jnp.ones((ROWS, HEAD), LOW)

    def kv_copy(slot):
        return send(r.kvo.at[slot], r.kvs.at[slot], r.kv_s.at[slot], r.kv_r.at[slot], s, sib)

    def project(slot):
        rows = r.nrm[slot]
        whole = dot(rows, r.dqkv[...])
        qs = (whole[:, :GROUP] + qkv_bias[0]).astype(LOW) * (1.0 / math.sqrt(HEAD))
        ks = whole[:, GROUP : 2 * GROUP].astype(LOW)
        vs = (whole[:, 2 * GROUP :] + qkv_bias[2]).astype(LOW)
        for h in range(3):
            r.q[h, pl.ds(slot * ROWS, ROWS), 0:HEAD] = qs[:, h * HEAD : (h + 1) * HEAD]
        r.kvo[slot, :, 0:GROUP] = ks
        r.kvo[slot, :, GROUP : 2 * GROUP] = vs
        kv_copy(slot).start()
        split_keys(r.kvo[slot], slot * ROWS)

    project(z)

    def arrivals(distance, carried):
        for side in range(2):
            for slot, there in ((z - distance, z >= distance), (z + distance, z + distance < CHIPS)):
                @pl.when(there)
                def _(slot=slot, side=side):
                    norm_copy(slot, side, True).wait_recv()
                    norm_forward(slot, side)

        for slot, there in ((z - distance, z >= distance), (z + distance, z + distance < CHIPS)):
            @pl.when(there)
            def _(slot=slot):
                project(slot)

        return carried

    lax.fori_loop(1, CHIPS, arrivals, 0)

    for item in seg_copies:
        item.wait_recv()
    for slot in range(CHIPS):
        for side, core in ((0, c), (1, 1 - c)):
            r.kseg[:, (side * CHIPS + slot) * ROWS : (side * CHIPS + slot + 1) * ROWS] = r.segs[
                core, slot, 0:1, :
            ]
        line = r.segs[c, slot, 0:1, :].astype(F32)
        r.qseg[slot * ROWS : (slot + 1) * ROWS, :] = jnp.transpose(
            jnp.broadcast_to(line, (128, ROWS))
        ).astype(jnp.int32)

    def take_sibling(slot, carried):
        kv_copy(slot).wait_recv()
        split_keys(r.kvs[slot], OWN + slot * ROWS)
        return carried

    lax.fori_loop(0, CHIPS, take_sibling, 0)

    r.kvt[:, :, 0:OWN] = jnp.transpose(r.kvo[...].reshape(OWN, 2 * GROUP)).reshape(6, HEAD, OWN)
    r.kvt[:, :, OWN:KEYS] = jnp.transpose(r.kvs[...].reshape(OWN, 2 * GROUP)).reshape(6, HEAD, OWN)
    BAND = 2 * ROWS

    def pack(ref, index, lane, value):
        width = value.shape[1]
        ref[index, :, lane : lane + width] = value[0:PACK]
        ref[index, :, GROUP + lane : GROUP + lane + width] = value[PACK:ROWS]

    def mg_copy(block):
        return send(r.mgs.at[block], r.mgr.at[z], r.mg_s.at[block], r.mg_r.at[z], s, 2 * block + c)

    def mg_arrival(slot):
        return send(r.mgs.at[slot], r.mgr.at[slot], r.mg_s.at[slot], r.mg_r.at[slot], s, 2 * slot + c)

    def forward_band(index, carried):
        h = index % 3
        band = (1 - upper) * (1 - index // 3) + upper * (index // 3)
        rows = pl.ds(pl.multiple_of(band * BAND, BAND), BAND)
        own_segs = r.qseg[rows, :]
        wide = jnp.concatenate([own_segs] * (KEYS // 128), axis=1)
        live = jnp.where(own_segs[:, :HEAD] != pad_number, 1.0, 0.0).astype(F32)
        raw = dot(r.q[h, rows, 0:HEAD], r.kvt[h])
        weights = jnp.where(wide == r.kseg[...], jnp.exp(raw), 0.0).astype(LOW)
        r.prob[h, rows, :] = weights
        total = dot(weights, r.vh[h])
        inverse = 1.0 / total[:, HEAD:]
        r.att[h, rows, 0:HEAD] = total[:, :HEAD] * inverse * live
        r.att[h, rows, HEAD : 2 * HEAD] = inverse

        @pl.when(h == 2)
        def _():
            for part in range(2):
                block = 2 * band + part
                block_rows = pl.ds(pl.multiple_of(block * ROWS, ROWS), ROWS)
                for head in range(3):
                    pack(r.mgs, block, head * HEAD, r.att[head, block_rows, 0:HEAD].astype(LOW))

                @pl.when(block != z)
                def _(block=block):
                    mg_copy(block).start()

                @pl.when(block == z)
                def _():
                    r.mgr[z] = r.mgs[z]

        return carried

    lax.fori_loop(0, 6, forward_band, 0)

    def others(fn):
        def run(index, carried):
            fn((z + 1 + index) % CHIPS)
            return carried

        lax.fori_loop(0, CHIPS - 1, run, 0)

    others(lambda slot: mg_arrival(slot).wait_recv())
    mgo_copy = send(r.mgr, r.mgo, r.mgo_s.at[0], r.mgo_r.at[0], s, sib)
    mgo_copy.start()
    pending.append(mgo_copy)

    for slot in range(CHIPS):
        r.mg[slot, 0:PACK, :] = r.mgr[slot, :, 0:GROUP]
        r.mg[slot, PACK:ROWS, :] = r.mgr[slot, :, GROUP : 2 * GROUP]

    loads[1].wait()

    def out_projection(index, carried):
        cols = pl.ds(pl.multiple_of(index * 256, 256), 256)
        total = tok[:, cols].astype(F32) + par[2:3, cols]
        for slot in range(CHIPS):
            total = total + dot(r.mg[slot], r.wo[slot * GROUP : (slot + 1) * GROUP, cols])
        r.resid[:, cols] = total
        return carried

    lax.fori_loop(0, 3, out_projection, 0)

    def second_norm(index, carried):
        rows = pl.ds(index * PIECE, PIECE)
        x = r.resid[rows, :]
        centre = x - jnp.mean(x, axis=-1, keepdims=True)
        spread = lax.rsqrt(jnp.mean(centre * centre, axis=-1, keepdims=True) + EPS)
        xhat = centre * spread
        r.xhat2[rows, :] = xhat
        r.rstd2[rows, :] = spread
        r.nt[c, rows, :] = (xhat * local_row(5) + local_row(6)).astype(LOW)
        return carried

    lax.fori_loop(0, 4, second_norm, 0)
    nt_copy = send(r.nt.at[c], r.nt.at[c], r.nt_s.at[0], r.nt_r.at[0], s, sib)
    nt_copy.start()
    pending.append(nt_copy)
    for item in loads[2:]:
        item.wait()
    og_copy.wait_recv()
    r.va[...] = jnp.zeros((8, D), F32)
    r.vb[...] = jnp.zeros((8, TILE), F32)
    r.va[3:4, :] = jnp.sum(ogi[...].astype(F32), axis=0, keepdims=True)
    nt_copy.wait_recv()

    def hop_one(unit):
        if isinstance(unit, int) and unit == TILES:
            one, two, to_one, to_two = r.oa, r.ob, r.roa, r.rob
        else:
            one, two, to_one, to_two = r.da.at[unit], r.db.at[unit], r.ra.at[unit], r.rb.at[unit]
        return (
            send(one.at[:, :, 1 - x], to_one, r.a1_s.at[unit], r.a1_r.at[unit], flip[1], b),
            send(two.at[:, 1 - y], to_two, r.b1_s.at[unit], r.b1_r.at[unit], flip[2], b),
        )

    def hop_two(unit):
        if isinstance(unit, int) and unit == TILES:
            one, two, to_one, to_two = r.oa2s, r.ob2s, r.oa2r, r.ob2r
        else:
            one, two, to_one, to_two = (
                r.a2s.at[unit], r.b2s.at[unit], r.a2r.at[unit], r.b2r.at[unit]
            )
        return (
            send(one, to_one, r.a2_s.at[unit], r.a2_r.at[unit], flip[2], b),
            send(two, to_two, r.b2_s.at[unit], r.b2_r.at[unit], flip[1], b),
        )

    is_end = jnp.logical_or(z == 0, z == 3)
    partner = z + 1 - 2 * (z % 2)
    inner = 3 - z
    outer = 3 - partner
    low_block = 1 - upper
    inner_of_end = 3 - partner

    def z_refs(unit):
        if isinstance(unit, int) and unit == TILES:
            return r.zo, r.rzo, r.zmo
        return r.zs.at[unit], r.rz.at[unit], r.zm.at[unit]

    def z_bundle(unit):
        here, there, _ = z_refs(unit)
        three = pl.ds(low_block, 3)
        return send(here.at[three], there.at[three], r.z_s.at[unit, 0], r.z_r.at[unit, partner],
                    s, 2 * partner + c)

    def z_near(unit):
        here, there, _ = z_refs(unit)
        return send(here.at[partner], there.at[z], r.z_s.at[unit, 1], r.z_r.at[unit, z],
                    s, 2 * partner + c)

    def z_inner(unit):
        _, there, merged = z_refs(unit)
        return send(merged.at[0], there.at[outer], r.z_s.at[unit, 2], r.z_r.at[unit, outer],
                    s, 2 * inner + c)

    def z_outer(unit):
        _, there, merged = z_refs(unit)
        return send(merged.at[1], there.at[z], r.z_s.at[unit, 3], r.z_r.at[unit, z],
                    s, 2 * outer + c)

    def z_three_arrival(unit):
        here, there, _ = z_refs(unit)
        three = pl.ds(low_block, 3)
        return send(here.at[three], there.at[three], r.z_s.at[unit, 0], r.z_r.at[unit, z],
                    s, 2 * partner + c)

    def z_arrival(unit, slot):
        here, there, _ = z_refs(unit)
        return send(here.at[slot], there.at[slot], r.z_s.at[unit, 0], r.z_r.at[unit, slot],
                    s, 2 * partner + c)

    owner = s // 2
    mine = 2 * z + owner

    def fin_copy(unit, step):
        if isinstance(unit, int) and unit == TILES:
            here, there = r.fo, out_fo.at[s % 2, c]
        else:
            here, there = r.fin.at[unit], out_fin.at[unit, s % 2, c]
        return send(here, there, r.f_s.at[unit, step], r.f_r.at[unit, 2 * (s % 2) + c],
                    s if step == 0 else flip[step], mine)

    def fin_arrival(unit, piece, core):
        if isinstance(unit, int) and unit == TILES:
            here, there = r.fo, out_fo.at[piece, core]
        else:
            here, there = r.fin.at[unit], out_fin.at[unit, piece, core]
        return send(here, there, r.f_s.at[unit, 0], r.f_r.at[unit, 2 * piece + core], s, sib)

    def mlp_grads(tile):
        cols = pl.ds(pl.multiple_of(tile * TILE, TILE), TILE)

        r.da[tile] = dot_tn(r.nt[...].reshape(2 * ROWS, D), r.hg[:, cols]).astype(LOW).reshape(
            CHIPS, 2, 2, PIECE, TILE
        )
        r.db[tile] = dot_tn(r.og[...].reshape(2 * ROWS, D), r.act[:, cols]).astype(LOW).reshape(
            CHIPS, 2, 2, PIECE, TILE
        )

    def service_zero(unit):
        for item in hop_one(unit):
            item.start()

    def service_one(unit):
        for item in hop_one(unit):
            item.wait_recv()
        if isinstance(unit, int) and unit == TILES:
            for block in range(2):
                r.oa2s[block] = (
                    r.oa[block, 1 - y, x].astype(F32) + r.roa[block, 1 - y].astype(F32)
                ).astype(LOW)
                r.ob2s[block] = (
                    r.ob[block, y, 1 - x].astype(F32) + r.rob[block, 1 - x].astype(F32)
                ).astype(LOW)
        else:
            def add(block, carried):
                r.a2s[unit, block] = (
                    r.da[unit, block, 1 - y, x].astype(F32) + r.ra[unit, block, 1 - y].astype(F32)
                ).astype(LOW)
                r.b2s[unit, block] = (
                    r.db[unit, block, y, 1 - x].astype(F32) + r.rb[unit, block, 1 - x].astype(F32)
                ).astype(LOW)
                return carried

            lax.fori_loop(0, CHIPS, add, 0)
        for item in hop_two(unit):
            item.start()

    def service_two(unit):
        for item in hop_two(unit):
            item.wait_recv()
        if isinstance(unit, int) and unit == TILES:
            for block in range(2):
                r.zo[block] = (
                    r.oa[block, y, x].astype(F32) + r.roa[block, y].astype(F32)
                    + r.oa2r[block].astype(F32)
                ).astype(LOW)
                r.zo[2 + block] = (
                    r.ob[block, y, x].astype(F32) + r.rob[block, x].astype(F32)
                    + r.ob2r[block].astype(F32)
                ).astype(LOW)
        else:
            def add(block, carried):
                r.zs[unit, block, 0] = (
                    r.da[unit, block, y, x].astype(F32) + r.ra[unit, block, y].astype(F32)
                    + r.a2r[unit, block].astype(F32)
                ).astype(LOW)
                r.zs[unit, block, 1] = (
                    r.db[unit, block, y, x].astype(F32) + r.rb[unit, block, x].astype(F32)
                    + r.b2r[unit, block].astype(F32)
                ).astype(LOW)
                return carried

            lax.fori_loop(0, CHIPS, add, 0)
        @pl.when(is_end)
        def _():
            z_bundle(unit).start()

        @pl.when(jnp.logical_not(is_end))
        def _():
            z_near(unit).start()

    def service_three(unit):
        here, there, merged = z_refs(unit)

        @pl.when(jnp.logical_not(is_end))
        def _():
            z_three_arrival(unit).wait_recv()
            merged[0] = (here[inner].astype(F32) + there[inner].astype(F32)).astype(LOW)
            merged[1] = (here[outer].astype(F32) + there[outer].astype(F32)).astype(LOW)
            z_inner(unit).start()
            z_outer(unit).start()

    def service_four(unit):
        here, there, _ = z_refs(unit)
        z_arrival(unit, partner).wait_recv()

        @pl.when(is_end)
        def _():
            z_arrival(unit, inner_of_end).wait_recv()

        second = jnp.where(is_end, inner_of_end, z)
        total = here[z].astype(F32) + there[partner].astype(F32) + there[second].astype(F32)
        if isinstance(unit, int) and unit == TILES:
            r.fo[...] = total.astype(LOW)
        else:
            r.fin[unit] = total.astype(LOW)
        for step in (1, 2, 3):
            fin_copy(unit, step).start()

        @pl.when(mine != b)
        def _():
            fin_copy(unit, 0).start()

        @pl.when(mine == b)
        def _():
            if isinstance(unit, int) and unit == TILES:
                out_fo[s % 2, c] = r.fo[...]
            else:
                out_fin[unit, s % 2, c] = r.fin[unit]

    def run_services(listed):
        for kind, unit in listed:
            (service_zero, service_one, service_two, service_three, service_four)[kind](unit)


    r.lo[...] = jnp.zeros((2, ROWS, D), F32)
    r.ng[...] = jnp.zeros((2, ROWS, D), F32)

    WIDE = 2 * TILE

    def mlp_tile(index, carried):
        cols = pl.ds(pl.multiple_of(index * WIDE, WIDE), WIDE)
        bias = b1[:, pl.ds(pl.multiple_of(c * HALF + index * WIDE, WIDE), WIDE)]
        w1 = jnp.concatenate(
            [r.da[2 * index + part].reshape(D, TILE) for part in range(2)], axis=1
        )
        w2 = r.w2[cols, :]
        hidden = dot(r.nt[...].reshape(2 * ROWS, D), w1) + bias
        gate = 0.5 * (1.0 + lax.erf(hidden * (1.0 / math.sqrt(2.0))))
        slope = gate + hidden * jnp.exp(-0.5 * hidden * hidden) * (1.0 / math.sqrt(2.0 * math.pi))
        active = (hidden * gate).astype(LOW)
        grad = (slope * dot_nt(r.og[...].reshape(2 * ROWS, D), w2)).astype(LOW)
        r.act[:, cols] = active
        r.hg[:, cols] = grad
        r.vh1[:, cols] = jnp.sum(grad.astype(F32), axis=0, keepdims=True)
        r.lo[...] += dot(active, w2).reshape(2, ROWS, D)
        r.ng[...] += dot_nt(grad, w1).reshape(2, ROWS, D)
        for part in range(2):
            tile = 2 * index + part

            @pl.when(tile < EARLY)
            def _(tile=tile):
                mlp_grads(tile)

            @pl.when(tile < STARTED)
            def _(tile=tile):
                service_zero(tile)

        return carried

    lax.fori_loop(0, TILES // 2, mlp_tile, 0)
    for part in range(2):
        r.va[pl.ds(4 + 2 * c + part, 1), :] = r.vh1[:, part * D : (part + 1) * D]
    ng_copy = send(r.ng.at[1 - c], r.ngr, r.ng_s.at[0], r.ng_r.at[0], s, sib)
    lo_copy = send(r.lo.at[1 - c], r.lor, r.lo_s.at[0], r.lo_r.at[0], s, sib)
    ng_copy.start()
    lo_copy.start()

    mlp_grads(4)
    run_services(PLAN["before_norm"])

    ng_copy.wait_recv()

    def second_back(index, carried):
        rows = pl.ds(index * PIECE, PIECE)
        grad = r.ng[c, rows, :] + r.ngr[rows, :]
        xhat = r.xhat2[rows, :]
        scaled = grad * local_row(5)
        mean_one = jnp.mean(scaled, axis=-1, keepdims=True)
        mean_two = jnp.mean(scaled * xhat, axis=-1, keepdims=True)
        through = r.rstd2[rows, :] * (scaled - mean_one - xhat * mean_two)
        resid_grad = ogi[rows, :].astype(F32) + through
        low = resid_grad.astype(LOW)
        r.xhat2[rows, :] = resid_grad
        r.bl[c, rows, :] = low
        r.va[0:1, :] += jnp.sum(low.astype(F32), axis=0, keepdims=True)
        r.va[1:2, :] += jnp.sum(grad * xhat, axis=0, keepdims=True)
        r.va[2:3, :] += jnp.sum(grad, axis=0, keepdims=True)
        return carried

    lax.fori_loop(0, 4, second_back, 0)
    bl_copy = send(r.bl.at[c], r.bl.at[c], r.bl_s.at[0], r.bl_r.at[0], s, sib)
    bl_copy.start()
    pending.append(bl_copy)

    def ag_copy(block):
        return send(r.ags.at[block], r.ag.at[z], r.ag_s.at[block], r.ag_r.at[z], s, 2 * block + c)

    def ag_arrival(slot):
        return send(r.ags.at[slot], r.ag.at[slot], r.ag_s.at[slot], r.ag_r.at[slot], s, 2 * slot + c)

    def attended_block(index, carried):
        block = (z + 1 + index) % CHIPS
        wide = pl.ds(pl.multiple_of(block * GROUP, GROUP), GROUP)
        pack(r.ags, block, 0, dot_nt(r.bl[c], r.wo[wide, :]).astype(LOW))

        @pl.when(block != z)
        def _():
            ag_copy(block).start()

        @pl.when(block == z)
        def _():
            r.ag[z] = r.ags[z]

        return carried

    lax.fori_loop(0, CHIPS, attended_block, 0)

    def vector_sums(mine_ref, pair_ref, z_ref, x_ref, send_sems, recv_sems):
        def pair():
            return send(mine_ref, pair_ref, send_sems.at[0], recv_sems.at[0], s, sib)

        def along(step):
            return send(z_ref.at[z], z_ref.at[z], send_sems.at[step], recv_sems.at[step],
                        s, (b + 2 * step) % 8)

        def over(step):
            return send(x_ref.at[s], x_ref.at[s], send_sems.at[3 + step], recv_sems.at[3 + step],
                        flip[step], b)

        def stage_one():
            pair().start()
            pending.append(pair())

        def stage_two():
            pair().wait_recv()
            r_first = jnp.where(c == 0, mine_ref[...], pair_ref[...])
            r_second = jnp.where(c == 0, pair_ref[...], mine_ref[...])
            z_ref[z] = r_first + r_second
            for step in (1, 2, 3):
                along(step).start()
                pending.append(along(step))

        def stage_three():
            for step in (1, 2, 3):
                along(step).wait_recv()
            x_ref[s] = z_ref[0] + z_ref[1] + z_ref[2] + z_ref[3]
            for step in (1, 2, 3):
                over(step).start()
                pending.append(over(step))

        def stage_four():
            for step in (1, 2, 3):
                over(step).wait_recv()
            return x_ref[0] + x_ref[1] + x_ref[2] + x_ref[3]

        return stage_one, stage_two, stage_three, stage_four

    va_stages = vector_sums(r.va, r.vap, r.vaz, r.vax, r.va_s, r.va_r)
    vq_stages = vector_sums(r.vq, r.vqp, r.vqz, r.vqx, r.vq_s, r.vq_r)
    va_stages[0]()

    run_services(PLAN["after_norm"])
    mlp_grads(5)
    mgo_copy.wait_recv()
    bl_copy.wait_recv()
    side = pl.ds(pl.multiple_of(c * OUT_HALF, OUT_HALF), OUT_HALF)
    for block in range(CHIPS):
        theirs = jnp.concatenate(
            [r.mgo[block, :, 0:GROUP], r.mgo[block, :, GROUP : 2 * GROUP]], axis=0
        )
        grad = dot_tn(r.mg[block], r.bl[c, :, side]) + dot_tn(theirs, r.bl[1 - c, :, side])
        low = grad.astype(LOW)
        home = r.oa if block < 2 else r.ob
        for piece in range(4):
            home[block % 2, piece // 2, piece % 2] = low[piece * PIECE : (piece + 1) * PIECE]
    va_stages[1]()

    lo_copy.wait_recv()

    def layer_rows(index, carried):
        rows = pl.ds(index * PIECE, PIECE)
        out_layer[rows, :] = (
            r.resid[rows, :] + r.lo[c, rows, :] + r.lor[rows, :] + local_row(7)
        ).astype(LOW)
        return carried

    lax.fori_loop(0, 4, layer_rows, 0)

    others(lambda slot: ag_arrival(slot).wait_recv())
    for h in range(3):
        for slot in range(CHIPS):
            for part in range(2):
                start = slot * ROWS + part * PACK
                r.agh[h, start : start + PACK, :] = r.ag[
                    slot, :, part * GROUP + h * HEAD : part * GROUP + (h + 1) * HEAD
                ]
    run_services(PLAN["before_loop"])

    ng_copy.wait_send()
    lo_copy.wait_send()
    key_sums, value_sums = r.ng, r.lo


    def pair_copies(h):
        return (send(r.dks.at[h], r.dkr.at[h], r.dk_s.at[h], r.dk_r.at[h], s, sib),)

    def dq_copy(h, block):
        return send(r.dqs.at[h, block], r.dqr.at[h, z], r.dq_s.at[h, block], r.dq_r.at[h, z],
                    s, 2 * block + c)

    def dq_arrival(h, slot):
        return send(r.dqs.at[h, slot], r.dqr.at[h, slot], r.dq_s.at[h, slot], r.dq_r.at[h, slot],
                    s, 2 * slot + c)

    def finish_head(h):
        for item in pair_copies(h):
            item.wait_recv()
        lines = slice(h * HEAD, (h + 1) * HEAD)
        key_grad = jnp.transpose((key_sums[0, lines, :] + r.dkr[h, 0].astype(F32)).astype(LOW))
        value_grad = jnp.transpose((value_sums[0, lines, :] + r.dkr[h, 1].astype(F32)).astype(LOW))
        for part, whole in enumerate((r.q[h, :, HEAD : 2 * HEAD], key_grad, value_grad)):
            lane = h * GROUP + part * HEAD
            r.dqkv[:, lane : lane + HEAD] = whole
            for block in range(CHIPS):
                pack(r.dqs.at[h], block, part * HEAD, whole[block * ROWS : (block + 1) * ROWS])
        others(lambda block: dq_copy(h, block).start())
        r.dqr[h, z] = r.dqs[h, z]

    def backward_band(index, carried):
        h = index // 2
        part = index % 2
        rows = pl.ds(pl.multiple_of(part * BAND, BAND), BAND)
        live = jnp.where(r.qseg[rows, :][:, :HEAD] != pad_number, 1.0, 0.0).astype(F32)
        grad = r.agh[h, rows, :].astype(F32) * live
        inverse = r.att[h, rows, HEAD : 2 * HEAD]
        correct = jnp.sum(grad * r.att[h, rows, 0:HEAD], axis=-1, keepdims=True) * inverse[:, 0:1]
        correct = correct.astype(LOW).astype(F32)
        scaled = (grad * inverse).astype(LOW)
        product = dot(scaled, r.kvt[3 + h])
        weights = r.prob[h, rows, :]
        slopes = (weights.astype(F32) * (product - correct)).astype(LOW)
        r.q[h, rows, HEAD : 2 * HEAD] = (
            dot(slopes, r.kh[h]) * (1.0 / math.sqrt(HEAD))
        ).astype(LOW)
        keys = dot(jnp.transpose(r.q[h, rows, 0:HEAD]), slopes)
        values = dot(jnp.transpose(scaled), weights)

        lines = pl.ds(pl.multiple_of(h * HEAD, HEAD), HEAD)

        @pl.when(part == 0)
        def _():
            for side in range(2):
                span = slice(side * OWN, (side + 1) * OWN)
                key_sums[side, lines, :] = keys[:, span]
                value_sums[side, lines, :] = values[:, span]

        @pl.when(part == 1)
        def _():
            key_sums[0, lines, :] += keys[:, 0:OWN]
            value_sums[0, lines, :] += values[:, 0:OWN]
            r.dks[h, 0] = (key_sums[1, lines, :] + keys[:, OWN:KEYS]).astype(LOW)
            r.dks[h, 1] = (value_sums[1, lines, :] + values[:, OWN:KEYS]).astype(LOW)
            for item in pair_copies(h):
                item.start()

        for turn, listed in PLAN["loop"]:
            @pl.when(index == turn)
            def _(listed=listed):
                run_services(listed)

        for turn, head in ((2, 0), (4, 1)):
            @pl.when(index == turn)
            def _(head=head):
                finish_head(head)

        return carried

    lax.fori_loop(0, 6, backward_band, 0)

    finish_head(2)
    run_services(PLAN["after_loop"])

    grad = dot_tn(r.nrm[...].reshape(OWN, D), r.dqkv[...])
    r.dwq[...] = grad.astype(LOW).reshape(CHIPS, 4, PIECE, QKV)
    q0_copy = send(
        r.dwq.at[pl.ds(2 * (1 - c), 2)], r.dwqr, r.q0_s.at[0], r.q0_r.at[0], s, sib
    )
    q0_copy.start()
    pending.append(q0_copy)
    column_sums = jnp.sum(r.dqkv[...].astype(F32), axis=0, keepdims=True)
    r.vq[...] = jnp.zeros((8, TILE), F32)
    for lane, row in ((0, 0), (2 * HEAD, CHIPS)):
        r.vq[pl.ds(row + z, 1), 0:GROUP] = jnp.concatenate(
            [
                column_sums[:, h * GROUP + lane : h * GROUP + lane + HEAD]
                for h in range(3)
            ],
            axis=1,
        )
    vq_stages[0]()
    va_stages[2]()
    q0_copy.wait_recv()
    for part in range(2):
        for piece in range(4):
            r.dwqx[part, piece] = (
                r.dwq[2 * c + part, piece].astype(F32) + r.dwqr[part, piece].astype(F32)
            ).astype(LOW)
    qx_copies = [
        send(r.dwqx.at[:, flip[step]], r.rxq.at[step - 1], r.qx_s.at[step - 1],
             r.qx_r.at[step - 1], flip[step], b)
        for step in (1, 2, 3)
    ]
    for item in qx_copies:
        item.start()
    pending.extend(qx_copies)

    run_services(PLAN["after_qkv"])
    vq_stages[1]()

    for h in range(3):
        others(lambda slot, h=h: dq_arrival(h, slot).wait_recv())
        for slot in range(CHIPS):
            for part in range(3):
                lane = part * D + slot * GROUP + h * HEAD
                for side in range(2):
                    start = side * GROUP + part * HEAD
                    r.rowg[side * PACK : (side + 1) * PACK, lane : lane + HEAD] = r.dqr[
                        h, slot, :, start : start + HEAD
                    ]

    def first_grads(index, carried):
        rows = pl.ds(pl.multiple_of(index * 256, 256), 256)
        r.ngr[:, rows] = dot_nt(r.rowg[...], r.wf[rows, :])
        return carried

    lax.fori_loop(0, 3, first_grads, 0)

    def first_back(index, carried):
        rows = pl.ds(index * PIECE, PIECE)
        grad = r.ngr[rows, :]
        xhat = r.xhat1[rows, :]
        scaled = grad * local_row(3)
        mean_one = jnp.mean(scaled, axis=-1, keepdims=True)
        mean_two = jnp.mean(scaled * xhat, axis=-1, keepdims=True)
        through = r.rstd1[rows, :] * (scaled - mean_one - xhat * mean_two)
        out_tok[rows, :] = (r.xhat2[rows, :] + through).astype(LOW)
        gains = jnp.sum(grad * xhat, axis=0, keepdims=True)
        shifts = jnp.sum(grad, axis=0, keepdims=True)
        for part in range(3):
            lanes = slice(part * TILE, (part + 1) * TILE)
            r.vb[part : part + 1, :] += gains[:, lanes]
            r.vb[4 + part : 5 + part, :] += shifts[:, lanes]
        return carried

    lax.fori_loop(0, 4, first_back, 0)

    vb_copies = [
        send(r.vb, r.vbr.at[b], r.vb_s.at[step - 1], r.vb_r.at[step - 1], s, (b + step) % 8)
        for step in range(1, 8)
    ]
    r.vbr[b] = r.vb[...]
    for item in vb_copies:
        item.start()
    pending.extend(vb_copies)

    run_services(PLAN["after_rows"])

    for item in qx_copies:
        item.wait_recv()
    def qz_copy(part):
        return send(r.zq.at[part], r.rzq.at[z], r.qz_s.at[part], r.qz_r.at[z],
                    s, 2 * (2 * c + part) + owner)

    for part in range(2):
        total = r.dwqx[part, s].astype(F32)
        for step in range(3):
            total = total + r.rxq[step, part].astype(F32)
        r.zq[part] = total.astype(LOW)
        there = 2 * (2 * c + part) + owner

        @pl.when(there != b)
        def _(part=part):
            qz_copy(part).start()

        @pl.when(there == b)
        def _(part=part):
            r.rzq[z] = r.zq[part]

    vq_stages[2]()
    run_services(PLAN["before_sums"])

    for item in vb_copies:
        item.wait_recv()
    total = r.vbr[0]
    for slot in range(1, 8):
        total = total + r.vbr[slot]
    r.vbx[s] = total
    vbx_copies = [
        send(r.vbx.at[s], r.vbx.at[s], r.vbx_s.at[step - 1], r.vbx_r.at[step - 1], flip[step], b)
        for step in (1, 2, 3)
    ]
    for item in vbx_copies:
        item.start()
    pending.extend(vbx_copies)

    run_services(PLAN["last"])

    def qf_copy(step):
        return send(r.rzq, out_finq.at[s % 2], r.qf_s.at[step - 1], r.qf_r.at[step - 1],
                    flip[step], b)

    def qz_arrival(slot):
        return send(r.zq.at[0], r.rzq.at[slot], r.qz_s.at[0], r.qz_r.at[slot], s, sib)

    @pl.when(owner == c)
    def _():
        for slot in range(CHIPS):
            @pl.when(jnp.logical_or(slot != z, z // 2 != c))
            def _(slot=slot):
                qz_arrival(slot).wait_recv()

        for step in (1, 2, 3):
            qf_copy(step).start()
        out_finq[s % 2] = r.rzq[...]

    for piece in range(2):
        for core in range(2):
            @pl.when(jnp.logical_or(2 * c + piece != s, core != c))
            def _(piece=piece, core=core):
                for unit in range(TILES + 1):
                    fin_arrival(unit, piece, core).wait_recv()

    for step in (1, 2, 3):
        @pl.when(flip[step] // 2 == c)
        def _(step=step):
            qf_copy(step).wait_recv()

    for item in vbx_copies:
        item.wait_recv()
    out_va[...] = va_stages[3]()
    out_vq[...] = vq_stages[3]()
    out_vb[...] = r.vbx[0] + r.vbx[1] + r.vbx[2] + r.vbx[3]

    for slot in range(CHIPS):
        for side in range(2):
            @pl.when(jnp.logical_and(slot <= z, z < 3))
            def _(slot=slot, side=side):
                norm_copy(slot, side, True).wait_send()

            @pl.when(jnp.logical_and(slot >= z, z > 0))
            def _(slot=slot, side=side):
                norm_copy(slot, side, False).wait_send()

        kv_copy(slot).wait_send()
    for make in (mg_copy, ag_copy):
        others(lambda slot, make=make: make(slot).wait_send())
    for h in range(3):
        others(lambda slot, h=h: dq_copy(h, slot).wait_send())
        for item in pair_copies(h):
            item.wait_send()
    for item in pending:
        item.wait_send()
    for unit in range(TILES + 1):
        for item in hop_one(unit) + hop_two(unit):
            item.wait_send()

        @pl.when(is_end)
        def _(unit=unit):
            z_bundle(unit).wait_send()

        @pl.when(jnp.logical_not(is_end))
        def _(unit=unit):
            z_near(unit).wait_send()
            z_inner(unit).wait_send()
            z_outer(unit).wait_send()

        for step in (1, 2, 3):
            fin_copy(unit, step).wait_send()

        @pl.when(mine != b)
        def _(unit=unit):
            fin_copy(unit, 0).wait_send()

    for part in range(2):
        @pl.when(2 * (2 * c + part) + owner != b)
        def _(part=part):
            qz_copy(part).wait_send()

    @pl.when(owner == c)
    def _():
        for step in (1, 2, 3):
            qf_copy(step).wait_send()


def finish_body(tok, layer, fin, fo, finq, va, vq, vb, *outs):
    (layer_out, tok_out, qkv_w, out_w, up_w, down_w, qb, v_b, ob, g1, s1, g2, s2, down_b, up_b) = outs
    layer_out[...] = layer[...]
    tok_out[...] = tok[...]
    for piece in range(2):
        rows = slice(piece * PIECE, (piece + 1) * PIECE)
        for core in range(2):
            out_w[rows, core * OUT_HALF : (core + 1) * OUT_HALF] = fo[piece, core].astype(F32)
            for tile in range(TILES):
                start = core * HALF + tile * TILE
                up_w[rows, start : start + TILE] = fin[tile, piece, core, 0].astype(F32)
                down_w[rows, start : start + TILE] = fin[tile, piece, core, 1].astype(F32)
        for slot in range(CHIPS):
            for h in range(3):
                for part in range(3):
                    lane = part * D + slot * GROUP + h * HEAD
                    source = h * GROUP + part * HEAD
                    qkv_w[rows, lane : lane + HEAD] = finq[
                        piece, slot, :, source : source + HEAD
                    ].astype(F32)
    b = lax.axis_index("blk")
    for index in range(8):
        @pl.when(b == index)
        def _(index=index):
            cols = slice(index * 96, (index + 1) * 96)
            for ref, row in ((ob, 0), (g2, 1), (s2, 2), (down_b, 3)):
                ref[...] = va[row, cols]
            for ref, row in ((g1, 0), (s1, 4)):
                whole = jnp.concatenate([vb[row + part : row + part + 1, :] for part in range(3)], axis=1)
                ref[...] = whole[0, cols]
            slot = index // 2
            half = slice((index % 2) * 96, (index % 2 + 1) * 96)
            qb[...] = vq[slot, half]
            v_b[...] = vq[CHIPS + slot, half]
            start = (index * 384) % D
            up_b[...] = va[4 + index * 384 // D, start : start + 384]


def chip_body(
    tokens, segment_ids, out_grad, query_key_value_weight, query_bias, value_bias,
    attention_output_weight, attention_output_bias, first_gain, first_shift,
    second_gain, second_shift, mlp_input_weight, mlp_input_bias, mlp_output_weight,
    mlp_output_bias,
):
    pad_number = tokens.shape[1] * lax.axis_size("blk") // SHORT_LO + 2
    names = scratch_list()
    any_space = pl.BlockSpec(memory_space=pl.ANY)
    in_vmem = pl.BlockSpec(memory_space=pltpu.VMEM)
    results = pl.pallas_call(
        functools.partial(kernel_body, tuple(names), pad_number),
        out_shape=(
            jax.ShapeDtypeStruct((ROWS, D), LOW),
            jax.ShapeDtypeStruct((ROWS, D), LOW),
            jax.ShapeDtypeStruct((TILES, 2, 2, 2, PIECE, TILE), LOW),
            jax.ShapeDtypeStruct((2, 2, PIECE, OUT_HALF), LOW),
            jax.ShapeDtypeStruct((2, CHIPS, PIECE, QKV), LOW),
            jax.ShapeDtypeStruct((8, D), F32),
            jax.ShapeDtypeStruct((8, TILE), F32),
            jax.ShapeDtypeStruct((8, TILE), F32),
        ),
        in_specs=[in_vmem] * 3 + [any_space] * 4 + [in_vmem] * 9,
        out_specs=(in_vmem,) * 8,
        scratch_shapes=list(names.values()),
        compiler_params=pltpu.CompilerParams(
            collective_id=0, has_side_effects=True, vmem_limit_bytes=VMEM_LIMIT
        ),
        name="encoder_block",
    )(
        tokens.reshape(ROWS, D), segment_ids, out_grad.reshape(ROWS, D),
        query_key_value_weight, attention_output_weight,
        mlp_input_weight.reshape(CHIPS, 2, 2, PIECE, FF), mlp_output_weight,
        query_bias, value_bias, attention_output_bias, first_gain, first_shift,
        second_gain, second_shift, mlp_output_bias, mlp_input_bias,
    )
    wide = [(96, 3 * D), (96, D), (96, FF), (96, FF)]
    shapes = (
        [jax.ShapeDtypeStruct((ROWS, D), LOW)] * 2
        + [jax.ShapeDtypeStruct(shape, F32) for shape in wide]
        + [jax.ShapeDtypeStruct((96,), F32)] * 8
        + [jax.ShapeDtypeStruct((384,), F32)]
    )
    (layer_out, tok_out, qkv_w, out_w, up_w, down_w, qb, vb, ob, g1, s1, g2, s2, down_b, up_b) = (
        pl.pallas_call(
            finish_body,
            out_shape=tuple(shapes),
            in_specs=[in_vmem] * 8,
            out_specs=(in_vmem,) * len(shapes),
            compiler_params=pltpu.CompilerParams(vmem_limit_bytes=VMEM_LIMIT),
            name="place_results",
        )(*results)
    )
    return (
        layer_out.reshape(tokens.shape), tok_out.reshape(tokens.shape), qkv_w, qb, vb, out_w, ob,
        g1, s1, g2, s2, up_w, up_b, jnp.transpose(down_w), down_b,
    )


def solution(mesh):
    placed = (
        P("seq", "blk", None),
        P("seq", "blk"),
        P("seq", "blk", None),
        P(),
        P(),
        P(),
        P(),
        P(),
        P(),
        P(),
        P(),
        P(),
        P(),
        P(),
        P(),
        P(),
    )
    chosen = chip_body if mesh.shape["seq"] == 4 and mesh.shape["blk"] == 8 else body
    return jax.shard_map(
        chosen,
        mesh=mesh,
        in_specs=placed,
        out_specs=(
            P("seq", "blk", None),
            P("seq", "blk", None),
            P("blk", None),
            P("blk"),
            P("blk"),
            P("blk", None),
            P("blk"),
            P("blk"),
            P("blk"),
            P("blk"),
            P("blk"),
            P("blk", None),
            P("blk"),
            P(None, "blk"),
            P("blk"),
        ),
        check_vma=False,
    )
```

```python
import functools
import math

import jax
import jax.numpy as jnp
from jax import lax
from jax.experimental import pallas as pl
from jax.experimental.pallas import tpu as pltpu
from jax.sharding import PartitionSpec as P

HEADS = 12
HEAD = 64
SHORT_LO = 25


EPS = 1e-06


def layer_norm(inputs, norm_gain, norm_shift):
    centre = inputs - jnp.mean(inputs, axis=-1, keepdims=True)
    spread = jnp.mean(centre * centre, axis=-1, keepdims=True)
    return centre * lax.rsqrt(spread + EPS) * norm_gain + norm_shift


def gelu_exact(inputs):
    return jax.nn.gelu(inputs, approximate=False)


def score_block(queries, query_segs, key_rows, key_segs):
    raw_scores = jnp.einsum("qhd,khd->hqk", queries, key_rows, preferred_element_type=jnp.float32)
    same_image = (query_segs[:, None] == key_segs[None, :])[None]
    return jnp.where(same_image, jnp.exp(raw_scores * (1.0 / math.sqrt(HEAD))), 0.0)


def forward_step(carried, queries, query_segs, key_rows, value_rows, key_segs):
    totals, summed = carried
    weights = score_block(queries, query_segs, key_rows, key_segs)
    totals = totals + jnp.transpose(jnp.sum(weights, axis=-1))
    summed = summed + jnp.einsum(
        "hqk,khd->qhd", weights.astype(jnp.bfloat16), value_rows, preferred_element_type=jnp.float32
    )
    return (totals, summed)


def back_step(queries, query_grads, query_corr, query_segs, key_rows, value_rows, key_segs):
    weights = score_block(queries, query_segs, key_rows, key_segs)
    product = jnp.einsum(
        "qhd,khd->hqk", query_grads, value_rows, preferred_element_type=jnp.float32
    )
    shifted = jnp.transpose(query_corr.astype(jnp.float32))[:, :, None]
    score_grads = (weights * (product - shifted) * (1.0 / math.sqrt(HEAD))).astype(jnp.bfloat16)
    return (weights.astype(jnp.bfloat16), score_grads)


def key_value_grads(queries, query_grads, query_corr, query_segs, key_rows, value_rows, key_segs):
    weights_low, score_grads = back_step(
        queries, query_grads, query_corr, query_segs, key_rows, value_rows, key_segs
    )
    key_part = jnp.einsum("hqk,qhd->khd", score_grads, queries, preferred_element_type=jnp.float32)
    value_part = jnp.einsum(
        "hqk,qhd->khd", weights_low, query_grads, preferred_element_type=jnp.float32
    )
    return (key_part, value_part)


def body(
    tokens,
    segment_ids,
    out_grad,
    query_key_value_weight,
    query_bias,
    value_bias,
    attention_output_weight,
    attention_output_bias,
    first_gain,
    first_shift,
    second_gain,
    second_shift,
    mlp_input_weight,
    mlp_input_bias,
    mlp_output_weight,
    mlp_output_bias,
):
    model_width = tokens.shape[-1]
    row_count = tokens.shape[0] * tokens.shape[1]
    head_shape = (row_count, HEADS, HEAD)
    pad_number = tokens.shape[1] * lax.axis_size("blk") // SHORT_LO + 2
    token_rows = tokens.reshape(row_count, model_width).astype(jnp.float32)
    seg_rows = segment_ids.reshape(row_count)
    live_rows = (seg_rows != pad_number).astype(jnp.float32)
    first_normed, first_back = jax.vjp(
        layer_norm, token_rows, first_gain.astype(jnp.float32), first_shift.astype(jnp.float32)
    )
    first_low = first_normed.astype(jnp.bfloat16)
    query_key_value_bias = jnp.concatenate(
        [
            query_bias.astype(jnp.float32),
            jnp.zeros((model_width,), jnp.float32),
            value_bias.astype(jnp.float32),
        ]
    )
    projected_rows = (
        jnp.dot(first_low, query_key_value_weight, preferred_element_type=jnp.float32)
        + query_key_value_bias
    )
    query_flat = projected_rows[:, :model_width].astype(jnp.bfloat16)
    key_flat = projected_rows[:, model_width : 2 * model_width].astype(jnp.bfloat16)
    value_flat = projected_rows[:, 2 * model_width :].astype(jnp.bfloat16)
    queries = query_flat.reshape(head_shape)
    gathered = (
        lax.all_gather(key_flat, "blk", axis=0, tiled=True),
        lax.all_gather(value_flat, "blk", axis=0, tiled=True),
        lax.all_gather(seg_rows, "blk", axis=0, tiled=True),
    )
    all_keys = gathered[0].reshape(-1, HEADS, HEAD)
    all_values = gathered[1].reshape(-1, HEADS, HEAD)
    all_segs = gathered[2]
    seq_rows = all_keys.shape[0]
    key_span = math.gcd(seq_rows, 2048)
    turns = seq_rows // key_span

    def forward_turn(index, carried):
        begin_row = index * key_span
        return forward_step(
            carried,
            queries,
            seg_rows,
            lax.dynamic_slice_in_dim(all_keys, begin_row, key_span, 0),
            lax.dynamic_slice_in_dim(all_values, begin_row, key_span, 0),
            lax.dynamic_slice_in_dim(all_segs, begin_row, key_span, 0),
        )

    totals, summed = lax.fori_loop(
        0,
        turns,
        forward_turn,
        (jnp.zeros((row_count, HEADS), jnp.float32), jnp.zeros(head_shape, jnp.float32)),
    )
    attended = summed / totals[:, :, None] * live_rows[:, None, None]
    merged_heads = attended.reshape(row_count, model_width).astype(jnp.bfloat16)
    residual = (
        token_rows
        + jnp.dot(merged_heads, attention_output_weight, preferred_element_type=jnp.float32)
        + attention_output_bias.astype(jnp.float32)
    )
    second_normed, second_back = jax.vjp(
        layer_norm, residual, second_gain.astype(jnp.float32), second_shift.astype(jnp.float32)
    )
    second_low = second_normed.astype(jnp.bfloat16)
    hidden_rows = jnp.dot(
        second_low, mlp_input_weight, preferred_element_type=jnp.float32
    ) + mlp_input_bias.astype(jnp.float32)
    gelu_active, gelu_back = jax.vjp(gelu_exact, hidden_rows)
    active_low = gelu_active.astype(jnp.bfloat16)
    layer_rows = (
        residual
        + jnp.dot(active_low, mlp_output_weight, preferred_element_type=jnp.float32)
        + mlp_output_bias.astype(jnp.float32)
    )
    layer_out = layer_rows.astype(jnp.bfloat16).reshape(tokens.shape)
    grad_rows = out_grad.reshape(row_count, model_width)
    down_weight_grad = jnp.einsum(
        "tf,td->fd", active_low, grad_rows, preferred_element_type=jnp.float32
    )
    down_bias_grad = jnp.sum(grad_rows.astype(jnp.float32), axis=0)
    active_grad = jnp.einsum(
        "td,fd->tf", grad_rows, mlp_output_weight, preferred_element_type=jnp.float32
    )
    (hidden_grad,) = gelu_back(active_grad)
    hidden_low = hidden_grad.astype(jnp.bfloat16)
    up_weight_grad = jnp.einsum(
        "td,tf->df", second_low, hidden_low, preferred_element_type=jnp.float32
    )
    up_bias_grad = jnp.sum(hidden_low.astype(jnp.float32), axis=0)
    normed_grad = jnp.einsum(
        "tf,df->td", hidden_low, mlp_input_weight, preferred_element_type=jnp.float32
    )
    resid_part, second_gain_grad, second_shift_grad = second_back(normed_grad)
    residual_grad = grad_rows.astype(jnp.float32) + resid_part
    branch_low = residual_grad.astype(jnp.bfloat16)
    out_weight_grad = jnp.einsum(
        "ti,to->io", merged_heads, branch_low, preferred_element_type=jnp.float32
    )
    out_bias_grad = jnp.sum(branch_low.astype(jnp.float32), axis=0)
    attended_grad = (
        jnp.einsum(
            "to,io->ti", branch_low, attention_output_weight, preferred_element_type=jnp.float32
        ).reshape(head_shape)
        * live_rows[:, None, None]
    )
    query_grads = (attended_grad / totals[:, :, None]).astype(jnp.bfloat16)
    corrections = (jnp.sum(attended_grad * attended, axis=-1) / totals).astype(jnp.bfloat16)

    def query_turn(index, carried):
        begin_row = index * key_span
        key_rows = lax.dynamic_slice_in_dim(all_keys, begin_row, key_span, 0)
        weights_low, score_grads = back_step(
            queries,
            query_grads,
            corrections,
            seg_rows,
            key_rows,
            lax.dynamic_slice_in_dim(all_values, begin_row, key_span, 0),
            lax.dynamic_slice_in_dim(all_segs, begin_row, key_span, 0),
        )
        return carried + jnp.einsum(
            "hqk,khd->qhd", score_grads, key_rows, preferred_element_type=jnp.float32
        )

    query_sum = lax.fori_loop(0, turns, query_turn, jnp.zeros(head_shape, jnp.float32))
    term_span = math.gcd(row_count * lax.axis_size("blk"), 2048)

    def term_block(index):
        begin_row = index * term_span
        key_part, value_part = key_value_grads(
            queries,
            query_grads,
            corrections,
            seg_rows,
            lax.dynamic_slice_in_dim(all_keys, begin_row, term_span, 0),
            lax.dynamic_slice_in_dim(all_values, begin_row, term_span, 0),
            lax.dynamic_slice_in_dim(all_segs, begin_row, term_span, 0),
        )
        return jnp.concatenate(
            [key_part.reshape(term_span, model_width), value_part.reshape(term_span, model_width)],
            axis=1,
        )

    blocks = lax.map(
        term_block, jnp.arange(row_count * lax.axis_size("blk") // term_span, dtype=jnp.int32)
    )
    key_terms = lax.psum_scatter(
        blocks.reshape(row_count * lax.axis_size("blk"), 2 * model_width),
        "blk",
        scatter_dimension=0,
        tiled=True,
    )
    query_low = query_sum.reshape(row_count, model_width).astype(jnp.bfloat16)
    key_low = key_terms[:, :model_width].astype(jnp.bfloat16)
    value_low = key_terms[:, model_width:].astype(jnp.bfloat16)
    qkv_grad = jnp.concatenate([query_low, key_low, value_low], axis=1)
    qkv_weight_grad = jnp.einsum(
        "td,tj->dj", first_low, qkv_grad, preferred_element_type=jnp.float32
    )
    query_bias_grad = jnp.sum(query_low.astype(jnp.float32), axis=0)
    value_bias_grad = jnp.sum(value_low.astype(jnp.float32), axis=0)
    first_grad = jnp.einsum(
        "tj,dj->td", qkv_grad, query_key_value_weight, preferred_element_type=jnp.float32
    )
    token_part, first_gain_grad, first_shift_grad = first_back(first_grad)
    tokens_grad = (residual_grad + token_part).astype(jnp.bfloat16).reshape(tokens.shape)
    local_grads = (
        qkv_weight_grad,
        query_bias_grad,
        value_bias_grad,
        out_weight_grad,
        out_bias_grad,
        first_gain_grad,
        first_shift_grad,
        second_gain_grad,
        second_shift_grad,
        up_weight_grad,
        up_bias_grad,
        down_weight_grad,
        down_bias_grad,
    )
    scattered = (
        lax.psum_scatter(local_grads[0], "blk", scatter_dimension=0, tiled=True),
        lax.psum_scatter(local_grads[1], "blk", scatter_dimension=0, tiled=True),
        lax.psum_scatter(local_grads[2], "blk", scatter_dimension=0, tiled=True),
        lax.psum_scatter(local_grads[3], "blk", scatter_dimension=0, tiled=True),
        lax.psum_scatter(local_grads[4], "blk", scatter_dimension=0, tiled=True),
        lax.psum_scatter(local_grads[5], "blk", scatter_dimension=0, tiled=True),
        lax.psum_scatter(local_grads[6], "blk", scatter_dimension=0, tiled=True),
        lax.psum_scatter(local_grads[7], "blk", scatter_dimension=0, tiled=True),
        lax.psum_scatter(local_grads[8], "blk", scatter_dimension=0, tiled=True),
        lax.psum_scatter(local_grads[9], "blk", scatter_dimension=0, tiled=True),
        lax.psum_scatter(local_grads[10], "blk", scatter_dimension=0, tiled=True),
        lax.psum_scatter(local_grads[11], "blk", scatter_dimension=1, tiled=True),
        lax.psum_scatter(local_grads[12], "blk", scatter_dimension=0, tiled=True),
    )
    summed_grads = lax.psum(
        (
            scattered[0],
            scattered[1],
            scattered[2],
            scattered[3],
            scattered[4],
            scattered[5],
            scattered[6],
            scattered[7],
            scattered[8],
            scattered[9],
            scattered[10],
            scattered[11],
            scattered[12],
        ),
        "seq",
    )
    return (layer_out, tokens_grad) + tuple(summed_grads)


VMEM_LIMIT = 64 * 1024 * 1024
D = 768
FF = 3072
ROWS = 192
CHIPS = 4
GROUP = 192
QKV = 3 * GROUP
HALF = FF // 2
OUT_HALF = D // 2
PIECE = 48
TILE = 256
TILES = HALF // TILE
PACK = ROWS // 2
SLOT = 2 * ROWS
KEYS = 1536
OWN = 768
LOW = jnp.bfloat16
F32 = jnp.float32
MESH = pl.DeviceIdType.MESH


def dot(a, b):
    return jnp.dot(a, b, preferred_element_type=F32)


def dot_nt(a, b):
    return lax.dot_general(a, b, (((1,), (1,)), ((), ())), preferred_element_type=F32)


def dot_tn(a, b):
    return lax.dot_general(a, b, (((0,), (0,)), ((), ())), preferred_element_type=F32)


def scratch_list():
    dma = pltpu.SemaphoreType.DMA
    vmem = pltpu.VMEM
    return dict(
        tok=vmem((ROWS, D), LOW),
        seg=vmem((1, ROWS), jnp.int32),
        vec0=vmem((D,), LOW), vec1=vmem((D,), LOW), vec2=vmem((D,), LOW), vec3=vmem((D,), LOW),
        vec4=vmem((D,), LOW), vec5=vmem((D,), LOW), vec6=vmem((D,), LOW), vec7=vmem((D,), LOW),
        vec8=vmem((FF,), LOW),
        layer=vmem((ROWS, D), LOW),
        tokg=vmem((ROWS, D), LOW),
        vec=vmem((3, 8, D), F32),
        in_sem=dma((12,)), out_sem=dma((5,)), own_sem=dma((TILES + 1,)),
        nrm=vmem((CHIPS, ROWS, D), LOW),
        xhat1=vmem((ROWS, D), F32),
        rstd1=vmem((ROWS, 1), F32),
        par=vmem((8, D), F32),
        qvb=vmem((2, CHIPS, GROUP), F32),
        b1=vmem((1, FF), F32),
        wf=vmem((D, 3 * D), LOW),
        wo=vmem((D, D), LOW),
        w2=vmem((HALF, D), LOW),
        q=vmem((3, OWN, 2 * HEAD), LOW),
        kvo=vmem((CHIPS, ROWS, 2 * GROUP), LOW),
        kvs=vmem((CHIPS, ROWS, 2 * GROUP), LOW),
        kh=vmem((3, KEYS, HEAD), LOW),
        vh=vmem((3, KEYS, 2 * HEAD), LOW),
        kvt=vmem((6, HEAD, KEYS), LOW),
        segs=vmem((2, CHIPS, 8, ROWS), jnp.int32),
        kseg=vmem((1, KEYS), jnp.int32),
        qseg=vmem((OWN, 128), jnp.int32),
        prob=vmem((3, OWN, KEYS), LOW),
        att=vmem((3, OWN, 2 * HEAD), F32),
        mgs=vmem((CHIPS, PACK, 2 * GROUP), LOW),
        mgr=vmem((CHIPS, PACK, 2 * GROUP), LOW),
        mgo=vmem((CHIPS, PACK, 2 * GROUP), LOW),
        mg=vmem((CHIPS, ROWS, GROUP), LOW),
        og=vmem((2, ROWS, D), LOW),
        nt=vmem((2, ROWS, D), LOW),
        bl=vmem((2, ROWS, D), LOW),
        resid=vmem((ROWS, D), F32),
        xhat2=vmem((ROWS, D), F32),
        rstd2=vmem((ROWS, 1), F32),
        act=vmem((2 * ROWS, HALF), LOW),
        hg=vmem((2 * ROWS, HALF), LOW),
        lo=vmem((2, ROWS, D), F32),
        ng=vmem((2, ROWS, D), F32),
        lor=vmem((ROWS, D), F32),
        ngr=vmem((ROWS, D), F32),
        ags=vmem((CHIPS, PACK, 2 * GROUP), LOW),
        ag=vmem((CHIPS, PACK, 2 * GROUP), LOW),
        agh=vmem((3, OWN, HEAD), LOW),
        dqs=vmem((3, CHIPS, PACK, 2 * GROUP), LOW),
        dqr=vmem((3, CHIPS, PACK, 2 * GROUP), LOW),
        rowg=vmem((ROWS, 3 * D), LOW),
        dkr=vmem((3, 2, HEAD, OWN), LOW),
        dks=vmem((3, 2, HEAD, OWN), LOW),
        dqkv=vmem((OWN, QKV), LOW),
        da=vmem((TILES, CHIPS, 2, 2, PIECE, TILE), LOW),
        db=vmem((TILES, CHIPS, 2, 2, PIECE, TILE), LOW),
        ra=vmem((TILES, CHIPS, 2, PIECE, TILE), LOW),
        rb=vmem((TILES, CHIPS, 2, PIECE, TILE), LOW),
        a2s=vmem((TILES, CHIPS, PIECE, TILE), LOW),
        b2s=vmem((TILES, CHIPS, PIECE, TILE), LOW),
        a2r=vmem((TILES, CHIPS, PIECE, TILE), LOW),
        b2r=vmem((TILES, CHIPS, PIECE, TILE), LOW),
        zs=vmem((TILES, CHIPS, 2, PIECE, TILE), LOW),
        rz=vmem((TILES, CHIPS, 2, PIECE, TILE), LOW),
        zm=vmem((TILES, 2, 2, PIECE, TILE), LOW),
        fin=vmem((TILES, 2, PIECE, TILE), LOW),
        oa=vmem((2, 2, 2, PIECE, OUT_HALF), LOW),
        ob=vmem((2, 2, 2, PIECE, OUT_HALF), LOW),
        roa=vmem((2, 2, PIECE, OUT_HALF), LOW),
        rob=vmem((2, 2, PIECE, OUT_HALF), LOW),
        oa2s=vmem((2, PIECE, OUT_HALF), LOW),
        ob2s=vmem((2, PIECE, OUT_HALF), LOW),
        oa2r=vmem((2, PIECE, OUT_HALF), LOW),
        ob2r=vmem((2, PIECE, OUT_HALF), LOW),
        zo=vmem((CHIPS, PIECE, OUT_HALF), LOW),
        rzo=vmem((CHIPS, PIECE, OUT_HALF), LOW),
        zmo=vmem((2, PIECE, OUT_HALF), LOW),
        fo=vmem((PIECE, OUT_HALF), LOW),
        dwq=vmem((CHIPS, 4, PIECE, QKV), LOW),
        dwqr=vmem((2, 4, PIECE, QKV), LOW),
        dwqx=vmem((2, 4, PIECE, QKV), LOW),
        rxq=vmem((3, 2, PIECE, QKV), LOW),
        zq=vmem((2, PIECE, QKV), LOW),
        rzq=vmem((CHIPS, PIECE, QKV), LOW),
        va=vmem((8, D), F32),
        vh1=vmem((1, HALF), F32),
        vap=vmem((8, D), F32),
        vaz=vmem((CHIPS, 8, D), F32),
        vax=vmem((4, 8, D), F32),
        vq=vmem((8, TILE), F32),
        vqp=vmem((8, TILE), F32),
        vqz=vmem((CHIPS, 8, TILE), F32),
        vqx=vmem((4, 8, TILE), F32),
        vb=vmem((8, TILE), F32),
        vbr=vmem((8, 8, TILE), F32),
        vbx=vmem((4, 8, TILE), F32),
        load_sem=dma((3 + TILES,)),
        seg_s=dma((7,)), seg_r=dma((7,)),
        og_s=dma((1,)), og_r=dma((1,)),
        nu_s=dma((CHIPS, 2)), nd_s=dma((CHIPS, 2)), n_r=dma((CHIPS, 2)),
        kv_s=dma((CHIPS,)), kv_r=dma((CHIPS,)),
        mg_s=dma((CHIPS,)), mg_r=dma((CHIPS,)),
        mgo_s=dma((1,)), mgo_r=dma((1,)),
        nt_s=dma((1,)), nt_r=dma((1,)),
        lo_s=dma((1,)), lo_r=dma((1,)),
        ng_s=dma((1,)), ng_r=dma((1,)),
        bl_s=dma((1,)), bl_r=dma((1,)),
        ag_s=dma((CHIPS,)), ag_r=dma((CHIPS,)),
        dk_s=dma((3,)), dk_r=dma((3,)),
        dq_s=dma((3, CHIPS)), dq_r=dma((3, CHIPS)),
        a1_s=dma((TILES + 1,)), a1_r=dma((TILES + 1,)),
        b1_s=dma((TILES + 1,)), b1_r=dma((TILES + 1,)),
        a2_s=dma((TILES + 1,)), a2_r=dma((TILES + 1,)),
        b2_s=dma((TILES + 1,)), b2_r=dma((TILES + 1,)),
        z_s=dma((TILES + 1, CHIPS)), z_r=dma((TILES + 1, CHIPS)),
        f_s=dma((TILES + 1, 4)), f_r=dma((TILES + 1, 4)),
        q0_s=dma((1,)), q0_r=dma((1,)),
        qx_s=dma((3,)), qx_r=dma((3,)),
        qz_s=dma((2,)), qz_r=dma((CHIPS,)),
        qf_s=dma((3,)), qf_r=dma((3,)),
        va_s=dma((7,)), va_r=dma((7,)),
        vq_s=dma((7,)), vq_r=dma((7,)),
        vb_s=dma((7,)), vb_r=dma((7,)),
        vbx_s=dma((3,)), vbx_r=dma((3,)),
    )


EARLY = 4
STARTED = 2
PLAN = dict(
    before_norm=((1, 0), (0, 2)),
    after_norm=(),
    middle=((1, 1), (0, 3)),
    before_loop=((2, 0),),
    loop=(
        (0, ((1, 2), (0, 4), (2, 1))),
        (1, ((3, 0),)),
        (2, ((1, 3), (0, 5))),
        (3, ((2, 2), (3, 1))),
        (5, ((1, 4), (0, 6))),
    ),
    after_loop=((2, 3), (4, 0), (1, 5)),
    after_qkv=((1, 6), (2, 4), (4, 1)),
    after_rows=((3, 2), (2, 5), (3, 3), (2, 6)),
    before_sums=((4, 2), (3, 4)),
    last=((3, 5), (3, 6), (4, 3), (4, 4), (4, 5), (4, 6)),
)


class Box:
    pass


def kernel_body(names, pad_number, *refs):
    (tok_h, seg_h, og_h, wqkv, wo_h, w1_h, w2_h) = refs[:7]
    (out_tok, out_layer, out_fin, out_fo, out_finq, out_vec) = refs[16:22]
    r = Box()
    for name, ref in zip(names, refs[22:]):
        setattr(r, name, ref)
    par, qvb, b1 = r.par, r.qvb, r.b1
    tok = r.tok

    s = lax.axis_index("seq")
    b = lax.axis_index("blk")
    z = b // 2
    c = b % 2
    sib = 2 * z + 1 - c
    flip = {1: s + 1 - 2 * (s % 2), 2: (s + 2) % 4, 3: 3 - s}
    x = s % 2
    y = s // 2
    is_end = jnp.logical_or(z == 0, z == 3)

    pending = []

    def send(src, dst, ssem, rsem, dev_s, dev_b):
        return pltpu.make_async_remote_copy(
            src_ref=src, dst_ref=dst, send_sem=ssem, recv_sem=rsem,
            device_id=(dev_s, dev_b), device_id_type=MESH,
        )

    def local_row(index):
        return par[index : index + 1, :]

    barrier = pltpu.get_barrier_semaphore()
    for step in range(1, 8):
        pl.semaphore_signal(barrier, inc=1, device_id=(s, (b + step) % 8), device_id_type=MESH)
    for step in (1, 2, 3):
        for core in range(2):
            pl.semaphore_signal(
                barrier, inc=1, device_id=(flip[step], 2 * z + core), device_id_type=MESH
            )

    vectors = [getattr(r, "vec%d" % index) for index in range(9)]
    first_loads = [
        pltpu.make_async_copy(source, target, r.in_sem.at[index])
        for index, (source, target) in enumerate(
            [(tok_h, r.tok), (seg_h, r.seg), (og_h, r.og.at[c])]
            + list(zip(refs[7:16], vectors))
        )
    ]
    for item in first_loads:
        item.start()

    loads = []
    loads.append(pltpu.make_async_copy(wqkv, r.wf, r.load_sem.at[0]))
    half = pl.multiple_of(c * HALF, 128)
    loads.append(pltpu.make_async_copy(wo_h, r.wo, r.load_sem.at[1]))
    loads.append(pltpu.make_async_copy(w2_h.at[pl.ds(half, HALF), :], r.w2, r.load_sem.at[2]))
    for tile in range(TILES):
        cols = pl.ds(pl.multiple_of(c * HALF + tile * TILE, TILE), TILE)
        loads.append(
            pltpu.make_async_copy(
                w1_h.at[:, :, :, :, cols], r.da.at[tile], r.load_sem.at[3 + tile]
            )
        )
    for item in loads:
        item.start()

    for item in first_loads:
        item.wait()
    for index, vector in enumerate(vectors[:8]):
        par[index : index + 1, :] = vector[...].astype(F32).reshape(1, D)
    for slot in range(CHIPS):
        part = slice(slot * GROUP, (slot + 1) * GROUP)
        qvb[0, slot : slot + 1, :] = par[0:1, part]
        qvb[1, slot : slot + 1, :] = par[1:2, part]
    b1[...] = vectors[8][...].astype(F32).reshape(1, FF)

    def first_norm(index, carried):
        rows = pl.ds(index * PIECE, PIECE)
        x = tok[rows, :].astype(F32)
        centre = x - jnp.mean(x, axis=-1, keepdims=True)
        spread = lax.rsqrt(jnp.mean(centre * centre, axis=-1, keepdims=True) + EPS)
        xhat = centre * spread
        r.xhat1[rows, :] = xhat
        r.rstd1[rows, :] = spread
        r.nrm[z, rows, :] = (xhat * local_row(3) + local_row(4)).astype(LOW)
        return carried

    lax.fori_loop(0, 4, first_norm, 0)

    pl.semaphore_wait(barrier, 13)

    def norm_copy(slot, side, up):
        part = r.nrm.at[slot, pl.ds(side * PACK, PACK)]
        sems = r.nu_s if up else r.nd_s
        return send(part, part, sems.at[slot, side], r.n_r.at[slot, side], s, b + 2 if up else b - 2)

    def norm_forward(slot, side):
        @pl.when(jnp.logical_and(slot <= z, z < 3))
        def _():
            norm_copy(slot, side, True).start()

        @pl.when(jnp.logical_and(slot >= z, z > 0))
        def _():
            norm_copy(slot, side, False).start()

    norm_forward(z, 0)
    norm_forward(z, 1)

    r.segs[c, z] = jnp.broadcast_to(r.seg[...], (8, ROWS))
    seg_copies = []
    for step in range(1, 8):
        seg_copies.append(
            send(r.segs.at[c, z], r.segs.at[c, z], r.seg_s.at[step - 1], r.seg_r.at[step - 1],
                 s, (b + step) % 8)
        )
    for item in seg_copies:
        item.start()
    pending.extend(seg_copies)


    og_copy = send(r.og.at[c], r.og.at[c], r.og_s.at[0], r.og_r.at[0], s, sib)
    og_copy.start()
    pending.append(og_copy)

    loads[0].wait()
    for part in range(3):
        start = pl.multiple_of(D * part + 384 * (z // 2) + 128 * (z % 2), 128)
        window = r.wf[:, pl.ds(start, 256)]
        r.dqkv[:, part * GROUP : (part + 1) * GROUP] = jnp.where(
            z % 2 == 1, window[:, 64:256], window[:, 0:192]
        )

    upper = z // 2
    qkv_bias = [qvb[0, pl.ds(z, 1), :], None, qvb[1, pl.ds(z, 1), :]]

    def split_keys(pair, row):
        for h in range(3):
            r.kh[h, pl.ds(row, ROWS), :] = pair[:, h * HEAD : (h + 1) * HEAD]
            r.vh[h, pl.ds(row, ROWS), 0:HEAD] = pair[:, GROUP + h * HEAD : GROUP + (h + 1) * HEAD]

    def kv_copy(slot):
        return send(r.kvo.at[slot], r.kvs.at[slot], r.kv_s.at[slot], r.kv_r.at[slot], s, sib)

    def project(slot):
        rows = r.nrm[slot]
        whole = dot(rows, r.dqkv[...])
        qs = (whole[:, :GROUP] + qkv_bias[0]).astype(LOW) * (1.0 / math.sqrt(HEAD))
        ks = whole[:, GROUP : 2 * GROUP].astype(LOW)
        vs = (whole[:, 2 * GROUP :] + qkv_bias[2]).astype(LOW)
        for h in range(3):
            r.q[h, pl.ds(slot * ROWS, ROWS), 0:HEAD] = qs[:, h * HEAD : (h + 1) * HEAD]
        r.kvo[slot, :, 0:GROUP] = ks
        r.kvo[slot, :, GROUP : 2 * GROUP] = vs
        kv_copy(slot).start()
        split_keys(r.kvo[slot], slot * SLOT)

    r.vh[:, :, HEAD : 2 * HEAD] = jnp.ones((3, KEYS, HEAD), LOW)
    project(z)

    def arrivals(distance, carried):
        for side in range(2):
            for slot, there in ((z - distance, z >= distance), (z + distance, z + distance < CHIPS)):
                @pl.when(there)
                def _(slot=slot, side=side):
                    norm_copy(slot, side, True).wait_recv()
                    norm_forward(slot, side)

        for slot, there in ((z - distance, z >= distance), (z + distance, z + distance < CHIPS)):
            @pl.when(there)
            def _(slot=slot):
                project(slot)

        return carried

    arrivals(1, 0)

    for item in seg_copies:
        item.wait_recv()
    for slot in range(CHIPS):
        for side, core in ((0, c), (1, 1 - c)):
            start = slot * SLOT + side * ROWS
            r.kseg[:, start : start + ROWS] = r.segs[core, slot, 0:1, :]
        line = r.segs[c, slot, 0:1, :].astype(F32)
        r.qseg[slot * ROWS : (slot + 1) * ROWS, :] = jnp.transpose(
            jnp.broadcast_to(line, (128, ROWS))
        ).astype(jnp.int32)

    loads[2].wait()
    og_copy.wait_recv()

    def active_grads(index, carried):
        cols = pl.ds(pl.multiple_of(index * 512, 512), 512)
        r.hg[:, cols] = dot_nt(r.og[...].reshape(2 * ROWS, D), r.w2[cols, :]).astype(LOW)
        return carried

    lax.fori_loop(0, HALF // 512, active_grads, 0)

    for slot, there in ((z - 2, z >= 2), (z + 2, z + 2 < CHIPS)):
        for side in range(2):
            @pl.when(there)
            def _(slot=slot, side=side):
                norm_copy(slot, side, True).wait_recv()
                norm_forward(slot, side)

        @pl.when(there)
        def _(slot=slot):
            project(slot)

    def take_sibling(slot, carried):
        kv_copy(slot).wait_recv()
        split_keys(r.kvs[slot], slot * SLOT + ROWS)
        both = jnp.concatenate([r.kvo[slot], r.kvs[slot]], axis=0)
        span = pl.ds(pl.multiple_of(slot * SLOT, 128), SLOT)
        r.kvt[:, :, span] = jnp.transpose(both).reshape(6, HEAD, SLOT)
        return carried

    lax.fori_loop(upper, upper + 3, take_sibling, 0)

    BAND = 2 * ROWS
    last = 3 * (1 - upper)

    def pack(ref, index, lane, value):
        width = value.shape[1]
        ref[index, :, lane : lane + width] = value[0:PACK]
        ref[index, :, GROUP + lane : GROUP + lane + width] = value[PACK:ROWS]

    def mg_copy(block):
        return send(r.mgs.at[block], r.mgr.at[z], r.mg_s.at[block], r.mg_r.at[z], s, 2 * block + c)

    def mg_arrival(slot):
        return send(r.mgs.at[slot], r.mgr.at[slot], r.mg_s.at[slot], r.mg_r.at[slot], s, 2 * slot + c)

    def weigh(h, rows, count, lanes, width):
        own_segs = r.qseg[rows, :]
        wide = jnp.concatenate([own_segs] * (width // 128), axis=1)
        raw = dot(r.q[h, rows, 0:HEAD], r.kvt[h, :, lanes])
        weights = jnp.where(wide == r.kseg[:, lanes], jnp.exp(raw), 0.0).astype(LOW)
        r.prob[h, rows, lanes] = weights
        return dot(weights, r.vh[h, lanes, :])

    def settle(h, rows, total):
        live = jnp.where(r.qseg[rows, :][:, :HEAD] != pad_number, 1.0, 0.0).astype(F32)
        inverse = 1.0 / total[:, HEAD:]
        r.att[h, rows, 0:HEAD] = total[:, :HEAD] * inverse * live
        r.att[h, rows, HEAD : 2 * HEAD] = inverse

    old_rows = pl.ds(pl.multiple_of(upper * ROWS, ROWS), 3 * ROWS)
    old_lanes = pl.ds(pl.multiple_of(upper * SLOT, 128), 3 * SLOT)
    last_rows = pl.ds(pl.multiple_of(last * ROWS, ROWS), ROWS)
    last_lanes = pl.ds(pl.multiple_of(last * SLOT, 128), SLOT)

    def forward_old(h, carried):
        r.att[h, old_rows, :] = weigh(h, old_rows, 3 * ROWS, old_lanes, 3 * SLOT)
        return carried

    lax.fori_loop(0, 3, forward_old, 0)

    @pl.when(is_end)
    def _():
        for side in range(2):
            norm_copy(last, side, True).wait_recv()
        project(last)

    take_sibling(last, 0)

    def give(block):
        block_rows = pl.ds(pl.multiple_of(block * ROWS, ROWS), ROWS)
        for head in range(3):
            pack(r.mgs, block, head * HEAD, r.att[head, block_rows, 0:HEAD].astype(LOW))

        @pl.when(block != z)
        def _():
            mg_copy(block).start()

        @pl.when(block == z)
        def _():
            r.mgr[z] = r.mgs[z]

    def forward_last(h, carried):
        settle(h, last_rows, weigh(h, last_rows, ROWS, slice(0, KEYS), KEYS))
        return carried

    lax.fori_loop(0, 3, forward_last, 0)
    give(last)

    def forward_rest(h, carried):
        settle(
            h, old_rows, r.att[h, old_rows, :] + weigh(h, old_rows, 3 * ROWS, last_lanes, SLOT)
        )
        return carried

    lax.fori_loop(0, 3, forward_rest, 0)

    for index in range(3):
        give(2 - index + upper * (2 * index - 1))

    def others(fn):
        def run(index, carried):
            fn((z + 1 + index) % CHIPS)
            return carried

        lax.fori_loop(0, CHIPS - 1, run, 0)

    others(lambda slot: mg_arrival(slot).wait_recv())
    mgo_copy = send(r.mgr, r.mgo, r.mgo_s.at[0], r.mgo_r.at[0], s, sib)
    mgo_copy.start()
    pending.append(mgo_copy)

    for slot in range(CHIPS):
        r.mg[slot, 0:PACK, :] = r.mgr[slot, :, 0:GROUP]
        r.mg[slot, PACK:ROWS, :] = r.mgr[slot, :, GROUP : 2 * GROUP]

    loads[1].wait()

    def out_projection(index, carried):
        cols = pl.ds(pl.multiple_of(index * 256, 256), 256)
        total = tok[:, cols].astype(F32) + par[2:3, cols]
        for slot in range(CHIPS):
            total = total + dot(r.mg[slot], r.wo[slot * GROUP : (slot + 1) * GROUP, cols])
        r.resid[:, cols] = total
        return carried

    lax.fori_loop(0, 3, out_projection, 0)

    def second_norm(index, carried):
        rows = pl.ds(index * PIECE, PIECE)
        x = r.resid[rows, :]
        centre = x - jnp.mean(x, axis=-1, keepdims=True)
        spread = lax.rsqrt(jnp.mean(centre * centre, axis=-1, keepdims=True) + EPS)
        xhat = centre * spread
        r.xhat2[rows, :] = xhat
        r.rstd2[rows, :] = spread
        r.nt[c, rows, :] = (xhat * local_row(5) + local_row(6)).astype(LOW)
        return carried

    lax.fori_loop(0, 4, second_norm, 0)
    nt_copy = send(r.nt.at[c], r.nt.at[c], r.nt_s.at[0], r.nt_r.at[0], s, sib)
    nt_copy.start()
    pending.append(nt_copy)
    for item in loads[3:]:
        item.wait()
    r.va[...] = jnp.zeros((8, D), F32)
    r.vb[...] = jnp.zeros((8, TILE), F32)
    r.va[3:4, :] = jnp.sum(r.og[c].astype(F32), axis=0, keepdims=True)
    nt_copy.wait_recv()

    def hop_one(unit):
        if isinstance(unit, int) and unit == TILES:
            one, two, to_one, to_two = r.oa, r.ob, r.roa, r.rob
        else:
            one, two, to_one, to_two = r.da.at[unit], r.db.at[unit], r.ra.at[unit], r.rb.at[unit]
        return (
            send(one.at[:, :, 1 - x], to_one, r.a1_s.at[unit], r.a1_r.at[unit], flip[1], b),
            send(two.at[:, 1 - y], to_two, r.b1_s.at[unit], r.b1_r.at[unit], flip[2], b),
        )

    def hop_two(unit):
        if isinstance(unit, int) and unit == TILES:
            one, two, to_one, to_two = r.oa2s, r.ob2s, r.oa2r, r.ob2r
        else:
            one, two, to_one, to_two = (
                r.a2s.at[unit], r.b2s.at[unit], r.a2r.at[unit], r.b2r.at[unit]
            )
        return (
            send(one, to_one, r.a2_s.at[unit], r.a2_r.at[unit], flip[2], b),
            send(two, to_two, r.b2_s.at[unit], r.b2_r.at[unit], flip[1], b),
        )

    partner = z + 1 - 2 * (z % 2)
    inner = 3 - z
    outer = 3 - partner
    low_block = 1 - upper
    inner_of_end = 3 - partner

    def z_refs(unit):
        if isinstance(unit, int) and unit == TILES:
            return r.zo, r.rzo, r.zmo
        return r.zs.at[unit], r.rz.at[unit], r.zm.at[unit]

    def z_bundle(unit):
        here, there, _ = z_refs(unit)
        three = pl.ds(low_block, 3)
        return send(here.at[three], there.at[three], r.z_s.at[unit, 0], r.z_r.at[unit, partner],
                    s, 2 * partner + c)

    def z_near(unit):
        here, there, _ = z_refs(unit)
        return send(here.at[partner], there.at[z], r.z_s.at[unit, 1], r.z_r.at[unit, z],
                    s, 2 * partner + c)

    def z_inner(unit):
        _, there, merged = z_refs(unit)
        return send(merged.at[0], there.at[outer], r.z_s.at[unit, 2], r.z_r.at[unit, outer],
                    s, 2 * inner + c)

    def z_outer(unit):
        _, there, merged = z_refs(unit)
        return send(merged.at[1], there.at[z], r.z_s.at[unit, 3], r.z_r.at[unit, z],
                    s, 2 * outer + c)

    def z_three_arrival(unit):
        here, there, _ = z_refs(unit)
        three = pl.ds(low_block, 3)
        return send(here.at[three], there.at[three], r.z_s.at[unit, 0], r.z_r.at[unit, z],
                    s, 2 * partner + c)

    def z_arrival(unit, slot):
        here, there, _ = z_refs(unit)
        return send(here.at[slot], there.at[slot], r.z_s.at[unit, 0], r.z_r.at[unit, slot],
                    s, 2 * partner + c)

    owner = s // 2
    mine = 2 * z + owner

    def fin_copy(unit, step):
        if isinstance(unit, int) and unit == TILES:
            here, there = r.fo, out_fo.at[s % 2, c]
        else:
            here, there = r.fin.at[unit], out_fin.at[unit, s % 2, c]
        return send(here, there, r.f_s.at[unit, step], r.f_r.at[unit, 2 * (s % 2) + c],
                    s if step == 0 else flip[step], mine)

    def fin_own(unit):
        if isinstance(unit, int) and unit == TILES:
            here, there = r.fo, out_fo.at[s % 2, c]
        else:
            here, there = r.fin.at[unit], out_fin.at[unit, s % 2, c]
        return pltpu.make_async_copy(here, there, r.own_sem.at[unit])

    def fin_arrival(unit, piece, core):
        if isinstance(unit, int) and unit == TILES:
            here, there = r.fo, out_fo.at[piece, core]
        else:
            here, there = r.fin.at[unit], out_fin.at[unit, piece, core]
        return send(here, there, r.f_s.at[unit, 0], r.f_r.at[unit, 2 * piece + core], s, sib)

    def mlp_grads(tile):
        cols = pl.ds(pl.multiple_of(tile * TILE, TILE), TILE)

        r.da[tile] = dot_tn(r.nt[...].reshape(2 * ROWS, D), r.hg[:, cols]).astype(LOW).reshape(
            CHIPS, 2, 2, PIECE, TILE
        )
        r.db[tile] = dot_tn(r.og[...].reshape(2 * ROWS, D), r.act[:, cols]).astype(LOW).reshape(
            CHIPS, 2, 2, PIECE, TILE
        )

    def service_zero(unit):
        for item in hop_one(unit):
            item.start()

    def service_one(unit):
        for item in hop_one(unit):
            item.wait_recv()
        if isinstance(unit, int) and unit == TILES:
            for block in range(2):
                r.oa2s[block] = (
                    r.oa[block, 1 - y, x].astype(F32) + r.roa[block, 1 - y].astype(F32)
                ).astype(LOW)
                r.ob2s[block] = (
                    r.ob[block, y, 1 - x].astype(F32) + r.rob[block, 1 - x].astype(F32)
                ).astype(LOW)
        else:
            def add(block, carried):
                r.a2s[unit, block] = (
                    r.da[unit, block, 1 - y, x].astype(F32) + r.ra[unit, block, 1 - y].astype(F32)
                ).astype(LOW)
                r.b2s[unit, block] = (
                    r.db[unit, block, y, 1 - x].astype(F32) + r.rb[unit, block, 1 - x].astype(F32)
                ).astype(LOW)
                return carried

            lax.fori_loop(0, CHIPS, add, 0)
        for item in hop_two(unit):
            item.start()

    def service_two(unit):
        for item in hop_two(unit):
            item.wait_recv()
        if isinstance(unit, int) and unit == TILES:
            for block in range(2):
                r.zo[block] = (
                    r.oa[block, y, x].astype(F32) + r.roa[block, y].astype(F32)
                    + r.oa2r[block].astype(F32)
                ).astype(LOW)
                r.zo[2 + block] = (
                    r.ob[block, y, x].astype(F32) + r.rob[block, x].astype(F32)
                    + r.ob2r[block].astype(F32)
                ).astype(LOW)
        else:
            def add(block, carried):
                r.zs[unit, block, 0] = (
                    r.da[unit, block, y, x].astype(F32) + r.ra[unit, block, y].astype(F32)
                    + r.a2r[unit, block].astype(F32)
                ).astype(LOW)
                r.zs[unit, block, 1] = (
                    r.db[unit, block, y, x].astype(F32) + r.rb[unit, block, x].astype(F32)
                    + r.b2r[unit, block].astype(F32)
                ).astype(LOW)
                return carried

            lax.fori_loop(0, CHIPS, add, 0)
        @pl.when(is_end)
        def _():
            z_bundle(unit).start()

        @pl.when(jnp.logical_not(is_end))
        def _():
            z_near(unit).start()

    def service_three(unit):
        here, there, merged = z_refs(unit)

        @pl.when(jnp.logical_not(is_end))
        def _():
            z_three_arrival(unit).wait_recv()
            merged[0] = (here[inner].astype(F32) + there[inner].astype(F32)).astype(LOW)
            merged[1] = (here[outer].astype(F32) + there[outer].astype(F32)).astype(LOW)
            z_inner(unit).start()
            z_outer(unit).start()

    def service_four(unit):
        here, there, _ = z_refs(unit)
        z_arrival(unit, partner).wait_recv()

        @pl.when(is_end)
        def _():
            z_arrival(unit, inner_of_end).wait_recv()

        second = jnp.where(is_end, inner_of_end, z)
        total = here[z].astype(F32) + there[partner].astype(F32) + there[second].astype(F32)
        if isinstance(unit, int) and unit == TILES:
            r.fo[...] = total.astype(LOW)
        else:
            r.fin[unit] = total.astype(LOW)
        for step in (1, 2, 3):
            fin_copy(unit, step).start()

        @pl.when(mine != b)
        def _():
            fin_copy(unit, 0).start()

        @pl.when(mine == b)
        def _():
            fin_own(unit).start()

    def run_services(listed):
        for kind, unit in listed:
            (service_zero, service_one, service_two, service_three, service_four)[kind](unit)


    r.lo[...] = jnp.zeros((2, ROWS, D), F32)
    r.ng[...] = jnp.zeros((2, ROWS, D), F32)

    WIDE = 2 * TILE

    def mlp_tile(index, carried):
        cols = pl.ds(pl.multiple_of(index * WIDE, WIDE), WIDE)
        bias = b1[:, pl.ds(pl.multiple_of(c * HALF + index * WIDE, WIDE), WIDE)]
        w1 = jnp.concatenate(
            [r.da[2 * index + part].reshape(D, TILE) for part in range(2)], axis=1
        )
        w2 = r.w2[cols, :]
        hidden = dot(r.nt[...].reshape(2 * ROWS, D), w1) + bias
        gate = 0.5 * (1.0 + lax.erf(hidden * (1.0 / math.sqrt(2.0))))
        slope = gate + hidden * jnp.exp(-0.5 * hidden * hidden) * (1.0 / math.sqrt(2.0 * math.pi))
        active = (hidden * gate).astype(LOW)
        grad = (slope * r.hg[:, cols].astype(F32)).astype(LOW)
        r.act[:, cols] = active
        r.hg[:, cols] = grad
        r.vh1[:, cols] = jnp.sum(grad.astype(F32), axis=0, keepdims=True)
        r.lo[...] += dot(active, w2).reshape(2, ROWS, D)
        r.ng[...] += dot_nt(grad, w1).reshape(2, ROWS, D)
        for part in range(2):
            tile = 2 * index + part

            @pl.when(tile < EARLY)
            def _(tile=tile):
                mlp_grads(tile)

            @pl.when(tile < STARTED)
            def _(tile=tile):
                service_zero(tile)

        return carried

    lax.fori_loop(0, TILES // 2, mlp_tile, 0)
    for part in range(2):
        r.va[pl.ds(4 + 2 * c + part, 1), :] = r.vh1[:, part * D : (part + 1) * D]
    ng_copy = send(r.ng.at[1 - c], r.ngr, r.ng_s.at[0], r.ng_r.at[0], s, sib)
    lo_copy = send(r.lo.at[1 - c], r.lor, r.lo_s.at[0], r.lo_r.at[0], s, sib)
    ng_copy.start()
    lo_copy.start()

    mlp_grads(4)
    run_services(PLAN["before_norm"])

    ng_copy.wait_recv()

    def second_back(index, carried):
        rows = pl.ds(index * PIECE, PIECE)
        grad = r.ng[c, rows, :] + r.ngr[rows, :]
        xhat = r.xhat2[rows, :]
        scaled = grad * local_row(5)
        mean_one = jnp.mean(scaled, axis=-1, keepdims=True)
        mean_two = jnp.mean(scaled * xhat, axis=-1, keepdims=True)
        through = r.rstd2[rows, :] * (scaled - mean_one - xhat * mean_two)
        resid_grad = r.og[c, rows, :].astype(F32) + through
        low = resid_grad.astype(LOW)
        r.xhat2[rows, :] = resid_grad
        r.bl[c, rows, :] = low
        r.va[0:1, :] += jnp.sum(low.astype(F32), axis=0, keepdims=True)
        r.va[1:2, :] += jnp.sum(grad * xhat, axis=0, keepdims=True)
        r.va[2:3, :] += jnp.sum(grad, axis=0, keepdims=True)
        return carried

    lax.fori_loop(0, 4, second_back, 0)
    bl_copy = send(r.bl.at[c], r.bl.at[c], r.bl_s.at[0], r.bl_r.at[0], s, sib)
    bl_copy.start()
    pending.append(bl_copy)

    def ag_copy(block):
        return send(r.ags.at[block], r.ag.at[z], r.ag_s.at[block], r.ag_r.at[z], s, 2 * block + c)

    def ag_arrival(slot):
        return send(r.ags.at[slot], r.ag.at[slot], r.ag_s.at[slot], r.ag_r.at[slot], s, 2 * slot + c)

    def attended_block(index, carried):
        block = (z + 1 + index) % CHIPS
        wide = pl.ds(pl.multiple_of(block * GROUP, GROUP), GROUP)
        pack(r.ags, block, 0, dot_nt(r.bl[c], r.wo[wide, :]).astype(LOW))

        @pl.when(block != z)
        def _():
            ag_copy(block).start()

        @pl.when(block == z)
        def _():
            r.ag[z] = r.ags[z]

        return carried

    lax.fori_loop(0, CHIPS, attended_block, 0)

    def vector_sums(mine_ref, pair_ref, z_ref, x_ref, send_sems, recv_sems):
        def pair():
            return send(mine_ref, pair_ref, send_sems.at[0], recv_sems.at[0], s, sib)

        def along(step):
            return send(z_ref.at[z], z_ref.at[z], send_sems.at[step], recv_sems.at[step],
                        s, (b + 2 * step) % 8)

        def over(step):
            return send(x_ref.at[s], x_ref.at[s], send_sems.at[3 + step], recv_sems.at[3 + step],
                        flip[step], b)

        def stage_one():
            pair().start()
            pending.append(pair())

        def stage_two():
            pair().wait_recv()
            r_first = jnp.where(c == 0, mine_ref[...], pair_ref[...])
            r_second = jnp.where(c == 0, pair_ref[...], mine_ref[...])
            z_ref[z] = r_first + r_second
            for step in (1, 2, 3):
                along(step).start()
                pending.append(along(step))

        def stage_three():
            for step in (1, 2, 3):
                along(step).wait_recv()
            x_ref[s] = z_ref[0] + z_ref[1] + z_ref[2] + z_ref[3]
            for step in (1, 2, 3):
                over(step).start()
                pending.append(over(step))

        def stage_four():
            for step in (1, 2, 3):
                over(step).wait_recv()
            return x_ref[0] + x_ref[1] + x_ref[2] + x_ref[3]

        return stage_one, stage_two, stage_three, stage_four

    va_stages = vector_sums(r.va, r.vap, r.vaz, r.vax, r.va_s, r.va_r)
    vq_stages = vector_sums(r.vq, r.vqp, r.vqz, r.vqx, r.vq_s, r.vq_r)
    va_stages[0]()

    run_services(PLAN["after_norm"])
    mlp_grads(5)
    run_services(PLAN["middle"])
    mgo_copy.wait_recv()
    bl_copy.wait_recv()
    side = pl.ds(pl.multiple_of(c * OUT_HALF, OUT_HALF), OUT_HALF)
    for block in range(CHIPS):
        theirs = jnp.concatenate(
            [r.mgo[block, :, 0:GROUP], r.mgo[block, :, GROUP : 2 * GROUP]], axis=0
        )
        grad = dot_tn(r.mg[block], r.bl[c, :, side]) + dot_tn(theirs, r.bl[1 - c, :, side])
        low = grad.astype(LOW)
        home = r.oa if block < 2 else r.ob
        for piece in range(4):
            home[block % 2, piece // 2, piece % 2] = low[piece * PIECE : (piece + 1) * PIECE]
    va_stages[1]()

    lo_copy.wait_recv()

    def layer_rows(index, carried):
        rows = pl.ds(index * PIECE, PIECE)
        r.layer[rows, :] = (
            r.resid[rows, :] + r.lo[c, rows, :] + r.lor[rows, :] + local_row(7)
        ).astype(LOW)
        return carried

    lax.fori_loop(0, 4, layer_rows, 0)
    results = [pltpu.make_async_copy(r.layer, out_layer, r.out_sem.at[0])]
    results[0].start()

    run_services(PLAN["before_loop"])
    others(lambda slot: ag_arrival(slot).wait_recv())
    for h in range(3):
        for slot in range(CHIPS):
            for part in range(2):
                start = slot * ROWS + part * PACK
                r.agh[h, start : start + PACK, :] = r.ag[
                    slot, :, part * GROUP + h * HEAD : part * GROUP + (h + 1) * HEAD
                ]
    ng_copy.wait_send()
    lo_copy.wait_send()
    key_sums, value_sums = r.ng, r.lo


    def pair_copies(h):
        return (send(r.dks.at[h], r.dkr.at[h], r.dk_s.at[h], r.dk_r.at[h], s, sib),)

    def dq_copy(h, block):
        return send(r.dqs.at[h, block], r.dqr.at[h, z], r.dq_s.at[h, block], r.dq_r.at[h, z],
                    s, 2 * block + c)

    def dq_arrival(h, slot):
        return send(r.dqs.at[h, slot], r.dqr.at[h, slot], r.dq_s.at[h, slot], r.dq_r.at[h, slot],
                    s, 2 * slot + c)

    def finish_head(h):
        for item in pair_copies(h):
            item.wait_recv()
        lines = slice(h * HEAD, (h + 1) * HEAD)
        key_grad = jnp.transpose((key_sums[0, lines, :] + r.dkr[h, 0].astype(F32)).astype(LOW))
        value_grad = jnp.transpose((value_sums[0, lines, :] + r.dkr[h, 1].astype(F32)).astype(LOW))
        for part, whole in enumerate((r.q[h, :, HEAD : 2 * HEAD], key_grad, value_grad)):
            lane = h * GROUP + part * HEAD
            r.dqkv[:, lane : lane + HEAD] = whole
            for block in range(CHIPS):
                pack(r.dqs.at[h], block, part * HEAD, whole[block * ROWS : (block + 1) * ROWS])
        others(lambda block: dq_copy(h, block).start())
        r.dqr[h, z] = r.dqs[h, z]

    def backward_band(index, carried):
        h = index // 2
        part = index % 2
        rows = pl.ds(pl.multiple_of(part * BAND, BAND), BAND)
        live = jnp.where(r.qseg[rows, :][:, :HEAD] != pad_number, 1.0, 0.0).astype(F32)
        grad = r.agh[h, rows, :].astype(F32) * live
        inverse = r.att[h, rows, HEAD : 2 * HEAD]
        correct = jnp.sum(grad * r.att[h, rows, 0:HEAD], axis=-1, keepdims=True) * inverse[:, 0:1]
        correct = correct.astype(LOW).astype(F32)
        scaled = (grad * inverse).astype(LOW)
        product = dot(scaled, r.kvt[3 + h])
        weights = r.prob[h, rows, :]
        slopes = (weights.astype(F32) * (product - correct)).astype(LOW)
        r.q[h, rows, HEAD : 2 * HEAD] = (
            dot(slopes, r.kh[h]) * (1.0 / math.sqrt(HEAD))
        ).astype(LOW)
        keys = dot(jnp.transpose(r.q[h, rows, 0:HEAD]), slopes)
        values = dot(jnp.transpose(scaled), weights)

        lines = pl.ds(pl.multiple_of(h * HEAD, HEAD), HEAD)

        halves = (slice(0, OWN), slice(OWN, KEYS))

        @pl.when(part == 0)
        def _():
            for side in range(2):
                key_sums[side, lines, :] = keys[:, halves[side]]
                value_sums[side, lines, :] = values[:, halves[side]]

        @pl.when(part == 1)
        def _():
            for place, (sums, value) in enumerate(((key_sums, keys), (value_sums, values))):
                whole = jnp.concatenate([sums[0, lines, :], sums[1, lines, :]], axis=1) + value
                own, theirs = (
                    jnp.concatenate(
                        [
                            whole[:, slot * SLOT + side * ROWS : slot * SLOT + (side + 1) * ROWS]
                            for slot in range(CHIPS)
                        ],
                        axis=1,
                    )
                    for side in range(2)
                )
                sums[0, lines, :] = own
                r.dks[h, place] = theirs.astype(LOW)
            for item in pair_copies(h):
                item.start()

        for turn, listed in PLAN["loop"]:
            @pl.when(index == turn)
            def _(listed=listed):
                run_services(listed)

        for turn, head in ((2, 0), (4, 1)):
            @pl.when(index == turn)
            def _(head=head):
                finish_head(head)

        return carried

    lax.fori_loop(0, 6, backward_band, 0)

    finish_head(2)
    run_services(PLAN["after_loop"])

    grad = dot_tn(r.nrm[...].reshape(OWN, D), r.dqkv[...])
    r.dwq[...] = grad.astype(LOW).reshape(CHIPS, 4, PIECE, QKV)
    q0_copy = send(
        r.dwq.at[pl.ds(2 * (1 - c), 2)], r.dwqr, r.q0_s.at[0], r.q0_r.at[0], s, sib
    )
    q0_copy.start()
    pending.append(q0_copy)
    column_sums = jnp.sum(r.dqkv[...].astype(F32), axis=0, keepdims=True)
    r.vq[...] = jnp.zeros((8, TILE), F32)
    for lane, row in ((0, 0), (2 * HEAD, CHIPS)):
        r.vq[pl.ds(row + z, 1), 0:GROUP] = jnp.concatenate(
            [
                column_sums[:, h * GROUP + lane : h * GROUP + lane + HEAD]
                for h in range(3)
            ],
            axis=1,
        )
    vq_stages[0]()
    va_stages[2]()
    q0_copy.wait_recv()
    for part in range(2):
        for piece in range(4):
            r.dwqx[part, piece] = (
                r.dwq[2 * c + part, piece].astype(F32) + r.dwqr[part, piece].astype(F32)
            ).astype(LOW)
    qx_copies = [
        send(r.dwqx.at[:, flip[step]], r.rxq.at[step - 1], r.qx_s.at[step - 1],
             r.qx_r.at[step - 1], flip[step], b)
        for step in (1, 2, 3)
    ]
    for item in qx_copies:
        item.start()
    pending.extend(qx_copies)

    run_services(PLAN["after_qkv"])
    vq_stages[1]()

    for h in range(3):
        others(lambda slot, h=h: dq_arrival(h, slot).wait_recv())
        for slot in range(CHIPS):
            for part in range(3):
                lane = part * D + slot * GROUP + h * HEAD
                for side in range(2):
                    start = side * GROUP + part * HEAD
                    r.rowg[side * PACK : (side + 1) * PACK, lane : lane + HEAD] = r.dqr[
                        h, slot, :, start : start + HEAD
                    ]

    def first_grads(index, carried):
        rows = pl.ds(pl.multiple_of(index * 256, 256), 256)
        r.ngr[:, rows] = dot_nt(r.rowg[...], r.wf[rows, :])
        return carried

    lax.fori_loop(0, 3, first_grads, 0)

    def first_back(index, carried):
        rows = pl.ds(index * PIECE, PIECE)
        grad = r.ngr[rows, :]
        xhat = r.xhat1[rows, :]
        scaled = grad * local_row(3)
        mean_one = jnp.mean(scaled, axis=-1, keepdims=True)
        mean_two = jnp.mean(scaled * xhat, axis=-1, keepdims=True)
        through = r.rstd1[rows, :] * (scaled - mean_one - xhat * mean_two)
        r.tokg[rows, :] = (r.xhat2[rows, :] + through).astype(LOW)
        gains = jnp.sum(grad * xhat, axis=0, keepdims=True)
        shifts = jnp.sum(grad, axis=0, keepdims=True)
        for part in range(3):
            lanes = slice(part * TILE, (part + 1) * TILE)
            r.vb[part : part + 1, :] += gains[:, lanes]
            r.vb[4 + part : 5 + part, :] += shifts[:, lanes]
        return carried

    lax.fori_loop(0, 4, first_back, 0)
    results.append(pltpu.make_async_copy(r.tokg, out_tok, r.out_sem.at[1]))
    results[1].start()

    vb_copies = [
        send(r.vb, r.vbr.at[b], r.vb_s.at[step - 1], r.vb_r.at[step - 1], s, (b + step) % 8)
        for step in range(1, 8)
    ]
    r.vbr[b] = r.vb[...]
    for item in vb_copies:
        item.start()
    pending.extend(vb_copies)

    run_services(PLAN["after_rows"])

    for item in qx_copies:
        item.wait_recv()
    def qz_copy(part):
        return send(r.zq.at[part], r.rzq.at[z], r.qz_s.at[part], r.qz_r.at[z],
                    s, 2 * (2 * c + part) + owner)

    for part in range(2):
        total = r.dwqx[part, s].astype(F32)
        for step in range(3):
            total = total + r.rxq[step, part].astype(F32)
        r.zq[part] = total.astype(LOW)
        there = 2 * (2 * c + part) + owner

        @pl.when(there != b)
        def _(part=part):
            qz_copy(part).start()

        @pl.when(there == b)
        def _(part=part):
            r.rzq[z] = r.zq[part]

    vq_stages[2]()
    run_services(PLAN["before_sums"])

    for item in vb_copies:
        item.wait_recv()
    total = r.vbr[0]
    for slot in range(1, 8):
        total = total + r.vbr[slot]
    r.vbx[s] = total
    vbx_copies = [
        send(r.vbx.at[s], r.vbx.at[s], r.vbx_s.at[step - 1], r.vbx_r.at[step - 1], flip[step], b)
        for step in (1, 2, 3)
    ]
    for item in vbx_copies:
        item.start()
    pending.extend(vbx_copies)

    run_services(PLAN["last"])

    finq_own = pltpu.make_async_copy(r.rzq, out_finq.at[s % 2], r.out_sem.at[2])

    def qf_copy(step):
        return send(r.rzq, out_finq.at[s % 2], r.qf_s.at[step - 1], r.qf_r.at[step - 1],
                    flip[step], b)

    def qz_arrival(slot):
        return send(r.zq.at[0], r.rzq.at[slot], r.qz_s.at[0], r.qz_r.at[slot], s, sib)

    @pl.when(owner == c)
    def _():
        for slot in range(CHIPS):
            @pl.when(jnp.logical_or(slot != z, z // 2 != c))
            def _(slot=slot):
                qz_arrival(slot).wait_recv()

        for step in (1, 2, 3):
            qf_copy(step).start()
        finq_own.start()

    for piece in range(2):
        for core in range(2):
            @pl.when(jnp.logical_or(2 * c + piece != s, core != c))
            def _(piece=piece, core=core):
                for unit in range(TILES + 1):
                    fin_arrival(unit, piece, core).wait_recv()

    for step in (1, 2, 3):
        @pl.when(flip[step] // 2 == c)
        def _(step=step):
            qf_copy(step).wait_recv()

    for item in vbx_copies:
        item.wait_recv()
    r.vec[0] = va_stages[3]()
    r.vec[1, :, 0:TILE] = vq_stages[3]()
    r.vec[2, :, 0:TILE] = r.vbx[0] + r.vbx[1] + r.vbx[2] + r.vbx[3]
    results.append(pltpu.make_async_copy(r.vec, out_vec, r.out_sem.at[3]))
    results[2].start()

    for slot in range(CHIPS):
        for side in range(2):
            @pl.when(jnp.logical_and(slot <= z, z < 3))
            def _(slot=slot, side=side):
                norm_copy(slot, side, True).wait_send()

            @pl.when(jnp.logical_and(slot >= z, z > 0))
            def _(slot=slot, side=side):
                norm_copy(slot, side, False).wait_send()

        kv_copy(slot).wait_send()
    for make in (mg_copy, ag_copy):
        others(lambda slot, make=make: make(slot).wait_send())
    for h in range(3):
        others(lambda slot, h=h: dq_copy(h, slot).wait_send())
        for item in pair_copies(h):
            item.wait_send()
    for item in pending:
        item.wait_send()
    for item in results:
        item.wait()
    for unit in range(TILES + 1):
        for item in hop_one(unit) + hop_two(unit):
            item.wait_send()

        @pl.when(is_end)
        def _(unit=unit):
            z_bundle(unit).wait_send()

        @pl.when(jnp.logical_not(is_end))
        def _(unit=unit):
            z_near(unit).wait_send()
            z_inner(unit).wait_send()
            z_outer(unit).wait_send()

        for step in (1, 2, 3):
            fin_copy(unit, step).wait_send()

        @pl.when(mine != b)
        def _(unit=unit):
            fin_copy(unit, 0).wait_send()

        @pl.when(mine == b)
        def _(unit=unit):
            fin_own(unit).wait()

    for part in range(2):
        @pl.when(2 * (2 * c + part) + owner != b)
        def _(part=part):
            qz_copy(part).wait_send()

    @pl.when(owner == c)
    def _():
        for step in (1, 2, 3):
            qf_copy(step).wait_send()
        finq_own.wait()


def finish_scratch():
    vmem = pltpu.VMEM
    return dict(
        fin=vmem((TILES, 2, 2, 2, PIECE, TILE), LOW),
        fo=vmem((2, 2, PIECE, OUT_HALF), LOW),
        finq=vmem((2, CHIPS, PIECE, QKV), LOW),
        vec=vmem((3, 8, D), F32),
        qkv=vmem((96, 3 * D), F32),
        out=vmem((96, D), F32),
        up=vmem((96, FF), F32),
        down=vmem((96, FF), F32),
        small0=vmem((96,), F32), small1=vmem((96,), F32), small2=vmem((96,), F32),
        small3=vmem((96,), F32), small4=vmem((96,), F32), small5=vmem((96,), F32),
        small6=vmem((96,), F32), small7=vmem((96,), F32), small8=vmem((384,), F32),
        layer=vmem((ROWS, D), LOW),
        tok=vmem((ROWS, D), LOW),
        in_sem=pltpu.SemaphoreType.DMA((5 + TILES,)),
        out_sem=pltpu.SemaphoreType.DMA((13 + 4 * TILES,)),
    )


def finish_body(names, tok, layer, fin, fo, finq, vec, *refs):
    outs = refs[:15]
    layer_out, tok_out, qkv_w, out_w, up_w, down_w = outs[:6]
    r = Box()
    for name, ref in zip(names, refs[15:]):
        setattr(r, name, ref)
    loads = [
        pltpu.make_async_copy(vec, r.vec, r.in_sem.at[0]),
        pltpu.make_async_copy(finq, r.finq, r.in_sem.at[1]),
        pltpu.make_async_copy(fo, r.fo, r.in_sem.at[2]),
        pltpu.make_async_copy(layer, r.layer, r.in_sem.at[3 + TILES]),
        pltpu.make_async_copy(tok, r.tok, r.in_sem.at[4 + TILES]),
    ] + [
        pltpu.make_async_copy(fin.at[tile], r.fin.at[tile], r.in_sem.at[3 + tile])
        for tile in range(TILES)
    ]
    for item in loads:
        item.start()
    stores = []

    def store(source, target):
        stores.append(pltpu.make_async_copy(source, target, r.out_sem.at[len(stores)]))
        stores[-1].start()

    loads[0].wait()
    small = [getattr(r, "small%d" % index) for index in range(9)]
    qb, v_b, ob, g1, s1, g2, s2, down_b, up_b = small
    b = lax.axis_index("blk")
    for index in range(8):
        @pl.when(b == index)
        def _(index=index):
            cols = slice(index * 96, (index + 1) * 96)
            for ref, row in ((ob, 0), (g2, 1), (s2, 2), (down_b, 3)):
                ref[...] = r.vec[0, row, cols]
            for ref, row in ((g1, 0), (s1, 4)):
                whole = jnp.concatenate(
                    [r.vec[2, row + part : row + part + 1, 0:TILE] for part in range(3)], axis=1
                )
                ref[...] = whole[0, cols]
            slot = index // 2
            half = slice((index % 2) * 96, (index % 2 + 1) * 96)
            qb[...] = r.vec[1, slot, half]
            v_b[...] = r.vec[1, CHIPS + slot, half]
            start = (index * 384) % D
            up_b[...] = r.vec[0, 4 + index * 384 // D, start : start + 384]

    for source, target in zip(small, outs[6:]):
        store(source, target)
    loads[3].wait()
    store(r.layer, layer_out)
    loads[4].wait()
    store(r.tok, tok_out)
    loads[1].wait()
    for piece in range(2):
        rows = slice(piece * PIECE, (piece + 1) * PIECE)
        for slot in range(CHIPS):
            for h in range(3):
                for part in range(3):
                    lane = part * D + slot * GROUP + h * HEAD
                    source = h * GROUP + part * HEAD
                    r.qkv[rows, lane : lane + HEAD] = r.finq[
                        piece, slot, :, source : source + HEAD
                    ].astype(F32)
    store(r.qkv, qkv_w)
    loads[2].wait()
    for piece in range(2):
        rows = slice(piece * PIECE, (piece + 1) * PIECE)
        for core in range(2):
            r.out[rows, core * OUT_HALF : (core + 1) * OUT_HALF] = r.fo[piece, core].astype(F32)
    store(r.out, out_w)
    for tile in range(TILES):
        loads[5 + tile].wait()
        for core in range(2):
            start = core * HALF + tile * TILE
            lanes = slice(start, start + TILE)
            for piece in range(2):
                rows = slice(piece * PIECE, (piece + 1) * PIECE)
                r.up[rows, lanes] = r.fin[tile, piece, core, 0].astype(F32)
                r.down[rows, lanes] = r.fin[tile, piece, core, 1].astype(F32)
            store(r.up.at[:, pl.ds(start, TILE)], up_w.at[:, pl.ds(start, TILE)])
            store(r.down.at[:, pl.ds(start, TILE)], down_w.at[:, pl.ds(start, TILE)])
    for item in stores:
        item.wait()


def chip_body(
    tokens, segment_ids, out_grad, query_key_value_weight, query_bias, value_bias,
    attention_output_weight, attention_output_bias, first_gain, first_shift,
    second_gain, second_shift, mlp_input_weight, mlp_input_bias, mlp_output_weight,
    mlp_output_bias,
):
    pad_number = tokens.shape[1] * lax.axis_size("blk") // SHORT_LO + 2
    names = scratch_list()
    any_space = pl.BlockSpec(memory_space=pl.ANY)
    finish_names = finish_scratch()
    results = pl.pallas_call(
        functools.partial(kernel_body, tuple(names), pad_number),
        out_shape=(
            jax.ShapeDtypeStruct((ROWS, D), LOW),
            jax.ShapeDtypeStruct((ROWS, D), LOW),
            jax.ShapeDtypeStruct((TILES, 2, 2, 2, PIECE, TILE), LOW),
            jax.ShapeDtypeStruct((2, 2, PIECE, OUT_HALF), LOW),
            jax.ShapeDtypeStruct((2, CHIPS, PIECE, QKV), LOW),
            jax.ShapeDtypeStruct((3, 8, D), F32),
        ),
        in_specs=[any_space] * 16,
        out_specs=(any_space,) * 6,
        scratch_shapes=list(names.values()),
        compiler_params=pltpu.CompilerParams(
            collective_id=0, has_side_effects=True, vmem_limit_bytes=VMEM_LIMIT
        ),
        name="encoder_block",
    )(
        tokens.reshape(ROWS, D), segment_ids, out_grad.reshape(ROWS, D),
        query_key_value_weight, attention_output_weight,
        mlp_input_weight.reshape(CHIPS, 2, 2, PIECE, FF), mlp_output_weight,
        query_bias, value_bias, attention_output_bias, first_gain, first_shift,
        second_gain, second_shift, mlp_output_bias, mlp_input_bias,
    )
    wide = [(96, 3 * D), (96, D), (96, FF), (96, FF)]
    shapes = (
        [jax.ShapeDtypeStruct((ROWS, D), LOW)] * 2
        + [jax.ShapeDtypeStruct(shape, F32) for shape in wide]
        + [jax.ShapeDtypeStruct((96,), F32)] * 8
        + [jax.ShapeDtypeStruct((384,), F32)]
    )
    (layer_out, tok_out, qkv_w, out_w, up_w, down_w, qb, vb, ob, g1, s1, g2, s2, down_b, up_b) = (
        pl.pallas_call(
            functools.partial(finish_body, tuple(finish_names)),
            out_shape=tuple(shapes),
            in_specs=[any_space] * 6,
            out_specs=(any_space,) * len(shapes),
            scratch_shapes=list(finish_names.values()),
            compiler_params=pltpu.CompilerParams(vmem_limit_bytes=VMEM_LIMIT),
            name="place_results",
        )(*results)
    )
    return (
        layer_out.reshape(tokens.shape), tok_out.reshape(tokens.shape), qkv_w, qb, vb, out_w, ob,
        g1, s1, g2, s2, up_w, up_b, jnp.transpose(down_w), down_b,
    )


def solution(mesh):
    placed = (
        P("seq", "blk", None),
        P("seq", "blk"),
        P("seq", "blk", None),
        P(),
        P(),
        P(),
        P(),
        P(),
        P(),
        P(),
        P(),
        P(),
        P(),
        P(),
        P(),
        P(),
    )
    chosen = chip_body if mesh.shape["seq"] == 4 and mesh.shape["blk"] == 8 else body
    return jax.shard_map(
        chosen,
        mesh=mesh,
        in_specs=placed,
        out_specs=(
            P("seq", "blk", None),
            P("seq", "blk", None),
            P("blk", None),
            P("blk"),
            P("blk"),
            P("blk", None),
            P("blk"),
            P("blk"),
            P("blk"),
            P("blk"),
            P("blk"),
            P("blk", None),
            P("blk"),
            P(None, "blk"),
            P("blk"),
        ),
        check_vma=False,
    )
```

```python
import functools
import math

import jax
import jax.numpy as jnp
from jax import lax
from jax.experimental import pallas as pl
from jax.experimental.pallas import tpu as pltpu
from jax.sharding import PartitionSpec as P

HEADS = 12
HEAD = 64
SHORT_LO = 25


EPS = 1e-06


def layer_norm(inputs, norm_gain, norm_shift):
    centre = inputs - jnp.mean(inputs, axis=-1, keepdims=True)
    spread = jnp.mean(centre * centre, axis=-1, keepdims=True)
    return centre * lax.rsqrt(spread + EPS) * norm_gain + norm_shift


def gelu_exact(inputs):
    return jax.nn.gelu(inputs, approximate=False)


def score_block(queries, query_segs, key_rows, key_segs):
    raw_scores = jnp.einsum("qhd,khd->hqk", queries, key_rows, preferred_element_type=jnp.float32)
    same_image = (query_segs[:, None] == key_segs[None, :])[None]
    return jnp.where(same_image, jnp.exp(raw_scores * (1.0 / math.sqrt(HEAD))), 0.0)


def forward_step(carried, queries, query_segs, key_rows, value_rows, key_segs):
    totals, summed = carried
    weights = score_block(queries, query_segs, key_rows, key_segs)
    totals = totals + jnp.transpose(jnp.sum(weights, axis=-1))
    summed = summed + jnp.einsum(
        "hqk,khd->qhd", weights.astype(jnp.bfloat16), value_rows, preferred_element_type=jnp.float32
    )
    return (totals, summed)


def back_step(queries, query_grads, query_corr, query_segs, key_rows, value_rows, key_segs):
    weights = score_block(queries, query_segs, key_rows, key_segs)
    product = jnp.einsum(
        "qhd,khd->hqk", query_grads, value_rows, preferred_element_type=jnp.float32
    )
    shifted = jnp.transpose(query_corr.astype(jnp.float32))[:, :, None]
    score_grads = (weights * (product - shifted) * (1.0 / math.sqrt(HEAD))).astype(jnp.bfloat16)
    return (weights.astype(jnp.bfloat16), score_grads)


def key_value_grads(queries, query_grads, query_corr, query_segs, key_rows, value_rows, key_segs):
    weights_low, score_grads = back_step(
        queries, query_grads, query_corr, query_segs, key_rows, value_rows, key_segs
    )
    key_part = jnp.einsum("hqk,qhd->khd", score_grads, queries, preferred_element_type=jnp.float32)
    value_part = jnp.einsum(
        "hqk,qhd->khd", weights_low, query_grads, preferred_element_type=jnp.float32
    )
    return (key_part, value_part)


def body(
    tokens,
    segment_ids,
    out_grad,
    query_key_value_weight,
    query_bias,
    value_bias,
    attention_output_weight,
    attention_output_bias,
    first_gain,
    first_shift,
    second_gain,
    second_shift,
    mlp_input_weight,
    mlp_input_bias,
    mlp_output_weight,
    mlp_output_bias,
):
    model_width = tokens.shape[-1]
    row_count = tokens.shape[0] * tokens.shape[1]
    head_shape = (row_count, HEADS, HEAD)
    pad_number = tokens.shape[1] * lax.axis_size("blk") // SHORT_LO + 2
    token_rows = tokens.reshape(row_count, model_width).astype(jnp.float32)
    seg_rows = segment_ids.reshape(row_count)
    live_rows = (seg_rows != pad_number).astype(jnp.float32)
    first_normed, first_back = jax.vjp(
        layer_norm, token_rows, first_gain.astype(jnp.float32), first_shift.astype(jnp.float32)
    )
    first_low = first_normed.astype(jnp.bfloat16)
    query_key_value_bias = jnp.concatenate(
        [
            query_bias.astype(jnp.float32),
            jnp.zeros((model_width,), jnp.float32),
            value_bias.astype(jnp.float32),
        ]
    )
    projected_rows = (
        jnp.dot(first_low, query_key_value_weight, preferred_element_type=jnp.float32)
        + query_key_value_bias
    )
    query_flat = projected_rows[:, :model_width].astype(jnp.bfloat16)
    key_flat = projected_rows[:, model_width : 2 * model_width].astype(jnp.bfloat16)
    value_flat = projected_rows[:, 2 * model_width :].astype(jnp.bfloat16)
    queries = query_flat.reshape(head_shape)
    gathered = (
        lax.all_gather(key_flat, "blk", axis=0, tiled=True),
        lax.all_gather(value_flat, "blk", axis=0, tiled=True),
        lax.all_gather(seg_rows, "blk", axis=0, tiled=True),
    )
    all_keys = gathered[0].reshape(-1, HEADS, HEAD)
    all_values = gathered[1].reshape(-1, HEADS, HEAD)
    all_segs = gathered[2]
    seq_rows = all_keys.shape[0]
    key_span = math.gcd(seq_rows, 2048)
    turns = seq_rows // key_span

    def forward_turn(index, carried):
        begin_row = index * key_span
        return forward_step(
            carried,
            queries,
            seg_rows,
            lax.dynamic_slice_in_dim(all_keys, begin_row, key_span, 0),
            lax.dynamic_slice_in_dim(all_values, begin_row, key_span, 0),
            lax.dynamic_slice_in_dim(all_segs, begin_row, key_span, 0),
        )

    totals, summed = lax.fori_loop(
        0,
        turns,
        forward_turn,
        (jnp.zeros((row_count, HEADS), jnp.float32), jnp.zeros(head_shape, jnp.float32)),
    )
    attended = summed / totals[:, :, None] * live_rows[:, None, None]
    merged_heads = attended.reshape(row_count, model_width).astype(jnp.bfloat16)
    residual = (
        token_rows
        + jnp.dot(merged_heads, attention_output_weight, preferred_element_type=jnp.float32)
        + attention_output_bias.astype(jnp.float32)
    )
    second_normed, second_back = jax.vjp(
        layer_norm, residual, second_gain.astype(jnp.float32), second_shift.astype(jnp.float32)
    )
    second_low = second_normed.astype(jnp.bfloat16)
    hidden_rows = jnp.dot(
        second_low, mlp_input_weight, preferred_element_type=jnp.float32
    ) + mlp_input_bias.astype(jnp.float32)
    gelu_active, gelu_back = jax.vjp(gelu_exact, hidden_rows)
    active_low = gelu_active.astype(jnp.bfloat16)
    layer_rows = (
        residual
        + jnp.dot(active_low, mlp_output_weight, preferred_element_type=jnp.float32)
        + mlp_output_bias.astype(jnp.float32)
    )
    layer_out = layer_rows.astype(jnp.bfloat16).reshape(tokens.shape)
    grad_rows = out_grad.reshape(row_count, model_width)
    down_weight_grad = jnp.einsum(
        "tf,td->fd", active_low, grad_rows, preferred_element_type=jnp.float32
    )
    down_bias_grad = jnp.sum(grad_rows.astype(jnp.float32), axis=0)
    active_grad = jnp.einsum(
        "td,fd->tf", grad_rows, mlp_output_weight, preferred_element_type=jnp.float32
    )
    (hidden_grad,) = gelu_back(active_grad)
    hidden_low = hidden_grad.astype(jnp.bfloat16)
    up_weight_grad = jnp.einsum(
        "td,tf->df", second_low, hidden_low, preferred_element_type=jnp.float32
    )
    up_bias_grad = jnp.sum(hidden_low.astype(jnp.float32), axis=0)
    normed_grad = jnp.einsum(
        "tf,df->td", hidden_low, mlp_input_weight, preferred_element_type=jnp.float32
    )
    resid_part, second_gain_grad, second_shift_grad = second_back(normed_grad)
    residual_grad = grad_rows.astype(jnp.float32) + resid_part
    branch_low = residual_grad.astype(jnp.bfloat16)
    out_weight_grad = jnp.einsum(
        "ti,to->io", merged_heads, branch_low, preferred_element_type=jnp.float32
    )
    out_bias_grad = jnp.sum(branch_low.astype(jnp.float32), axis=0)
    attended_grad = (
        jnp.einsum(
            "to,io->ti", branch_low, attention_output_weight, preferred_element_type=jnp.float32
        ).reshape(head_shape)
        * live_rows[:, None, None]
    )
    query_grads = (attended_grad / totals[:, :, None]).astype(jnp.bfloat16)
    corrections = (jnp.sum(attended_grad * attended, axis=-1) / totals).astype(jnp.bfloat16)

    def query_turn(index, carried):
        begin_row = index * key_span
        key_rows = lax.dynamic_slice_in_dim(all_keys, begin_row, key_span, 0)
        weights_low, score_grads = back_step(
            queries,
            query_grads,
            corrections,
            seg_rows,
            key_rows,
            lax.dynamic_slice_in_dim(all_values, begin_row, key_span, 0),
            lax.dynamic_slice_in_dim(all_segs, begin_row, key_span, 0),
        )
        return carried + jnp.einsum(
            "hqk,khd->qhd", score_grads, key_rows, preferred_element_type=jnp.float32
        )

    query_sum = lax.fori_loop(0, turns, query_turn, jnp.zeros(head_shape, jnp.float32))
    term_span = math.gcd(row_count * lax.axis_size("blk"), 2048)

    def term_block(index):
        begin_row = index * term_span
        key_part, value_part = key_value_grads(
            queries,
            query_grads,
            corrections,
            seg_rows,
            lax.dynamic_slice_in_dim(all_keys, begin_row, term_span, 0),
            lax.dynamic_slice_in_dim(all_values, begin_row, term_span, 0),
            lax.dynamic_slice_in_dim(all_segs, begin_row, term_span, 0),
        )
        return jnp.concatenate(
            [key_part.reshape(term_span, model_width), value_part.reshape(term_span, model_width)],
            axis=1,
        )

    blocks = lax.map(
        term_block, jnp.arange(row_count * lax.axis_size("blk") // term_span, dtype=jnp.int32)
    )
    key_terms = lax.psum_scatter(
        blocks.reshape(row_count * lax.axis_size("blk"), 2 * model_width),
        "blk",
        scatter_dimension=0,
        tiled=True,
    )
    query_low = query_sum.reshape(row_count, model_width).astype(jnp.bfloat16)
    key_low = key_terms[:, :model_width].astype(jnp.bfloat16)
    value_low = key_terms[:, model_width:].astype(jnp.bfloat16)
    qkv_grad = jnp.concatenate([query_low, key_low, value_low], axis=1)
    qkv_weight_grad = jnp.einsum(
        "td,tj->dj", first_low, qkv_grad, preferred_element_type=jnp.float32
    )
    query_bias_grad = jnp.sum(query_low.astype(jnp.float32), axis=0)
    value_bias_grad = jnp.sum(value_low.astype(jnp.float32), axis=0)
    first_grad = jnp.einsum(
        "tj,dj->td", qkv_grad, query_key_value_weight, preferred_element_type=jnp.float32
    )
    token_part, first_gain_grad, first_shift_grad = first_back(first_grad)
    tokens_grad = (residual_grad + token_part).astype(jnp.bfloat16).reshape(tokens.shape)
    local_grads = (
        qkv_weight_grad,
        query_bias_grad,
        value_bias_grad,
        out_weight_grad,
        out_bias_grad,
        first_gain_grad,
        first_shift_grad,
        second_gain_grad,
        second_shift_grad,
        up_weight_grad,
        up_bias_grad,
        down_weight_grad,
        down_bias_grad,
    )
    scattered = (
        lax.psum_scatter(local_grads[0], "blk", scatter_dimension=0, tiled=True),
        lax.psum_scatter(local_grads[1], "blk", scatter_dimension=0, tiled=True),
        lax.psum_scatter(local_grads[2], "blk", scatter_dimension=0, tiled=True),
        lax.psum_scatter(local_grads[3], "blk", scatter_dimension=0, tiled=True),
        lax.psum_scatter(local_grads[4], "blk", scatter_dimension=0, tiled=True),
        lax.psum_scatter(local_grads[5], "blk", scatter_dimension=0, tiled=True),
        lax.psum_scatter(local_grads[6], "blk", scatter_dimension=0, tiled=True),
        lax.psum_scatter(local_grads[7], "blk", scatter_dimension=0, tiled=True),
        lax.psum_scatter(local_grads[8], "blk", scatter_dimension=0, tiled=True),
        lax.psum_scatter(local_grads[9], "blk", scatter_dimension=0, tiled=True),
        lax.psum_scatter(local_grads[10], "blk", scatter_dimension=0, tiled=True),
        lax.psum_scatter(local_grads[11], "blk", scatter_dimension=1, tiled=True),
        lax.psum_scatter(local_grads[12], "blk", scatter_dimension=0, tiled=True),
    )
    summed_grads = lax.psum(
        (
            scattered[0],
            scattered[1],
            scattered[2],
            scattered[3],
            scattered[4],
            scattered[5],
            scattered[6],
            scattered[7],
            scattered[8],
            scattered[9],
            scattered[10],
            scattered[11],
            scattered[12],
        ),
        "seq",
    )
    return (layer_out, tokens_grad) + tuple(summed_grads)


VMEM_LIMIT = 64 * 1024 * 1024
D = 768
FF = 3072
ROWS = 192
CHIPS = 4
GROUP = 192
QKV = 3 * GROUP
HALF = FF // 2
OUT_HALF = D // 2
PIECE = 48
TILE = 256
TILES = HALF // TILE
PACK = ROWS // 2
SLOT = 2 * ROWS
KEYS = 1536
OWN = 768
LOW = jnp.bfloat16
F32 = jnp.float32
MESH = pl.DeviceIdType.MESH


def dot(a, b):
    return jnp.dot(a, b, preferred_element_type=F32)


def dot_nt(a, b):
    return lax.dot_general(a, b, (((1,), (1,)), ((), ())), preferred_element_type=F32)


def dot_tn(a, b):
    return lax.dot_general(a, b, (((0,), (0,)), ((), ())), preferred_element_type=F32)


def scratch_list():
    dma = pltpu.SemaphoreType.DMA
    vmem = pltpu.VMEM
    return dict(
        tok=vmem((ROWS, D), LOW),
        seg=vmem((1, ROWS), jnp.int32),
        vec0=vmem((D,), LOW), vec1=vmem((D,), LOW), vec2=vmem((D,), LOW), vec3=vmem((D,), LOW),
        vec4=vmem((D,), LOW), vec5=vmem((D,), LOW), vec6=vmem((D,), LOW), vec7=vmem((D,), LOW),
        vec8=vmem((FF,), LOW),
        layer=vmem((ROWS, D), LOW),
        tokg=vmem((ROWS, D), LOW),
        vec=vmem((3, 8, D), F32),
        in_sem=dma((12,)), out_sem=dma((5,)), own_sem=dma((TILES + 1,)),
        nrm=vmem((CHIPS, ROWS, D), LOW),
        xhat1=vmem((ROWS, D), F32),
        rstd1=vmem((ROWS, 1), F32),
        par=vmem((8, D), F32),
        qvb=vmem((2, CHIPS, GROUP), F32),
        b1=vmem((1, FF), F32),
        wf=vmem((D, 3 * D), LOW),
        wo=vmem((D, D), LOW),
        w2=vmem((HALF, D), LOW),
        q=vmem((3, OWN, 2 * HEAD), LOW),
        kvo=vmem((CHIPS, ROWS, 2 * GROUP), LOW),
        kvs=vmem((CHIPS, ROWS, 2 * GROUP), LOW),
        kh=vmem((3, KEYS, HEAD), LOW),
        vh=vmem((3, KEYS, 2 * HEAD), LOW),
        kvt=vmem((6, HEAD, KEYS), LOW),
        segs=vmem((8, 8, ROWS), jnp.int32),
        kseg=vmem((1, KEYS), jnp.int32),
        qseg=vmem((OWN, 128), jnp.int32),
        prob=vmem((3, OWN, KEYS), LOW),
        att=vmem((3, OWN, 2 * HEAD), F32),
        mgs=vmem((CHIPS, PACK, 2 * GROUP), LOW),
        mgr=vmem((CHIPS, PACK, 2 * GROUP), LOW),
        mgo=vmem((CHIPS, PACK, 2 * GROUP), LOW),
        mg=vmem((CHIPS, ROWS, GROUP), LOW),
        og=vmem((2, ROWS, D), LOW),
        nt=vmem((2, ROWS, D), LOW),
        bl=vmem((2, ROWS, D), LOW),
        resid=vmem((ROWS, D), F32),
        xhat2=vmem((ROWS, D), F32),
        rstd2=vmem((ROWS, 1), F32),
        act=vmem((2 * ROWS, HALF), LOW),
        hg=vmem((2 * ROWS, HALF), LOW),
        lo=vmem((2, ROWS, D), F32),
        ng=vmem((2, ROWS, D), F32),
        lor=vmem((ROWS, D), F32),
        ngr=vmem((ROWS, D), F32),
        ags=vmem((CHIPS, PACK, 2 * GROUP), LOW),
        ag=vmem((CHIPS, PACK, 2 * GROUP), LOW),
        agh=vmem((3, OWN, HEAD), LOW),
        dqs=vmem((3, CHIPS, PACK, 2 * GROUP), LOW),
        dqr=vmem((3, CHIPS, PACK, 2 * GROUP), LOW),
        rowg=vmem((ROWS, 3 * D), LOW),
        dkr=vmem((3, 2, HEAD, OWN), LOW),
        dks=vmem((3, 2, HEAD, OWN), LOW),
        dqkv=vmem((OWN, QKV), LOW),
        da=vmem((TILES, CHIPS, 2, 2, PIECE, TILE), LOW),
        db=vmem((TILES, CHIPS, 2, 2, PIECE, TILE), LOW),
        ra=vmem((TILES, CHIPS, 2, PIECE, TILE), LOW),
        rb=vmem((TILES, CHIPS, 2, PIECE, TILE), LOW),
        a2s=vmem((TILES, CHIPS, PIECE, TILE), LOW),
        b2s=vmem((TILES, CHIPS, PIECE, TILE), LOW),
        a2r=vmem((TILES, CHIPS, PIECE, TILE), LOW),
        b2r=vmem((TILES, CHIPS, PIECE, TILE), LOW),
        zs=vmem((TILES, CHIPS, 2, PIECE, TILE), LOW),
        rz=vmem((TILES, CHIPS, 2, PIECE, TILE), LOW),
        zm=vmem((TILES, 2, 2, PIECE, TILE), LOW),
        fin=vmem((TILES, 2, PIECE, TILE), LOW),
        oa=vmem((2, 2, 2, PIECE, OUT_HALF), LOW),
        ob=vmem((2, 2, 2, PIECE, OUT_HALF), LOW),
        roa=vmem((2, 2, PIECE, OUT_HALF), LOW),
        rob=vmem((2, 2, PIECE, OUT_HALF), LOW),
        oa2s=vmem((2, PIECE, OUT_HALF), LOW),
        ob2s=vmem((2, PIECE, OUT_HALF), LOW),
        oa2r=vmem((2, PIECE, OUT_HALF), LOW),
        ob2r=vmem((2, PIECE, OUT_HALF), LOW),
        zo=vmem((CHIPS, PIECE, OUT_HALF), LOW),
        rzo=vmem((CHIPS, PIECE, OUT_HALF), LOW),
        zmo=vmem((2, PIECE, OUT_HALF), LOW),
        fo=vmem((PIECE, OUT_HALF), LOW),
        dwq=vmem((CHIPS, 4, PIECE, QKV), LOW),
        dwqr=vmem((2, 4, PIECE, QKV), LOW),
        dwqx=vmem((2, 4, PIECE, QKV), LOW),
        rxq=vmem((3, 2, PIECE, QKV), LOW),
        zq=vmem((2, PIECE, QKV), LOW),
        rzq=vmem((CHIPS, PIECE, QKV), LOW),
        va=vmem((8, D), F32),
        vh1=vmem((1, HALF), F32),
        vap=vmem((8, D), F32),
        vaz=vmem((CHIPS, 8, D), F32),
        vax=vmem((4, 8, D), F32),
        vq=vmem((8, TILE), F32),
        vqp=vmem((8, TILE), F32),
        vqz=vmem((CHIPS, 8, TILE), F32),
        vqx=vmem((4, 8, TILE), F32),
        vb=vmem((8, TILE), F32),
        vbr=vmem((8, 8, TILE), F32),
        vbx=vmem((4, 8, TILE), F32),
        load_sem=dma((3 + TILES,)),
        seg_s=dma((1,)), seg_r=dma((1,)),
        og_s=dma((1,)), og_r=dma((1,)),
        n_s=dma((1,)), n_r=dma((CHIPS, 2)),
        kv_s=dma((CHIPS,)), kv_r=dma((CHIPS,)),
        mg_s=dma((1,)), mg_r=dma((1,)),
        mgo_s=dma((1,)), mgo_r=dma((1,)),
        nt_s=dma((1,)), nt_r=dma((1,)),
        lo_s=dma((1,)), lo_r=dma((1,)),
        ng_s=dma((1,)), ng_r=dma((1,)),
        bl_s=dma((1,)), bl_r=dma((1,)),
        ag_s=dma((1,)), ag_r=dma((1,)),
        dk_s=dma((3,)), dk_r=dma((3,)),
        dq_s=dma((3,)), dq_r=dma((3,)),
        h_s=dma((TILES + 2,)), h1_r=dma((TILES + 1,)), h2_r=dma((TILES + 1,)),
        z_s=dma((TILES + 1,)), z_r=dma((TILES + 1, 2)),
        f_s=dma((TILES + 1,)), f_r=dma((TILES + 1,)),
        q0_s=dma((1,)), q0_r=dma((1,)),
        qx_s=dma((1,)), qx_r=dma((1,)),
        qz_s=dma((2,)), qz_r=dma((CHIPS,)),
        qf_s=dma((3,)), qf_r=dma((3,)),
        va_s=dma((3,)), va_r=dma((3,)),
        vq_s=dma((3,)), vq_r=dma((3,)),
        vb_s=dma((1,)), vb_r=dma((1,)),
        vbx_s=dma((1,)), vbx_r=dma((1,)),
    )


EARLY = 4
STARTED = 2
PLAN = dict(
    before_norm=((1, 0), (0, 2)),
    after_norm=(),
    middle=((1, 1), (0, 3)),
    before_loop=((2, 0),),
    loop=(
        (0, ((1, 2), (0, 4), (2, 1))),
        (1, ((3, 0),)),
        (2, ((1, 3), (0, 5))),
        (3, ((2, 2), (3, 1))),
        (5, ((1, 4), (0, 6))),
    ),
    after_loop=((2, 3), (4, 0), (1, 5)),
    after_qkv=((1, 6), (2, 4), (4, 1)),
    after_rows=((3, 2), (2, 5), (3, 3), (2, 6)),
    before_sums=((4, 2), (3, 4)),
    last=((3, 5), (3, 6), (4, 3), (4, 4), (4, 5), (4, 6)),
)


class Box:
    pass


def kernel_body(names, pad_number, *refs):
    (tok_h, seg_h, og_h, wqkv, wo_h, w1_h, w2_h) = refs[:7]
    (out_tok, out_layer, out_fin, out_fo, out_finq, out_vec) = refs[16:22]
    r = Box()
    for name, ref in zip(names, refs[22:]):
        setattr(r, name, ref)
    par, qvb, b1 = r.par, r.qvb, r.b1
    tok = r.tok

    s = lax.axis_index("seq")
    b = lax.axis_index("blk")
    z = b // 2
    c = b % 2
    sib = 2 * z + 1 - c
    flip = {1: s + 1 - 2 * (s % 2), 2: (s + 2) % 4, 3: 3 - s}
    x = s % 2
    y = s // 2
    is_end = jnp.logical_or(z == 0, z == 3)

    pending = []

    def send(src, dst, ssem, rsem, dev_s, dev_b):
        return pltpu.make_async_remote_copy(
            src_ref=src, dst_ref=dst, send_sem=ssem, recv_sem=rsem,
            device_id=(dev_s, dev_b), device_id_type=MESH,
        )

    def all_of(ref, ssem, rsem):
        return send(ref, ref, ssem, rsem, s, sib)

    def local_row(index):
        return par[index : index + 1, :]

    barrier = pltpu.get_barrier_semaphore()
    for step in range(1, 8):
        pl.semaphore_signal(barrier, inc=1, device_id=(s, (b + step) % 8), device_id_type=MESH)
    for step in (1, 2, 3):
        for core in range(2):
            pl.semaphore_signal(
                barrier, inc=1, device_id=(flip[step], 2 * z + core), device_id_type=MESH
            )

    vectors = [getattr(r, "vec%d" % index) for index in range(9)]
    first_loads = [
        pltpu.make_async_copy(source, target, r.in_sem.at[index])
        for index, (source, target) in enumerate(
            [(tok_h, r.tok), (seg_h, r.seg), (og_h, r.og.at[c])]
            + list(zip(refs[7:16], vectors))
        )
    ]
    for item in first_loads:
        item.start()

    loads = []
    loads.append(pltpu.make_async_copy(wqkv, r.wf, r.load_sem.at[0]))
    half = pl.multiple_of(c * HALF, 128)
    loads.append(pltpu.make_async_copy(wo_h, r.wo, r.load_sem.at[1]))
    loads.append(pltpu.make_async_copy(w2_h.at[pl.ds(half, HALF), :], r.w2, r.load_sem.at[2]))
    for tile in range(TILES):
        cols = pl.ds(pl.multiple_of(c * HALF + tile * TILE, TILE), TILE)
        loads.append(
            pltpu.make_async_copy(
                w1_h.at[:, :, :, :, cols], r.da.at[tile], r.load_sem.at[3 + tile]
            )
        )
    for item in loads:
        item.start()

    for item in first_loads:
        item.wait()
    for index, vector in enumerate(vectors[:8]):
        par[index : index + 1, :] = vector[...].astype(F32).reshape(1, D)
    for slot in range(CHIPS):
        part = slice(slot * GROUP, (slot + 1) * GROUP)
        qvb[0, slot : slot + 1, :] = par[0:1, part]
        qvb[1, slot : slot + 1, :] = par[1:2, part]
    b1[...] = vectors[8][...].astype(F32).reshape(1, FF)

    def first_norm(index, carried):
        rows = pl.ds(index * PIECE, PIECE)
        x = tok[rows, :].astype(F32)
        centre = x - jnp.mean(x, axis=-1, keepdims=True)
        spread = lax.rsqrt(jnp.mean(centre * centre, axis=-1, keepdims=True) + EPS)
        xhat = centre * spread
        r.xhat1[rows, :] = xhat
        r.rstd1[rows, :] = spread
        r.nrm[z, rows, :] = (xhat * local_row(3) + local_row(4)).astype(LOW)
        return carried

    lax.fori_loop(0, 4, first_norm, 0)

    pl.semaphore_wait(barrier, 13)

    def norm_copy(slot, side, up):
        part = r.nrm.at[slot, pl.ds(side * PACK, PACK)]
        return send(part, part, r.n_s.at[0], r.n_r.at[slot, side], s, b + 2 if up else b - 2)

    def norm_forward(slot, side):
        @pl.when(jnp.logical_and(slot <= z, z < 3))
        def _():
            norm_copy(slot, side, True).start()

        @pl.when(jnp.logical_and(slot >= z, z > 0))
        def _():
            norm_copy(slot, side, False).start()

    norm_forward(z, 0)
    norm_forward(z, 1)

    r.segs[CHIPS * c + z] = jnp.broadcast_to(r.seg[...], (8, ROWS))
    seg_copies = []
    for step in range(1, 8):
        seg_copies.append(
            send(r.segs.at[CHIPS * c + z], r.segs.at[CHIPS * c + z], r.seg_s.at[0], r.seg_r.at[0],
                 s, (b + step) % 8)
        )
    for item in seg_copies:
        item.start()
    seg_all = all_of(r.segs.at[pl.ds(0, 7)], r.seg_s.at[0], r.seg_r.at[0])
    pending.append(seg_all)


    og_copy = send(r.og.at[c], r.og.at[c], r.og_s.at[0], r.og_r.at[0], s, sib)
    og_copy.start()
    pending.append(og_copy)

    loads[0].wait()
    for part in range(3):
        start = pl.multiple_of(D * part + 384 * (z // 2) + 128 * (z % 2), 128)
        window = r.wf[:, pl.ds(start, 256)]
        r.dqkv[:, part * GROUP : (part + 1) * GROUP] = jnp.where(
            z % 2 == 1, window[:, 64:256], window[:, 0:192]
        )

    upper = z // 2
    qkv_bias = [qvb[0, pl.ds(z, 1), :], None, qvb[1, pl.ds(z, 1), :]]

    def split_keys(pair, row):
        for h in range(3):
            r.kh[h, pl.ds(row, ROWS), :] = pair[:, h * HEAD : (h + 1) * HEAD]
            r.vh[h, pl.ds(row, ROWS), 0:HEAD] = pair[:, GROUP + h * HEAD : GROUP + (h + 1) * HEAD]

    def kv_copy(slot):
        return send(r.kvo.at[slot], r.kvs.at[slot], r.kv_s.at[slot], r.kv_r.at[slot], s, sib)

    def project(slot):
        rows = r.nrm[slot]
        whole = dot(rows, r.dqkv[...])
        qs = (whole[:, :GROUP] + qkv_bias[0]).astype(LOW) * (1.0 / math.sqrt(HEAD))
        ks = whole[:, GROUP : 2 * GROUP].astype(LOW)
        vs = (whole[:, 2 * GROUP :] + qkv_bias[2]).astype(LOW)
        for h in range(3):
            r.q[h, pl.ds(slot * ROWS, ROWS), 0:HEAD] = qs[:, h * HEAD : (h + 1) * HEAD]
        r.kvo[slot, :, 0:GROUP] = ks
        r.kvo[slot, :, GROUP : 2 * GROUP] = vs
        kv_copy(slot).start()
        split_keys(r.kvo[slot], slot * SLOT)

    r.vh[:, :, HEAD : 2 * HEAD] = jnp.ones((3, KEYS, HEAD), LOW)
    project(z)

    def arrivals(distance, carried):
        for side in range(2):
            for slot, there in ((z - distance, z >= distance), (z + distance, z + distance < CHIPS)):
                @pl.when(there)
                def _(slot=slot, side=side):
                    norm_copy(slot, side, True).wait_recv()
                    norm_forward(slot, side)

        for slot, there in ((z - distance, z >= distance), (z + distance, z + distance < CHIPS)):
            @pl.when(there)
            def _(slot=slot):
                project(slot)

        return carried

    arrivals(1, 0)

    seg_all.wait_recv()
    for slot in range(CHIPS):
        for side, core in ((0, c), (1, 1 - c)):
            start = slot * SLOT + side * ROWS
            r.kseg[:, start : start + ROWS] = r.segs[CHIPS * core + slot, 0:1, :]
        line = r.segs[CHIPS * c + slot, 0:1, :].astype(F32)
        r.qseg[slot * ROWS : (slot + 1) * ROWS, :] = jnp.transpose(
            jnp.broadcast_to(line, (128, ROWS))
        ).astype(jnp.int32)

    loads[2].wait()
    og_copy.wait_recv()

    def active_grads(index, carried):
        cols = pl.ds(pl.multiple_of(index * 512, 512), 512)
        r.hg[:, cols] = dot_nt(r.og[...].reshape(2 * ROWS, D), r.w2[cols, :]).astype(LOW)
        return carried

    lax.fori_loop(0, HALF // 512, active_grads, 0)

    for slot, there in ((z - 2, z >= 2), (z + 2, z + 2 < CHIPS)):
        for side in range(2):
            @pl.when(there)
            def _(slot=slot, side=side):
                norm_copy(slot, side, True).wait_recv()
                norm_forward(slot, side)

        @pl.when(there)
        def _(slot=slot):
            project(slot)

    def take_sibling(slot, carried):
        kv_copy(slot).wait_recv()
        split_keys(r.kvs[slot], slot * SLOT + ROWS)
        both = jnp.concatenate([r.kvo[slot], r.kvs[slot]], axis=0)
        span = pl.ds(pl.multiple_of(slot * SLOT, 128), SLOT)
        r.kvt[:, :, span] = jnp.transpose(both).reshape(6, HEAD, SLOT)
        return carried

    lax.fori_loop(upper, upper + 3, take_sibling, 0)

    BAND = 2 * ROWS
    last = 3 * (1 - upper)

    def pack(ref, index, lane, value):
        width = value.shape[1]
        ref[index, :, lane : lane + width] = value[0:PACK]
        ref[index, :, GROUP + lane : GROUP + lane + width] = value[PACK:ROWS]

    def mg_copy(block):
        return send(r.mgs.at[block], r.mgr.at[z], r.mg_s.at[0], r.mg_r.at[0], s, 2 * block + c)

    mg_all = all_of(r.mgs.at[pl.ds(0, 3)], r.mg_s.at[0], r.mg_r.at[0])

    def weigh(h, rows, count, lanes, width):
        own_segs = r.qseg[rows, :]
        wide = jnp.concatenate([own_segs] * (width // 128), axis=1)
        raw = dot(r.q[h, rows, 0:HEAD], r.kvt[h, :, lanes])
        weights = jnp.where(wide == r.kseg[:, lanes], jnp.exp(raw), 0.0).astype(LOW)
        r.prob[h, rows, lanes] = weights
        return dot(weights, r.vh[h, lanes, :])

    def settle(h, rows, total):
        live = jnp.where(r.qseg[rows, :][:, :HEAD] != pad_number, 1.0, 0.0).astype(F32)
        inverse = 1.0 / total[:, HEAD:]
        r.att[h, rows, 0:HEAD] = total[:, :HEAD] * inverse * live
        r.att[h, rows, HEAD : 2 * HEAD] = inverse

    old_rows = pl.ds(pl.multiple_of(upper * ROWS, ROWS), 3 * ROWS)
    old_lanes = pl.ds(pl.multiple_of(upper * SLOT, 128), 3 * SLOT)
    last_rows = pl.ds(pl.multiple_of(last * ROWS, ROWS), ROWS)
    last_lanes = pl.ds(pl.multiple_of(last * SLOT, 128), SLOT)

    def forward_old(h, carried):
        r.att[h, old_rows, :] = weigh(h, old_rows, 3 * ROWS, old_lanes, 3 * SLOT)
        return carried

    lax.fori_loop(0, 3, forward_old, 0)

    @pl.when(is_end)
    def _():
        for side in range(2):
            norm_copy(last, side, True).wait_recv()
        project(last)

    take_sibling(last, 0)

    def give(block):
        block_rows = pl.ds(pl.multiple_of(block * ROWS, ROWS), ROWS)
        for head in range(3):
            pack(r.mgs, block, head * HEAD, r.att[head, block_rows, 0:HEAD].astype(LOW))

        @pl.when(block != z)
        def _():
            mg_copy(block).start()

        @pl.when(block == z)
        def _():
            r.mgr[z] = r.mgs[z]

    def forward_last(h, carried):
        settle(h, last_rows, weigh(h, last_rows, ROWS, slice(0, KEYS), KEYS))
        return carried

    lax.fori_loop(0, 3, forward_last, 0)
    give(last)

    def forward_rest(h, carried):
        settle(
            h, old_rows, r.att[h, old_rows, :] + weigh(h, old_rows, 3 * ROWS, last_lanes, SLOT)
        )
        return carried

    lax.fori_loop(0, 3, forward_rest, 0)

    for index in range(3):
        give(2 - index + upper * (2 * index - 1))

    def others(fn):
        def run(index, carried):
            fn((z + 1 + index) % CHIPS)
            return carried

        lax.fori_loop(0, CHIPS - 1, run, 0)

    mg_all.wait_recv()
    mgo_copy = send(r.mgr, r.mgo, r.mgo_s.at[0], r.mgo_r.at[0], s, sib)
    mgo_copy.start()
    pending.append(mgo_copy)

    for slot in range(CHIPS):
        r.mg[slot, 0:PACK, :] = r.mgr[slot, :, 0:GROUP]
        r.mg[slot, PACK:ROWS, :] = r.mgr[slot, :, GROUP : 2 * GROUP]

    loads[1].wait()

    def out_projection(index, carried):
        cols = pl.ds(pl.multiple_of(index * 256, 256), 256)
        total = tok[:, cols].astype(F32) + par[2:3, cols]
        for slot in range(CHIPS):
            total = total + dot(r.mg[slot], r.wo[slot * GROUP : (slot + 1) * GROUP, cols])
        r.resid[:, cols] = total
        return carried

    lax.fori_loop(0, 3, out_projection, 0)

    def second_norm(index, carried):
        rows = pl.ds(index * PIECE, PIECE)
        x = r.resid[rows, :]
        centre = x - jnp.mean(x, axis=-1, keepdims=True)
        spread = lax.rsqrt(jnp.mean(centre * centre, axis=-1, keepdims=True) + EPS)
        xhat = centre * spread
        r.xhat2[rows, :] = xhat
        r.rstd2[rows, :] = spread
        r.nt[c, rows, :] = (xhat * local_row(5) + local_row(6)).astype(LOW)
        return carried

    lax.fori_loop(0, 4, second_norm, 0)
    nt_copy = send(r.nt.at[c], r.nt.at[c], r.nt_s.at[0], r.nt_r.at[0], s, sib)
    nt_copy.start()
    pending.append(nt_copy)
    for item in loads[3:]:
        item.wait()
    r.va[...] = jnp.zeros((8, D), F32)
    r.vb[...] = jnp.zeros((8, TILE), F32)
    r.va[3:4, :] = jnp.sum(r.og[c].astype(F32), axis=0, keepdims=True)
    nt_copy.wait_recv()

    def hop_one(unit):
        if isinstance(unit, int) and unit == TILES:
            one, two, to_one, to_two = r.oa, r.ob, r.roa, r.rob
        else:
            one, two, to_one, to_two = r.da.at[unit], r.db.at[unit], r.ra.at[unit], r.rb.at[unit]
        return (
            send(one.at[:, :, 1 - x], to_one, r.h_s.at[unit], r.h1_r.at[unit], flip[1], b),
            send(two.at[:, 1 - y], to_two, r.h_s.at[unit], r.h1_r.at[unit], flip[2], b),
        )

    def hop_two(unit):
        later = TILES + 1 if isinstance(unit, int) and unit == TILES else unit
        if isinstance(unit, int) and unit == TILES:
            one, two, to_one, to_two = r.oa2s, r.ob2s, r.oa2r, r.ob2r
        else:
            one, two, to_one, to_two = (
                r.a2s.at[unit], r.b2s.at[unit], r.a2r.at[unit], r.b2r.at[unit]
            )
        return (
            send(one, to_one, r.h_s.at[later], r.h2_r.at[unit], flip[2], b),
            send(two, to_two, r.h_s.at[later], r.h2_r.at[unit], flip[1], b),
        )

    def hop_one_all(unit):
        last_unit = isinstance(unit, int) and unit == TILES
        return all_of(r.oa if last_unit else r.da.at[unit], r.h_s.at[unit], r.h1_r.at[unit])

    def hop_two_all(unit):
        last_unit = isinstance(unit, int) and unit == TILES
        return all_of(r.roa if last_unit else r.ra.at[unit], r.h_s.at[TILES + 1], r.h2_r.at[unit])

    partner = z + 1 - 2 * (z % 2)
    inner = 3 - z
    outer = 3 - partner
    low_block = 1 - upper
    inner_of_end = 3 - partner

    def z_refs(unit):
        if isinstance(unit, int) and unit == TILES:
            return r.zo, r.rzo, r.zmo
        return r.zs.at[unit], r.rz.at[unit], r.zm.at[unit]

    def z_bundle(unit):
        here, there, _ = z_refs(unit)
        three = pl.ds(low_block, 3)
        return send(here.at[three], there.at[three], r.z_s.at[unit], r.z_r.at[unit, 0],
                    s, 2 * partner + c)

    def z_near(unit):
        here, there, _ = z_refs(unit)
        return send(here.at[partner], there.at[z], r.z_s.at[unit], r.z_r.at[unit, 0],
                    s, 2 * partner + c)

    def z_inner(unit):
        _, there, merged = z_refs(unit)
        return send(merged.at[0], there.at[outer], r.z_s.at[unit], r.z_r.at[unit, 1],
                    s, 2 * inner + c)

    def z_outer(unit):
        _, there, merged = z_refs(unit)
        return send(merged.at[1], there.at[z], r.z_s.at[unit], r.z_r.at[unit, 1],
                    s, 2 * outer + c)

    def z_three_arrival(unit):
        here, there, _ = z_refs(unit)
        three = pl.ds(low_block, 3)
        return send(here.at[three], there.at[three], r.z_s.at[unit], r.z_r.at[unit, 0],
                    s, 2 * partner + c)

    def z_arrival(unit, level):
        here, _, _ = z_refs(unit)
        return all_of(here.at[0], r.z_s.at[unit], r.z_r.at[unit, level])

    def z_sent(unit):
        here, _, _ = z_refs(unit)
        return all_of(here.at[pl.ds(0, 3)], r.z_s.at[unit], r.z_r.at[unit, 0])

    owner = s // 2
    mine = 2 * z + owner

    def fin_copy(unit, step):
        if isinstance(unit, int) and unit == TILES:
            here, there = r.fo, out_fo.at[s % 2, c]
        else:
            here, there = r.fin.at[unit], out_fin.at[unit, s % 2, c]
        return send(here, there, r.f_s.at[unit], r.f_r.at[unit],
                    s if step == 0 else flip[step], mine)

    def fin_own(unit):
        if isinstance(unit, int) and unit == TILES:
            here, there = r.fo, out_fo.at[s % 2, c]
        else:
            here, there = r.fin.at[unit], out_fin.at[unit, s % 2, c]
        return pltpu.make_async_copy(here, there, r.own_sem.at[unit])

    def fin_all(unit, count):
        whole = r.zo if unit == TILES else r.zs.at[unit]
        return all_of(whole.at[pl.ds(0, count)], r.f_s.at[unit], r.f_r.at[unit])

    def mlp_grads(tile):
        cols = pl.ds(pl.multiple_of(tile * TILE, TILE), TILE)

        r.da[tile] = dot_tn(r.nt[...].reshape(2 * ROWS, D), r.hg[:, cols]).astype(LOW).reshape(
            CHIPS, 2, 2, PIECE, TILE
        )
        r.db[tile] = dot_tn(r.og[...].reshape(2 * ROWS, D), r.act[:, cols]).astype(LOW).reshape(
            CHIPS, 2, 2, PIECE, TILE
        )

    def service_zero(unit):
        for item in hop_one(unit):
            item.start()

    def service_one(unit):
        hop_one_all(unit).wait_recv()
        if isinstance(unit, int) and unit == TILES:
            for block in range(2):
                r.oa2s[block] = (
                    r.oa[block, 1 - y, x].astype(F32) + r.roa[block, 1 - y].astype(F32)
                ).astype(LOW)
                r.ob2s[block] = (
                    r.ob[block, y, 1 - x].astype(F32) + r.rob[block, 1 - x].astype(F32)
                ).astype(LOW)
        else:
            def add(block, carried):
                r.a2s[unit, block] = (
                    r.da[unit, block, 1 - y, x].astype(F32) + r.ra[unit, block, 1 - y].astype(F32)
                ).astype(LOW)
                r.b2s[unit, block] = (
                    r.db[unit, block, y, 1 - x].astype(F32) + r.rb[unit, block, 1 - x].astype(F32)
                ).astype(LOW)
                return carried

            lax.fori_loop(0, CHIPS, add, 0)
        for item in hop_two(unit):
            item.start()

    def service_two(unit):
        hop_two_all(unit).wait_recv()
        if isinstance(unit, int) and unit == TILES:
            for block in range(2):
                r.zo[block] = (
                    r.oa[block, y, x].astype(F32) + r.roa[block, y].astype(F32)
                    + r.oa2r[block].astype(F32)
                ).astype(LOW)
                r.zo[2 + block] = (
                    r.ob[block, y, x].astype(F32) + r.rob[block, x].astype(F32)
                    + r.ob2r[block].astype(F32)
                ).astype(LOW)
        else:
            def add(block, carried):
                r.zs[unit, block, 0] = (
                    r.da[unit, block, y, x].astype(F32) + r.ra[unit, block, y].astype(F32)
                    + r.a2r[unit, block].astype(F32)
                ).astype(LOW)
                r.zs[unit, block, 1] = (
                    r.db[unit, block, y, x].astype(F32) + r.rb[unit, block, x].astype(F32)
                    + r.b2r[unit, block].astype(F32)
                ).astype(LOW)
                return carried

            lax.fori_loop(0, CHIPS, add, 0)
        @pl.when(is_end)
        def _():
            z_bundle(unit).start()

        @pl.when(jnp.logical_not(is_end))
        def _():
            z_near(unit).start()

    def service_three(unit):
        here, there, merged = z_refs(unit)

        @pl.when(jnp.logical_not(is_end))
        def _():
            z_three_arrival(unit).wait_recv()
            merged[0] = (here[inner].astype(F32) + there[inner].astype(F32)).astype(LOW)
            merged[1] = (here[outer].astype(F32) + there[outer].astype(F32)).astype(LOW)
            z_inner(unit).start()
            z_outer(unit).start()

    def service_four(unit):
        here, there, _ = z_refs(unit)
        z_arrival(unit, 1).wait_recv()

        @pl.when(is_end)
        def _():
            z_arrival(unit, 0).wait_recv()

        second = jnp.where(is_end, inner_of_end, z)
        total = here[z].astype(F32) + there[partner].astype(F32) + there[second].astype(F32)
        if isinstance(unit, int) and unit == TILES:
            r.fo[...] = total.astype(LOW)
        else:
            r.fin[unit] = total.astype(LOW)
        for step in (1, 2, 3):
            fin_copy(unit, step).start()

        @pl.when(mine != b)
        def _():
            fin_copy(unit, 0).start()

        @pl.when(mine == b)
        def _():
            fin_own(unit).start()

    def run_services(listed):
        for kind, unit in listed:
            (service_zero, service_one, service_two, service_three, service_four)[kind](unit)


    r.lo[...] = jnp.zeros((2, ROWS, D), F32)
    r.ng[...] = jnp.zeros((2, ROWS, D), F32)

    WIDE = 2 * TILE

    def mlp_tile(index, carried):
        cols = pl.ds(pl.multiple_of(index * WIDE, WIDE), WIDE)
        bias = b1[:, pl.ds(pl.multiple_of(c * HALF + index * WIDE, WIDE), WIDE)]
        w1 = jnp.concatenate(
            [r.da[2 * index + part].reshape(D, TILE) for part in range(2)], axis=1
        )
        w2 = r.w2[cols, :]
        hidden = dot(r.nt[...].reshape(2 * ROWS, D), w1) + bias
        gate = 0.5 * (1.0 + lax.erf(hidden * (1.0 / math.sqrt(2.0))))
        slope = gate + hidden * jnp.exp(-0.5 * hidden * hidden) * (1.0 / math.sqrt(2.0 * math.pi))
        active = (hidden * gate).astype(LOW)
        grad = (slope * r.hg[:, cols].astype(F32)).astype(LOW)
        r.act[:, cols] = active
        r.hg[:, cols] = grad
        r.vh1[:, cols] = jnp.sum(grad.astype(F32), axis=0, keepdims=True)
        r.lo[...] += dot(active, w2).reshape(2, ROWS, D)
        r.ng[...] += dot_nt(grad, w1).reshape(2, ROWS, D)
        for part in range(2):
            tile = 2 * index + part

            @pl.when(tile < EARLY)
            def _(tile=tile):
                mlp_grads(tile)

            @pl.when(tile < STARTED)
            def _(tile=tile):
                service_zero(tile)

        return carried

    lax.fori_loop(0, TILES // 2, mlp_tile, 0)
    for part in range(2):
        r.va[pl.ds(4 + 2 * c + part, 1), :] = r.vh1[:, part * D : (part + 1) * D]
    ng_copy = send(r.ng.at[1 - c], r.ngr, r.ng_s.at[0], r.ng_r.at[0], s, sib)
    lo_copy = send(r.lo.at[1 - c], r.lor, r.lo_s.at[0], r.lo_r.at[0], s, sib)
    ng_copy.start()
    lo_copy.start()

    mlp_grads(4)
    run_services(PLAN["before_norm"])

    ng_copy.wait_recv()

    def second_back(index, carried):
        rows = pl.ds(index * PIECE, PIECE)
        grad = r.ng[c, rows, :] + r.ngr[rows, :]
        xhat = r.xhat2[rows, :]
        scaled = grad * local_row(5)
        mean_one = jnp.mean(scaled, axis=-1, keepdims=True)
        mean_two = jnp.mean(scaled * xhat, axis=-1, keepdims=True)
        through = r.rstd2[rows, :] * (scaled - mean_one - xhat * mean_two)
        resid_grad = r.og[c, rows, :].astype(F32) + through
        low = resid_grad.astype(LOW)
        r.xhat2[rows, :] = resid_grad
        r.bl[c, rows, :] = low
        r.va[0:1, :] += jnp.sum(low.astype(F32), axis=0, keepdims=True)
        r.va[1:2, :] += jnp.sum(grad * xhat, axis=0, keepdims=True)
        r.va[2:3, :] += jnp.sum(grad, axis=0, keepdims=True)
        return carried

    lax.fori_loop(0, 4, second_back, 0)
    bl_copy = send(r.bl.at[c], r.bl.at[c], r.bl_s.at[0], r.bl_r.at[0], s, sib)
    bl_copy.start()
    pending.append(bl_copy)

    def ag_copy(block):
        return send(r.ags.at[block], r.ag.at[z], r.ag_s.at[0], r.ag_r.at[0], s, 2 * block + c)

    ag_all = all_of(r.ags.at[pl.ds(0, 3)], r.ag_s.at[0], r.ag_r.at[0])

    def attended_block(index, carried):
        block = (z + 1 + index) % CHIPS
        wide = pl.ds(pl.multiple_of(block * GROUP, GROUP), GROUP)
        pack(r.ags, block, 0, dot_nt(r.bl[c], r.wo[wide, :]).astype(LOW))

        @pl.when(block != z)
        def _():
            ag_copy(block).start()

        @pl.when(block == z)
        def _():
            r.ag[z] = r.ags[z]

        return carried

    lax.fori_loop(0, CHIPS, attended_block, 0)

    def vector_sums(mine_ref, pair_ref, z_ref, x_ref, send_sems, recv_sems):
        def pair():
            return send(mine_ref, pair_ref, send_sems.at[0], recv_sems.at[0], s, sib)

        def along(step):
            return send(z_ref.at[z], z_ref.at[z], send_sems.at[1], recv_sems.at[1],
                        s, (b + 2 * step) % 8)

        def over(step):
            return send(x_ref.at[s], x_ref.at[s], send_sems.at[2], recv_sems.at[2],
                        flip[step], b)

        along_all = all_of(z_ref.at[pl.ds(0, 3)], send_sems.at[1], recv_sems.at[1])
        over_all = all_of(x_ref.at[pl.ds(0, 3)], send_sems.at[2], recv_sems.at[2])

        def stage_one():
            pair().start()
            pending.append(pair())

        def stage_two():
            pair().wait_recv()
            r_first = jnp.where(c == 0, mine_ref[...], pair_ref[...])
            r_second = jnp.where(c == 0, pair_ref[...], mine_ref[...])
            z_ref[z] = r_first + r_second
            for step in (1, 2, 3):
                along(step).start()
            pending.append(along_all)

        def stage_three():
            along_all.wait_recv()
            x_ref[s] = z_ref[0] + z_ref[1] + z_ref[2] + z_ref[3]
            for step in (1, 2, 3):
                over(step).start()
            pending.append(over_all)

        def stage_four():
            over_all.wait_recv()
            return x_ref[0] + x_ref[1] + x_ref[2] + x_ref[3]

        return stage_one, stage_two, stage_three, stage_four

    va_stages = vector_sums(r.va, r.vap, r.vaz, r.vax, r.va_s, r.va_r)
    vq_stages = vector_sums(r.vq, r.vqp, r.vqz, r.vqx, r.vq_s, r.vq_r)
    va_stages[0]()

    run_services(PLAN["after_norm"])
    mlp_grads(5)
    run_services(PLAN["middle"])
    mgo_copy.wait_recv()
    bl_copy.wait_recv()
    side = pl.ds(pl.multiple_of(c * OUT_HALF, OUT_HALF), OUT_HALF)
    for block in range(CHIPS):
        theirs = jnp.concatenate(
            [r.mgo[block, :, 0:GROUP], r.mgo[block, :, GROUP : 2 * GROUP]], axis=0
        )
        grad = dot_tn(r.mg[block], r.bl[c, :, side]) + dot_tn(theirs, r.bl[1 - c, :, side])
        low = grad.astype(LOW)
        home = r.oa if block < 2 else r.ob
        for piece in range(4):
            home[block % 2, piece // 2, piece % 2] = low[piece * PIECE : (piece + 1) * PIECE]
    va_stages[1]()

    lo_copy.wait_recv()

    def layer_rows(index, carried):
        rows = pl.ds(index * PIECE, PIECE)
        r.layer[rows, :] = (
            r.resid[rows, :] + r.lo[c, rows, :] + r.lor[rows, :] + local_row(7)
        ).astype(LOW)
        return carried

    lax.fori_loop(0, 4, layer_rows, 0)
    results = [pltpu.make_async_copy(r.layer, out_layer, r.out_sem.at[0])]
    results[0].start()

    run_services(PLAN["before_loop"])
    ag_all.wait_recv()
    for h in range(3):
        for slot in range(CHIPS):
            for part in range(2):
                start = slot * ROWS + part * PACK
                r.agh[h, start : start + PACK, :] = r.ag[
                    slot, :, part * GROUP + h * HEAD : part * GROUP + (h + 1) * HEAD
                ]
    ng_copy.wait_send()
    lo_copy.wait_send()
    key_sums, value_sums = r.ng, r.lo


    def pair_copies(h):
        return (send(r.dks.at[h], r.dkr.at[h], r.dk_s.at[h], r.dk_r.at[h], s, sib),)

    def dq_copy(h, block):
        return send(r.dqs.at[h, block], r.dqr.at[h, z], r.dq_s.at[h], r.dq_r.at[h],
                    s, 2 * block + c)

    def dq_all(h):
        return all_of(r.dqs.at[h, pl.ds(0, 3)], r.dq_s.at[h], r.dq_r.at[h])

    def finish_head(h):
        for item in pair_copies(h):
            item.wait_recv()
        lines = slice(h * HEAD, (h + 1) * HEAD)
        key_grad = jnp.transpose((key_sums[0, lines, :] + r.dkr[h, 0].astype(F32)).astype(LOW))
        value_grad = jnp.transpose((value_sums[0, lines, :] + r.dkr[h, 1].astype(F32)).astype(LOW))
        for part, whole in enumerate((r.q[h, :, HEAD : 2 * HEAD], key_grad, value_grad)):
            lane = h * GROUP + part * HEAD
            r.dqkv[:, lane : lane + HEAD] = whole
            for block in range(CHIPS):
                pack(r.dqs.at[h], block, part * HEAD, whole[block * ROWS : (block + 1) * ROWS])
        others(lambda block: dq_copy(h, block).start())
        r.dqr[h, z] = r.dqs[h, z]

    def backward_band(index, carried):
        h = index // 2
        part = index % 2
        rows = pl.ds(pl.multiple_of(part * BAND, BAND), BAND)
        live = jnp.where(r.qseg[rows, :][:, :HEAD] != pad_number, 1.0, 0.0).astype(F32)
        grad = r.agh[h, rows, :].astype(F32) * live
        inverse = r.att[h, rows, HEAD : 2 * HEAD]
        correct = jnp.sum(grad * r.att[h, rows, 0:HEAD], axis=-1, keepdims=True) * inverse[:, 0:1]
        correct = correct.astype(LOW).astype(F32)
        scaled = (grad * inverse).astype(LOW)
        product = dot(scaled, r.kvt[3 + h])
        weights = r.prob[h, rows, :]
        slopes = (weights.astype(F32) * (product - correct)).astype(LOW)
        r.q[h, rows, HEAD : 2 * HEAD] = (
            dot(slopes, r.kh[h]) * (1.0 / math.sqrt(HEAD))
        ).astype(LOW)
        keys = dot(jnp.transpose(r.q[h, rows, 0:HEAD]), slopes)
        values = dot(jnp.transpose(scaled), weights)

        lines = pl.ds(pl.multiple_of(h * HEAD, HEAD), HEAD)

        halves = (slice(0, OWN), slice(OWN, KEYS))

        @pl.when(part == 0)
        def _():
            for side in range(2):
                key_sums[side, lines, :] = keys[:, halves[side]]
                value_sums[side, lines, :] = values[:, halves[side]]

        @pl.when(part == 1)
        def _():
            for place, (sums, value) in enumerate(((key_sums, keys), (value_sums, values))):
                whole = jnp.concatenate([sums[0, lines, :], sums[1, lines, :]], axis=1) + value
                own, theirs = (
                    jnp.concatenate(
                        [
                            whole[:, slot * SLOT + side * ROWS : slot * SLOT + (side + 1) * ROWS]
                            for slot in range(CHIPS)
                        ],
                        axis=1,
                    )
                    for side in range(2)
                )
                sums[0, lines, :] = own
                r.dks[h, place] = theirs.astype(LOW)
            for item in pair_copies(h):
                item.start()

        for turn, listed in PLAN["loop"]:
            @pl.when(index == turn)
            def _(listed=listed):
                run_services(listed)

        for turn, head in ((2, 0), (4, 1)):
            @pl.when(index == turn)
            def _(head=head):
                finish_head(head)

        return carried

    lax.fori_loop(0, 6, backward_band, 0)

    finish_head(2)
    run_services(PLAN["after_loop"])

    grad = dot_tn(r.nrm[...].reshape(OWN, D), r.dqkv[...])
    r.dwq[...] = grad.astype(LOW).reshape(CHIPS, 4, PIECE, QKV)
    q0_copy = send(
        r.dwq.at[pl.ds(2 * (1 - c), 2)], r.dwqr, r.q0_s.at[0], r.q0_r.at[0], s, sib
    )
    q0_copy.start()
    pending.append(q0_copy)
    column_sums = jnp.sum(r.dqkv[...].astype(F32), axis=0, keepdims=True)
    r.vq[...] = jnp.zeros((8, TILE), F32)
    for lane, row in ((0, 0), (2 * HEAD, CHIPS)):
        r.vq[pl.ds(row + z, 1), 0:GROUP] = jnp.concatenate(
            [
                column_sums[:, h * GROUP + lane : h * GROUP + lane + HEAD]
                for h in range(3)
            ],
            axis=1,
        )
    vq_stages[0]()
    va_stages[2]()
    q0_copy.wait_recv()
    for part in range(2):
        for piece in range(4):
            r.dwqx[part, piece] = (
                r.dwq[2 * c + part, piece].astype(F32) + r.dwqr[part, piece].astype(F32)
            ).astype(LOW)
    qx_copies = [
        send(r.dwqx.at[:, flip[step]], r.rxq.at[step - 1], r.qx_s.at[0],
             r.qx_r.at[0], flip[step], b)
        for step in (1, 2, 3)
    ]
    for item in qx_copies:
        item.start()
    qx_all = all_of(r.rxq, r.qx_s.at[0], r.qx_r.at[0])
    pending.append(qx_all)

    run_services(PLAN["after_qkv"])
    vq_stages[1]()

    for h in range(3):
        dq_all(h).wait_recv()
        for slot in range(CHIPS):
            for part in range(3):
                lane = part * D + slot * GROUP + h * HEAD
                for side in range(2):
                    start = side * GROUP + part * HEAD
                    r.rowg[side * PACK : (side + 1) * PACK, lane : lane + HEAD] = r.dqr[
                        h, slot, :, start : start + HEAD
                    ]

    def first_grads(index, carried):
        rows = pl.ds(pl.multiple_of(index * 256, 256), 256)
        r.ngr[:, rows] = dot_nt(r.rowg[...], r.wf[rows, :])
        return carried

    lax.fori_loop(0, 3, first_grads, 0)

    def first_back(index, carried):
        rows = pl.ds(index * PIECE, PIECE)
        grad = r.ngr[rows, :]
        xhat = r.xhat1[rows, :]
        scaled = grad * local_row(3)
        mean_one = jnp.mean(scaled, axis=-1, keepdims=True)
        mean_two = jnp.mean(scaled * xhat, axis=-1, keepdims=True)
        through = r.rstd1[rows, :] * (scaled - mean_one - xhat * mean_two)
        r.tokg[rows, :] = (r.xhat2[rows, :] + through).astype(LOW)
        gains = jnp.sum(grad * xhat, axis=0, keepdims=True)
        shifts = jnp.sum(grad, axis=0, keepdims=True)
        for part in range(3):
            lanes = slice(part * TILE, (part + 1) * TILE)
            r.vb[part : part + 1, :] += gains[:, lanes]
            r.vb[4 + part : 5 + part, :] += shifts[:, lanes]
        return carried

    lax.fori_loop(0, 4, first_back, 0)
    results.append(pltpu.make_async_copy(r.tokg, out_tok, r.out_sem.at[1]))
    results[1].start()

    vb_copies = [
        send(r.vb, r.vbr.at[b], r.vb_s.at[0], r.vb_r.at[0], s, (b + step) % 8)
        for step in range(1, 8)
    ]
    r.vbr[b] = r.vb[...]
    for item in vb_copies:
        item.start()
    vb_all = all_of(r.vbr.at[pl.ds(0, 7)], r.vb_s.at[0], r.vb_r.at[0])
    pending.append(vb_all)

    run_services(PLAN["after_rows"])

    qx_all.wait_recv()
    def qz_copy(part):
        return send(r.zq.at[part], r.rzq.at[z], r.qz_s.at[part], r.qz_r.at[z],
                    s, 2 * (2 * c + part) + owner)

    for part in range(2):
        total = r.dwqx[part, s].astype(F32)
        for step in range(3):
            total = total + r.rxq[step, part].astype(F32)
        r.zq[part] = total.astype(LOW)
        there = 2 * (2 * c + part) + owner

        @pl.when(there != b)
        def _(part=part):
            qz_copy(part).start()

        @pl.when(there == b)
        def _(part=part):
            r.rzq[z] = r.zq[part]

    vq_stages[2]()
    run_services(PLAN["before_sums"])

    vb_all.wait_recv()
    total = r.vbr[0]
    for slot in range(1, 8):
        total = total + r.vbr[slot]
    r.vbx[s] = total
    vbx_copies = [
        send(r.vbx.at[s], r.vbx.at[s], r.vbx_s.at[0], r.vbx_r.at[0], flip[step], b)
        for step in (1, 2, 3)
    ]
    for item in vbx_copies:
        item.start()
    vbx_all = all_of(r.vbx.at[pl.ds(0, 3)], r.vbx_s.at[0], r.vbx_r.at[0])
    pending.append(vbx_all)

    run_services(PLAN["last"])

    finq_own = pltpu.make_async_copy(r.rzq, out_finq.at[s % 2], r.out_sem.at[2])

    def qf_copy(step):
        return send(r.rzq, out_finq.at[s % 2], r.qf_s.at[step - 1], r.qf_r.at[step - 1],
                    flip[step], b)

    def qz_arrival(slot):
        return send(r.zq.at[0], r.rzq.at[slot], r.qz_s.at[0], r.qz_r.at[slot], s, sib)

    @pl.when(owner == c)
    def _():
        for slot in range(CHIPS):
            @pl.when(jnp.logical_or(slot != z, z // 2 != c))
            def _(slot=slot):
                qz_arrival(slot).wait_recv()

        for step in (1, 2, 3):
            qf_copy(step).start()
        finq_own.start()

    for count, there in ((3, mine == b), (4, mine != b)):
        @pl.when(there)
        def _(count=count):
            for unit in range(TILES + 1):
                fin_all(unit, count).wait_recv()

    for step in (1, 2, 3):
        @pl.when(flip[step] // 2 == c)
        def _(step=step):
            qf_copy(step).wait_recv()

    vbx_all.wait_recv()
    r.vec[0] = va_stages[3]()
    r.vec[1, :, 0:TILE] = vq_stages[3]()
    r.vec[2, :, 0:TILE] = r.vbx[0] + r.vbx[1] + r.vbx[2] + r.vbx[3]
    results.append(pltpu.make_async_copy(r.vec, out_vec, r.out_sem.at[3]))
    results[2].start()

    for slot in range(CHIPS):
        kv_copy(slot).wait_send()

    @pl.when(is_end)
    def _():
        all_of(r.nrm.at[0], r.n_s.at[0], r.n_r.at[0, 0]).wait_send()

    @pl.when(jnp.logical_not(is_end))
    def _():
        all_of(r.w2.at[pl.ds(0, 5 * ROWS)], r.n_s.at[0], r.n_r.at[0, 0]).wait_send()

    for item in (mg_all, ag_all):
        item.wait_send()
    for h in range(3):
        dq_all(h).wait_send()
        for item in pair_copies(h):
            item.wait_send()
    for item in pending:
        item.wait_send()
    for item in results:
        item.wait()
    for unit in range(TILES + 1):
        if unit == TILES:
            hop_one_all(unit).wait_send()
            hop_two_all(unit).wait_send()
        else:
            all_of(r.ra.at[pl.ds(0, 3)], r.h_s.at[unit], r.h1_r.at[unit]).wait_send()
        z_sent(unit).wait_send()
        @pl.when(mine != b)
        def _(unit=unit):
            fin_all(unit, 4).wait_send()

        @pl.when(mine == b)
        def _(unit=unit):
            fin_all(unit, 3).wait_send()
            fin_own(unit).wait()

    for part in range(2):
        @pl.when(2 * (2 * c + part) + owner != b)
        def _(part=part):
            qz_copy(part).wait_send()

    @pl.when(owner == c)
    def _():
        for step in (1, 2, 3):
            qf_copy(step).wait_send()
        finq_own.wait()


def finish_scratch():
    vmem = pltpu.VMEM
    return dict(
        fin=vmem((TILES, 2, 2, 2, PIECE, TILE), LOW),
        fo=vmem((2, 2, PIECE, OUT_HALF), LOW),
        finq=vmem((2, CHIPS, PIECE, QKV), LOW),
        vec=vmem((3, 8, D), F32),
        qkv=vmem((96, 3 * D), F32),
        out=vmem((96, D), F32),
        up=vmem((96, FF), F32),
        down=vmem((96, FF), F32),
        small0=vmem((96,), F32), small1=vmem((96,), F32), small2=vmem((96,), F32),
        small3=vmem((96,), F32), small4=vmem((96,), F32), small5=vmem((96,), F32),
        small6=vmem((96,), F32), small7=vmem((96,), F32), small8=vmem((384,), F32),
        layer=vmem((ROWS, D), LOW),
        tok=vmem((ROWS, D), LOW),
        in_sem=pltpu.SemaphoreType.DMA((5 + TILES,)),
        out_sem=pltpu.SemaphoreType.DMA((15,)),
    )


def finish_body(names, tok, layer, fin, fo, finq, vec, *refs):
    outs = refs[:15]
    layer_out, tok_out, qkv_w, out_w, up_w, down_w = outs[:6]
    r = Box()
    for name, ref in zip(names, refs[15:]):
        setattr(r, name, ref)
    loads = [
        pltpu.make_async_copy(vec, r.vec, r.in_sem.at[0]),
        pltpu.make_async_copy(finq, r.finq, r.in_sem.at[1]),
        pltpu.make_async_copy(fo, r.fo, r.in_sem.at[2]),
        pltpu.make_async_copy(layer, r.layer, r.in_sem.at[3 + TILES]),
        pltpu.make_async_copy(tok, r.tok, r.in_sem.at[4 + TILES]),
    ] + [
        pltpu.make_async_copy(fin.at[tile], r.fin.at[tile], r.in_sem.at[3 + tile])
        for tile in range(TILES)
    ]
    for item in loads:
        item.start()
    stores = []

    def store(source, target):
        stores.append(pltpu.make_async_copy(source, target, r.out_sem.at[len(stores)]))
        stores[-1].start()

    loads[0].wait()
    small = [getattr(r, "small%d" % index) for index in range(9)]
    qb, v_b, ob, g1, s1, g2, s2, down_b, up_b = small
    b = lax.axis_index("blk")
    for index in range(8):
        @pl.when(b == index)
        def _(index=index):
            cols = slice(index * 96, (index + 1) * 96)
            for ref, row in ((ob, 0), (g2, 1), (s2, 2), (down_b, 3)):
                ref[...] = r.vec[0, row, cols]
            for ref, row in ((g1, 0), (s1, 4)):
                whole = jnp.concatenate(
                    [r.vec[2, row + part : row + part + 1, 0:TILE] for part in range(3)], axis=1
                )
                ref[...] = whole[0, cols]
            slot = index // 2
            half = slice((index % 2) * 96, (index % 2 + 1) * 96)
            qb[...] = r.vec[1, slot, half]
            v_b[...] = r.vec[1, CHIPS + slot, half]
            start = (index * 384) % D
            up_b[...] = r.vec[0, 4 + index * 384 // D, start : start + 384]

    for source, target in zip(small, outs[6:]):
        store(source, target)
    loads[3].wait()
    store(r.layer, layer_out)
    loads[4].wait()
    store(r.tok, tok_out)
    loads[1].wait()
    for piece in range(2):
        rows = slice(piece * PIECE, (piece + 1) * PIECE)
        for slot in range(CHIPS):
            for h in range(3):
                for part in range(3):
                    lane = part * D + slot * GROUP + h * HEAD
                    source = h * GROUP + part * HEAD
                    r.qkv[rows, lane : lane + HEAD] = r.finq[
                        piece, slot, :, source : source + HEAD
                    ].astype(F32)
    store(r.qkv, qkv_w)
    loads[2].wait()
    for piece in range(2):
        rows = slice(piece * PIECE, (piece + 1) * PIECE)
        for core in range(2):
            r.out[rows, core * OUT_HALF : (core + 1) * OUT_HALF] = r.fo[piece, core].astype(F32)
    store(r.out, out_w)
    for tile in range(TILES):
        loads[5 + tile].wait()
        for core in range(2):
            start = core * HALF + tile * TILE
            lanes = slice(start, start + TILE)
            for piece in range(2):
                rows = slice(piece * PIECE, (piece + 1) * PIECE)
                r.up[rows, lanes] = r.fin[tile, piece, core, 0].astype(F32)
                r.down[rows, lanes] = r.fin[tile, piece, core, 1].astype(F32)
            for index, (source, target) in enumerate(((r.up, up_w), (r.down, down_w))):
                part = pl.ds(start, TILE)
                pltpu.make_async_copy(
                    source.at[:, part], target.at[:, part], r.out_sem.at[13 + index]
                ).start()
    for item in stores:
        item.wait()
    pltpu.make_async_copy(r.up, up_w, r.out_sem.at[13]).wait()
    pltpu.make_async_copy(r.down, down_w, r.out_sem.at[14]).wait()


def chip_body(
    tokens, segment_ids, out_grad, query_key_value_weight, query_bias, value_bias,
    attention_output_weight, attention_output_bias, first_gain, first_shift,
    second_gain, second_shift, mlp_input_weight, mlp_input_bias, mlp_output_weight,
    mlp_output_bias,
):
    pad_number = tokens.shape[1] * lax.axis_size("blk") // SHORT_LO + 2
    names = scratch_list()
    any_space = pl.BlockSpec(memory_space=pl.ANY)
    finish_names = finish_scratch()
    results = pl.pallas_call(
        functools.partial(kernel_body, tuple(names), pad_number),
        out_shape=(
            jax.ShapeDtypeStruct((ROWS, D), LOW),
            jax.ShapeDtypeStruct((ROWS, D), LOW),
            jax.ShapeDtypeStruct((TILES, 2, 2, 2, PIECE, TILE), LOW),
            jax.ShapeDtypeStruct((2, 2, PIECE, OUT_HALF), LOW),
            jax.ShapeDtypeStruct((2, CHIPS, PIECE, QKV), LOW),
            jax.ShapeDtypeStruct((3, 8, D), F32),
        ),
        in_specs=[any_space] * 16,
        out_specs=(any_space,) * 6,
        scratch_shapes=list(names.values()),
        compiler_params=pltpu.CompilerParams(
            collective_id=0, has_side_effects=True, vmem_limit_bytes=VMEM_LIMIT
        ),
        name="encoder_block",
    )(
        tokens.reshape(ROWS, D), segment_ids, out_grad.reshape(ROWS, D),
        query_key_value_weight, attention_output_weight,
        mlp_input_weight.reshape(CHIPS, 2, 2, PIECE, FF), mlp_output_weight,
        query_bias, value_bias, attention_output_bias, first_gain, first_shift,
        second_gain, second_shift, mlp_output_bias, mlp_input_bias,
    )
    wide = [(96, 3 * D), (96, D), (96, FF), (96, FF)]
    shapes = (
        [jax.ShapeDtypeStruct((ROWS, D), LOW)] * 2
        + [jax.ShapeDtypeStruct(shape, F32) for shape in wide]
        + [jax.ShapeDtypeStruct((96,), F32)] * 8
        + [jax.ShapeDtypeStruct((384,), F32)]
    )
    (layer_out, tok_out, qkv_w, out_w, up_w, down_w, qb, vb, ob, g1, s1, g2, s2, down_b, up_b) = (
        pl.pallas_call(
            functools.partial(finish_body, tuple(finish_names)),
            out_shape=tuple(shapes),
            in_specs=[any_space] * 6,
            out_specs=(any_space,) * len(shapes),
            scratch_shapes=list(finish_names.values()),
            compiler_params=pltpu.CompilerParams(vmem_limit_bytes=VMEM_LIMIT),
            name="place_results",
        )(*results)
    )
    return (
        layer_out.reshape(tokens.shape), tok_out.reshape(tokens.shape), qkv_w, qb, vb, out_w, ob,
        g1, s1, g2, s2, up_w, up_b, jnp.transpose(down_w), down_b,
    )


def solution(mesh):
    placed = (
        P("seq", "blk", None),
        P("seq", "blk"),
        P("seq", "blk", None),
        P(),
        P(),
        P(),
        P(),
        P(),
        P(),
        P(),
        P(),
        P(),
        P(),
        P(),
        P(),
        P(),
    )
    chosen = chip_body if mesh.shape["seq"] == 4 and mesh.shape["blk"] == 8 else body
    return jax.shard_map(
        chosen,
        mesh=mesh,
        in_specs=placed,
        out_specs=(
            P("seq", "blk", None),
            P("seq", "blk", None),
            P("blk", None),
            P("blk"),
            P("blk"),
            P("blk", None),
            P("blk"),
            P("blk"),
            P("blk"),
            P("blk"),
            P("blk"),
            P("blk", None),
            P("blk"),
            P(None, "blk"),
            P("blk"),
        ),
        check_vma=False,
    )
```

```python
import functools
import math

import jax
import jax.numpy as jnp
from jax import lax
from jax.experimental import pallas as pl
from jax.experimental.pallas import tpu as pltpu
from jax.sharding import PartitionSpec as P

HEADS = 12
HEAD = 64
SHORT_LO = 25


EPS = 1e-06


def layer_norm(inputs, norm_gain, norm_shift):
    centre = inputs - jnp.mean(inputs, axis=-1, keepdims=True)
    spread = jnp.mean(centre * centre, axis=-1, keepdims=True)
    return centre * lax.rsqrt(spread + EPS) * norm_gain + norm_shift


def gelu_exact(inputs):
    return jax.nn.gelu(inputs, approximate=False)


def score_block(queries, query_segs, key_rows, key_segs):
    raw_scores = jnp.einsum("qhd,khd->hqk", queries, key_rows, preferred_element_type=jnp.float32)
    same_image = (query_segs[:, None] == key_segs[None, :])[None]
    return jnp.where(same_image, jnp.exp(raw_scores * (1.0 / math.sqrt(HEAD))), 0.0)


def forward_step(carried, queries, query_segs, key_rows, value_rows, key_segs):
    totals, summed = carried
    weights = score_block(queries, query_segs, key_rows, key_segs)
    totals = totals + jnp.transpose(jnp.sum(weights, axis=-1))
    summed = summed + jnp.einsum(
        "hqk,khd->qhd", weights.astype(jnp.bfloat16), value_rows, preferred_element_type=jnp.float32
    )
    return (totals, summed)


def back_step(queries, query_grads, query_corr, query_segs, key_rows, value_rows, key_segs):
    weights = score_block(queries, query_segs, key_rows, key_segs)
    product = jnp.einsum(
        "qhd,khd->hqk", query_grads, value_rows, preferred_element_type=jnp.float32
    )
    shifted = jnp.transpose(query_corr.astype(jnp.float32))[:, :, None]
    score_grads = (weights * (product - shifted) * (1.0 / math.sqrt(HEAD))).astype(jnp.bfloat16)
    return (weights.astype(jnp.bfloat16), score_grads)


def key_value_grads(queries, query_grads, query_corr, query_segs, key_rows, value_rows, key_segs):
    weights_low, score_grads = back_step(
        queries, query_grads, query_corr, query_segs, key_rows, value_rows, key_segs
    )
    key_part = jnp.einsum("hqk,qhd->khd", score_grads, queries, preferred_element_type=jnp.float32)
    value_part = jnp.einsum(
        "hqk,qhd->khd", weights_low, query_grads, preferred_element_type=jnp.float32
    )
    return (key_part, value_part)


def body(
    tokens,
    segment_ids,
    out_grad,
    query_key_value_weight,
    query_bias,
    value_bias,
    attention_output_weight,
    attention_output_bias,
    first_gain,
    first_shift,
    second_gain,
    second_shift,
    mlp_input_weight,
    mlp_input_bias,
    mlp_output_weight,
    mlp_output_bias,
):
    model_width = tokens.shape[-1]
    row_count = tokens.shape[0] * tokens.shape[1]
    head_shape = (row_count, HEADS, HEAD)
    pad_number = tokens.shape[1] * lax.axis_size("blk") // SHORT_LO + 2
    token_rows = tokens.reshape(row_count, model_width).astype(jnp.float32)
    seg_rows = segment_ids.reshape(row_count)
    live_rows = (seg_rows != pad_number).astype(jnp.float32)
    first_normed, first_back = jax.vjp(
        layer_norm, token_rows, first_gain.astype(jnp.float32), first_shift.astype(jnp.float32)
    )
    first_low = first_normed.astype(jnp.bfloat16)
    query_key_value_bias = jnp.concatenate(
        [
            query_bias.astype(jnp.float32),
            jnp.zeros((model_width,), jnp.float32),
            value_bias.astype(jnp.float32),
        ]
    )
    projected_rows = (
        jnp.dot(first_low, query_key_value_weight, preferred_element_type=jnp.float32)
        + query_key_value_bias
    )
    query_flat = projected_rows[:, :model_width].astype(jnp.bfloat16)
    key_flat = projected_rows[:, model_width : 2 * model_width].astype(jnp.bfloat16)
    value_flat = projected_rows[:, 2 * model_width :].astype(jnp.bfloat16)
    queries = query_flat.reshape(head_shape)
    gathered = (
        lax.all_gather(key_flat, "blk", axis=0, tiled=True),
        lax.all_gather(value_flat, "blk", axis=0, tiled=True),
        lax.all_gather(seg_rows, "blk", axis=0, tiled=True),
    )
    all_keys = gathered[0].reshape(-1, HEADS, HEAD)
    all_values = gathered[1].reshape(-1, HEADS, HEAD)
    all_segs = gathered[2]
    seq_rows = all_keys.shape[0]
    key_span = math.gcd(seq_rows, 2048)
    turns = seq_rows // key_span

    def forward_turn(index, carried):
        begin_row = index * key_span
        return forward_step(
            carried,
            queries,
            seg_rows,
            lax.dynamic_slice_in_dim(all_keys, begin_row, key_span, 0),
            lax.dynamic_slice_in_dim(all_values, begin_row, key_span, 0),
            lax.dynamic_slice_in_dim(all_segs, begin_row, key_span, 0),
        )

    totals, summed = lax.fori_loop(
        0,
        turns,
        forward_turn,
        (jnp.zeros((row_count, HEADS), jnp.float32), jnp.zeros(head_shape, jnp.float32)),
    )
    attended = summed / totals[:, :, None] * live_rows[:, None, None]
    merged_heads = attended.reshape(row_count, model_width).astype(jnp.bfloat16)
    residual = (
        token_rows
        + jnp.dot(merged_heads, attention_output_weight, preferred_element_type=jnp.float32)
        + attention_output_bias.astype(jnp.float32)
    )
    second_normed, second_back = jax.vjp(
        layer_norm, residual, second_gain.astype(jnp.float32), second_shift.astype(jnp.float32)
    )
    second_low = second_normed.astype(jnp.bfloat16)
    hidden_rows = jnp.dot(
        second_low, mlp_input_weight, preferred_element_type=jnp.float32
    ) + mlp_input_bias.astype(jnp.float32)
    gelu_active, gelu_back = jax.vjp(gelu_exact, hidden_rows)
    active_low = gelu_active.astype(jnp.bfloat16)
    layer_rows = (
        residual
        + jnp.dot(active_low, mlp_output_weight, preferred_element_type=jnp.float32)
        + mlp_output_bias.astype(jnp.float32)
    )
    layer_out = layer_rows.astype(jnp.bfloat16).reshape(tokens.shape)
    grad_rows = out_grad.reshape(row_count, model_width)
    down_weight_grad = jnp.einsum(
        "tf,td->fd", active_low, grad_rows, preferred_element_type=jnp.float32
    )
    down_bias_grad = jnp.sum(grad_rows.astype(jnp.float32), axis=0)
    active_grad = jnp.einsum(
        "td,fd->tf", grad_rows, mlp_output_weight, preferred_element_type=jnp.float32
    )
    (hidden_grad,) = gelu_back(active_grad)
    hidden_low = hidden_grad.astype(jnp.bfloat16)
    up_weight_grad = jnp.einsum(
        "td,tf->df", second_low, hidden_low, preferred_element_type=jnp.float32
    )
    up_bias_grad = jnp.sum(hidden_low.astype(jnp.float32), axis=0)
    normed_grad = jnp.einsum(
        "tf,df->td", hidden_low, mlp_input_weight, preferred_element_type=jnp.float32
    )
    resid_part, second_gain_grad, second_shift_grad = second_back(normed_grad)
    residual_grad = grad_rows.astype(jnp.float32) + resid_part
    branch_low = residual_grad.astype(jnp.bfloat16)
    out_weight_grad = jnp.einsum(
        "ti,to->io", merged_heads, branch_low, preferred_element_type=jnp.float32
    )
    out_bias_grad = jnp.sum(branch_low.astype(jnp.float32), axis=0)
    attended_grad = (
        jnp.einsum(
            "to,io->ti", branch_low, attention_output_weight, preferred_element_type=jnp.float32
        ).reshape(head_shape)
        * live_rows[:, None, None]
    )
    query_grads = (attended_grad / totals[:, :, None]).astype(jnp.bfloat16)
    corrections = (jnp.sum(attended_grad * attended, axis=-1) / totals).astype(jnp.bfloat16)

    def query_turn(index, carried):
        begin_row = index * key_span
        key_rows = lax.dynamic_slice_in_dim(all_keys, begin_row, key_span, 0)
        weights_low, score_grads = back_step(
            queries,
            query_grads,
            corrections,
            seg_rows,
            key_rows,
            lax.dynamic_slice_in_dim(all_values, begin_row, key_span, 0),
            lax.dynamic_slice_in_dim(all_segs, begin_row, key_span, 0),
        )
        return carried + jnp.einsum(
            "hqk,khd->qhd", score_grads, key_rows, preferred_element_type=jnp.float32
        )

    query_sum = lax.fori_loop(0, turns, query_turn, jnp.zeros(head_shape, jnp.float32))
    term_span = math.gcd(row_count * lax.axis_size("blk"), 2048)

    def term_block(index):
        begin_row = index * term_span
        key_part, value_part = key_value_grads(
            queries,
            query_grads,
            corrections,
            seg_rows,
            lax.dynamic_slice_in_dim(all_keys, begin_row, term_span, 0),
            lax.dynamic_slice_in_dim(all_values, begin_row, term_span, 0),
            lax.dynamic_slice_in_dim(all_segs, begin_row, term_span, 0),
        )
        return jnp.concatenate(
            [key_part.reshape(term_span, model_width), value_part.reshape(term_span, model_width)],
            axis=1,
        )

    blocks = lax.map(
        term_block, jnp.arange(row_count * lax.axis_size("blk") // term_span, dtype=jnp.int32)
    )
    key_terms = lax.psum_scatter(
        blocks.reshape(row_count * lax.axis_size("blk"), 2 * model_width),
        "blk",
        scatter_dimension=0,
        tiled=True,
    )
    query_low = query_sum.reshape(row_count, model_width).astype(jnp.bfloat16)
    key_low = key_terms[:, :model_width].astype(jnp.bfloat16)
    value_low = key_terms[:, model_width:].astype(jnp.bfloat16)
    qkv_grad = jnp.concatenate([query_low, key_low, value_low], axis=1)
    qkv_weight_grad = jnp.einsum(
        "td,tj->dj", first_low, qkv_grad, preferred_element_type=jnp.float32
    )
    query_bias_grad = jnp.sum(query_low.astype(jnp.float32), axis=0)
    value_bias_grad = jnp.sum(value_low.astype(jnp.float32), axis=0)
    first_grad = jnp.einsum(
        "tj,dj->td", qkv_grad, query_key_value_weight, preferred_element_type=jnp.float32
    )
    token_part, first_gain_grad, first_shift_grad = first_back(first_grad)
    tokens_grad = (residual_grad + token_part).astype(jnp.bfloat16).reshape(tokens.shape)
    local_grads = (
        qkv_weight_grad,
        query_bias_grad,
        value_bias_grad,
        out_weight_grad,
        out_bias_grad,
        first_gain_grad,
        first_shift_grad,
        second_gain_grad,
        second_shift_grad,
        up_weight_grad,
        up_bias_grad,
        down_weight_grad,
        down_bias_grad,
    )
    scattered = (
        lax.psum_scatter(local_grads[0], "blk", scatter_dimension=0, tiled=True),
        lax.psum_scatter(local_grads[1], "blk", scatter_dimension=0, tiled=True),
        lax.psum_scatter(local_grads[2], "blk", scatter_dimension=0, tiled=True),
        lax.psum_scatter(local_grads[3], "blk", scatter_dimension=0, tiled=True),
        lax.psum_scatter(local_grads[4], "blk", scatter_dimension=0, tiled=True),
        lax.psum_scatter(local_grads[5], "blk", scatter_dimension=0, tiled=True),
        lax.psum_scatter(local_grads[6], "blk", scatter_dimension=0, tiled=True),
        lax.psum_scatter(local_grads[7], "blk", scatter_dimension=0, tiled=True),
        lax.psum_scatter(local_grads[8], "blk", scatter_dimension=0, tiled=True),
        lax.psum_scatter(local_grads[9], "blk", scatter_dimension=0, tiled=True),
        lax.psum_scatter(local_grads[10], "blk", scatter_dimension=0, tiled=True),
        lax.psum_scatter(local_grads[11], "blk", scatter_dimension=1, tiled=True),
        lax.psum_scatter(local_grads[12], "blk", scatter_dimension=0, tiled=True),
    )
    summed_grads = lax.psum(
        (
            scattered[0],
            scattered[1],
            scattered[2],
            scattered[3],
            scattered[4],
            scattered[5],
            scattered[6],
            scattered[7],
            scattered[8],
            scattered[9],
            scattered[10],
            scattered[11],
            scattered[12],
        ),
        "seq",
    )
    return (layer_out, tokens_grad) + tuple(summed_grads)


VMEM_LIMIT = 64 * 1024 * 1024
D = 768
FF = 3072
ROWS = 192
CHIPS = 4
GROUP = 192
QKV = 3 * GROUP
HALF = FF // 2
OUT_HALF = D // 2
PIECE = 48
TILE = 256
TILES = HALF // TILE
PACK = ROWS // 2
SLOT = 2 * ROWS
KEYS = 1536
OWN = 768
LOW = jnp.bfloat16
F32 = jnp.float32
MESH = pl.DeviceIdType.MESH


def dot(a, b):
    return jnp.dot(a, b, preferred_element_type=F32)


def dot_nt(a, b):
    return lax.dot_general(a, b, (((1,), (1,)), ((), ())), preferred_element_type=F32)


def dot_tn(a, b):
    return lax.dot_general(a, b, (((0,), (0,)), ((), ())), preferred_element_type=F32)


def scratch_list():
    dma = pltpu.SemaphoreType.DMA
    vmem = pltpu.VMEM
    return dict(
        tok=vmem((ROWS, D), LOW),
        seg=vmem((1, ROWS), jnp.int32),
        vec0=vmem((D,), LOW), vec1=vmem((D,), LOW), vec2=vmem((D,), LOW), vec3=vmem((D,), LOW),
        vec4=vmem((D,), LOW), vec5=vmem((D,), LOW), vec6=vmem((D,), LOW), vec7=vmem((D,), LOW),
        vec8=vmem((FF,), LOW),
        layer=vmem((ROWS, D), LOW),
        tokg=vmem((ROWS, D), LOW),
        vec=vmem((3, 8, D), F32),
        in_sem=dma((12,)), out_sem=dma((5,)), own_sem=dma((TILES + 1,)),
        nrm=vmem((CHIPS, ROWS, D), LOW),
        xhat1=vmem((ROWS, D), F32),
        rstd1=vmem((ROWS, 1), F32),
        par=vmem((8, D), F32),
        qvb=vmem((2, CHIPS, GROUP), F32),
        b1=vmem((1, FF), F32),
        wf=vmem((D, 3 * D), LOW),
        wo=vmem((D, D), LOW),
        w2=vmem((HALF, D), LOW),
        q=vmem((3, OWN, 2 * HEAD), LOW),
        kvo=vmem((CHIPS, ROWS, 2 * GROUP), LOW),
        kvs=vmem((CHIPS, ROWS, 2 * GROUP), LOW),
        kh=vmem((3, KEYS, HEAD), LOW),
        vh=vmem((3, KEYS, 2 * HEAD), LOW),
        kvt=vmem((6, HEAD, KEYS), LOW),
        segs=vmem((8, 8, ROWS), jnp.int32),
        kseg=vmem((1, KEYS), jnp.int32),
        qseg=vmem((OWN, 128), jnp.int32),
        prob=vmem((3, OWN, KEYS), LOW),
        att=vmem((3, OWN, 2 * HEAD), F32),
        mgs=vmem((CHIPS, PACK, 2 * GROUP), LOW),
        mgr=vmem((CHIPS, PACK, 2 * GROUP), LOW),
        mgo=vmem((CHIPS, PACK, 2 * GROUP), LOW),
        mg=vmem((CHIPS, ROWS, GROUP), LOW),
        og=vmem((2, ROWS, D), LOW),
        nt=vmem((2, ROWS, D), LOW),
        bl=vmem((2, ROWS, D), LOW),
        resid=vmem((ROWS, D), F32),
        xhat2=vmem((ROWS, D), F32),
        rstd2=vmem((ROWS, 1), F32),
        act=vmem((2 * ROWS, HALF), LOW),
        hg=vmem((2 * ROWS, HALF), LOW),
        lo=vmem((2, ROWS, D), F32),
        ng=vmem((2, ROWS, D), F32),
        lor=vmem((ROWS, D), F32),
        ngr=vmem((ROWS, D), F32),
        ags=vmem((CHIPS, PACK, 2 * GROUP), LOW),
        ag=vmem((CHIPS, PACK, 2 * GROUP), LOW),
        agh=vmem((3, OWN, HEAD), LOW),
        dqs=vmem((3, CHIPS, PACK, 2 * GROUP), LOW),
        dqr=vmem((3, CHIPS, PACK, 2 * GROUP), LOW),
        rowg=vmem((ROWS, 3 * D), LOW),
        dkr=vmem((3, 2, HEAD, OWN), LOW),
        dks=vmem((3, 2, HEAD, OWN), LOW),
        dqkv=vmem((OWN, QKV), LOW),
        da=vmem((TILES, CHIPS, 2, 2, PIECE, TILE), LOW),
        db=vmem((TILES, CHIPS, 2, 2, PIECE, TILE), LOW),
        ra=vmem((TILES, CHIPS, 2, PIECE, TILE), LOW),
        rb=vmem((TILES, CHIPS, 2, PIECE, TILE), LOW),
        a2s=vmem((TILES, CHIPS, PIECE, TILE), LOW),
        b2s=vmem((TILES, CHIPS, PIECE, TILE), LOW),
        a2r=vmem((TILES, CHIPS, PIECE, TILE), LOW),
        b2r=vmem((TILES, CHIPS, PIECE, TILE), LOW),
        zs=vmem((TILES, CHIPS, 2, PIECE, TILE), LOW),
        rz=vmem((TILES, CHIPS, 2, PIECE, TILE), LOW),
        zm=vmem((TILES, 2, 2, PIECE, TILE), LOW),
        fin=vmem((TILES, 2, PIECE, TILE), LOW),
        oa=vmem((2, 2, 2, PIECE, OUT_HALF), LOW),
        ob=vmem((2, 2, 2, PIECE, OUT_HALF), LOW),
        roa=vmem((2, 2, PIECE, OUT_HALF), LOW),
        rob=vmem((2, 2, PIECE, OUT_HALF), LOW),
        oa2s=vmem((2, PIECE, OUT_HALF), LOW),
        ob2s=vmem((2, PIECE, OUT_HALF), LOW),
        oa2r=vmem((2, PIECE, OUT_HALF), LOW),
        ob2r=vmem((2, PIECE, OUT_HALF), LOW),
        zo=vmem((CHIPS, PIECE, OUT_HALF), LOW),
        rzo=vmem((CHIPS, PIECE, OUT_HALF), LOW),
        zmo=vmem((2, PIECE, OUT_HALF), LOW),
        fo=vmem((PIECE, OUT_HALF), LOW),
        dwq=vmem((CHIPS, 4, PIECE, QKV), LOW),
        dwqr=vmem((2, 4, PIECE, QKV), LOW),
        dwqx=vmem((2, 4, PIECE, QKV), LOW),
        rxq=vmem((3, 2, PIECE, QKV), LOW),
        zq=vmem((2, PIECE, QKV), LOW),
        rzq=vmem((CHIPS, PIECE, QKV), LOW),
        va=vmem((8, D), F32),
        vh1=vmem((1, HALF), F32),
        vap=vmem((8, D), F32),
        vaz=vmem((CHIPS, 8, D), F32),
        vax=vmem((4, 8, D), F32),
        vq=vmem((8, TILE), F32),
        vqp=vmem((8, TILE), F32),
        vqz=vmem((CHIPS, 8, TILE), F32),
        vqx=vmem((4, 8, TILE), F32),
        vb=vmem((8, TILE), F32),
        vbr=vmem((8, 8, TILE), F32),
        vbx=vmem((4, 8, TILE), F32),
        load_sem=dma((3 + TILES,)),
        seg_s=dma((1,)), seg_r=dma((1,)),
        og_s=dma((1,)), og_r=dma((1,)),
        n_s=dma((1,)), n_r=dma((CHIPS, 2)),
        kv_s=dma((CHIPS,)), kv_r=dma((CHIPS,)),
        mg_s=dma((1,)), mg_r=dma((1,)),
        mgo_s=dma((1,)), mgo_r=dma((1,)),
        nt_s=dma((1,)), nt_r=dma((1,)),
        lo_s=dma((1,)), lo_r=dma((1,)),
        ng_s=dma((1,)), ng_r=dma((1,)),
        bl_s=dma((1,)), bl_r=dma((1,)),
        ag_s=dma((1,)), ag_r=dma((1,)),
        dk_s=dma((3,)), dk_r=dma((3,)),
        dq_s=dma((3,)), dq_r=dma((3,)),
        h_s=dma((TILES + 2,)), h1_r=dma((TILES + 1,)), h2_r=dma((TILES + 1,)),
        z_s=dma((TILES + 1,)), z_r=dma((TILES + 1, 2)),
        f_s=dma((TILES + 1,)), f_r=dma((TILES + 1,)),
        q0_s=dma((1,)), q0_r=dma((1,)),
        qx_s=dma((1,)), qx_r=dma((1,)),
        qz_s=dma((2,)), qz_r=dma((CHIPS,)),
        qf_s=dma((3,)), qf_r=dma((3,)),
        va_s=dma((3,)), va_r=dma((3,)),
        vq_s=dma((3,)), vq_r=dma((3,)),
        vb_s=dma((1,)), vb_r=dma((1,)),
        vbx_s=dma((1,)), vbx_r=dma((1,)),
    )


EARLY = 2
STARTED = 2
PLAN = dict(
    before_norm=((1, 0), (0, 2)),
    after_norm=(),
    middle=((1, 1), (0, 3)),
    before_loop=((2, 0),),
    loop=(
        (0, ((1, 2), (0, 4), (2, 1))),
        (1, ((3, 0),)),
        (2, ((1, 3), (0, 5))),
        (3, ((2, 2), (3, 1))),
        (5, ((1, 4), (0, 6))),
    ),
    after_loop=((2, 3), (4, 0), (1, 5), (3, 2)),
    after_qkv=((1, 6), (2, 4), (4, 1)),
    after_rows=((4, 2), (2, 5), (3, 3), (2, 6), (3, 4)),
    before_sums=((4, 3), (3, 5)),
    last=((4, 4), (3, 6), (4, 5), (4, 6)),
)


class Box:
    pass


def kernel_body(names, pad_number, *refs):
    (tok_h, seg_h, og_h, wqkv, wo_h, w1_h, w2_h) = refs[:7]
    (out_tok, out_layer, out_fin, out_fo, out_finq, out_vec) = refs[16:22]
    r = Box()
    for name, ref in zip(names, refs[22:]):
        setattr(r, name, ref)
    par, qvb, b1 = r.par, r.qvb, r.b1
    tok = r.tok

    s = lax.axis_index("seq")
    b = lax.axis_index("blk")
    z = b // 2
    c = b % 2
    sib = 2 * z + 1 - c
    flip = {1: s + 1 - 2 * (s % 2), 2: (s + 2) % 4, 3: 3 - s}
    x = s % 2
    y = s // 2
    is_end = jnp.logical_or(z == 0, z == 3)

    pending = []

    def send(src, dst, ssem, rsem, dev_s, dev_b):
        return pltpu.make_async_remote_copy(
            src_ref=src, dst_ref=dst, send_sem=ssem, recv_sem=rsem,
            device_id=(dev_s, dev_b), device_id_type=MESH,
        )

    def all_of(ref, ssem, rsem):
        return send(ref, ref, ssem, rsem, s, sib)

    def local_row(index):
        return par[index : index + 1, :]

    barrier = pltpu.get_barrier_semaphore()
    for step in range(1, 8):
        pl.semaphore_signal(barrier, inc=1, device_id=(s, (b + step) % 8), device_id_type=MESH)
    for step in (1, 2, 3):
        for core in range(2):
            pl.semaphore_signal(
                barrier, inc=1, device_id=(flip[step], 2 * z + core), device_id_type=MESH
            )

    vectors = [getattr(r, "vec%d" % index) for index in range(9)]
    first_loads = [
        pltpu.make_async_copy(source, target, r.in_sem.at[index])
        for index, (source, target) in enumerate(
            [(tok_h, r.tok), (seg_h, r.seg), (og_h, r.og.at[c])]
            + list(zip(refs[7:16], vectors))
        )
    ]
    for item in first_loads:
        item.start()

    loads = []
    loads.append(pltpu.make_async_copy(wqkv, r.wf, r.load_sem.at[0]))
    half = pl.multiple_of(c * HALF, 128)
    loads.append(pltpu.make_async_copy(wo_h, r.wo, r.load_sem.at[1]))
    loads.append(pltpu.make_async_copy(w2_h.at[pl.ds(half, HALF), :], r.w2, r.load_sem.at[2]))
    for tile in range(TILES):
        cols = pl.ds(pl.multiple_of(c * HALF + tile * TILE, TILE), TILE)
        loads.append(
            pltpu.make_async_copy(
                w1_h.at[:, :, :, :, cols], r.da.at[tile], r.load_sem.at[3 + tile]
            )
        )
    for item in loads:
        item.start()

    for item in first_loads:
        item.wait()
    for index, vector in enumerate(vectors[:8]):
        par[index : index + 1, :] = vector[...].astype(F32).reshape(1, D)
    for slot in range(CHIPS):
        part = slice(slot * GROUP, (slot + 1) * GROUP)
        qvb[0, slot : slot + 1, :] = par[0:1, part]
        qvb[1, slot : slot + 1, :] = par[1:2, part]
    b1[...] = vectors[8][...].astype(F32).reshape(1, FF)

    def first_norm(index, carried):
        rows = pl.ds(index * PIECE, PIECE)
        x = tok[rows, :].astype(F32)
        centre = x - jnp.mean(x, axis=-1, keepdims=True)
        spread = lax.rsqrt(jnp.mean(centre * centre, axis=-1, keepdims=True) + EPS)
        xhat = centre * spread
        r.xhat1[rows, :] = xhat
        r.rstd1[rows, :] = spread
        r.nrm[z, rows, :] = (xhat * local_row(3) + local_row(4)).astype(LOW)
        return carried

    lax.fori_loop(0, 4, first_norm, 0)

    pl.semaphore_wait(barrier, 13)

    def norm_copy(slot, side, up):
        part = r.nrm.at[slot, pl.ds(side * PACK, PACK)]
        return send(part, part, r.n_s.at[0], r.n_r.at[slot, side], s, b + 2 if up else b - 2)

    def norm_forward(slot, side):
        @pl.when(jnp.logical_and(slot <= z, z < 3))
        def _():
            norm_copy(slot, side, True).start()

        @pl.when(jnp.logical_and(slot >= z, z > 0))
        def _():
            norm_copy(slot, side, False).start()

    norm_forward(z, 0)
    norm_forward(z, 1)

    r.segs[CHIPS * c + z] = jnp.broadcast_to(r.seg[...], (8, ROWS))
    seg_copies = []
    for step in range(1, 8):
        seg_copies.append(
            send(r.segs.at[CHIPS * c + z], r.segs.at[CHIPS * c + z], r.seg_s.at[0], r.seg_r.at[0],
                 s, (b + step) % 8)
        )
    for item in seg_copies:
        item.start()
    seg_all = all_of(r.segs.at[pl.ds(0, 7)], r.seg_s.at[0], r.seg_r.at[0])
    pending.append(seg_all)


    og_copy = send(r.og.at[c], r.og.at[c], r.og_s.at[0], r.og_r.at[0], s, sib)
    og_copy.start()
    pending.append(og_copy)

    loads[0].wait()
    for part in range(3):
        start = pl.multiple_of(D * part + 384 * (z // 2) + 128 * (z % 2), 128)
        window = r.wf[:, pl.ds(start, 256)]
        r.dqkv[:, part * GROUP : (part + 1) * GROUP] = jnp.where(
            z % 2 == 1, window[:, 64:256], window[:, 0:192]
        )

    upper = z // 2
    qkv_bias = [qvb[0, pl.ds(z, 1), :], None, qvb[1, pl.ds(z, 1), :]]

    def split_keys(pair, row):
        for h in range(3):
            r.kh[h, pl.ds(row, ROWS), :] = pair[:, h * HEAD : (h + 1) * HEAD]
            r.vh[h, pl.ds(row, ROWS), 0:HEAD] = pair[:, GROUP + h * HEAD : GROUP + (h + 1) * HEAD]

    def kv_copy(slot):
        return send(r.kvo.at[slot], r.kvs.at[slot], r.kv_s.at[slot], r.kv_r.at[slot], s, sib)

    def project(slot):
        rows = r.nrm[slot]
        whole = dot(rows, r.dqkv[...])
        qs = (whole[:, :GROUP] + qkv_bias[0]).astype(LOW) * (1.0 / math.sqrt(HEAD))
        ks = whole[:, GROUP : 2 * GROUP].astype(LOW)
        vs = (whole[:, 2 * GROUP :] + qkv_bias[2]).astype(LOW)
        for h in range(3):
            r.q[h, pl.ds(slot * ROWS, ROWS), 0:HEAD] = qs[:, h * HEAD : (h + 1) * HEAD]
        r.kvo[slot, :, 0:GROUP] = ks
        r.kvo[slot, :, GROUP : 2 * GROUP] = vs
        kv_copy(slot).start()
        split_keys(r.kvo[slot], slot * SLOT)

    r.vh[:, :, HEAD : 2 * HEAD] = jnp.ones((3, KEYS, HEAD), LOW)
    project(z)

    def arrivals(distance, carried):
        for side in range(2):
            for slot, there in ((z - distance, z >= distance), (z + distance, z + distance < CHIPS)):
                @pl.when(there)
                def _(slot=slot, side=side):
                    norm_copy(slot, side, True).wait_recv()
                    norm_forward(slot, side)

        for slot, there in ((z - distance, z >= distance), (z + distance, z + distance < CHIPS)):
            @pl.when(there)
            def _(slot=slot):
                project(slot)

        return carried

    arrivals(1, 0)

    seg_all.wait_recv()
    for slot in range(CHIPS):
        for side, core in ((0, c), (1, 1 - c)):
            start = slot * SLOT + side * ROWS
            r.kseg[:, start : start + ROWS] = r.segs[CHIPS * core + slot, 0:1, :]
        line = r.segs[CHIPS * c + slot, 0:1, :].astype(F32)
        r.qseg[slot * ROWS : (slot + 1) * ROWS, :] = jnp.transpose(
            jnp.broadcast_to(line, (128, ROWS))
        ).astype(jnp.int32)

    loads[2].wait()
    og_copy.wait_recv()

    def active_grads(index, carried):
        cols = pl.ds(pl.multiple_of(index * 512, 512), 512)
        r.hg[:, cols] = dot_nt(r.og[...].reshape(2 * ROWS, D), r.w2[cols, :]).astype(LOW)
        return carried

    lax.fori_loop(0, HALF // 512, active_grads, 0)

    for slot, there in ((z - 2, z >= 2), (z + 2, z + 2 < CHIPS)):
        for side in range(2):
            @pl.when(there)
            def _(slot=slot, side=side):
                norm_copy(slot, side, True).wait_recv()
                norm_forward(slot, side)

        @pl.when(there)
        def _(slot=slot):
            project(slot)

    def take_sibling(slot, carried):
        kv_copy(slot).wait_recv()
        split_keys(r.kvs[slot], slot * SLOT + ROWS)
        both = jnp.concatenate([r.kvo[slot], r.kvs[slot]], axis=0)
        span = pl.ds(pl.multiple_of(slot * SLOT, 128), SLOT)
        r.kvt[:, :, span] = jnp.transpose(both).reshape(6, HEAD, SLOT)
        return carried

    lax.fori_loop(upper, upper + 3, take_sibling, 0)

    BAND = 2 * ROWS
    last = 3 * (1 - upper)

    def pack(ref, index, lane, value):
        width = value.shape[1]
        ref[index, :, lane : lane + width] = value[0:PACK]
        ref[index, :, GROUP + lane : GROUP + lane + width] = value[PACK:ROWS]

    def mg_copy(block):
        return send(r.mgs.at[block], r.mgr.at[z], r.mg_s.at[0], r.mg_r.at[0], s, 2 * block + c)

    mg_all = all_of(r.mgs.at[pl.ds(0, 3)], r.mg_s.at[0], r.mg_r.at[0])

    def weigh(h, rows, count, lanes, width):
        own_segs = r.qseg[rows, :]
        wide = jnp.concatenate([own_segs] * (width // 128), axis=1)
        raw = dot(r.q[h, rows, 0:HEAD], r.kvt[h, :, lanes])
        weights = jnp.where(wide == r.kseg[:, lanes], jnp.exp(raw), 0.0).astype(LOW)
        r.prob[h, rows, lanes] = weights
        return dot(weights, r.vh[h, lanes, :])

    def settle(h, rows, total):
        live = jnp.where(r.qseg[rows, :][:, :HEAD] != pad_number, 1.0, 0.0).astype(F32)
        inverse = 1.0 / total[:, HEAD:]
        r.att[h, rows, 0:HEAD] = total[:, :HEAD] * inverse * live
        r.att[h, rows, HEAD : 2 * HEAD] = inverse

    old_rows = pl.ds(pl.multiple_of(upper * ROWS, ROWS), 3 * ROWS)
    old_lanes = pl.ds(pl.multiple_of(upper * SLOT, 128), 3 * SLOT)
    last_rows = pl.ds(pl.multiple_of(last * ROWS, ROWS), ROWS)
    last_lanes = pl.ds(pl.multiple_of(last * SLOT, 128), SLOT)

    def forward_old(h, carried):
        r.att[h, old_rows, :] = weigh(h, old_rows, 3 * ROWS, old_lanes, 3 * SLOT)
        return carried

    lax.fori_loop(0, 3, forward_old, 0)

    @pl.when(is_end)
    def _():
        for side in range(2):
            norm_copy(last, side, True).wait_recv()
        project(last)

    take_sibling(last, 0)

    def give(block):
        block_rows = pl.ds(pl.multiple_of(block * ROWS, ROWS), ROWS)
        for head in range(3):
            pack(r.mgs, block, head * HEAD, r.att[head, block_rows, 0:HEAD].astype(LOW))

        @pl.when(block != z)
        def _():
            mg_copy(block).start()

        @pl.when(block == z)
        def _():
            r.mgr[z] = r.mgs[z]

    def forward_last(h, carried):
        settle(h, last_rows, weigh(h, last_rows, ROWS, slice(0, KEYS), KEYS))
        return carried

    lax.fori_loop(0, 3, forward_last, 0)
    give(last)

    def forward_rest(h, carried):
        settle(
            h, old_rows, r.att[h, old_rows, :] + weigh(h, old_rows, 3 * ROWS, last_lanes, SLOT)
        )
        return carried

    lax.fori_loop(0, 3, forward_rest, 0)

    for index in range(3):
        give(2 - index + upper * (2 * index - 1))

    def others(fn):
        def run(index, carried):
            fn((z + 1 + index) % CHIPS)
            return carried

        lax.fori_loop(0, CHIPS - 1, run, 0)

    mg_all.wait_recv()
    mgo_copy = send(r.mgr, r.mgo, r.mgo_s.at[0], r.mgo_r.at[0], s, sib)
    mgo_copy.start()
    pending.append(mgo_copy)

    for slot in range(CHIPS):
        r.mg[slot, 0:PACK, :] = r.mgr[slot, :, 0:GROUP]
        r.mg[slot, PACK:ROWS, :] = r.mgr[slot, :, GROUP : 2 * GROUP]

    loads[1].wait()

    def out_projection(index, carried):
        cols = pl.ds(pl.multiple_of(index * 256, 256), 256)
        total = tok[:, cols].astype(F32) + par[2:3, cols]
        for slot in range(CHIPS):
            total = total + dot(r.mg[slot], r.wo[slot * GROUP : (slot + 1) * GROUP, cols])
        r.resid[:, cols] = total
        return carried

    lax.fori_loop(0, 3, out_projection, 0)

    def second_norm(index, carried):
        rows = pl.ds(index * PIECE, PIECE)
        x = r.resid[rows, :]
        centre = x - jnp.mean(x, axis=-1, keepdims=True)
        spread = lax.rsqrt(jnp.mean(centre * centre, axis=-1, keepdims=True) + EPS)
        xhat = centre * spread
        r.xhat2[rows, :] = xhat
        r.rstd2[rows, :] = spread
        r.nt[c, rows, :] = (xhat * local_row(5) + local_row(6)).astype(LOW)
        return carried

    lax.fori_loop(0, 4, second_norm, 0)
    nt_copy = send(r.nt.at[c], r.nt.at[c], r.nt_s.at[0], r.nt_r.at[0], s, sib)
    nt_copy.start()
    pending.append(nt_copy)
    for item in loads[3:]:
        item.wait()
    r.va[...] = jnp.zeros((8, D), F32)
    r.vb[...] = jnp.zeros((8, TILE), F32)
    r.va[3:4, :] = jnp.sum(r.og[c].astype(F32), axis=0, keepdims=True)
    nt_copy.wait_recv()

    def hop_one(unit):
        if isinstance(unit, int) and unit == TILES:
            one, two, to_one, to_two = r.oa, r.ob, r.roa, r.rob
        else:
            one, two, to_one, to_two = r.da.at[unit], r.db.at[unit], r.ra.at[unit], r.rb.at[unit]
        return (
            send(one.at[:, :, 1 - x], to_one, r.h_s.at[unit], r.h1_r.at[unit], flip[1], b),
            send(two.at[:, 1 - y], to_two, r.h_s.at[unit], r.h1_r.at[unit], flip[2], b),
        )

    def hop_two(unit):
        later = TILES + 1 if isinstance(unit, int) and unit == TILES else unit
        if isinstance(unit, int) and unit == TILES:
            one, two, to_one, to_two = r.oa2s, r.ob2s, r.oa2r, r.ob2r
        else:
            one, two, to_one, to_two = (
                r.a2s.at[unit], r.b2s.at[unit], r.a2r.at[unit], r.b2r.at[unit]
            )
        return (
            send(one, to_one, r.h_s.at[later], r.h2_r.at[unit], flip[2], b),
            send(two, to_two, r.h_s.at[later], r.h2_r.at[unit], flip[1], b),
        )

    def hop_one_all(unit):
        last_unit = isinstance(unit, int) and unit == TILES
        return all_of(r.oa if last_unit else r.da.at[unit], r.h_s.at[unit], r.h1_r.at[unit])

    def hop_two_all(unit):
        last_unit = isinstance(unit, int) and unit == TILES
        return all_of(r.roa if last_unit else r.ra.at[unit], r.h_s.at[TILES + 1], r.h2_r.at[unit])

    partner = z + 1 - 2 * (z % 2)
    inner = 3 - z
    outer = 3 - partner
    low_block = 1 - upper
    inner_of_end = 3 - partner

    def z_refs(unit):
        if isinstance(unit, int) and unit == TILES:
            return r.zo, r.rzo, r.zmo
        return r.zs.at[unit], r.rz.at[unit], r.zm.at[unit]

    def z_bundle(unit):
        here, there, _ = z_refs(unit)
        three = pl.ds(low_block, 3)
        return send(here.at[three], there.at[three], r.z_s.at[unit], r.z_r.at[unit, 0],
                    s, 2 * partner + c)

    def z_near(unit):
        here, there, _ = z_refs(unit)
        return send(here.at[partner], there.at[z], r.z_s.at[unit], r.z_r.at[unit, 0],
                    s, 2 * partner + c)

    def z_inner(unit):
        _, there, merged = z_refs(unit)
        return send(merged.at[0], there.at[outer], r.z_s.at[unit], r.z_r.at[unit, 1],
                    s, 2 * inner + c)

    def z_outer(unit):
        _, there, merged = z_refs(unit)
        return send(merged.at[1], there.at[z], r.z_s.at[unit], r.z_r.at[unit, 1],
                    s, 2 * outer + c)

    def z_three_arrival(unit):
        here, there, _ = z_refs(unit)
        three = pl.ds(low_block, 3)
        return send(here.at[three], there.at[three], r.z_s.at[unit], r.z_r.at[unit, 0],
                    s, 2 * partner + c)

    def z_arrival(unit, level):
        here, _, _ = z_refs(unit)
        return all_of(here.at[0], r.z_s.at[unit], r.z_r.at[unit, level])

    def z_sent(unit):
        here, _, _ = z_refs(unit)
        return all_of(here.at[pl.ds(0, 3)], r.z_s.at[unit], r.z_r.at[unit, 0])

    owner = s // 2
    mine = 2 * z + owner

    def fin_copy(unit, step):
        if isinstance(unit, int) and unit == TILES:
            here, there = r.fo, out_fo.at[s % 2, c]
        else:
            here, there = r.fin.at[unit], out_fin.at[unit, s % 2, c]
        return send(here, there, r.f_s.at[unit], r.f_r.at[unit],
                    s if step == 0 else flip[step], mine)

    def fin_own(unit):
        if isinstance(unit, int) and unit == TILES:
            here, there = r.fo, out_fo.at[s % 2, c]
        else:
            here, there = r.fin.at[unit], out_fin.at[unit, s % 2, c]
        return pltpu.make_async_copy(here, there, r.own_sem.at[unit])

    def fin_all(unit, count):
        whole = r.zo if unit == TILES else r.zs.at[unit]
        return all_of(whole.at[pl.ds(0, count)], r.f_s.at[unit], r.f_r.at[unit])

    def mlp_grads(tile):
        cols = pl.ds(pl.multiple_of(tile * TILE, TILE), TILE)

        r.da[tile] = dot_tn(r.nt[...].reshape(2 * ROWS, D), r.hg[:, cols]).astype(LOW).reshape(
            CHIPS, 2, 2, PIECE, TILE
        )
        r.db[tile] = dot_tn(r.og[...].reshape(2 * ROWS, D), r.act[:, cols]).astype(LOW).reshape(
            CHIPS, 2, 2, PIECE, TILE
        )

    def service_zero(unit):
        for item in hop_one(unit):
            item.start()

    def service_one(unit):
        hop_one_all(unit).wait_recv()
        if isinstance(unit, int) and unit == TILES:
            for block in range(2):
                r.oa2s[block] = (
                    r.oa[block, 1 - y, x].astype(F32) + r.roa[block, 1 - y].astype(F32)
                ).astype(LOW)
                r.ob2s[block] = (
                    r.ob[block, y, 1 - x].astype(F32) + r.rob[block, 1 - x].astype(F32)
                ).astype(LOW)
        else:
            def add(block, carried):
                r.a2s[unit, block] = (
                    r.da[unit, block, 1 - y, x].astype(F32) + r.ra[unit, block, 1 - y].astype(F32)
                ).astype(LOW)
                r.b2s[unit, block] = (
                    r.db[unit, block, y, 1 - x].astype(F32) + r.rb[unit, block, 1 - x].astype(F32)
                ).astype(LOW)
                return carried

            lax.fori_loop(0, CHIPS, add, 0)
        for item in hop_two(unit):
            item.start()

    def service_two(unit):
        hop_two_all(unit).wait_recv()
        if isinstance(unit, int) and unit == TILES:
            for block in range(2):
                r.zo[block] = (
                    r.oa[block, y, x].astype(F32) + r.roa[block, y].astype(F32)
                    + r.oa2r[block].astype(F32)
                ).astype(LOW)
                r.zo[2 + block] = (
                    r.ob[block, y, x].astype(F32) + r.rob[block, x].astype(F32)
                    + r.ob2r[block].astype(F32)
                ).astype(LOW)
        else:
            def add(block, carried):
                r.zs[unit, block, 0] = (
                    r.da[unit, block, y, x].astype(F32) + r.ra[unit, block, y].astype(F32)
                    + r.a2r[unit, block].astype(F32)
                ).astype(LOW)
                r.zs[unit, block, 1] = (
                    r.db[unit, block, y, x].astype(F32) + r.rb[unit, block, x].astype(F32)
                    + r.b2r[unit, block].astype(F32)
                ).astype(LOW)
                return carried

            lax.fori_loop(0, CHIPS, add, 0)
        @pl.when(is_end)
        def _():
            z_bundle(unit).start()

        @pl.when(jnp.logical_not(is_end))
        def _():
            z_near(unit).start()

    def service_three(unit):
        here, there, merged = z_refs(unit)

        @pl.when(jnp.logical_not(is_end))
        def _():
            z_three_arrival(unit).wait_recv()
            merged[0] = (here[inner].astype(F32) + there[inner].astype(F32)).astype(LOW)
            merged[1] = (here[outer].astype(F32) + there[outer].astype(F32)).astype(LOW)
            z_inner(unit).start()
            z_outer(unit).start()

    def service_four(unit):
        here, there, _ = z_refs(unit)
        z_arrival(unit, 1).wait_recv()

        @pl.when(is_end)
        def _():
            z_arrival(unit, 0).wait_recv()

        second = jnp.where(is_end, inner_of_end, z)
        total = here[z].astype(F32) + there[partner].astype(F32) + there[second].astype(F32)
        if isinstance(unit, int) and unit == TILES:
            r.fo[...] = total.astype(LOW)
        else:
            r.fin[unit] = total.astype(LOW)
        for step in (1, 2, 3):
            fin_copy(unit, step).start()

        @pl.when(mine != b)
        def _():
            fin_copy(unit, 0).start()

        @pl.when(mine == b)
        def _():
            fin_own(unit).start()

    def run_services(listed):
        for kind, unit in listed:
            (service_zero, service_one, service_two, service_three, service_four)[kind](unit)


    r.ng[...] = jnp.zeros((2, ROWS, D), F32)

    WIDE = 2 * TILE

    def mlp_tile(index, carried):
        cols = pl.ds(pl.multiple_of(index * WIDE, WIDE), WIDE)
        bias = b1[:, pl.ds(pl.multiple_of(c * HALF + index * WIDE, WIDE), WIDE)]
        w1 = jnp.concatenate(
            [r.da[2 * index + part].reshape(D, TILE) for part in range(2)], axis=1
        )
        hidden = dot(r.nt[...].reshape(2 * ROWS, D), w1) + bias
        gate = 0.5 * (1.0 + lax.erf(hidden * (1.0 / math.sqrt(2.0))))
        slope = gate + hidden * jnp.exp(-0.5 * hidden * hidden) * (1.0 / math.sqrt(2.0 * math.pi))
        active = (hidden * gate).astype(LOW)
        grad = (slope * r.hg[:, cols].astype(F32)).astype(LOW)
        r.act[:, cols] = active
        r.hg[:, cols] = grad
        r.vh1[:, cols] = jnp.sum(grad.astype(F32), axis=0, keepdims=True)
        r.ng[...] += dot_nt(grad, w1).reshape(2, ROWS, D)
        for part in range(2):
            tile = 2 * index + part

            @pl.when(tile < EARLY)
            def _(tile=tile):
                mlp_grads(tile)

            @pl.when(tile < STARTED)
            def _(tile=tile):
                service_zero(tile)

        return carried

    lax.fori_loop(0, TILES // 2, mlp_tile, 0)
    for part in range(2):
        r.va[pl.ds(4 + 2 * c + part, 1), :] = r.vh1[:, part * D : (part + 1) * D]
    ng_copy = send(r.ng.at[1 - c], r.ngr, r.ng_s.at[0], r.ng_r.at[0], s, sib)
    ng_copy.start()

    mlp_grads(2)
    run_services(PLAN["before_norm"])

    ng_copy.wait_recv()

    def second_back(index, carried):
        rows = pl.ds(index * PIECE, PIECE)
        grad = r.ng[c, rows, :] + r.ngr[rows, :]
        xhat = r.xhat2[rows, :]
        scaled = grad * local_row(5)
        mean_one = jnp.mean(scaled, axis=-1, keepdims=True)
        mean_two = jnp.mean(scaled * xhat, axis=-1, keepdims=True)
        through = r.rstd2[rows, :] * (scaled - mean_one - xhat * mean_two)
        resid_grad = r.og[c, rows, :].astype(F32) + through
        low = resid_grad.astype(LOW)
        r.xhat2[rows, :] = resid_grad
        r.bl[c, rows, :] = low
        r.va[0:1, :] += jnp.sum(low.astype(F32), axis=0, keepdims=True)
        r.va[1:2, :] += jnp.sum(grad * xhat, axis=0, keepdims=True)
        r.va[2:3, :] += jnp.sum(grad, axis=0, keepdims=True)
        return carried

    lax.fori_loop(0, 4, second_back, 0)
    bl_copy = send(r.bl.at[c], r.bl.at[c], r.bl_s.at[0], r.bl_r.at[0], s, sib)
    bl_copy.start()
    pending.append(bl_copy)

    def ag_copy(block):
        return send(r.ags.at[block], r.ag.at[z], r.ag_s.at[0], r.ag_r.at[0], s, 2 * block + c)

    ag_all = all_of(r.ags.at[pl.ds(0, 3)], r.ag_s.at[0], r.ag_r.at[0])

    def attended_block(index, carried):
        block = (z + 1 + index) % CHIPS
        wide = pl.ds(pl.multiple_of(block * GROUP, GROUP), GROUP)
        pack(r.ags, block, 0, dot_nt(r.bl[c], r.wo[wide, :]).astype(LOW))

        @pl.when(block != z)
        def _():
            ag_copy(block).start()

        @pl.when(block == z)
        def _():
            r.ag[z] = r.ags[z]

        return carried

    lax.fori_loop(0, CHIPS, attended_block, 0)

    def vector_sums(mine_ref, pair_ref, z_ref, x_ref, send_sems, recv_sems):
        def pair():
            return send(mine_ref, pair_ref, send_sems.at[0], recv_sems.at[0], s, sib)

        def along(step):
            return send(z_ref.at[z], z_ref.at[z], send_sems.at[1], recv_sems.at[1],
                        s, (b + 2 * step) % 8)

        def over(step):
            return send(x_ref.at[s], x_ref.at[s], send_sems.at[2], recv_sems.at[2],
                        flip[step], b)

        along_all = all_of(z_ref.at[pl.ds(0, 3)], send_sems.at[1], recv_sems.at[1])
        over_all = all_of(x_ref.at[pl.ds(0, 3)], send_sems.at[2], recv_sems.at[2])

        def stage_one():
            pair().start()
            pending.append(pair())

        def stage_two():
            pair().wait_recv()
            r_first = jnp.where(c == 0, mine_ref[...], pair_ref[...])
            r_second = jnp.where(c == 0, pair_ref[...], mine_ref[...])
            z_ref[z] = r_first + r_second
            for step in (1, 2, 3):
                along(step).start()
            pending.append(along_all)

        def stage_three():
            along_all.wait_recv()
            x_ref[s] = z_ref[0] + z_ref[1] + z_ref[2] + z_ref[3]
            for step in (1, 2, 3):
                over(step).start()
            pending.append(over_all)

        def stage_four():
            over_all.wait_recv()
            return x_ref[0] + x_ref[1] + x_ref[2] + x_ref[3]

        return stage_one, stage_two, stage_three, stage_four

    va_stages = vector_sums(r.va, r.vap, r.vaz, r.vax, r.va_s, r.va_r)
    vq_stages = vector_sums(r.vq, r.vqp, r.vqz, r.vqx, r.vq_s, r.vq_r)
    va_stages[0]()

    run_services(PLAN["after_norm"])
    mlp_grads(3)
    run_services(PLAN["middle"])
    mlp_grads(4)
    mlp_grads(5)
    mgo_copy.wait_recv()
    bl_copy.wait_recv()
    side = pl.ds(pl.multiple_of(c * OUT_HALF, OUT_HALF), OUT_HALF)
    for block in range(CHIPS):
        theirs = jnp.concatenate(
            [r.mgo[block, :, 0:GROUP], r.mgo[block, :, GROUP : 2 * GROUP]], axis=0
        )
        grad = dot_tn(r.mg[block], r.bl[c, :, side]) + dot_tn(theirs, r.bl[1 - c, :, side])
        low = grad.astype(LOW)
        home = r.oa if block < 2 else r.ob
        for piece in range(4):
            home[block % 2, piece // 2, piece % 2] = low[piece * PIECE : (piece + 1) * PIECE]
    va_stages[1]()

    def layer_sums(index, carried):
        cols = pl.ds(pl.multiple_of(index * 256, 256), 256)
        r.lo[:, :, cols] = dot(r.act[...], r.w2[:, cols]).reshape(2, ROWS, 256)
        return carried

    lax.fori_loop(0, D // 256, layer_sums, 0)
    lo_copy = send(r.lo.at[1 - c], r.lor, r.lo_s.at[0], r.lo_r.at[0], s, sib)
    lo_copy.start()
    run_services(PLAN["before_loop"])
    lo_copy.wait_recv()

    def layer_rows(index, carried):
        rows = pl.ds(index * PIECE, PIECE)
        r.layer[rows, :] = (
            r.resid[rows, :] + r.lo[c, rows, :] + r.lor[rows, :] + local_row(7)
        ).astype(LOW)
        return carried

    lax.fori_loop(0, 4, layer_rows, 0)
    results = [pltpu.make_async_copy(r.layer, out_layer, r.out_sem.at[0])]
    results[0].start()

    ag_all.wait_recv()
    for h in range(3):
        for slot in range(CHIPS):
            for part in range(2):
                start = slot * ROWS + part * PACK
                r.agh[h, start : start + PACK, :] = r.ag[
                    slot, :, part * GROUP + h * HEAD : part * GROUP + (h + 1) * HEAD
                ]
    ng_copy.wait_send()
    lo_copy.wait_send()
    key_sums, value_sums = r.ng, r.lo


    def pair_copies(h):
        return (send(r.dks.at[h], r.dkr.at[h], r.dk_s.at[h], r.dk_r.at[h], s, sib),)

    def dq_copy(h, block):
        return send(r.dqs.at[h, block], r.dqr.at[h, z], r.dq_s.at[h], r.dq_r.at[h],
                    s, 2 * block + c)

    def dq_all(h):
        return all_of(r.dqs.at[h, pl.ds(0, 3)], r.dq_s.at[h], r.dq_r.at[h])

    def finish_head(h):
        for item in pair_copies(h):
            item.wait_recv()
        lines = slice(h * HEAD, (h + 1) * HEAD)
        key_grad = jnp.transpose((key_sums[0, lines, :] + r.dkr[h, 0].astype(F32)).astype(LOW))
        value_grad = jnp.transpose((value_sums[0, lines, :] + r.dkr[h, 1].astype(F32)).astype(LOW))
        for part, whole in enumerate((r.q[h, :, HEAD : 2 * HEAD], key_grad, value_grad)):
            lane = h * GROUP + part * HEAD
            r.dqkv[:, lane : lane + HEAD] = whole
            for block in range(CHIPS):
                pack(r.dqs.at[h], block, part * HEAD, whole[block * ROWS : (block + 1) * ROWS])
        others(lambda block: dq_copy(h, block).start())
        r.dqr[h, z] = r.dqs[h, z]

    def backward_band(index, carried):
        h = index // 2
        part = index % 2
        rows = pl.ds(pl.multiple_of(part * BAND, BAND), BAND)
        live = jnp.where(r.qseg[rows, :][:, :HEAD] != pad_number, 1.0, 0.0).astype(F32)
        grad = r.agh[h, rows, :].astype(F32) * live
        inverse = r.att[h, rows, HEAD : 2 * HEAD]
        correct = jnp.sum(grad * r.att[h, rows, 0:HEAD], axis=-1, keepdims=True) * inverse[:, 0:1]
        correct = correct.astype(LOW).astype(F32)
        scaled = (grad * inverse).astype(LOW)
        product = dot(scaled, r.kvt[3 + h])
        weights = r.prob[h, rows, :]
        slopes = (weights.astype(F32) * (product - correct)).astype(LOW)
        r.q[h, rows, HEAD : 2 * HEAD] = (
            dot(slopes, r.kh[h]) * (1.0 / math.sqrt(HEAD))
        ).astype(LOW)
        keys = dot(jnp.transpose(r.q[h, rows, 0:HEAD]), slopes)
        values = dot(jnp.transpose(scaled), weights)

        lines = pl.ds(pl.multiple_of(h * HEAD, HEAD), HEAD)

        halves = (slice(0, OWN), slice(OWN, KEYS))

        @pl.when(part == 0)
        def _():
            for side in range(2):
                key_sums[side, lines, :] = keys[:, halves[side]]
                value_sums[side, lines, :] = values[:, halves[side]]

        @pl.when(part == 1)
        def _():
            for place, (sums, value) in enumerate(((key_sums, keys), (value_sums, values))):
                whole = jnp.concatenate([sums[0, lines, :], sums[1, lines, :]], axis=1) + value
                own, theirs = (
                    jnp.concatenate(
                        [
                            whole[:, slot * SLOT + side * ROWS : slot * SLOT + (side + 1) * ROWS]
                            for slot in range(CHIPS)
                        ],
                        axis=1,
                    )
                    for side in range(2)
                )
                sums[0, lines, :] = own
                r.dks[h, place] = theirs.astype(LOW)
            for item in pair_copies(h):
                item.start()

        for turn, listed in PLAN["loop"]:
            @pl.when(index == turn)
            def _(listed=listed):
                run_services(listed)

        for turn, head in ((2, 0), (4, 1)):
            @pl.when(index == turn)
            def _(head=head):
                finish_head(head)

        return carried

    lax.fori_loop(0, 6, backward_band, 0)

    finish_head(2)
    run_services(PLAN["after_loop"])

    grad = dot_tn(r.nrm[...].reshape(OWN, D), r.dqkv[...])
    r.dwq[...] = grad.astype(LOW).reshape(CHIPS, 4, PIECE, QKV)
    q0_copy = send(
        r.dwq.at[pl.ds(2 * (1 - c), 2)], r.dwqr, r.q0_s.at[0], r.q0_r.at[0], s, sib
    )
    q0_copy.start()
    pending.append(q0_copy)
    column_sums = jnp.sum(r.dqkv[...].astype(F32), axis=0, keepdims=True)
    r.vq[...] = jnp.zeros((8, TILE), F32)
    for lane, row in ((0, 0), (2 * HEAD, CHIPS)):
        r.vq[pl.ds(row + z, 1), 0:GROUP] = jnp.concatenate(
            [
                column_sums[:, h * GROUP + lane : h * GROUP + lane + HEAD]
                for h in range(3)
            ],
            axis=1,
        )
    vq_stages[0]()
    va_stages[2]()
    q0_copy.wait_recv()
    for part in range(2):
        for piece in range(4):
            r.dwqx[part, piece] = (
                r.dwq[2 * c + part, piece].astype(F32) + r.dwqr[part, piece].astype(F32)
            ).astype(LOW)
    qx_copies = [
        send(r.dwqx.at[:, flip[step]], r.rxq.at[step - 1], r.qx_s.at[0],
             r.qx_r.at[0], flip[step], b)
        for step in (1, 2, 3)
    ]
    for item in qx_copies:
        item.start()
    qx_all = all_of(r.rxq, r.qx_s.at[0], r.qx_r.at[0])
    pending.append(qx_all)

    run_services(PLAN["after_qkv"])
    vq_stages[1]()

    for h in range(3):
        dq_all(h).wait_recv()
        for slot in range(CHIPS):
            for part in range(3):
                lane = part * D + slot * GROUP + h * HEAD
                for side in range(2):
                    start = side * GROUP + part * HEAD
                    r.rowg[side * PACK : (side + 1) * PACK, lane : lane + HEAD] = r.dqr[
                        h, slot, :, start : start + HEAD
                    ]

    def first_grads(index, carried):
        rows = pl.ds(pl.multiple_of(index * 256, 256), 256)
        r.ngr[:, rows] = dot_nt(r.rowg[...], r.wf[rows, :])
        return carried

    lax.fori_loop(0, 3, first_grads, 0)

    def first_back(index, carried):
        rows = pl.ds(index * PIECE, PIECE)
        grad = r.ngr[rows, :]
        xhat = r.xhat1[rows, :]
        scaled = grad * local_row(3)
        mean_one = jnp.mean(scaled, axis=-1, keepdims=True)
        mean_two = jnp.mean(scaled * xhat, axis=-1, keepdims=True)
        through = r.rstd1[rows, :] * (scaled - mean_one - xhat * mean_two)
        r.tokg[rows, :] = (r.xhat2[rows, :] + through).astype(LOW)
        gains = jnp.sum(grad * xhat, axis=0, keepdims=True)
        shifts = jnp.sum(grad, axis=0, keepdims=True)
        for part in range(3):
            lanes = slice(part * TILE, (part + 1) * TILE)
            r.vb[part : part + 1, :] += gains[:, lanes]
            r.vb[4 + part : 5 + part, :] += shifts[:, lanes]
        return carried

    lax.fori_loop(0, 4, first_back, 0)
    results.append(pltpu.make_async_copy(r.tokg, out_tok, r.out_sem.at[1]))
    results[1].start()

    vb_copies = [
        send(r.vb, r.vbr.at[b], r.vb_s.at[0], r.vb_r.at[0], s, (b + step) % 8)
        for step in range(1, 8)
    ]
    r.vbr[b] = r.vb[...]
    for item in vb_copies:
        item.start()
    vb_all = all_of(r.vbr.at[pl.ds(0, 7)], r.vb_s.at[0], r.vb_r.at[0])
    pending.append(vb_all)

    run_services(PLAN["after_rows"])

    qx_all.wait_recv()
    def qz_copy(part):
        return send(r.zq.at[part], r.rzq.at[z], r.qz_s.at[part], r.qz_r.at[z],
                    s, 2 * (2 * c + part) + owner)

    for part in range(2):
        total = r.dwqx[part, s].astype(F32)
        for step in range(3):
            total = total + r.rxq[step, part].astype(F32)
        r.zq[part] = total.astype(LOW)
        there = 2 * (2 * c + part) + owner

        @pl.when(there != b)
        def _(part=part):
            qz_copy(part).start()

        @pl.when(there == b)
        def _(part=part):
            r.rzq[z] = r.zq[part]

    vq_stages[2]()
    run_services(PLAN["before_sums"])

    vb_all.wait_recv()
    total = r.vbr[0]
    for slot in range(1, 8):
        total = total + r.vbr[slot]
    r.vbx[s] = total
    vbx_copies = [
        send(r.vbx.at[s], r.vbx.at[s], r.vbx_s.at[0], r.vbx_r.at[0], flip[step], b)
        for step in (1, 2, 3)
    ]
    for item in vbx_copies:
        item.start()
    vbx_all = all_of(r.vbx.at[pl.ds(0, 3)], r.vbx_s.at[0], r.vbx_r.at[0])
    pending.append(vbx_all)

    run_services(PLAN["last"])

    finq_own = pltpu.make_async_copy(r.rzq, out_finq.at[s % 2], r.out_sem.at[2])

    def qf_copy(step):
        return send(r.rzq, out_finq.at[s % 2], r.qf_s.at[step - 1], r.qf_r.at[step - 1],
                    flip[step], b)

    def qz_arrival(slot):
        return send(r.zq.at[0], r.rzq.at[slot], r.qz_s.at[0], r.qz_r.at[slot], s, sib)

    @pl.when(owner == c)
    def _():
        for slot in range(CHIPS):
            @pl.when(jnp.logical_or(slot != z, z // 2 != c))
            def _(slot=slot):
                qz_arrival(slot).wait_recv()

        for step in (1, 2, 3):
            qf_copy(step).start()
        finq_own.start()

    for count, there in ((3, mine == b), (4, mine != b)):
        @pl.when(there)
        def _(count=count):
            for unit in range(TILES + 1):
                fin_all(unit, count).wait_recv()

    for step in (1, 2, 3):
        @pl.when(flip[step] // 2 == c)
        def _(step=step):
            qf_copy(step).wait_recv()

    vbx_all.wait_recv()
    r.vec[0] = va_stages[3]()
    r.vec[1, :, 0:TILE] = vq_stages[3]()
    r.vec[2, :, 0:TILE] = r.vbx[0] + r.vbx[1] + r.vbx[2] + r.vbx[3]
    results.append(pltpu.make_async_copy(r.vec, out_vec, r.out_sem.at[3]))
    results[2].start()

    for slot in range(CHIPS):
        kv_copy(slot).wait_send()

    @pl.when(is_end)
    def _():
        all_of(r.nrm.at[0], r.n_s.at[0], r.n_r.at[0, 0]).wait_send()

    @pl.when(jnp.logical_not(is_end))
    def _():
        all_of(r.w2.at[pl.ds(0, 5 * ROWS)], r.n_s.at[0], r.n_r.at[0, 0]).wait_send()

    for item in (mg_all, ag_all):
        item.wait_send()
    for h in range(3):
        dq_all(h).wait_send()
        for item in pair_copies(h):
            item.wait_send()
    for item in pending:
        item.wait_send()
    for item in results:
        item.wait()
    for unit in range(TILES + 1):
        if unit == TILES:
            hop_one_all(unit).wait_send()
            hop_two_all(unit).wait_send()
        else:
            all_of(r.ra.at[pl.ds(0, 3)], r.h_s.at[unit], r.h1_r.at[unit]).wait_send()
        z_sent(unit).wait_send()
        @pl.when(mine != b)
        def _(unit=unit):
            fin_all(unit, 4).wait_send()

        @pl.when(mine == b)
        def _(unit=unit):
            fin_all(unit, 3).wait_send()
            fin_own(unit).wait()

    for part in range(2):
        @pl.when(2 * (2 * c + part) + owner != b)
        def _(part=part):
            qz_copy(part).wait_send()

    @pl.when(owner == c)
    def _():
        for step in (1, 2, 3):
            qf_copy(step).wait_send()
        finq_own.wait()


def finish_scratch():
    vmem = pltpu.VMEM
    return dict(
        fin=vmem((TILES, 2, 2, 2, PIECE, TILE), LOW),
        fo=vmem((2, 2, PIECE, OUT_HALF), LOW),
        finq=vmem((2, CHIPS, PIECE, QKV), LOW),
        vec=vmem((3, 8, D), F32),
        qkv=vmem((96, 3 * D), F32),
        out=vmem((96, D), F32),
        up=vmem((96, FF), F32),
        down=vmem((96, FF), F32),
        small0=vmem((96,), F32), small1=vmem((96,), F32), small2=vmem((96,), F32),
        small3=vmem((96,), F32), small4=vmem((96,), F32), small5=vmem((96,), F32),
        small6=vmem((96,), F32), small7=vmem((96,), F32), small8=vmem((384,), F32),
        layer=vmem((ROWS, D), LOW),
        tok=vmem((ROWS, D), LOW),
        in_sem=pltpu.SemaphoreType.DMA((5 + TILES,)),
        out_sem=pltpu.SemaphoreType.DMA((15,)),
    )


def finish_body(names, tok, layer, fin, fo, finq, vec, *refs):
    outs = refs[:15]
    layer_out, tok_out, qkv_w, out_w, up_w, down_w = outs[:6]
    r = Box()
    for name, ref in zip(names, refs[15:]):
        setattr(r, name, ref)
    loads = [
        pltpu.make_async_copy(vec, r.vec, r.in_sem.at[0]),
        pltpu.make_async_copy(finq, r.finq, r.in_sem.at[1]),
        pltpu.make_async_copy(fo, r.fo, r.in_sem.at[2]),
        pltpu.make_async_copy(layer, r.layer, r.in_sem.at[3 + TILES]),
        pltpu.make_async_copy(tok, r.tok, r.in_sem.at[4 + TILES]),
    ] + [
        pltpu.make_async_copy(fin.at[tile], r.fin.at[tile], r.in_sem.at[3 + tile])
        for tile in range(TILES)
    ]
    for item in loads:
        item.start()
    stores = []

    def store(source, target):
        stores.append(pltpu.make_async_copy(source, target, r.out_sem.at[len(stores)]))
        stores[-1].start()

    for tile in range(TILES):
        loads[5 + tile].wait()
        for core in range(2):
            start = core * HALF + tile * TILE
            lanes = slice(start, start + TILE)
            for piece in range(2):
                rows = slice(piece * PIECE, (piece + 1) * PIECE)
                r.up[rows, lanes] = r.fin[tile, piece, core, 0].astype(F32)
                r.down[rows, lanes] = r.fin[tile, piece, core, 1].astype(F32)
            for index, (source, target) in enumerate(((r.up, up_w), (r.down, down_w))):
                part = pl.ds(start, TILE)
                pltpu.make_async_copy(
                    source.at[:, part], target.at[:, part], r.out_sem.at[13 + index]
                ).start()
    loads[3].wait()
    store(r.layer, layer_out)
    loads[4].wait()
    store(r.tok, tok_out)
    loads[1].wait()
    for piece in range(2):
        rows = slice(piece * PIECE, (piece + 1) * PIECE)
        for slot in range(CHIPS):
            for h in range(3):
                for part in range(3):
                    lane = part * D + slot * GROUP + h * HEAD
                    source = h * GROUP + part * HEAD
                    r.qkv[rows, lane : lane + HEAD] = r.finq[
                        piece, slot, :, source : source + HEAD
                    ].astype(F32)
    store(r.qkv, qkv_w)
    loads[2].wait()
    for piece in range(2):
        rows = slice(piece * PIECE, (piece + 1) * PIECE)
        for core in range(2):
            r.out[rows, core * OUT_HALF : (core + 1) * OUT_HALF] = r.fo[piece, core].astype(F32)
    store(r.out, out_w)
    loads[0].wait()
    small = [getattr(r, "small%d" % index) for index in range(9)]
    qb, v_b, ob, g1, s1, g2, s2, down_b, up_b = small
    b = lax.axis_index("blk")
    for index in range(8):
        @pl.when(b == index)
        def _(index=index):
            cols = slice(index * 96, (index + 1) * 96)
            for ref, row in ((ob, 0), (g2, 1), (s2, 2), (down_b, 3)):
                ref[...] = r.vec[0, row, cols]
            for ref, row in ((g1, 0), (s1, 4)):
                whole = jnp.concatenate(
                    [r.vec[2, row + part : row + part + 1, 0:TILE] for part in range(3)], axis=1
                )
                ref[...] = whole[0, cols]
            slot = index // 2
            half = slice((index % 2) * 96, (index % 2 + 1) * 96)
            qb[...] = r.vec[1, slot, half]
            v_b[...] = r.vec[1, CHIPS + slot, half]
            start = (index * 384) % D
            up_b[...] = r.vec[0, 4 + index * 384 // D, start : start + 384]

    for source, target in zip(small, outs[6:]):
        store(source, target)
    for item in stores:
        item.wait()
    pltpu.make_async_copy(r.up, up_w, r.out_sem.at[13]).wait()
    pltpu.make_async_copy(r.down, down_w, r.out_sem.at[14]).wait()


def chip_body(
    tokens, segment_ids, out_grad, query_key_value_weight, query_bias, value_bias,
    attention_output_weight, attention_output_bias, first_gain, first_shift,
    second_gain, second_shift, mlp_input_weight, mlp_input_bias, mlp_output_weight,
    mlp_output_bias,
):
    pad_number = tokens.shape[1] * lax.axis_size("blk") // SHORT_LO + 2
    names = scratch_list()
    any_space = pl.BlockSpec(memory_space=pl.ANY)
    finish_names = finish_scratch()
    results = pl.pallas_call(
        functools.partial(kernel_body, tuple(names), pad_number),
        out_shape=(
            jax.ShapeDtypeStruct((ROWS, D), LOW),
            jax.ShapeDtypeStruct((ROWS, D), LOW),
            jax.ShapeDtypeStruct((TILES, 2, 2, 2, PIECE, TILE), LOW),
            jax.ShapeDtypeStruct((2, 2, PIECE, OUT_HALF), LOW),
            jax.ShapeDtypeStruct((2, CHIPS, PIECE, QKV), LOW),
            jax.ShapeDtypeStruct((3, 8, D), F32),
        ),
        in_specs=[any_space] * 16,
        out_specs=(any_space,) * 6,
        scratch_shapes=list(names.values()),
        compiler_params=pltpu.CompilerParams(
            collective_id=0, has_side_effects=True, vmem_limit_bytes=VMEM_LIMIT
        ),
        name="encoder_block",
    )(
        tokens.reshape(ROWS, D), segment_ids, out_grad.reshape(ROWS, D),
        query_key_value_weight, attention_output_weight,
        mlp_input_weight.reshape(CHIPS, 2, 2, PIECE, FF), mlp_output_weight,
        query_bias, value_bias, attention_output_bias, first_gain, first_shift,
        second_gain, second_shift, mlp_output_bias, mlp_input_bias,
    )
    wide = [(96, 3 * D), (96, D), (96, FF), (96, FF)]
    shapes = (
        [jax.ShapeDtypeStruct((ROWS, D), LOW)] * 2
        + [jax.ShapeDtypeStruct(shape, F32) for shape in wide]
        + [jax.ShapeDtypeStruct((96,), F32)] * 8
        + [jax.ShapeDtypeStruct((384,), F32)]
    )
    (layer_out, tok_out, qkv_w, out_w, up_w, down_w, qb, vb, ob, g1, s1, g2, s2, down_b, up_b) = (
        pl.pallas_call(
            functools.partial(finish_body, tuple(finish_names)),
            out_shape=tuple(shapes),
            in_specs=[any_space] * 6,
            out_specs=(any_space,) * len(shapes),
            scratch_shapes=list(finish_names.values()),
            compiler_params=pltpu.CompilerParams(vmem_limit_bytes=VMEM_LIMIT),
            name="place_results",
        )(*results)
    )
    return (
        layer_out.reshape(tokens.shape), tok_out.reshape(tokens.shape), qkv_w, qb, vb, out_w, ob,
        g1, s1, g2, s2, up_w, up_b, jnp.transpose(down_w), down_b,
    )


def solution(mesh):
    placed = (
        P("seq", "blk", None),
        P("seq", "blk"),
        P("seq", "blk", None),
        P(),
        P(),
        P(),
        P(),
        P(),
        P(),
        P(),
        P(),
        P(),
        P(),
        P(),
        P(),
        P(),
    )
    chosen = chip_body if mesh.shape["seq"] == 4 and mesh.shape["blk"] == 8 else body
    return jax.shard_map(
        chosen,
        mesh=mesh,
        in_specs=placed,
        out_specs=(
            P("seq", "blk", None),
            P("seq", "blk", None),
            P("blk", None),
            P("blk"),
            P("blk"),
            P("blk", None),
            P("blk"),
            P("blk"),
            P("blk"),
            P("blk"),
            P("blk"),
            P("blk", None),
            P("blk"),
            P(None, "blk"),
            P("blk"),
        ),
        check_vma=False,
    )
```
